32 devices in a mesh: ctx: 8 (over z, core), wt: 4 (over y, x).
Axes of the slice: x: 2, y: 2, z: 4, core: 2. Of those that a mesh axis runs over, the one named last changes fastest.
Arguments:
- hidden: bfloat16 [4, 2048, 1536], P('wt', 'ctx'), may hold values from -6 to 6
- segment_ids: int32 [4, 2048], P('wt'), may hold values from 0 to 2, as said below
- routes: int32 [4, 2048, 6], P('wt', 'ctx'), may hold values from 0 to 63, all different within a row; in each aligned block of 256 rows (0 to 255, 256 to 511, ..., all dimensions but the last counted through in order) at most 40 rows name the same one
- gates: float32 [4, 2048, 6], P('wt', 'ctx'), may hold values from 0.08 to 0.25
- cotangent: bfloat16 [4, 2048, 1536], P('wt', 'ctx'), may hold values from -6 to 6
- norm_one_gain: bfloat16 [1536], P('wt'), may hold values from 0.25 to 1.75
- w_query: bfloat16 [1536, 1536], P('wt'), may hold values from -0.3125 to 0.3125
- w_key: bfloat16 [1536, 512], P('wt'), may hold values from -0.15625 to 0.15625
- w_value: bfloat16 [1536, 512], P('wt'), may hold values from -0.15625 to 0.15625
- w_out: bfloat16 [1536, 1536], P('wt'), may hold values from -0.75 to 0.75
- norm_two_gain: bfloat16 [1536], P('wt'), may hold values from 0.25 to 1.75
- shared_gate: bfloat16 [1536, 1024], P('wt'), may hold values from -0.15625 to 0.15625
- shared_up: bfloat16 [1536, 1024], P('wt'), may hold values from -0.15625 to 0.15625
- shared_down: bfloat16 [1024, 1536], P('wt'), may hold values from -0.1875 to 0.1875
- expert_gate: bfloat16 [64, 1536, 512], P('ctx', 'wt'), may hold values from -0.15625 to 0.15625
- expert_up: bfloat16 [64, 1536, 512], P('ctx', 'wt'), may hold values from -0.15625 to 0.15625
- expert_down: bfloat16 [64, 512, 1536], P('ctx', None, 'wt'), may hold values from -0.25 to 0.25
Outputs:
- output: bfloat16 [4, 2048, 1536], P('wt', 'ctx')
- grad_hidden: float32 [4, 2048, 1536], P('wt', 'ctx')
- grad_norm_one_gain: float32 [1536], P('wt')
- grad_w_query: float32 [1536, 1536], P('wt')
- grad_w_key: float32 [1536, 512], P('wt')
- grad_w_value: float32 [1536, 512], P('wt')
- grad_w_out: float32 [1536, 1536], P('wt')
- grad_norm_two_gain: float32 [1536], P('wt')
- grad_shared_gate: float32 [1536, 1024], P('wt')
- grad_shared_up: float32 [1536, 1024], P('wt')
- grad_shared_down: float32 [1024, 1536], P('wt')
- grad_expert_gate: float32 [64, 1536, 512], P('ctx', 'wt')
- grad_expert_up: float32 [64, 1536, 512], P('ctx', 'wt')
- grad_expert_down: float32 [64, 512, 1536], P('ctx', None, 'wt')
The draws below stay inside these ranges and needn't reach their ends.
Inputs may be any that keep to these rules, and one draw needn't show every extreme that they name: `routes`: each row names 6 different experts; of the 256 rows of one device at most 40 name any one expert. `segment_ids`: along each pack the ids never fall; id 0 covers the first 1 to 255 tokens, id 2 the last 1 to 255 tokens, id 1 all others.
All inputs are finite; a program needn't handle non-finite values.
Results may differ from the reference program's by a relative error of at most 0.024.
Values may be sent and summed in bfloat16 or wider, within the bound.
A program may use at most 384 MiB of HBM per device.

```python
import math
import jax
import jax.numpy as jnp
import numpy as np
from jax import lax

D = 1536
HEADS = 12
KV_HEADS = 4
HEAD_DIM = 128
EXPERTS = 64
EXPERT_FF = 512
SHARED_FF = 1024
TOPK = 6
TOK_DEV = 256
PACKS = 4
PACK_LEN = 2048
CAP = 40
N_CTX = 8


def draw_segment_ids(key, part):
    key = jax.random.fold_in(key, 11)
    first_key, last_key = jax.random.split(key)
    first = jax.random.randint(first_key, (PACKS, 1), 1, TOK_DEV, dtype=jnp.int32)
    last = jax.random.randint(last_key, (PACKS, 1), 1, TOK_DEV, dtype=jnp.int32)
    spots = jnp.arange(PACK_LEN, dtype=jnp.int32)[None, :]
    return (spots >= first).astype(jnp.int32) + (spots >= PACK_LEN - last).astype(jnp.int32)


def steps_of(key, shape, cuts, smallest, high):
    loudness = 1.0
    for position, blocks in cuts:
        heights = jax.random.uniform(jax.random.fold_in(jax.random.fold_in(key, 6), position), (blocks,), jnp.float32, smallest / len(cuts), high / len(cuts))
        loudness = loudness * jnp.repeat(jnp.exp(heights), shape[position] // blocks).reshape((-1,) + (1,) * (len(shape) - 1 - position))
    return loudness


def assign_block(key, own, number, rows, number_of, top, most, skew):
    order = jax.random.permutation(key, number_of)
    heavy_load, common = portions_of(number_of, rows * top, most, skew, True), portions_of(number_of, rows * top, most, skew, False)
    places = jnp.arange(number_of)

    def named(lengths, turn):
        used = int((lengths > 0).sum())
        fixed = max(1, used // 4)
        shifted = fixed + (places - fixed + turn * (used - fixed)) % max(1, number_of - fixed)
        return jnp.zeros((number_of,), jnp.int32).at[order[jnp.where(places < fixed, places, shifted)]].set(jnp.asarray(lengths, jnp.int32))

    lengths = jnp.where(number % 4 == 0, named(heavy_load, number // 4), named(common, number - number // 4 - 1))
    mixed = jax.random.permutation(jax.random.fold_in(own, 3), number_of)
    giver, sink = mixed[0:number_of // 2 * 2:2], mixed[1:number_of // 2 * 2:2]
    slack = jnp.minimum(lengths[giver] - 1, most - lengths[sink]) // 2
    slack = jnp.where((giver == order[0]) | (sink == order[0]) | (lengths[sink] == 0), 0, jnp.maximum(slack, 0))
    shifted = jax.random.randint(jax.random.fold_in(own, 4), (number_of // 2,), 0, 1 << 20) % (slack + 1)
    lengths = lengths.at[giver].add(-shifted).at[sink].add(shifted)
    items = jnp.searchsorted(jnp.cumsum(lengths), jnp.arange(rows * top), side="right").astype(jnp.int32)
    table = items.reshape(top, rows).T
    table = table[jax.random.permutation(jax.random.fold_in(own, 1), rows)]
    turn = jax.random.randint(jax.random.fold_in(own, 2), (rows, 1), 0, top)
    return jnp.take_along_axis(table, (jnp.arange(top)[None, :] + turn) % top, axis=1)


def portions_of(number_of, total, most, slope, full):
    weights = [(1 << 20) // math.isqrt(standing ** slope) + 1 for standing in range(1, number_of + 1)]
    largest = most if full else min(most, max(-(-total // number_of), total * weights[0] // sum(weights)))
    least = 1 if total - largest >= number_of - 1 else 0
    given, surplus = [largest] + [least] * (number_of - 1), total - largest - least * (number_of - 1)
    while surplus > 0:
        movable = [i for i in range(1, number_of) if given[i] < largest] or [i for i in range(1, number_of) if given[i] < most]
        mass, left = sum([weights[i] for i in movable]), surplus
        for i in movable:
            more = min(most - given[i], max(1, left * weights[i] // mass), surplus)
            given[i] = given[i] + more
            surplus = surplus - more
    return np.array(given)


def bell_draw(key, extent, scale, bound, pieces=(), kind=jnp.bfloat16):
    drawn = scale * jax.random.normal(key, extent, jnp.float32)
    if pieces:
        drawn = drawn * steps_of(key, extent, pieces, -0.22, 0.18)
    return jnp.clip(drawn, -bound, bound).astype(kind)


def setup_inputs(seed: int = 0) -> dict:
    key_of = jax.random.split(jax.random.key(seed), 18)
    hidden = bell_draw(key_of[0], (PACKS, PACK_LEN, D), 1.0, 6.0, ((0, 4), (1, 8)))
    segment_ids = draw_segment_ids(jax.random.fold_in(key_of[17], 71), 0)
    routes_keys = jax.random.split(jax.random.fold_in(key_of[2], 1), PACKS * PACK_LEN // TOK_DEV)
    routes_turns = jax.random.permutation(jax.random.fold_in(key_of[2], 3), PACKS * PACK_LEN // TOK_DEV)
    routes = jax.vmap(lambda own, number: assign_block(jax.random.fold_in(key_of[2], 2), own, number, TOK_DEV, EXPERTS, TOPK, CAP, 1))(routes_keys, routes_turns).reshape((PACKS, PACK_LEN, TOPK))
    gates = jnp.clip(0.08 + 0.17 * jax.random.uniform(key_of[3], (PACKS, PACK_LEN, TOPK), jnp.float32) ** steps_of(key_of[3], (PACKS, PACK_LEN, TOPK), ((0, 4), (1, 8)), -0.2, 0.2), 0.08, 0.25)
    cotangent = bell_draw(key_of[4], (PACKS, PACK_LEN, D), 1.0, 6.0, ((0, 4), (1, 8)))
    norm_one_gain = jnp.clip(1.0 + 0.15 * jax.random.normal(key_of[5], (D,), jnp.float32), 0.25, 1.75).astype(jnp.bfloat16)
    w_query = bell_draw(key_of[6], (D, HEADS * HEAD_DIM), (D // 4) ** -0.5, 0.3125, ((0, 4),))
    w_key = bell_draw(key_of[7], (D, KV_HEADS * HEAD_DIM), D ** -0.5, 0.15625, ((0, 4),))
    w_value = bell_draw(key_of[8], (D, KV_HEADS * HEAD_DIM), D ** -0.5, 0.15625, ((0, 4),))
    w_out = bell_draw(key_of[9], (HEADS * HEAD_DIM, D), 64 ** -0.5, 0.75, ((0, 4),))
    norm_two_gain = jnp.clip(1.0 + 0.15 * jax.random.normal(key_of[10], (D,), jnp.float32), 0.25, 1.75).astype(jnp.bfloat16)
    shared_gate = bell_draw(key_of[11], (D, SHARED_FF), D ** -0.5, 0.15625, ((0, 4),))
    shared_up = bell_draw(key_of[12], (D, SHARED_FF), D ** -0.5, 0.15625, ((0, 4),))
    shared_down = bell_draw(key_of[13], (SHARED_FF, D), SHARED_FF ** -0.5, 0.1875, ((0, 4),))
    expert_gate = bell_draw(key_of[14], (EXPERTS, D, EXPERT_FF), D ** -0.5, 0.15625, ((0, 8), (1, 4)))
    expert_up = bell_draw(key_of[15], (EXPERTS, D, EXPERT_FF), D ** -0.5, 0.15625, ((0, 8), (1, 4)))
    expert_down = bell_draw(key_of[16], (EXPERTS, EXPERT_FF, D), EXPERT_FF ** -0.5, 0.25, ((0, 8), (2, 4)))
    return dict(hidden=hidden, segment_ids=segment_ids, routes=routes, gates=gates, cotangent=cotangent, norm_one_gain=norm_one_gain, w_query=w_query, w_key=w_key, w_value=w_value, w_out=w_out, norm_two_gain=norm_two_gain, shared_gate=shared_gate, shared_up=shared_up, shared_down=shared_down, expert_gate=expert_gate, expert_up=expert_up, expert_down=expert_down)


@jax.custom_vjp
def low(v):
    return lax.optimization_barrier(v.astype(jnp.bfloat16)).astype(jnp.float32)

@jax.custom_vjp
def low_back(v):
    return v

def low_keep(v):
    return (low(v), None)

def low_pass(kept, grad):
    return (grad,)

def back_keep(v):
    return (v, None)

def back_low(kept, grad):
    return (low(grad),)
low.defvjp(low_keep, low_pass)
low_back.defvjp(back_keep, back_low)
epsilon = 1e-05
masked_value = -1e+30
highest = lax.Precision.HIGHEST

def inverse_rms(rows):
    return lax.rsqrt(lax.optimization_barrier(jnp.mean(rows * rows, axis=-1, keepdims=True)) + epsilon)

def product(left, right):
    return jnp.dot(left, right, precision=highest, preferred_element_type=jnp.float32)

def block_ranks(route_rows):
    flat_routes = route_rows.reshape(-1)
    onehot = (flat_routes[:, None] == jnp.arange(EXPERTS, dtype=jnp.int32)[None, :]).astype(jnp.int32)
    earlier = jnp.cumsum(onehot, axis=0) - onehot
    return lax.optimization_barrier(jnp.sum(earlier * onehot, axis=1))

def attention(queries, keys, values, segments):
    group = HEADS // KV_HEADS
    scale = HEAD_DIM ** (-0.5)
    width = math.gcd(PACK_LEN, 512)
    grouped = queries.reshape(PACK_LEN // width, width, KV_HEADS, group, HEAD_DIM)
    key_rows = keys.reshape(PACK_LEN, KV_HEADS, HEAD_DIM)
    value_rows = values.reshape(PACK_LEN, KV_HEADS, HEAD_DIM)
    positions = jnp.arange(PACK_LEN, dtype=jnp.int32)

    def one_block(block):
        query_block, query_pos, query_seg = block
        scores = jnp.einsum('qkgd,skd->kgqs', query_block, key_rows, precision=highest) * scale
        scores = low_back(scores)
        allowed = (positions[None, :] <= query_pos[:, None]) & (segments[None, :] == query_seg[:, None])
        scores = jnp.where(allowed[None, None], scores, masked_value)
        weights = low(jax.nn.softmax(scores, axis=-1))
        return jnp.einsum('kgqs,skd->qkgd', weights, value_rows, precision=highest)
    blocks = lax.map(jax.checkpoint(one_block), (grouped, positions.reshape(-1, width), segments.reshape(-1, width)))
    return blocks.reshape(PACK_LEN, HEADS * HEAD_DIM)

def pack_forward(weights, hidden, segments, routes, gates):
    gain_one, query_weight, key_weight, value_weight, out_weight, gain_two, gate_weight, up_weight, down_weight, experts_gate, experts_up, experts_down = weights
    normed = low(hidden * inverse_rms(hidden) * gain_one)
    queries = low_back(low(product(normed, query_weight)))
    keys = low_back(low(product(normed, key_weight)))
    values = low_back(low(product(normed, value_weight)))
    attended = low_back(low(attention(queries, keys, values, segments)))
    middle = hidden + low_back(product(attended, out_weight))
    normed_two = low(middle * inverse_rms(middle) * gain_two)
    shared_gate_part = low_back(product(normed_two, gate_weight))
    shared_up_part = low_back(product(normed_two, up_weight))
    shared_inner = low(jax.nn.silu(shared_gate_part) * shared_up_part)
    shared_result = low_back(product(shared_inner, down_weight))
    ranks = jax.vmap(block_ranks)(routes.reshape(N_CTX, TOK_DEV, TOPK)).reshape(-1)
    experts_flat = routes.reshape(-1)
    blocks_flat = jnp.arange(PACK_LEN * TOPK, dtype=jnp.int32) // (TOK_DEV * TOPK)
    bucket = N_CTX * CAP
    slots = experts_flat * bucket + blocks_flat * CAP + ranks
    owners = jnp.full((EXPERTS * bucket,), PACK_LEN, jnp.int32).at[slots].set(jnp.arange(PACK_LEN * TOPK, dtype=jnp.int32) // TOPK)
    padded = jnp.concatenate([normed_two, jnp.zeros((1, D), jnp.float32)], axis=0)
    dispatch = low_back(padded[owners]).reshape(EXPERTS, bucket, D)
    gate_part = low_back(jnp.einsum('ecd,edf->ecf', dispatch, experts_gate, precision=highest))
    up_part = low_back(jnp.einsum('ecd,edf->ecf', dispatch, experts_up, precision=highest))
    inner_rows = low(jax.nn.silu(gate_part) * up_part)
    result = low_back(low(jnp.einsum('ecf,efd->ecd', inner_rows, experts_down, precision=highest)))
    picked = result.reshape(EXPERTS * bucket, D)[slots].reshape(PACK_LEN, TOPK, D)
    routed = lax.optimization_barrier(jnp.sum(gates[:, :, None] * picked, axis=1))
    return middle + shared_result + routed

def reference(hidden, segment_ids, routes, gates, cotangent, norm_one_gain, w_query, w_key, w_value, w_out, norm_two_gain, shared_gate, shared_up, shared_down, expert_gate, expert_up, expert_down):
    weights = (norm_one_gain.astype(jnp.float32), w_query.astype(jnp.float32), w_key.astype(jnp.float32), w_value.astype(jnp.float32), w_out.astype(jnp.float32), norm_two_gain.astype(jnp.float32), shared_gate.astype(jnp.float32), shared_up.astype(jnp.float32), shared_down.astype(jnp.float32), expert_gate.astype(jnp.float32), expert_up.astype(jnp.float32), expert_down.astype(jnp.float32))
    inputs = hidden.astype(jnp.float32)
    gate_rows = gates.astype(jnp.float32)

    def whole(weights, inputs):

        def one_pack(carry, pack):
            pack_hidden, pack_segments, pack_routes, pack_gates = pack
            return (carry, jax.checkpoint(pack_forward)(weights, pack_hidden, pack_segments, pack_routes, pack_gates))
        _, outputs = lax.scan(one_pack, jnp.zeros((), jnp.float32), (inputs, segment_ids, routes, gate_rows))
        return outputs
    outputs, pullback = jax.vjp(whole, weights, inputs)
    weight_grads, input_grad = pullback(cotangent.astype(jnp.float32))
    grad_gain_one, grad_query, grad_key, grad_value, grad_out, grad_gain_two, grad_gate, grad_up, grad_down, grad_experts_gate, grad_experts_up, grad_experts_down = weight_grads
    return (outputs.astype(jnp.bfloat16), input_grad, grad_gain_one, grad_query, grad_key, grad_value, grad_out, grad_gain_two, grad_gate, grad_up, grad_down, grad_experts_gate, grad_experts_up, grad_experts_down)
```

```python
import functools
import math

import jax
import jax.numpy as jnp
from jax import lax
from jax.experimental import pallas as pl
from jax.experimental.pallas import tpu as pltpu
from jax.sharding import PartitionSpec as P

HEADS = 12
KV_HEADS = 4
HEAD_DIM = 128
EXPERTS = 64
TOPK = 6
CAP = 40


epsilon = 1e-05
masked_value = -1e30


def inverse_rms(rows):
    return lax.rsqrt(jnp.mean(rows * rows, axis=-1, keepdims=True) + epsilon)


def silu_slope(gate_part):
    sigmoid = jax.nn.sigmoid(gate_part)
    return sigmoid * (1.0 + gate_part * (1.0 - sigmoid))


def block_mask(begin, width, query_pos, query_seg, seg_all):
    key_pos = begin + jnp.arange(width, dtype=jnp.int32)
    key_seg = lax.dynamic_slice_in_dim(seg_all, begin, width)
    return (key_pos[None, :] <= query_pos[:, None]) & (key_seg[None, :] == query_seg[:, None])


def forward_piece(state, piece, grouped, query_pos, query_seg, seg_all, last_query):
    piece_keys, piece_values = piece
    count = piece_keys.shape[0]
    width = math.gcd(count, 512)
    scale = HEAD_DIM ** (-0.5)

    def forward_inner(carry, index):
        begin = index * width

        def forward_compute(current):
            best, total, accum = current
            block_keys = lax.dynamic_slice_in_dim(piece_keys, begin, width).reshape(
                width, KV_HEADS, HEAD_DIM
            )
            block_values = lax.dynamic_slice_in_dim(piece_values, begin, width).reshape(
                width, KV_HEADS, HEAD_DIM
            )
            allowed = block_mask(begin, width, query_pos, query_seg, seg_all)
            scores = (
                jnp.einsum(
                    "qkgd,skd->kgqs", grouped, block_keys, preferred_element_type=jnp.float32
                )
                * scale
            )
            scores = jnp.where(allowed[None, None], scores, masked_value)
            newest = jnp.maximum(best, jnp.max(scores, axis=-1))
            factor = jnp.exp(best - newest)
            weights = jnp.exp(scores - newest[..., None])
            total = total * factor + jnp.sum(weights, axis=-1)
            accum = accum * factor[..., None] + jnp.einsum(
                "kgqs,skd->kgqd",
                weights.astype(jnp.bfloat16),
                block_values,
                preferred_element_type=jnp.float32,
            )
            return (newest, total, accum)

        def forward_keep(current):
            return current

        return (lax.cond(begin <= last_query, forward_compute, forward_keep, carry), None)

    state, _ = lax.scan(forward_inner, state, jnp.arange(count // width, dtype=jnp.int32))
    return state


def backward_piece(
    state,
    piece,
    grouped,
    grad_grouped,
    log_totals,
    deltas,
    query_pos,
    query_seg,
    seg_all,
    last_query,
):
    piece_keys, piece_values = piece
    count = piece_keys.shape[0]
    width = math.gcd(count, 512)
    scale = HEAD_DIM ** (-0.5)
    grad_queries, keys_grad, values_grad = state
    kv_width = piece_keys.shape[1]

    def backward_inner(carry, index):
        begin = index * width

        def backward_compute(current):
            block_keys = lax.dynamic_slice_in_dim(piece_keys, begin, width).reshape(
                width, KV_HEADS, HEAD_DIM
            )
            block_values = lax.dynamic_slice_in_dim(piece_values, begin, width).reshape(
                width, KV_HEADS, HEAD_DIM
            )
            allowed = block_mask(begin, width, query_pos, query_seg, seg_all)
            scores = (
                jnp.einsum(
                    "qkgd,skd->kgqs", grouped, block_keys, preferred_element_type=jnp.float32
                )
                * scale
            )
            scores = jnp.where(allowed[None, None], scores, masked_value)
            probs = jnp.exp(scores - log_totals[..., None])
            grad_probs = jnp.einsum(
                "qkgd,skd->kgqs", grad_grouped, block_values, preferred_element_type=jnp.float32
            )
            grad_scores = (probs * (grad_probs - deltas[..., None])).astype(jnp.bfloat16)
            updated = (
                current
                + jnp.einsum(
                    "kgqs,skd->qkgd", grad_scores, block_keys, preferred_element_type=jnp.float32
                )
                * scale
            )
            key_term = (
                jnp.einsum(
                    "kgqs,qkgd->skd", grad_scores, grouped, preferred_element_type=jnp.float32
                )
                * scale
            )
            value_term = jnp.einsum(
                "kgqs,qkgd->skd",
                probs.astype(jnp.bfloat16),
                grad_grouped,
                preferred_element_type=jnp.float32,
            )
            return (updated, key_term.reshape(width, kv_width), value_term.reshape(width, kv_width))

        def backward_keep(current):
            empty = jnp.zeros((width, kv_width), jnp.float32)
            return (current, empty, empty)

        updated, key_term, value_term = lax.cond(
            begin <= last_query, backward_compute, backward_keep, carry
        )
        return (updated, (key_term, value_term))

    grad_queries, (key_terms, value_terms) = lax.scan(
        backward_inner, grad_queries, jnp.arange(count // width, dtype=jnp.int32)
    )
    keys_grad = key_terms.reshape(count, -1)
    values_grad = value_terms.reshape(count, -1)
    return (grad_queries, keys_grad, values_grad)


MESH = pl.DeviceIdType.MESH
WIDE = 56 * 2**20


def flip(index, distance):
    result = index
    bit = 1
    while bit <= distance:
        if distance // bit % 2:
            result = result + bit - 2 * bit * (index // bit % 2)
        bit *= 2
    return result


def remote(src, dst, send_sem, recv_sem, device):
    return pltpu.make_async_remote_copy(
        src_ref=src,
        dst_ref=dst,
        send_sem=send_sem,
        recv_sem=recv_sem,
        device_id=device,
        device_id_type=MESH,
    )


def greet(devices):
    barrier = pltpu.get_barrier_semaphore()
    for device in devices:
        pl.semaphore_signal(barrier, inc=1, device_id=device, device_id_type=MESH)
    pl.semaphore_wait(barrier, len(devices))


class Slabs:
    def __init__(self, count, sources, targets, here, send, recv, near_send, near_recv):
        self.c, self.w = lax.axis_index("ctx"), lax.axis_index("wt")
        self.core = lax.rem(self.c, 2)
        self.near = (flip(self.c, 1), self.w)
        self.peers = [flip(self.w, d) for d in range(1, count)]
        self.pairs = list(zip(sources, targets))
        self.here, self.send, self.recv = here, send, recv
        self.near_send, self.near_recv = near_send, near_recv

    def devices(self):
        return [(self.c, p) for p in self.peers]

    def half(self, source, core):
        rows = source.shape[0] // 2
        return pl.ds(pl.multiple_of(core * rows, 16), rows)

    def push(self, i, s):
        source, target = self.pairs[s]
        part = self.half(source, self.core)
        return remote(
            source.at[part], target.at[self.w, part], self.send.at[s, i], self.recv.at[s, i], (self.c, self.peers[i])
        )

    def arrival(self, i, s):
        source, target = self.pairs[s]
        spot = target.at[self.peers[i], self.half(source, self.core)]
        return remote(spot, spot, self.send.at[s, i], self.recv.at[s, i], (self.c, self.peers[i]))

    def hand(self, i, s, core):
        source, target = self.pairs[s]
        spot = target.at[self.peers[i], self.half(source, core)]
        return remote(spot, spot, self.near_send.at[s, i], self.near_recv.at[s, i], self.near)

    def keep(self, s):
        source, target = self.pairs[s]
        return pltpu.make_async_copy(source, target.at[self.w], self.here.at[s])

    def every(self):
        return [(i, s) for s in range(len(self.pairs)) for i in range(len(self.peers))]

    def start(self):
        for i, s in self.every():
            self.push(i, s).start()
        for s in range(len(self.pairs)):
            self.keep(s).start()

    def relay(self):
        for i, s in self.every():
            self.arrival(i, s).wait_recv()
            self.hand(i, s, self.core).start()

    def finish(self):
        for i, s in self.every():
            self.hand(i, s, 1 - self.core).wait_recv()
            self.hand(i, s, self.core).wait_send()
            self.push(i, s).wait_send()
        for s in range(len(self.pairs)):
            self.keep(s).wait()

    @staticmethod
    def scratch(slabs, count):
        dma = pltpu.SemaphoreType.DMA
        return [dma((slabs,))] + [dma((slabs, count - 1))] * 4

    @staticmethod
    def shapes(slabs, count):
        return tuple(jax.ShapeDtypeStruct((count,) + s.shape, s.dtype) for s in slabs)


def weights_kernel(count, slabs, *refs):
    sources, targets, zero_ref = refs[:slabs], refs[slabs : 2 * slabs], refs[2 * slabs]
    plan = Slabs(count, sources, targets, *refs[2 * slabs + 1 :])
    greet(plan.devices() + [plan.near])
    plan.start()
    zero_ref[...] = jnp.zeros_like(zero_ref)
    plan.relay()
    plan.finish()


def gather_weights(slabs):
    count = lax.axis_size("wt")
    return pl.pallas_call(
        functools.partial(weights_kernel, count, len(slabs)),
        out_shape=Slabs.shapes(slabs, count) + (jax.ShapeDtypeStruct((8, 128), jnp.int32),),
        in_specs=[pl.BlockSpec(memory_space=pl.ANY)] * len(slabs),
        out_specs=(pl.BlockSpec(memory_space=pl.ANY),) * len(slabs)
        + (pl.BlockSpec(memory_space=pltpu.VMEM),),
        scratch_shapes=Slabs.scratch(len(slabs), count),
        compiler_params=pltpu.CompilerParams(
            collective_id=1, has_side_effects=True, vmem_limit_bytes=WIDE
        ),
        cost_estimate=pl.CostEstimate(flops=0, bytes_accessed=150_000_000, transcendentals=0),
        name="gather_weights",
    )(*slabs)


def gather_kernel(chips, downward, paired, count, slabs, rows_ref, *refs):
    sources, out_ref, targets = refs[:slabs], refs[slabs], refs[slabs + 1 : 2 * slabs + 1]
    here, up_send, up_recv, down_send, down_recv, pair_send, pair_recv, near_send, near_recv = refs[
        2 * slabs + 1 : 2 * slabs + 10
    ]
    plan = Slabs(count, sources, targets, *refs[2 * slabs + 10 :]) if slabs else None
    c, w = lax.axis_index("ctx"), lax.axis_index("wt")
    z = c // 2
    core = lax.rem(c, 2)
    side = lax.rem(w, 2) if paired else 0
    near, partner = (flip(c, 1), w), (c, flip(w, 1))
    above = (lax.rem(c + 2, 2 * chips), w)
    below = (lax.rem(c + 2 * chips - 2, 2 * chips), w)
    greet([near, above, below] + ([partner] if paired else []) + (plan.devices() if plan else []))

    def spot(chip, which, parity):
        return out_ref.at[chip, which, parity]

    def lift(chip, source):
        return remote(source, spot(chip, side, core), up_send.at[chip], up_recv.at[chip], above)

    def drop(chip, source):
        return remote(source, spot(chip, side, core), down_send.at[chip], down_recv.at[chip], below)

    def give(chip, source):
        return remote(source, spot(chip, side, core), pair_send.at[chip], pair_recv.at[chip], partner)

    def taken(chip):
        return remote(
            spot(chip, 1 - side, core), spot(chip, 1 - side, core), pair_send.at[chip], pair_recv.at[chip], partner
        )

    def hand(chip, which, source):
        return remote(source, spot(chip, which, core), near_send.at[chip, which], near_recv.at[chip, which], near)

    def handed(chip, which):
        there = spot(chip, which, 1 - core)
        return remote(there, there, near_send.at[chip, which], near_recv.at[chip, which], near)

    def settle_pair(chip):
        taken(chip).wait_recv()
        hand(chip, 1 - side, spot(chip, 1 - side, core)).start()

    keep = pltpu.make_async_copy(rows_ref, spot(z, side, core), here)
    keep.start()
    pl.when(z < chips - 1)(lambda: lift(z, rows_ref).start())
    if downward:
        pl.when(z > 0)(lambda: drop(z, rows_ref).start())
    if paired:
        give(z, rows_ref).start()
    hand(z, side, rows_ref).start()
    if plan:
        plan.start()
    for step in range(1, chips):
        low, high = z - step, z + step

        @pl.when(low >= 0)
        def _():
            lift(low, spot(low, side, core)).wait_recv()
            pl.when(z < chips - 1)(lambda: lift(low, spot(low, side, core)).start())
            if paired:
                give(low, spot(low, side, core)).start()
            hand(low, side, spot(low, side, core)).start()

        if downward:

            @pl.when(high < chips)
            def _():
                drop(high, spot(high, side, core)).wait_recv()
                pl.when(z > 0)(lambda: drop(high, spot(high, side, core)).start())
                if paired:
                    give(high, spot(high, side, core)).start()
                hand(high, side, spot(high, side, core)).start()

        if paired:
            if step == 1:
                settle_pair(z)
            else:
                pl.when(z - step + 1 >= 0)(lambda: settle_pair(z - step + 1))
                pl.when(z + step - 1 < chips)(lambda: settle_pair(z + step - 1))
    if paired:
        pl.when(z - chips + 1 >= 0)(lambda: settle_pair(z - chips + 1))
        pl.when(z + chips - 1 < chips)(lambda: settle_pair(z + chips - 1))
    keep.wait()
    if plan:
        plan.relay()
        plan.finish()

    def finish(chip):
        here_now = spot(chip, side, core)
        pl.when((z < chips - 1) & (chip <= z))(lambda: lift(chip, here_now).wait_send())
        if downward:
            pl.when((z > 0) & (chip >= z))(lambda: drop(chip, here_now).wait_send())
        if paired:
            give(chip, here_now).wait_send()
            for which in range(2):
                hand(chip, which, spot(chip, which, core)).wait_send()
                handed(chip, which).wait_recv()
        else:
            hand(chip, side, here_now).wait_send()
            handed(chip, side).wait_recv()

    for chip in range(chips):
        if downward:
            finish(chip)
        else:
            pl.when(chip <= z)(lambda: finish(chip))


def gather_rows(rows, collective_id, downward, paired, name, slabs=()):
    chips = lax.axis_size("ctx") // 2
    count = lax.axis_size("wt")
    line = pltpu.SemaphoreType.DMA((chips,))
    both = pltpu.SemaphoreType.DMA((chips, 2))
    shape = jax.ShapeDtypeStruct((chips, 2 if paired else 1, 2) + rows.shape, rows.dtype)
    return pl.pallas_call(
        functools.partial(gather_kernel, chips, downward, paired, count, len(slabs)),
        out_shape=(shape,) + Slabs.shapes(slabs, count),
        in_specs=[pl.BlockSpec(memory_space=pl.ANY)] * (1 + len(slabs)),
        out_specs=(pl.BlockSpec(memory_space=pl.ANY),) * (1 + len(slabs)),
        scratch_shapes=[pltpu.SemaphoreType.DMA]
        + [line] * 6
        + [both] * 2
        + (Slabs.scratch(len(slabs), count) if slabs else []),
        compiler_params=pltpu.CompilerParams(
            collective_id=collective_id, has_side_effects=True, vmem_limit_bytes=WIDE
        ),
        cost_estimate=pl.CostEstimate(flops=0, bytes_accessed=250_000_000, transcendentals=0),
        name=name,
    )(rows, *slabs)


def scatter_kernel(chips, upward, paired, pieces, partial_ref, out_ref, own, sib, mate, low_in, high_in, load, near_send, near_recv, pair_send, pair_recv, up_send, up_recv, down_send, down_recv):
    c, w = lax.axis_index("ctx"), lax.axis_index("wt")
    z = c // 2
    core = lax.rem(c, 2)
    side = lax.rem(w, 2) if paired else 0
    sides = 2 if paired else 1
    near, partner = (flip(c, 1), w), (c, flip(w, 1))
    above = (lax.rem(c + 2, 2 * chips), w)
    below = (lax.rem(c + 2 * chips - 2, 2 * chips), w)
    rows = own.shape[2] // pieces
    greet([near, above, below] + ([partner] if paired else []))
    order = []
    for i in range(chips // 2):
        order += [chips - 1 - i, i]
    if chips % 2:
        order.append(chips // 2)
    if not upward:
        order = list(range(chips))

    def wanted(chip, action):
        if upward:
            action()
        else:
            pl.when(chip <= z)(action)

    def fetch(chip, which):
        return pltpu.make_async_copy(
            partial_ref.at[chip, which, core], own.at[chip, which], load.at[chip, which]
        )

    def hand(chip, which):
        return remote(
            partial_ref.at[chip, which, 1 - core],
            sib.at[chip, which],
            near_send.at[chip, which],
            near_recv.at[chip, which],
            near,
        )

    def cut(piece):
        return pl.ds(piece * rows, rows)

    def give(chip, piece):
        return remote(
            own.at[chip, 1 - side, cut(piece)],
            mate.at[chip, cut(piece)],
            pair_send.at[chip, piece],
            pair_recv.at[chip, piece],
            partner,
        )

    def lift(chip, piece):
        return remote(
            own.at[chip, side, cut(piece)],
            low_in.at[chip, cut(piece)],
            up_send.at[chip, piece],
            up_recv.at[chip, piece],
            above,
        )

    def drop(chip, piece):
        return remote(
            own.at[chip, side, cut(piece)],
            high_in.at[chip, cut(piece)],
            down_send.at[chip, piece],
            down_recv.at[chip, piece],
            below,
        )

    def add_into(chip, which, piece, other):
        spot = own.at[chip, which, cut(piece)]
        spot[...] = (spot[...].astype(jnp.float32) + other[...].astype(jnp.float32)).astype(spot.dtype)

    for chip in order:

        def begin(chip=chip):
            for which in range(sides):
                hand(chip, which).start()
                fetch(chip, which).start()

        wanted(chip, begin)

    def meet(chip):
        for which in range(sides):
            fetch(chip, which).wait()
            hand(chip, which).wait_recv()
        for piece in range(pieces):
            if paired:
                add_into(chip, 1 - side, piece, sib.at[chip, 1 - side, cut(piece)])
                give(chip, piece).start()
            add_into(chip, side, piece, sib.at[chip, side, cut(piece)])

    def travel(chip):
        for piece in range(pieces):
            if paired:
                give(chip, piece).wait_recv()
                add_into(chip, side, piece, mate.at[chip, cut(piece)])
            if upward:

                @pl.when(z < chip)
                def _():
                    @pl.when(z > 0)
                    def _():
                        lift(chip, piece).wait_recv()
                        add_into(chip, side, piece, low_in.at[chip, cut(piece)])

                    lift(chip, piece).start()

            @pl.when(z > chip)
            def _():
                @pl.when(z < chips - 1)
                def _():
                    drop(chip, piece).wait_recv()
                    add_into(chip, side, piece, high_in.at[chip, cut(piece)])

                drop(chip, piece).start()

    for i, chip in enumerate(order):
        wanted(chip, lambda: meet(chip))
        if i >= 1:
            wanted(order[i - 1], lambda: travel(order[i - 1]))
    wanted(order[-1], lambda: travel(order[-1]))
    for piece in range(pieces):
        out_ref[cut(piece), :] = own.at[z, side, cut(piece)][...].astype(jnp.float32)
    for piece in range(pieces):
        if upward:

            @pl.when(z > 0)
            def _():
                lift(z, piece).wait_recv()
                out_ref[cut(piece), :] += low_in.at[z, cut(piece)][...].astype(jnp.float32)

        @pl.when(z < chips - 1)
        def _():
            drop(z, piece).wait_recv()
            out_ref[cut(piece), :] += high_in.at[z, cut(piece)][...].astype(jnp.float32)

    def finish(chip):
        for which in range(sides):
            hand(chip, which).wait_send()
        for piece in range(pieces):
            if paired:
                give(chip, piece).wait_send()
            if upward:
                pl.when(z < chip)(lambda: lift(chip, piece).wait_send())
            pl.when(z > chip)(lambda: drop(chip, piece).wait_send())

    for chip in order:
        wanted(chip, lambda: finish(chip))


def scatter_rows(partial, collective_id, upward, paired, name):
    chips, sides, _, tokens, width = partial.shape
    pieces = 2
    dma = pltpu.SemaphoreType.DMA
    block = (tokens, width)
    return pl.pallas_call(
        functools.partial(scatter_kernel, chips, upward, paired, pieces),
        out_shape=jax.ShapeDtypeStruct(block, jnp.float32),
        in_specs=[pl.BlockSpec(memory_space=pl.ANY)],
        out_specs=pl.BlockSpec(memory_space=pltpu.VMEM),
        scratch_shapes=[
            pltpu.VMEM((chips, sides) + block, jnp.bfloat16),
            pltpu.VMEM((chips, sides) + block, jnp.bfloat16),
            pltpu.VMEM((chips if paired else 1,) + block, jnp.bfloat16),
            pltpu.VMEM((chips if upward else 1,) + block, jnp.bfloat16),
            pltpu.VMEM((chips,) + block, jnp.bfloat16),
            dma((chips, 2)),
            dma((chips, 2)),
            dma((chips, 2)),
        ]
        + [dma((chips, pieces))] * 6,
        compiler_params=pltpu.CompilerParams(
            collective_id=collective_id, has_side_effects=True, vmem_limit_bytes=WIDE
        ),
        cost_estimate=pl.CostEstimate(
            flops=0, bytes_accessed=300_000_000 if paired else 150_000_000, transcendentals=0
        ),
        name=name,
    )(partial)


def pick_kernel(scaled, slot_ref, gate_ref, rows_ref, out_ref, scale_ref=None):
    local, depth = out_ref.shape[2], out_ref.shape[3]
    tokens = rows_ref.shape[3]
    place = lax.broadcasted_iota(jnp.int32, (depth, tokens), 0)
    total, weight = None, None
    for core in range(2):
        span = slice(core * tokens, (core + 1) * tokens)
        chosen = [slot_ref[0, 0, e : e + 1, span] == place for e in range(local)]
        ones = jnp.concatenate([c.astype(jnp.float32) for c in chosen], axis=0).astype(jnp.bfloat16)
        rows = rows_ref[0, core, 0] if scaled else rows_ref[0, 0, core]
        term = jnp.dot(ones, rows, preferred_element_type=jnp.float32)
        total = term if total is None else total + term
        if scaled:
            gates = jnp.concatenate(
                [
                    jnp.sum(jnp.where(c, gate_ref[0, 0, e : e + 1, span], 0.0), axis=1, keepdims=True)
                    for e, c in enumerate(chosen)
                ],
                axis=0,
            )
            weight = gates if weight is None else weight + gates
    if scaled:
        total = total * weight
        scale_ref[0, 0] = jnp.broadcast_to(weight, (local * depth, 128)).reshape(local, depth, 128)
    out_ref[0, 0] = total.astype(jnp.bfloat16).reshape(local, depth, total.shape[1])


def pick_rows(rows, slots, gates, scaled):
    chips, sides, local, both = slots.shape
    tokens, width = both // 2, rows.shape[4]
    depth = 2 * CAP
    table = pl.BlockSpec((1, 1, local, both), lambda z, s: (z, s, 0, 0))
    shapes = [jax.ShapeDtypeStruct((chips, sides, local, depth, width), jnp.bfloat16)]
    specs = [pl.BlockSpec((1, 1, local, depth, width), lambda z, s: (z, s, 0, 0, 0))]
    if scaled:
        shapes.append(jax.ShapeDtypeStruct((chips, sides, local, depth, 128), jnp.float32))
        specs.append(pl.BlockSpec((1, 1, local, depth, 128), lambda z, s: (z, s, 0, 0, 0)))
        source = pl.BlockSpec((1, 2, 1, tokens, width), lambda z, s: (z, 0, s, 0, 0))
    else:
        source = pl.BlockSpec((1, 1, 2, tokens, width), lambda z, s: (z, s, 0, 0, 0))
    return pl.pallas_call(
        functools.partial(pick_kernel, scaled),
        grid=(chips, sides),
        out_shape=shapes,
        in_specs=[table, table, source],
        out_specs=specs,
        compiler_params=pltpu.CompilerParams(vmem_limit_bytes=WIDE),
        cost_estimate=pl.CostEstimate(
            flops=4 * chips * sides * local * depth * both * width // 2,
            bytes_accessed=40_000_000,
            transcendentals=0,
        ),
        name="pick_grads" if scaled else "pick_tokens",
    )(slots, gates, rows)


def spread_kernel(slot_ref, rows_ref, out_ref):
    local, depth, width = rows_ref.shape[2:]
    tokens = out_ref.shape[3]
    place = lax.broadcasted_iota(jnp.int32, (depth, tokens), 0)
    rows = rows_ref[0, 0].reshape(local * depth, width)
    for core in range(2):
        span = slice(core * tokens, (core + 1) * tokens)
        ones = jnp.concatenate(
            [(slot_ref[0, 0, e : e + 1, span] == place).astype(jnp.float32) for e in range(local)], axis=0
        ).astype(jnp.bfloat16)
        out_ref[0, 0, core] = lax.dot_general(
            ones, rows, (((0,), (0,)), ((), ())), preferred_element_type=jnp.float32
        ).astype(jnp.bfloat16)


def spread_rows(rows, slots, name):
    chips, sides, local, both = slots.shape
    depth, width = rows.shape[3:]
    tokens = both // 2
    return pl.pallas_call(
        spread_kernel,
        grid=(chips, sides),
        out_shape=jax.ShapeDtypeStruct((chips, sides, 2, tokens, width), jnp.bfloat16),
        in_specs=[
            pl.BlockSpec((1, 1, local, both), lambda z, s: (z, s, 0, 0)),
            pl.BlockSpec((1, 1, local, depth, width), lambda z, s: (z, s, 0, 0, 0)),
        ],
        out_specs=pl.BlockSpec((1, 1, 2, tokens, width), lambda z, s: (z, s, 0, 0, 0)),
        compiler_params=pltpu.CompilerParams(vmem_limit_bytes=WIDE),
        cost_estimate=pl.CostEstimate(
            flops=2 * chips * sides * local * depth * both * width,
            bytes_accessed=40_000_000,
            transcendentals=0,
        ),
        name=name,
    )(slots, rows)


def expert_kernel(blocks, x_ref, g_ref, scale_ref, *refs):
    gate_refs, up_refs, down_refs = refs[:blocks], refs[blocks : 2 * blocks], refs[2 * blocks : 3 * blocks]
    result_ref, back_ref, grad_gate_ref, grad_up_ref, grad_down_ref = refs[3 * blocks :]
    w = lax.axis_index("wt")
    chips, sides, _, depth, width = x_ref.shape
    rows = chips * sides * depth
    part = gate_refs[0].shape[1]
    nn, nt, tn = (((1,), (0,)), ((), ())), (((1,), (1,)), ((), ())), (((0,), (0,)), ((), ()))

    def dot(a, b, dims):
        return lax.dot_general(a, b, dims, preferred_element_type=jnp.float32)

    def columns(ref, q):
        if blocks == 1:
            return ref.at[:, :, 0]
        span = pl.ds(pl.multiple_of(flip(w, q) * part, 128), part)
        return ref.at[:, :, 0, :, span]

    def piece(ref, q):
        return columns(ref, q)[...].reshape(rows, part)

    gate, up, grad_inner = None, None, None
    for q in range(blocks):
        x = piece(x_ref, q)
        more_gate, more_up = dot(x, gate_refs[q][0], nn), dot(x, up_refs[q][0], nn)
        gate, up = (more_gate, more_up) if q == 0 else (gate + more_gate, up + more_up)
    for q in range(blocks):
        more = dot(piece(g_ref, q), down_refs[q][0], nt)
        grad_inner = more if q == 0 else grad_inner + more
    sigmoid = jax.nn.sigmoid(gate)
    activated = gate * sigmoid
    inner = (activated * up).astype(jnp.bfloat16)
    grad_gate = (grad_inner * up * (sigmoid * (1.0 + gate * (1.0 - sigmoid)))).astype(jnp.bfloat16)
    grad_up = (grad_inner * activated).astype(jnp.bfloat16)
    scale = scale_ref[...].reshape(rows, 128)[:, :1]
    for q in range(blocks):
        result = dot(inner, down_refs[q][0], nn) * scale
        columns(result_ref, q)[...] = result.astype(jnp.bfloat16).reshape(chips, sides, depth, part)
        back = dot(grad_gate, gate_refs[q][0], nt) + dot(grad_up, up_refs[q][0], nt)
        columns(back_ref, q)[...] = back.astype(jnp.bfloat16).reshape(chips, sides, depth, part)
        grad_down_ref[q, 0] = dot(inner, piece(g_ref, q), tn).astype(jnp.bfloat16)
        x = piece(x_ref, q)
        grad_gate_ref[q, 0] = dot(x, grad_gate, tn).astype(jnp.bfloat16)
        grad_up_ref[q, 0] = dot(x, grad_up, tn).astype(jnp.bfloat16)


def run_experts(x, g, scale, gates, ups, downs):
    chips, sides, local, depth, width = x.shape
    blocks = len(gates)
    part, inner = gates[0].shape[1:]
    large = chips * sides * depth > 1024
    rows = pl.BlockSpec((chips, sides, 1, depth, width), lambda e: (0, 0, e, 0, 0))
    sources = pl.BlockSpec(
        (chips, sides, 1, depth, width),
        lambda e: (0, 0, e, 0, 0),
        pipeline_mode=pl.Buffered(1 if large else 2),
    )
    scales = pl.BlockSpec((chips, sides, 1, depth, 128), lambda e: (0, 0, e, 0, 0))
    tall = pl.BlockSpec((1, part, inner), lambda e: (e, 0, 0))
    flat = pl.BlockSpec((1, inner, part), lambda e: (e, 0, 0))
    tall_out = pl.BlockSpec((blocks, 1, part, inner), lambda e: (0, e, 0, 0))
    flat_out = pl.BlockSpec((blocks, 1, inner, part), lambda e: (0, e, 0, 0))
    total = chips * sides * local * depth
    return pl.pallas_call(
        functools.partial(expert_kernel, blocks),
        grid=(local,),
        out_shape=(
            jax.ShapeDtypeStruct(x.shape, jnp.bfloat16),
            jax.ShapeDtypeStruct(x.shape, jnp.bfloat16),
            jax.ShapeDtypeStruct((blocks, local, part, inner), jnp.bfloat16),
            jax.ShapeDtypeStruct((blocks, local, part, inner), jnp.bfloat16),
            jax.ShapeDtypeStruct((blocks, local, inner, part), jnp.bfloat16),
        ),
        in_specs=[sources, sources, scales] + [tall] * (2 * blocks) + [flat] * blocks,
        out_specs=(rows, rows, tall_out, tall_out, flat_out),
        compiler_params=pltpu.CompilerParams(vmem_limit_bytes=60 * 2**20),
        cost_estimate=pl.CostEstimate(
            flops=18 * total * width * inner, bytes_accessed=70_000_000, transcendentals=total * inner
        ),
        name="experts",
    )(x, g, scale, *gates, *ups, *downs)


def swap_pairs(value, axis, distance):
    count = lax.axis_size(axis)
    return lax.ppermute(value, axis, [(i, i ^ distance) for i in range(count)])


def own_and_other(stacked, mine):
    return (
        lax.dynamic_index_in_dim(stacked, mine, 0, keepdims=False),
        lax.dynamic_index_in_dim(stacked, 1 - mine, 0, keepdims=False),
    )


def in_order(own, other, mine):
    first = jnp.where(mine == 0, own, other)
    second = jnp.where(mine == 0, other, own)
    return jnp.stack([first, second])


def collect_expert(shard, side, pairs):
    local = shard.shape[0]
    kept, given = own_and_other(shard.reshape((2, local // 2) + shard.shape[1:]), side)
    blocks = [kept, swap_pairs(given, "wt", 1)]
    for d in range(1, pairs):
        blocks += [swap_pairs(blocks[0], "wt", 2 * d), swap_pairs(blocks[1], "wt", 2 * d)]
    return blocks


def settle_blocks(blocks, index, axis):
    stacked = jnp.stack(blocks)
    return jnp.concatenate(
        [
            lax.dynamic_index_in_dim(stacked, jnp.bitwise_xor(j, index), 0, False)
            for j in range(len(blocks))
        ],
        axis=axis,
    )


def split_blocks(whole, index, count, axis):
    parts = jnp.stack(jnp.split(whole, count, axis=axis))
    return jnp.stack(
        [
            lax.dynamic_index_in_dim(parts, jnp.bitwise_xor(q, index), 0, False)
            for q in range(count)
        ]
    )


def scatter_expert(grads, side, pairs):
    total = grads[:2].astype(jnp.float32)
    for d in range(1, pairs):
        total = total + swap_pairs(grads[2 * d : 2 * d + 2], "wt", 2 * d).astype(jnp.float32)
    other = swap_pairs(total[1].astype(jnp.bfloat16), "wt", 1).astype(jnp.float32)
    both = in_order(total[0], other, side)
    return both.reshape((-1,) + both.shape[2:])


def gather_side(rows, side):
    both = in_order(rows, swap_pairs(rows, "wt", 1), side)
    return lax.all_gather(both, "ctx", axis=0)


def body(
    hidden,
    segment_ids,
    routes,
    gates,
    cotangent,
    norm_one_gain,
    w_query,
    w_key,
    w_value,
    w_out,
    norm_two_gain,
    shared_gate,
    shared_up,
    shared_down,
    expert_gate,
    expert_up,
    expert_down,
):
    wt_index = lax.axis_index("wt")
    wt_count = lax.axis_size("wt")
    ctx_count = lax.axis_size("ctx")
    chips = ctx_count // 2
    pairs = wt_count // 2
    tokens, width_model = hidden.shape[1:]
    wide, kv_width = w_query.shape[1], w_key.shape[1]
    shared_width = shared_gate.shape[1]
    slab, gains, zero = gather_weights(
        (
            jnp.concatenate([w_query, w_key, w_value], axis=1),
            jnp.concatenate(
                [
                    norm_one_gain[None],
                    norm_two_gain[None],
                    jnp.zeros((30, norm_one_gain.shape[0]), jnp.bfloat16),
                ]
            ),
        )
    )
    side = lax.rem(wt_index, 2)
    later = side + zero[0, 0]
    slab = slab.reshape(-1, slab.shape[2])
    gain_one, gain_two = gains[:, 0].reshape(-1), gains[:, 1].reshape(-1)
    tables = jnp.concatenate(
        [jnp.swapaxes(routes[0], 0, 1).astype(jnp.float32), jnp.swapaxes(gates[0], 0, 1)], axis=0
    )
    all_tables = gather_side(tables, side)
    gate_blocks = collect_expert(expert_gate, later, pairs)
    up_blocks = collect_expert(expert_up, later, pairs)
    down_blocks = collect_expert(expert_down, later, pairs)
    local = expert_gate.shape[0] // 2
    first_expert = (lax.axis_index("ctx") * 2 + side) * local

    inputs = hidden[0].astype(jnp.float32)
    offset = lax.axis_index("ctx") * tokens
    query_pos = offset + jnp.arange(tokens, dtype=jnp.int32)
    last_query = offset + tokens - 1
    seg_all = segment_ids[0]
    query_seg = lax.dynamic_slice_in_dim(seg_all, offset, tokens)
    group = HEADS // KV_HEADS
    scale_one = inverse_rms(inputs)
    gain_one_full = gain_one.astype(jnp.float32)
    normed = (inputs * scale_one * gain_one_full).astype(jnp.bfloat16)
    projected = jnp.dot(normed, slab, preferred_element_type=jnp.float32).astype(jnp.bfloat16)
    queries = projected[:, :wide]
    both, out_weight, both_weight, down_weight = gather_rows(
        projected[:, wide:],
        2,
        False,
        False,
        "gather_keys",
        (w_out, jnp.concatenate([shared_gate, shared_up], axis=1), shared_down),
    )
    out_weight = out_weight.reshape(-1, out_weight.shape[2])
    both_weight = both_weight.reshape(-1, both_weight.shape[2])
    down_weight = down_weight.reshape(-1, down_weight.shape[2])
    both = both.reshape(-1, 2 * kv_width)
    all_keys, all_values = both[:, :kv_width], both[:, kv_width:]

    table_shape = (chips, 2, 2, 2 * TOPK, tokens)
    ordered_tables = jnp.transpose(all_tables.reshape(table_shape), (0, 2, 3, 1, 4)).reshape(
        chips, 2, 2 * TOPK, 2 * tokens
    )
    experts_here = (first_expert + jnp.arange(local, dtype=jnp.int32)).astype(jnp.float32)
    named = ordered_tables[:, :, None, :TOPK] == experts_here[None, None, :, None, None]
    member = jnp.any(named, axis=3)
    slot_gates = jnp.sum(jnp.where(named, ordered_tables[:, :, None, TOPK:], 0.0), axis=3)
    earlier = (
        jnp.arange(2 * tokens)[:, None] < jnp.arange(2 * tokens)[None, :]
    ).astype(jnp.bfloat16)
    rank = jnp.dot(member.astype(jnp.bfloat16), earlier, preferred_element_type=jnp.float32)
    slots = jnp.where(member, rank.astype(jnp.int32), -1)

    grad_rows = cotangent[0]
    all_grads = gather_side(
        lax.dynamic_index_in_dim(jnp.stack([grad_rows, grad_rows]), later - side, 0, False), side
    ).reshape(chips, 2, 2, tokens, width_model)

    grouped = queries.reshape(tokens, KV_HEADS, group, HEAD_DIM)
    start_state = (
        jnp.full((KV_HEADS, group, tokens), masked_value, jnp.float32),
        jnp.zeros((KV_HEADS, group, tokens), jnp.float32),
        jnp.zeros((KV_HEADS, group, tokens, HEAD_DIM), jnp.float32),
    )
    best, total, accum = forward_piece(
        start_state, (all_keys, all_values), grouped, query_pos, query_seg, seg_all, last_query
    )
    log_totals = best + jnp.log(total)
    attended_full = jnp.transpose(accum / total[..., None], (2, 0, 1, 3)).reshape(
        tokens, HEADS * HEAD_DIM
    )
    attended = attended_full.astype(jnp.bfloat16)
    middle = inputs + jnp.dot(attended, out_weight, preferred_element_type=jnp.float32)
    scale_two = inverse_rms(middle)
    gain_two_full = gain_two.astype(jnp.float32)
    normed_two = (middle * scale_two * gain_two_full).astype(jnp.bfloat16)

    (all_rows,) = gather_rows(normed_two, 3, True, True, "gather_tokens")
    (received_rows,) = pick_rows(all_rows, slots, slot_gates, False)
    grad_received, row_gates = pick_rows(all_grads, slots, slot_gates, True)
    if gate_blocks[0].shape[1] % 128:
        results, backs, grads_gate, grads_up, grads_down = run_experts(
            received_rows,
            grad_received,
            row_gates,
            [settle_blocks(gate_blocks, wt_index, 1)],
            [settle_blocks(up_blocks, wt_index, 1)],
            [settle_blocks(down_blocks, wt_index, 2)],
        )
        grads_gate = split_blocks(grads_gate[0], wt_index, wt_count, 1)
        grads_up = split_blocks(grads_up[0], wt_index, wt_count, 1)
        grads_down = split_blocks(grads_down[0], wt_index, wt_count, 2)
    else:
        results, backs, grads_gate, grads_up, grads_down = run_experts(
            received_rows, grad_received, row_gates, gate_blocks, up_blocks, down_blocks
        )
    sum_experts_gate = scatter_expert(grads_gate, side, pairs)
    sum_experts_up = scatter_expert(grads_up, side, pairs)
    sum_experts_down = scatter_expert(grads_down, side, pairs)
    routed_grad = scatter_rows(
        spread_rows(backs, slots, "spread_grads"), 5, True, True, "scatter_grads"
    )
    routed = scatter_rows(
        spread_rows(results, slots, "spread_results"), 4, True, True, "scatter_results"
    )

    shared_parts = jnp.dot(normed_two, both_weight, preferred_element_type=jnp.float32)
    shared_gate_part, shared_up_part = shared_parts[:, :shared_width], shared_parts[:, shared_width:]
    shared_inner = (jax.nn.silu(shared_gate_part) * shared_up_part).astype(jnp.bfloat16)
    shared_result = jnp.dot(shared_inner, down_weight, preferred_element_type=jnp.float32)
    output = (middle + shared_result + routed).astype(jnp.bfloat16)
    grad_out = grad_rows.astype(jnp.float32)
    grad_shared_down = jnp.einsum(
        "tf,td->fd", shared_inner, grad_rows, preferred_element_type=jnp.float32
    )
    grad_shared_inner = jnp.einsum(
        "td,fd->tf", grad_rows, down_weight, preferred_element_type=jnp.float32
    )
    grad_shared_gate_part = (
        grad_shared_inner * shared_up_part * silu_slope(shared_gate_part)
    ).astype(jnp.bfloat16)
    grad_shared_up_part = (grad_shared_inner * jax.nn.silu(shared_gate_part)).astype(jnp.bfloat16)
    grad_shared_parts = jnp.concatenate([grad_shared_gate_part, grad_shared_up_part], axis=1)
    grad_shared_both = jnp.einsum(
        "td,tf->df", normed_two, grad_shared_parts, preferred_element_type=jnp.float32
    )
    grad_normed_two = (
        jnp.einsum("tf,df->td", grad_shared_parts, both_weight, preferred_element_type=jnp.float32)
        + routed_grad
    )
    grad_gain_two = jnp.sum(grad_normed_two * middle * scale_two, axis=0)
    scaled_two = grad_normed_two * gain_two_full
    grad_middle = (
        grad_out
        + scale_two * scaled_two
        - middle * scale_two**3 * jnp.mean(scaled_two * middle, axis=-1, keepdims=True)
    )
    grad_branch = grad_middle.astype(jnp.bfloat16)
    grad_out_weight = jnp.einsum(
        "tq,td->qd", attended, grad_branch, preferred_element_type=jnp.float32
    )
    grad_attended = jnp.einsum(
        "td,qd->tq", grad_branch, out_weight, preferred_element_type=jnp.float32
    ).astype(jnp.bfloat16)
    grad_grouped = grad_attended.reshape(tokens, KV_HEADS, group, HEAD_DIM)
    deltas = jnp.transpose(
        jnp.sum(
            grad_grouped.astype(jnp.float32)
            * attended_full.reshape(tokens, KV_HEADS, group, HEAD_DIM),
            axis=-1,
        ),
        (1, 2, 0),
    )
    pack_len = seg_all.shape[0]
    back_state = (
        jnp.zeros((tokens, KV_HEADS, group, HEAD_DIM), jnp.float32),
        jnp.zeros((pack_len, kv_width), jnp.float32),
        jnp.zeros((pack_len, kv_width), jnp.float32),
    )
    grad_queries_full, keys_terms, values_terms = backward_piece(
        back_state,
        (all_keys, all_values),
        grouped,
        grad_grouped,
        log_totals,
        deltas,
        query_pos,
        query_seg,
        seg_all,
        last_query,
    )
    grad_both = scatter_rows(
        jnp.concatenate([keys_terms, values_terms], axis=1)
        .astype(jnp.bfloat16)
        .reshape(chips, 1, 2, tokens, 2 * kv_width),
        6,
        False,
        False,
        "scatter_keys",
    ).astype(jnp.bfloat16)
    grad_queries = grad_queries_full.reshape(tokens, HEADS * HEAD_DIM).astype(jnp.bfloat16)
    grad_projected = jnp.concatenate([grad_queries, grad_both], axis=1)
    grad_slab = jnp.einsum("tc,tq->cq", normed, grad_projected, preferred_element_type=jnp.float32)
    grad_normed = jnp.einsum(
        "tq,cq->tc", grad_projected, slab, preferred_element_type=jnp.float32
    )
    grad_gain_one = jnp.sum(grad_normed * inputs * scale_one, axis=0)
    scaled_one = grad_normed * gain_one_full
    grad_inputs = (
        grad_middle
        + scale_one * scaled_one
        - inputs * scale_one**3 * jnp.mean(scaled_one * inputs, axis=-1, keepdims=True)
    )

    def reduced(grad):
        part = lax.psum_scatter(grad.astype(jnp.bfloat16), "wt", scatter_dimension=0, tiled=True)
        return lax.psum(part, "ctx").astype(jnp.float32)

    final_shared = reduced(grad_shared_both)
    final_gate, final_up = final_shared[:, :shared_width], final_shared[:, shared_width:]
    final_down = reduced(grad_shared_down)
    final_out = reduced(grad_out_weight)
    final_slab = reduced(grad_slab)
    final_query = final_slab[:, :wide]
    final_key = final_slab[:, wide : wide + kv_width]
    final_value = final_slab[:, wide + kv_width :]
    final_gains = reduced(jnp.stack([grad_gain_one, grad_gain_two], axis=1))
    final_gain_one, final_gain_two = final_gains[:, 0], final_gains[:, 1]
    return (
        output[None],
        grad_inputs[None],
        final_gain_one,
        final_query,
        final_key,
        final_value,
        final_out,
        final_gain_two,
        final_gate,
        final_up,
        final_down,
        sum_experts_gate,
        sum_experts_up,
        sum_experts_down,
    )


def solution(mesh):
    placed = (
        P("wt", "ctx", None),
        P("wt", None),
        P("wt", "ctx", None),
        P("wt", "ctx", None),
        P("wt", "ctx", None),
        P("wt"),
        P("wt", None),
        P("wt", None),
        P("wt", None),
        P("wt", None),
        P("wt"),
        P("wt", None),
        P("wt", None),
        P("wt", None),
        P("ctx", "wt", None),
        P("ctx", "wt", None),
        P("ctx", None, "wt"),
    )
    return jax.shard_map(
        body,
        mesh=mesh,
        in_specs=placed,
        out_specs=(
            P("wt", "ctx", None),
            P("wt", "ctx", None),
            P("wt"),
            P("wt", None),
            P("wt", None),
            P("wt", None),
            P("wt", None),
            P("wt"),
            P("wt", None),
            P("wt", None),
            P("wt", None),
            P("ctx", "wt", None),
            P("ctx", "wt", None),
            P("ctx", None, "wt"),
        ),
        check_vma=False,
    )
```

```python
import functools
import math

import jax
import jax.numpy as jnp
from jax import lax
from jax.experimental import pallas as pl
from jax.experimental.pallas import tpu as pltpu
from jax.sharding import PartitionSpec as P

HEADS = 12
KV_HEADS = 4
HEAD_DIM = 128
EXPERTS = 64
TOPK = 6
CAP = 40


epsilon = 1e-05
masked_value = -1e30


def inverse_rms(rows):
    return lax.rsqrt(jnp.mean(rows * rows, axis=-1, keepdims=True) + epsilon)


def silu_slope(gate_part):
    sigmoid = jax.nn.sigmoid(gate_part)
    return sigmoid * (1.0 + gate_part * (1.0 - sigmoid))


def block_mask(begin, width, query_pos, query_seg, seg_all):
    key_pos = begin + jnp.arange(width, dtype=jnp.int32)
    key_seg = lax.dynamic_slice_in_dim(seg_all, begin, width)
    return (key_pos[None, :] <= query_pos[:, None]) & (key_seg[None, :] == query_seg[:, None])


def forward_piece(state, piece, grouped, query_pos, query_seg, seg_all, last_query):
    piece_keys, piece_values = piece
    count = piece_keys.shape[0]
    width = math.gcd(count, 512)
    scale = HEAD_DIM ** (-0.5)

    def forward_inner(carry, index):
        begin = index * width

        def forward_compute(current):
            best, total, accum = current
            block_keys = lax.dynamic_slice_in_dim(piece_keys, begin, width).reshape(
                width, KV_HEADS, HEAD_DIM
            )
            block_values = lax.dynamic_slice_in_dim(piece_values, begin, width).reshape(
                width, KV_HEADS, HEAD_DIM
            )
            allowed = block_mask(begin, width, query_pos, query_seg, seg_all)
            scores = (
                jnp.einsum(
                    "qkgd,skd->kgqs", grouped, block_keys, preferred_element_type=jnp.float32
                )
                * scale
            )
            scores = jnp.where(allowed[None, None], scores, masked_value)
            newest = jnp.maximum(best, jnp.max(scores, axis=-1))
            factor = jnp.exp(best - newest)
            weights = jnp.exp(scores - newest[..., None])
            total = total * factor + jnp.sum(weights, axis=-1)
            accum = accum * factor[..., None] + jnp.einsum(
                "kgqs,skd->kgqd",
                weights.astype(jnp.bfloat16),
                block_values,
                preferred_element_type=jnp.float32,
            )
            return (newest, total, accum)

        def forward_keep(current):
            return current

        return (lax.cond(begin <= last_query, forward_compute, forward_keep, carry), None)

    state, _ = lax.scan(forward_inner, state, jnp.arange(count // width, dtype=jnp.int32))
    return state


def backward_piece(
    state,
    piece,
    grouped,
    grad_grouped,
    log_totals,
    deltas,
    query_pos,
    query_seg,
    seg_all,
    last_query,
):
    piece_keys, piece_values = piece
    count = piece_keys.shape[0]
    width = math.gcd(count, 512)
    scale = HEAD_DIM ** (-0.5)
    grad_queries, keys_grad, values_grad = state
    kv_width = piece_keys.shape[1]

    def backward_inner(carry, index):
        begin = index * width

        def backward_compute(current):
            block_keys = lax.dynamic_slice_in_dim(piece_keys, begin, width).reshape(
                width, KV_HEADS, HEAD_DIM
            )
            block_values = lax.dynamic_slice_in_dim(piece_values, begin, width).reshape(
                width, KV_HEADS, HEAD_DIM
            )
            allowed = block_mask(begin, width, query_pos, query_seg, seg_all)
            scores = (
                jnp.einsum(
                    "qkgd,skd->kgqs", grouped, block_keys, preferred_element_type=jnp.float32
                )
                * scale
            )
            scores = jnp.where(allowed[None, None], scores, masked_value)
            probs = jnp.exp(scores - log_totals[..., None])
            grad_probs = jnp.einsum(
                "qkgd,skd->kgqs", grad_grouped, block_values, preferred_element_type=jnp.float32
            )
            grad_scores = (probs * (grad_probs - deltas[..., None])).astype(jnp.bfloat16)
            updated = (
                current
                + jnp.einsum(
                    "kgqs,skd->qkgd", grad_scores, block_keys, preferred_element_type=jnp.float32
                )
                * scale
            )
            key_term = (
                jnp.einsum(
                    "kgqs,qkgd->skd", grad_scores, grouped, preferred_element_type=jnp.float32
                )
                * scale
            )
            value_term = jnp.einsum(
                "kgqs,qkgd->skd",
                probs.astype(jnp.bfloat16),
                grad_grouped,
                preferred_element_type=jnp.float32,
            )
            return (updated, key_term.reshape(width, kv_width), value_term.reshape(width, kv_width))

        def backward_keep(current):
            empty = jnp.zeros((width, kv_width), jnp.float32)
            return (current, empty, empty)

        updated, key_term, value_term = lax.cond(
            begin <= last_query, backward_compute, backward_keep, carry
        )
        return (updated, (key_term, value_term))

    grad_queries, (key_terms, value_terms) = lax.scan(
        backward_inner, grad_queries, jnp.arange(count // width, dtype=jnp.int32)
    )
    keys_grad = key_terms.reshape(count, -1)
    values_grad = value_terms.reshape(count, -1)
    return (grad_queries, keys_grad, values_grad)


MESH = pl.DeviceIdType.MESH
WIDE = 56 * 2**20
LONG = pl.CostEstimate(flops=0, bytes_accessed=2_000_000_000, transcendentals=0)
CHEAP = pl.CostEstimate(flops=0, bytes_accessed=4096, transcendentals=0)


def flip(index, distance):
    result = index
    bit = 1
    while bit <= distance:
        if distance // bit % 2:
            result = result + bit - 2 * bit * (index // bit % 2)
        bit *= 2
    return result


def remote(src, dst, send_sem, recv_sem, device):
    return pltpu.make_async_remote_copy(
        src_ref=src,
        dst_ref=dst,
        send_sem=send_sem,
        recv_sem=recv_sem,
        device_id=device,
        device_id_type=MESH,
    )


def greet(devices):
    barrier = pltpu.get_barrier_semaphore()
    for device in devices:
        pl.semaphore_signal(barrier, inc=1, device_id=device, device_id_type=MESH)
    pl.semaphore_wait(barrier, len(devices))


class Slabs:
    def __init__(self, count, sources, targets, here, send, recv, near_send, near_recv):
        self.c, self.w = lax.axis_index("ctx"), lax.axis_index("wt")
        self.core = lax.rem(self.c, 2)
        self.near = (flip(self.c, 1), self.w)
        self.peers = [flip(self.w, d) for d in range(1, count)]
        self.pairs = list(zip(sources, targets))
        self.here, self.send, self.recv = here, send, recv
        self.near_send, self.near_recv = near_send, near_recv

    def devices(self):
        return [(self.c, p) for p in self.peers]

    def half(self, source, core):
        rows = source.shape[0] // 2
        return pl.ds(pl.multiple_of(core * rows, 16), rows)

    def push(self, i, s):
        source, target = self.pairs[s]
        part = self.half(source, self.core)
        return remote(
            source.at[part], target.at[self.w, part], self.send.at[s, i], self.recv.at[s, i], (self.c, self.peers[i])
        )

    def arrival(self, i, s):
        source, target = self.pairs[s]
        spot = target.at[self.peers[i], self.half(source, self.core)]
        return remote(spot, spot, self.send.at[s, i], self.recv.at[s, i], (self.c, self.peers[i]))

    def hand(self, i, s, core):
        source, target = self.pairs[s]
        spot = target.at[self.peers[i], self.half(source, core)]
        return remote(spot, spot, self.near_send.at[s, i], self.near_recv.at[s, i], self.near)

    def keep(self, s):
        source, target = self.pairs[s]
        return pltpu.make_async_copy(source, target.at[self.w], self.here.at[s])

    def every(self):
        return [(i, s) for s in range(len(self.pairs)) for i in range(len(self.peers))]

    def start(self):
        for i, s in self.every():
            self.push(i, s).start()
        for s in range(len(self.pairs)):
            self.keep(s).start()

    def relay(self):
        for i, s in self.every():
            self.arrival(i, s).wait_recv()
            self.hand(i, s, self.core).start()

    def finish(self):
        for i, s in self.every():
            self.hand(i, s, 1 - self.core).wait_recv()
            self.hand(i, s, self.core).wait_send()
            self.push(i, s).wait_send()
        for s in range(len(self.pairs)):
            self.keep(s).wait()

    @staticmethod
    def scratch(slabs, count):
        dma = pltpu.SemaphoreType.DMA
        return [dma((slabs,))] + [dma((slabs, count - 1))] * 4

    @staticmethod
    def shapes(slabs, count):
        return tuple(jax.ShapeDtypeStruct((count,) + s.shape, s.dtype) for s in slabs)


def weights_kernel(count, slabs, *refs):
    sources, targets, zero_ref = refs[:slabs], refs[slabs : 2 * slabs], refs[2 * slabs]
    plan = Slabs(count, sources, targets, *refs[2 * slabs + 1 :])
    greet(plan.devices() + [plan.near])
    plan.start()
    zero_ref[...] = jnp.zeros_like(zero_ref)
    plan.relay()
    plan.finish()


def gather_weights(slabs):
    count = lax.axis_size("wt")
    return pl.pallas_call(
        functools.partial(weights_kernel, count, len(slabs)),
        out_shape=Slabs.shapes(slabs, count) + (jax.ShapeDtypeStruct((8, 128), jnp.int32),),
        in_specs=[pl.BlockSpec(memory_space=pl.ANY)] * len(slabs),
        out_specs=(pl.BlockSpec(memory_space=pl.ANY),) * len(slabs)
        + (pl.BlockSpec(memory_space=pltpu.VMEM),),
        scratch_shapes=Slabs.scratch(len(slabs), count),
        compiler_params=pltpu.CompilerParams(
            collective_id=1, has_side_effects=True, vmem_limit_bytes=WIDE
        ),
        cost_estimate=CHEAP,
        name="gather_weights",
    )(*slabs)


def gather_kernel(chips, downward, paired, count, slabs, passed, rows_ref, *refs):
    refs = list(refs)

    def take(number):
        taken = refs[:number]
        del refs[:number]
        return taken

    hops = count // 2 - 1
    sources, moved = take(slabs), take(passed)
    (out_ref,), targets, landed, (zero_ref,) = take(1), take(slabs), take(passed * hops), take(1)
    here, up_send, up_recv, down_send, down_recv, pair_send, pair_recv, near_send, near_recv = take(9)
    plan = Slabs(count, sources, targets, *take(5)) if slabs else None
    pass_send, pass_recv = take(2) if passed else (None, None)
    zero_ref[...] = jnp.zeros_like(zero_ref)
    c, w = lax.axis_index("ctx"), lax.axis_index("wt")
    z = c // 2
    core = lax.rem(c, 2)
    side = lax.rem(w, 2) if paired else 0
    near, partner = (flip(c, 1), w), (c, flip(w, 1))
    above = (lax.rem(c + 2, 2 * chips), w)
    below = (lax.rem(c + 2 * chips - 2, 2 * chips), w)
    far = [(c, flip(w, 2 * d + 2)) for d in range(hops)]
    greet([near, above, below] + ([partner] if paired else []) + (plan.devices() if plan else []) + (far if passed else []))

    def onward(i, d):
        return remote(
            moved[i], landed[i * hops + d], pass_send.at[i, d], pass_recv.at[i, d], far[d]
        )

    def spot(chip, which, parity):
        return out_ref.at[chip, which, parity]

    def lift(chip, source):
        return remote(source, spot(chip, side, core), up_send.at[chip], up_recv.at[chip], above)

    def drop(chip, source):
        return remote(source, spot(chip, side, core), down_send.at[chip], down_recv.at[chip], below)

    def give(chip, source):
        return remote(source, spot(chip, side, core), pair_send.at[chip], pair_recv.at[chip], partner)

    def taken(chip):
        return remote(
            spot(chip, 1 - side, core), spot(chip, 1 - side, core), pair_send.at[chip], pair_recv.at[chip], partner
        )

    def hand(chip, which, source):
        return remote(source, spot(chip, which, core), near_send.at[chip, which], near_recv.at[chip, which], near)

    def handed(chip, which):
        there = spot(chip, which, 1 - core)
        return remote(there, there, near_send.at[chip, which], near_recv.at[chip, which], near)

    def settle_pair(chip):
        taken(chip).wait_recv()
        hand(chip, 1 - side, spot(chip, 1 - side, core)).start()

    keep = pltpu.make_async_copy(rows_ref, spot(z, side, core), here)
    keep.start()
    pl.when(z < chips - 1)(lambda: lift(z, rows_ref).start())
    if downward:
        pl.when(z > 0)(lambda: drop(z, rows_ref).start())
    if paired:
        give(z, rows_ref).start()
    hand(z, side, rows_ref).start()
    if plan:
        plan.start()
    for d in range(hops):
        for i in range(passed):
            onward(i, d).start()
    for step in range(1, chips):
        low, high = z - step, z + step

        @pl.when(low >= 0)
        def _():
            lift(low, spot(low, side, core)).wait_recv()
            pl.when(z < chips - 1)(lambda: lift(low, spot(low, side, core)).start())
            if paired:
                give(low, spot(low, side, core)).start()
            hand(low, side, spot(low, side, core)).start()

        if downward:

            @pl.when(high < chips)
            def _():
                drop(high, spot(high, side, core)).wait_recv()
                pl.when(z > 0)(lambda: drop(high, spot(high, side, core)).start())
                if paired:
                    give(high, spot(high, side, core)).start()
                hand(high, side, spot(high, side, core)).start()

        if paired:
            if step == 1:
                settle_pair(z)
            else:
                pl.when(z - step + 1 >= 0)(lambda: settle_pair(z - step + 1))
                pl.when(z + step - 1 < chips)(lambda: settle_pair(z + step - 1))
    if paired:
        pl.when(z - chips + 1 >= 0)(lambda: settle_pair(z - chips + 1))
        pl.when(z + chips - 1 < chips)(lambda: settle_pair(z + chips - 1))
    keep.wait()
    if plan:
        plan.relay()
        plan.finish()

    def finish(chip):
        here_now = spot(chip, side, core)
        pl.when((z < chips - 1) & (chip <= z))(lambda: lift(chip, here_now).wait_send())
        if downward:
            pl.when((z > 0) & (chip >= z))(lambda: drop(chip, here_now).wait_send())
        if paired:
            give(chip, here_now).wait_send()
            for which in range(2):
                hand(chip, which, spot(chip, which, core)).wait_send()
                handed(chip, which).wait_recv()
        else:
            hand(chip, side, here_now).wait_send()
            handed(chip, side).wait_recv()

    for chip in range(chips):
        if downward:
            finish(chip)
        else:
            pl.when(chip <= z)(lambda: finish(chip))
    for d in range(hops):
        for i in range(passed):
            onward(i, d).wait()


def gather_rows(rows, collective_id, downward, paired, name, slabs=(), moved=()):
    chips = lax.axis_size("ctx") // 2
    count = lax.axis_size("wt")
    hops = count // 2 - 1
    line = pltpu.SemaphoreType.DMA((chips,))
    both = pltpu.SemaphoreType.DMA((chips, 2))
    shape = jax.ShapeDtypeStruct((chips, 2 if paired else 1, 2) + rows.shape, rows.dtype)
    landed = tuple(jax.ShapeDtypeStruct(m.shape, m.dtype) for m in moved for _ in range(hops))
    shapes = (shape,) + Slabs.shapes(slabs, count) + landed
    *results, zero = pl.pallas_call(
        functools.partial(gather_kernel, chips, downward, paired, count, len(slabs), len(moved)),
        out_shape=shapes + (jax.ShapeDtypeStruct((8, 128), jnp.int32),),
        in_specs=[pl.BlockSpec(memory_space=pl.ANY)] * (1 + len(slabs) + len(moved)),
        out_specs=(pl.BlockSpec(memory_space=pl.ANY),) * len(shapes)
        + (pl.BlockSpec(memory_space=pltpu.VMEM),),
        scratch_shapes=[pltpu.SemaphoreType.DMA]
        + [line] * 6
        + [both] * 2
        + (Slabs.scratch(len(slabs), count) if slabs else [])
        + ([pltpu.SemaphoreType.DMA((len(moved), hops))] * 2 if moved else []),
        compiler_params=pltpu.CompilerParams(
            collective_id=collective_id, has_side_effects=True, vmem_limit_bytes=WIDE
        ),
        cost_estimate=LONG,
        name=name,
    )(rows, *slabs, *moved)
    return results + [zero[0, 0]]


def scatter_kernel(chips, upward, paired, pieces, partial_ref, out_ref, own, sib, mate, low_in, high_in, load, near_send, near_recv, pair_send, pair_recv, up_send, up_recv, down_send, down_recv):
    c, w = lax.axis_index("ctx"), lax.axis_index("wt")
    z = c // 2
    core = lax.rem(c, 2)
    side = lax.rem(w, 2) if paired else 0
    sides = 2 if paired else 1
    near, partner = (flip(c, 1), w), (c, flip(w, 1))
    above = (lax.rem(c + 2, 2 * chips), w)
    below = (lax.rem(c + 2 * chips - 2, 2 * chips), w)
    rows = own.shape[2] // pieces
    greet([near, above, below] + ([partner] if paired else []))
    order = []
    for i in range(chips // 2):
        order += [chips - 1 - i, i]
    if chips % 2:
        order.append(chips // 2)
    if not upward:
        order = list(range(chips))

    def wanted(chip, action):
        if upward:
            action()
        else:
            pl.when(chip <= z)(action)

    def fetch(chip, which):
        return pltpu.make_async_copy(
            partial_ref.at[chip, which, core], own.at[chip, which], load.at[chip, which]
        )

    def hand(chip, which):
        return remote(
            partial_ref.at[chip, which, 1 - core],
            sib.at[chip, which],
            near_send.at[chip, which],
            near_recv.at[chip, which],
            near,
        )

    def cut(piece):
        return pl.ds(piece * rows, rows)

    def give(chip, piece):
        return remote(
            own.at[chip, 1 - side, cut(piece)],
            mate.at[chip, cut(piece)],
            pair_send.at[chip, piece],
            pair_recv.at[chip, piece],
            partner,
        )

    def lift(chip, piece):
        return remote(
            own.at[chip, side, cut(piece)],
            low_in.at[chip, cut(piece)],
            up_send.at[chip, piece],
            up_recv.at[chip, piece],
            above,
        )

    def drop(chip, piece):
        return remote(
            own.at[chip, side, cut(piece)],
            high_in.at[chip, cut(piece)],
            down_send.at[chip, piece],
            down_recv.at[chip, piece],
            below,
        )

    def add_into(chip, which, piece, other):
        spot = own.at[chip, which, cut(piece)]
        spot[...] = (spot[...].astype(jnp.float32) + other[...].astype(jnp.float32)).astype(spot.dtype)

    for chip in order:

        def begin(chip=chip):
            for which in range(sides):
                hand(chip, which).start()
                fetch(chip, which).start()

        wanted(chip, begin)

    def meet(chip):
        for which in range(sides):
            fetch(chip, which).wait()
            hand(chip, which).wait_recv()
        for piece in range(pieces):
            if paired:
                add_into(chip, 1 - side, piece, sib.at[chip, 1 - side, cut(piece)])
                give(chip, piece).start()
            add_into(chip, side, piece, sib.at[chip, side, cut(piece)])

    def travel(chip):
        for piece in range(pieces):
            if paired:
                give(chip, piece).wait_recv()
                add_into(chip, side, piece, mate.at[chip, cut(piece)])
            if upward:

                @pl.when(z < chip)
                def _():
                    @pl.when(z > 0)
                    def _():
                        lift(chip, piece).wait_recv()
                        add_into(chip, side, piece, low_in.at[chip, cut(piece)])

                    lift(chip, piece).start()

            @pl.when(z > chip)
            def _():
                @pl.when(z < chips - 1)
                def _():
                    drop(chip, piece).wait_recv()
                    add_into(chip, side, piece, high_in.at[chip, cut(piece)])

                drop(chip, piece).start()

    for i, chip in enumerate(order):
        wanted(chip, lambda: meet(chip))
        if i >= 1:
            wanted(order[i - 1], lambda: travel(order[i - 1]))
    wanted(order[-1], lambda: travel(order[-1]))
    for piece in range(pieces):
        out_ref[cut(piece), :] = own.at[z, side, cut(piece)][...].astype(jnp.float32)
    for piece in range(pieces):
        if upward:

            @pl.when(z > 0)
            def _():
                lift(z, piece).wait_recv()
                out_ref[cut(piece), :] += low_in.at[z, cut(piece)][...].astype(jnp.float32)

        @pl.when(z < chips - 1)
        def _():
            drop(z, piece).wait_recv()
            out_ref[cut(piece), :] += high_in.at[z, cut(piece)][...].astype(jnp.float32)

    def finish(chip):
        for which in range(sides):
            hand(chip, which).wait_send()
        for piece in range(pieces):
            if paired:
                give(chip, piece).wait_send()
            if upward:
                pl.when(z < chip)(lambda: lift(chip, piece).wait_send())
            pl.when(z > chip)(lambda: drop(chip, piece).wait_send())

    for chip in order:
        wanted(chip, lambda: finish(chip))


def scatter_rows(partial, collective_id, upward, paired, name):
    chips, sides, _, tokens, width = partial.shape
    pieces = 2
    dma = pltpu.SemaphoreType.DMA
    block = (tokens, width)
    return pl.pallas_call(
        functools.partial(scatter_kernel, chips, upward, paired, pieces),
        out_shape=jax.ShapeDtypeStruct(block, jnp.float32),
        in_specs=[pl.BlockSpec(memory_space=pl.ANY)],
        out_specs=pl.BlockSpec(memory_space=pltpu.VMEM),
        scratch_shapes=[
            pltpu.VMEM((chips, sides) + block, jnp.bfloat16),
            pltpu.VMEM((chips, sides) + block, jnp.bfloat16),
            pltpu.VMEM((chips if paired else 1,) + block, jnp.bfloat16),
            pltpu.VMEM((chips if upward else 1,) + block, jnp.bfloat16),
            pltpu.VMEM((chips,) + block, jnp.bfloat16),
            dma((chips, 2)),
            dma((chips, 2)),
            dma((chips, 2)),
        ]
        + [dma((chips, pieces))] * 6,
        compiler_params=pltpu.CompilerParams(
            collective_id=collective_id, has_side_effects=True, vmem_limit_bytes=WIDE
        ),
        cost_estimate=LONG,
        name=name,
    )(partial)


def pick_kernel(scaled, slot_ref, gate_ref, rows_ref, out_ref, scale_ref=None):
    local, depth = out_ref.shape[2], out_ref.shape[3]
    tokens = rows_ref.shape[3]
    place = lax.broadcasted_iota(jnp.int32, (depth, tokens), 0)
    total, weight = None, None
    for core in range(2):
        span = slice(core * tokens, (core + 1) * tokens)
        chosen = [slot_ref[0, 0, e : e + 1, span] == place for e in range(local)]
        ones = jnp.concatenate([c.astype(jnp.float32) for c in chosen], axis=0).astype(jnp.bfloat16)
        rows = rows_ref[0, core, 0] if scaled else rows_ref[0, 0, core]
        term = jnp.dot(ones, rows, preferred_element_type=jnp.float32)
        total = term if total is None else total + term
        if scaled:
            gates = jnp.concatenate(
                [
                    jnp.sum(jnp.where(c, gate_ref[0, 0, e : e + 1, span], 0.0), axis=1, keepdims=True)
                    for e, c in enumerate(chosen)
                ],
                axis=0,
            )
            weight = gates if weight is None else weight + gates
    if scaled:
        total = total * weight
        scale_ref[0, 0] = jnp.broadcast_to(weight, (local * depth, 128)).reshape(local, depth, 128)
    out_ref[0, 0] = total.astype(jnp.bfloat16).reshape(local, depth, total.shape[1])


def pick_rows(rows, slots, gates, scaled):
    chips, sides, local, both = slots.shape
    tokens, width = both // 2, rows.shape[4]
    depth = 2 * CAP
    table = pl.BlockSpec((1, 1, local, both), lambda z, s: (z, s, 0, 0))
    shapes = [jax.ShapeDtypeStruct((chips, sides, local, depth, width), jnp.bfloat16)]
    specs = [pl.BlockSpec((1, 1, local, depth, width), lambda z, s: (z, s, 0, 0, 0))]
    if scaled:
        shapes.append(jax.ShapeDtypeStruct((chips, sides, local, depth, 128), jnp.float32))
        specs.append(pl.BlockSpec((1, 1, local, depth, 128), lambda z, s: (z, s, 0, 0, 0)))
        source = pl.BlockSpec((1, 2, 1, tokens, width), lambda z, s: (z, 0, s, 0, 0))
    else:
        source = pl.BlockSpec((1, 1, 2, tokens, width), lambda z, s: (z, s, 0, 0, 0))
    return pl.pallas_call(
        functools.partial(pick_kernel, scaled),
        grid=(chips, sides),
        out_shape=shapes,
        in_specs=[table, table, source],
        out_specs=specs,
        compiler_params=pltpu.CompilerParams(vmem_limit_bytes=WIDE),
        cost_estimate=CHEAP,
        name="pick_grads" if scaled else "pick_tokens",
    )(slots, gates, rows)


def spread_kernel(slot_ref, rows_ref, out_ref):
    local, depth, width = rows_ref.shape[2:]
    tokens = out_ref.shape[3]
    place = lax.broadcasted_iota(jnp.int32, (depth, tokens), 0)
    rows = rows_ref[0, 0].reshape(local * depth, width)
    for core in range(2):
        span = slice(core * tokens, (core + 1) * tokens)
        ones = jnp.concatenate(
            [(slot_ref[0, 0, e : e + 1, span] == place).astype(jnp.float32) for e in range(local)], axis=0
        ).astype(jnp.bfloat16)
        out_ref[0, 0, core] = lax.dot_general(
            ones, rows, (((0,), (0,)), ((), ())), preferred_element_type=jnp.float32
        ).astype(jnp.bfloat16)


def spread_rows(rows, slots, name):
    chips, sides, local, both = slots.shape
    depth, width = rows.shape[3:]
    tokens = both // 2
    return pl.pallas_call(
        spread_kernel,
        grid=(chips, sides),
        out_shape=jax.ShapeDtypeStruct((chips, sides, 2, tokens, width), jnp.bfloat16),
        in_specs=[
            pl.BlockSpec((1, 1, local, both), lambda z, s: (z, s, 0, 0)),
            pl.BlockSpec((1, 1, local, depth, width), lambda z, s: (z, s, 0, 0, 0)),
        ],
        out_specs=pl.BlockSpec((1, 1, 2, tokens, width), lambda z, s: (z, s, 0, 0, 0)),
        compiler_params=pltpu.CompilerParams(vmem_limit_bytes=WIDE),
        cost_estimate=CHEAP,
        name=name,
    )(slots, rows)


def expert_kernel(blocks, x_ref, g_ref, scale_ref, *refs):
    gate_refs, up_refs, down_refs = refs[:blocks], refs[blocks : 2 * blocks], refs[2 * blocks : 3 * blocks]
    result_ref, back_ref, grad_gate_ref, grad_up_ref, grad_down_ref = refs[3 * blocks :]
    w = lax.axis_index("wt")
    chips, sides, _, depth, width = x_ref.shape
    rows = chips * sides * depth
    part = gate_refs[0].shape[1]
    nn, nt, tn = (((1,), (0,)), ((), ())), (((1,), (1,)), ((), ())), (((0,), (0,)), ((), ()))

    def dot(a, b, dims):
        return lax.dot_general(a, b, dims, preferred_element_type=jnp.float32)

    def columns(ref, q):
        if blocks == 1:
            return ref.at[:, :, 0]
        span = pl.ds(pl.multiple_of(flip(w, q) * part, 128), part)
        return ref.at[:, :, 0, :, span]

    def piece(ref, q):
        return columns(ref, q)[...].reshape(rows, part)

    gate, up, grad_inner = None, None, None
    for q in range(blocks):
        x = piece(x_ref, q)
        more_gate, more_up = dot(x, gate_refs[q][0], nn), dot(x, up_refs[q][0], nn)
        gate, up = (more_gate, more_up) if q == 0 else (gate + more_gate, up + more_up)
    for q in range(blocks):
        more = dot(piece(g_ref, q), down_refs[q][0], nt)
        grad_inner = more if q == 0 else grad_inner + more
    sigmoid = jax.nn.sigmoid(gate)
    activated = gate * sigmoid
    inner = (activated * up).astype(jnp.bfloat16)
    grad_gate = (grad_inner * up * (sigmoid * (1.0 + gate * (1.0 - sigmoid)))).astype(jnp.bfloat16)
    grad_up = (grad_inner * activated).astype(jnp.bfloat16)
    scale = scale_ref[...].reshape(rows, 128)[:, :1]
    for q in range(blocks):
        result = dot(inner, down_refs[q][0], nn) * scale
        columns(result_ref, q)[...] = result.astype(jnp.bfloat16).reshape(chips, sides, depth, part)
        back = dot(grad_gate, gate_refs[q][0], nt) + dot(grad_up, up_refs[q][0], nt)
        columns(back_ref, q)[...] = back.astype(jnp.bfloat16).reshape(chips, sides, depth, part)
        grad_down_ref[q, 0] = dot(inner, piece(g_ref, q), tn).astype(jnp.bfloat16)
        x = piece(x_ref, q)
        grad_gate_ref[q, 0] = dot(x, grad_gate, tn).astype(jnp.bfloat16)
        grad_up_ref[q, 0] = dot(x, grad_up, tn).astype(jnp.bfloat16)


def run_experts(x, g, scale, gates, ups, downs):
    chips, sides, local, depth, width = x.shape
    blocks = len(gates)
    part, inner = gates[0].shape[1:]
    large = chips * sides * depth > 1024
    rows = pl.BlockSpec((chips, sides, 1, depth, width), lambda e: (0, 0, e, 0, 0))
    sources = pl.BlockSpec(
        (chips, sides, 1, depth, width),
        lambda e: (0, 0, e, 0, 0),
        pipeline_mode=pl.Buffered(1 if large else 2),
    )
    scales = pl.BlockSpec((chips, sides, 1, depth, 128), lambda e: (0, 0, e, 0, 0))
    tall = pl.BlockSpec((1, part, inner), lambda e: (e, 0, 0))
    flat = pl.BlockSpec((1, inner, part), lambda e: (e, 0, 0))
    tall_out = pl.BlockSpec((blocks, 1, part, inner), lambda e: (0, e, 0, 0))
    flat_out = pl.BlockSpec((blocks, 1, inner, part), lambda e: (0, e, 0, 0))
    total = chips * sides * local * depth
    return pl.pallas_call(
        functools.partial(expert_kernel, blocks),
        grid=(local,),
        out_shape=(
            jax.ShapeDtypeStruct(x.shape, jnp.bfloat16),
            jax.ShapeDtypeStruct(x.shape, jnp.bfloat16),
            jax.ShapeDtypeStruct((blocks, local, part, inner), jnp.bfloat16),
            jax.ShapeDtypeStruct((blocks, local, part, inner), jnp.bfloat16),
            jax.ShapeDtypeStruct((blocks, local, inner, part), jnp.bfloat16),
        ),
        in_specs=[sources, sources, scales] + [tall] * (2 * blocks) + [flat] * blocks,
        out_specs=(rows, rows, tall_out, tall_out, flat_out),
        compiler_params=pltpu.CompilerParams(vmem_limit_bytes=60 * 2**20),
        cost_estimate=CHEAP,
        name="experts",
    )(x, g, scale, *gates, *ups, *downs)


def swap_pairs(value, axis, distance):
    count = lax.axis_size(axis)
    return lax.ppermute(value, axis, [(i, i ^ distance) for i in range(count)])


def own_and_other(stacked, mine):
    return (
        lax.dynamic_index_in_dim(stacked, mine, 0, keepdims=False),
        lax.dynamic_index_in_dim(stacked, 1 - mine, 0, keepdims=False),
    )


def in_order(own, other, mine):
    first = jnp.where(mine == 0, own, other)
    second = jnp.where(mine == 0, other, own)
    return jnp.stack([first, second])


def collect_expert(shard, side, pairs):
    local = shard.shape[0]
    kept, given = own_and_other(shard.reshape((2, local // 2) + shard.shape[1:]), side)
    return kept, swap_pairs(given, "wt", 1), [swap_pairs(kept, "wt", 2 * d) for d in range(1, pairs)]


def settle_blocks(blocks, index, axis):
    stacked = jnp.stack(blocks)
    return jnp.concatenate(
        [
            lax.dynamic_index_in_dim(stacked, jnp.bitwise_xor(j, index), 0, False)
            for j in range(len(blocks))
        ],
        axis=axis,
    )


def split_blocks(whole, index, count, axis):
    parts = jnp.stack(jnp.split(whole, count, axis=axis))
    return jnp.stack(
        [
            lax.dynamic_index_in_dim(parts, jnp.bitwise_xor(q, index), 0, False)
            for q in range(count)
        ]
    )


def scatter_expert(grads, arrived, side):
    total = grads[:2].astype(jnp.float32)
    for more in arrived:
        total = total + more.astype(jnp.float32)
    other = swap_pairs(total[1].astype(jnp.bfloat16), "wt", 1).astype(jnp.float32)
    both = in_order(total[0], other, side)
    return both.reshape((-1,) + both.shape[2:])


def gather_side(rows, side):
    both = in_order(rows, swap_pairs(rows, "wt", 1), side)
    return lax.all_gather(both, "ctx", axis=0)


def body(
    hidden,
    segment_ids,
    routes,
    gates,
    cotangent,
    norm_one_gain,
    w_query,
    w_key,
    w_value,
    w_out,
    norm_two_gain,
    shared_gate,
    shared_up,
    shared_down,
    expert_gate,
    expert_up,
    expert_down,
):
    wt_index = lax.axis_index("wt")
    wt_count = lax.axis_size("wt")
    ctx_count = lax.axis_size("ctx")
    chips = ctx_count // 2
    pairs = wt_count // 2
    tokens, width_model = hidden.shape[1:]
    wide, kv_width = w_query.shape[1], w_key.shape[1]
    shared_width = shared_gate.shape[1]
    slab, gains, zero = gather_weights(
        (
            jnp.concatenate([w_query, w_key, w_value], axis=1),
            jnp.concatenate(
                [
                    norm_one_gain[None],
                    norm_two_gain[None],
                    jnp.zeros((30, norm_one_gain.shape[0]), jnp.bfloat16),
                ]
            ),
        )
    )
    side = lax.rem(wt_index, 2)
    later = side + zero[0, 0]
    slab = slab.reshape(-1, slab.shape[2])
    gain_one, gain_two = gains[:, 0].reshape(-1), gains[:, 1].reshape(-1)
    tables = jnp.concatenate(
        [jnp.swapaxes(routes[0], 0, 1).astype(jnp.float32), jnp.swapaxes(gates[0], 0, 1)], axis=0
    )
    all_tables = gather_side(tables, side)
    collected = [collect_expert(e, later, pairs) for e in (expert_gate, expert_up, expert_down)]
    local = expert_gate.shape[0] // 2
    first_expert = (lax.axis_index("ctx") * 2 + side) * local

    inputs = hidden[0].astype(jnp.float32)
    offset = lax.axis_index("ctx") * tokens
    query_pos = offset + jnp.arange(tokens, dtype=jnp.int32)
    last_query = offset + tokens - 1
    seg_all = segment_ids[0]
    query_seg = lax.dynamic_slice_in_dim(seg_all, offset, tokens)
    group = HEADS // KV_HEADS
    scale_one = inverse_rms(inputs)
    gain_one_full = gain_one.astype(jnp.float32)
    normed = (inputs * scale_one * gain_one_full).astype(jnp.bfloat16)
    projected = jnp.dot(normed, slab, preferred_element_type=jnp.float32).astype(jnp.bfloat16)
    queries = projected[:, :wide]
    both, out_weight, both_weight, down_weight, zero = gather_rows(
        projected[:, wide:],
        2,
        False,
        False,
        "gather_keys",
        (w_out, jnp.concatenate([shared_gate, shared_up], axis=1), shared_down),
    )
    out_weight = out_weight.reshape(-1, out_weight.shape[2])
    both_weight = both_weight.reshape(-1, both_weight.shape[2])
    down_weight = down_weight.reshape(-1, down_weight.shape[2])
    both = both.reshape(-1, 2 * kv_width)
    all_keys, all_values = both[:, :kv_width], both[:, kv_width:]

    table_shape = (chips, 2, 2, 2 * TOPK, tokens)
    ordered_tables = jnp.transpose(all_tables.reshape(table_shape), (0, 2, 3, 1, 4)).reshape(
        chips, 2, 2 * TOPK, 2 * tokens
    )
    experts_here = (first_expert + jnp.arange(local, dtype=jnp.int32)).astype(jnp.float32)
    named = ordered_tables[:, :, None, :TOPK] == experts_here[None, None, :, None, None]
    member = jnp.any(named, axis=3)
    slot_gates = jnp.sum(jnp.where(named, ordered_tables[:, :, None, TOPK:], 0.0), axis=3)
    earlier = (
        jnp.arange(2 * tokens)[:, None] < jnp.arange(2 * tokens)[None, :]
    ).astype(jnp.bfloat16)
    rank = jnp.dot(member.astype(jnp.bfloat16), earlier, preferred_element_type=jnp.float32)
    slots = jnp.where(member, rank.astype(jnp.int32), -1)

    grad_rows = cotangent[0]
    all_grads = gather_side(
        lax.dynamic_index_in_dim(jnp.stack([grad_rows, grad_rows]), zero, 0, False), side
    ).reshape(chips, 2, 2, tokens, width_model)

    grouped = queries.reshape(tokens, KV_HEADS, group, HEAD_DIM)
    start_state = (
        jnp.full((KV_HEADS, group, tokens), masked_value, jnp.float32),
        jnp.zeros((KV_HEADS, group, tokens), jnp.float32),
        jnp.zeros((KV_HEADS, group, tokens, HEAD_DIM), jnp.float32),
    )
    best, total, accum = forward_piece(
        start_state, (all_keys, all_values), grouped, query_pos, query_seg, seg_all, last_query
    )
    log_totals = best + jnp.log(total)
    attended_full = jnp.transpose(accum / total[..., None], (2, 0, 1, 3)).reshape(
        tokens, HEADS * HEAD_DIM
    )
    attended = attended_full.astype(jnp.bfloat16)
    attended, collected = lax.optimization_barrier((attended, collected))
    middle = inputs + jnp.dot(attended, out_weight, preferred_element_type=jnp.float32)
    scale_two = inverse_rms(middle)
    gain_two_full = gain_two.astype(jnp.float32)
    normed_two = (middle * scale_two * gain_two_full).astype(jnp.bfloat16)

    all_rows, *landed, zero = gather_rows(
        normed_two, 3, True, True, "gather_tokens", (), [c[1] for c in collected]
    )

    def blocks_of(i):
        kept, paired, straight = collected[i]
        blocks = [kept, paired]
        for d in range(pairs - 1):
            blocks += [straight[d], landed[i * (pairs - 1) + d]]
        return blocks

    gate_blocks, up_blocks, down_blocks = blocks_of(0), blocks_of(1), blocks_of(2)
    (received_rows,) = pick_rows(all_rows, slots, slot_gates, False)
    grad_received, row_gates = pick_rows(all_grads, slots, slot_gates, True)
    if gate_blocks[0].shape[1] % 128:
        results, backs, grads_gate, grads_up, grads_down = run_experts(
            received_rows,
            grad_received,
            row_gates,
            [settle_blocks(gate_blocks, wt_index, 1)],
            [settle_blocks(up_blocks, wt_index, 1)],
            [settle_blocks(down_blocks, wt_index, 2)],
        )
        grads_gate = split_blocks(grads_gate[0], wt_index, wt_count, 1)
        grads_up = split_blocks(grads_up[0], wt_index, wt_count, 1)
        grads_down = split_blocks(grads_down[0], wt_index, wt_count, 2)
    else:
        results, backs, grads_gate, grads_up, grads_down = run_experts(
            received_rows, grad_received, row_gates, gate_blocks, up_blocks, down_blocks
        )
    expert_grads = (grads_gate, grads_up, grads_down)
    arrived = [
        [swap_pairs(g[2 * d : 2 * d + 2], "wt", 2 * d) for d in range(1, pairs)] for g in expert_grads
    ]
    routed_grad = scatter_rows(
        spread_rows(backs, slots, "spread_grads"), 5, True, True, "scatter_grads"
    )
    spread = spread_rows(results, slots, "spread_results")
    partial = lax.psum_scatter(
        jnp.swapaxes(spread, 1, 2).reshape(ctx_count, 2, tokens, width_model),
        "ctx",
        scatter_dimension=0,
        tiled=True,
    )[0]
    kept, given = own_and_other(partial, side)
    routed = kept.astype(jnp.float32) + swap_pairs(given, "wt", 1).astype(jnp.float32)

    shared_parts = jnp.dot(normed_two, both_weight, preferred_element_type=jnp.float32)
    shared_gate_part, shared_up_part = shared_parts[:, :shared_width], shared_parts[:, shared_width:]
    shared_inner = (jax.nn.silu(shared_gate_part) * shared_up_part).astype(jnp.bfloat16)
    shared_result = jnp.dot(shared_inner, down_weight, preferred_element_type=jnp.float32)
    output = (middle + shared_result + routed).astype(jnp.bfloat16)
    grad_out = grad_rows.astype(jnp.float32)
    grad_shared_down = jnp.einsum(
        "tf,td->fd", shared_inner, grad_rows, preferred_element_type=jnp.float32
    )
    grad_shared_inner = jnp.einsum(
        "td,fd->tf", grad_rows, down_weight, preferred_element_type=jnp.float32
    )
    grad_shared_gate_part = (
        grad_shared_inner * shared_up_part * silu_slope(shared_gate_part)
    ).astype(jnp.bfloat16)
    grad_shared_up_part = (grad_shared_inner * jax.nn.silu(shared_gate_part)).astype(jnp.bfloat16)
    grad_shared_parts = jnp.concatenate([grad_shared_gate_part, grad_shared_up_part], axis=1)
    grad_shared_both = jnp.einsum(
        "td,tf->df", normed_two, grad_shared_parts, preferred_element_type=jnp.float32
    )
    grad_normed_two = (
        jnp.einsum("tf,df->td", grad_shared_parts, both_weight, preferred_element_type=jnp.float32)
        + routed_grad
    )
    grad_gain_two = jnp.sum(grad_normed_two * middle * scale_two, axis=0)
    scaled_two = grad_normed_two * gain_two_full
    grad_middle = (
        grad_out
        + scale_two * scaled_two
        - middle * scale_two**3 * jnp.mean(scaled_two * middle, axis=-1, keepdims=True)
    )
    grad_branch = grad_middle.astype(jnp.bfloat16)
    grad_out_weight = jnp.einsum(
        "tq,td->qd", attended, grad_branch, preferred_element_type=jnp.float32
    )
    grad_attended = jnp.einsum(
        "td,qd->tq", grad_branch, out_weight, preferred_element_type=jnp.float32
    ).astype(jnp.bfloat16)
    grad_grouped = grad_attended.reshape(tokens, KV_HEADS, group, HEAD_DIM)
    deltas = jnp.transpose(
        jnp.sum(
            grad_grouped.astype(jnp.float32)
            * attended_full.reshape(tokens, KV_HEADS, group, HEAD_DIM),
            axis=-1,
        ),
        (1, 2, 0),
    )
    pack_len = seg_all.shape[0]
    back_state = (
        jnp.zeros((tokens, KV_HEADS, group, HEAD_DIM), jnp.float32),
        jnp.zeros((pack_len, kv_width), jnp.float32),
        jnp.zeros((pack_len, kv_width), jnp.float32),
    )
    grad_queries_full, keys_terms, values_terms = backward_piece(
        back_state,
        (all_keys, all_values),
        grouped,
        grad_grouped,
        log_totals,
        deltas,
        query_pos,
        query_seg,
        seg_all,
        last_query,
    )
    grad_both = scatter_rows(
        jnp.concatenate([keys_terms, values_terms], axis=1)
        .astype(jnp.bfloat16)
        .reshape(chips, 1, 2, tokens, 2 * kv_width),
        6,
        False,
        False,
        "scatter_keys",
    ).astype(jnp.bfloat16)
    grad_both, arrived = lax.optimization_barrier((grad_both, arrived))
    sum_experts_gate, sum_experts_up, sum_experts_down = [
        scatter_expert(g, a, side) for g, a in zip(expert_grads, arrived)
    ]
    grad_queries = grad_queries_full.reshape(tokens, HEADS * HEAD_DIM).astype(jnp.bfloat16)
    grad_projected = jnp.concatenate([grad_queries, grad_both], axis=1)
    grad_slab = jnp.einsum("tc,tq->cq", normed, grad_projected, preferred_element_type=jnp.float32)
    grad_normed = jnp.einsum(
        "tq,cq->tc", grad_projected, slab, preferred_element_type=jnp.float32
    )
    grad_gain_one = jnp.sum(grad_normed * inputs * scale_one, axis=0)
    scaled_one = grad_normed * gain_one_full
    grad_inputs = (
        grad_middle
        + scale_one * scaled_one
        - inputs * scale_one**3 * jnp.mean(scaled_one * inputs, axis=-1, keepdims=True)
    )

    def reduced(grad):
        part = lax.psum_scatter(grad.astype(jnp.bfloat16), "wt", scatter_dimension=0, tiled=True)
        return lax.psum(part, "ctx").astype(jnp.float32)

    final_shared = reduced(grad_shared_both)
    final_gate, final_up = final_shared[:, :shared_width], final_shared[:, shared_width:]
    final_down = reduced(grad_shared_down)
    final_out = reduced(grad_out_weight)
    final_slab = reduced(grad_slab)
    final_query = final_slab[:, :wide]
    final_key = final_slab[:, wide : wide + kv_width]
    final_value = final_slab[:, wide + kv_width :]
    final_gains = reduced(jnp.stack([grad_gain_one, grad_gain_two], axis=1))
    final_gain_one, final_gain_two = final_gains[:, 0], final_gains[:, 1]
    return (
        output[None],
        grad_inputs[None],
        final_gain_one,
        final_query,
        final_key,
        final_value,
        final_out,
        final_gain_two,
        final_gate,
        final_up,
        final_down,
        sum_experts_gate,
        sum_experts_up,
        sum_experts_down,
    )


def solution(mesh):
    placed = (
        P("wt", "ctx", None),
        P("wt", None),
        P("wt", "ctx", None),
        P("wt", "ctx", None),
        P("wt", "ctx", None),
        P("wt"),
        P("wt", None),
        P("wt", None),
        P("wt", None),
        P("wt", None),
        P("wt"),
        P("wt", None),
        P("wt", None),
        P("wt", None),
        P("ctx", "wt", None),
        P("ctx", "wt", None),
        P("ctx", None, "wt"),
    )
    return jax.shard_map(
        body,
        mesh=mesh,
        in_specs=placed,
        out_specs=(
            P("wt", "ctx", None),
            P("wt", "ctx", None),
            P("wt"),
            P("wt", None),
            P("wt", None),
            P("wt", None),
            P("wt", None),
            P("wt"),
            P("wt", None),
            P("wt", None),
            P("wt", None),
            P("ctx", "wt", None),
            P("ctx", "wt", None),
            P("ctx", None, "wt"),
        ),
        check_vma=False,
    )
```

```python
import functools
import math

import jax
import jax.numpy as jnp
from jax import lax
from jax.experimental import pallas as pl
from jax.experimental.pallas import tpu as pltpu
from jax.sharding import PartitionSpec as P

HEADS = 12
KV_HEADS = 4
HEAD_DIM = 128
EXPERTS = 64
TOPK = 6
CAP = 40


epsilon = 1e-05
masked_value = -1e30


def inverse_rms(rows):
    return lax.rsqrt(jnp.mean(rows * rows, axis=-1, keepdims=True) + epsilon)


def silu_slope(gate_part):
    sigmoid = jax.nn.sigmoid(gate_part)
    return sigmoid * (1.0 + gate_part * (1.0 - sigmoid))


MESH = pl.DeviceIdType.MESH
WIDE = 56 * 2**20
LONG = pl.CostEstimate(flops=0, bytes_accessed=2_000_000_000, transcendentals=0)
CHEAP = pl.CostEstimate(flops=0, bytes_accessed=4096, transcendentals=0)


def flip(index, distance):
    result = index
    bit = 1
    while bit <= distance:
        if distance // bit % 2:
            result = result + bit - 2 * bit * (index // bit % 2)
        bit *= 2
    return result


def remote(src, dst, send_sem, recv_sem, device):
    return pltpu.make_async_remote_copy(
        src_ref=src,
        dst_ref=dst,
        send_sem=send_sem,
        recv_sem=recv_sem,
        device_id=device,
        device_id_type=MESH,
    )


def greet(devices):
    barrier = pltpu.get_barrier_semaphore()
    for device in devices:
        pl.semaphore_signal(barrier, inc=1, device_id=device, device_id_type=MESH)
    pl.semaphore_wait(barrier, len(devices))


class Slabs:
    def __init__(self, count, sources, targets, here, there, send, recv, near_send, near_recv, *stages):
        self.c, self.w = lax.axis_index("ctx"), lax.axis_index("wt")
        self.core = lax.rem(self.c, 2)
        self.near = (flip(self.c, 1), self.w)
        self.peers = [flip(self.w, d) for d in range(1, count)]
        self.pairs = list(zip(sources, targets))
        self.here, self.there, self.send, self.recv = here, there, send, recv
        self.stages = stages
        self.near_send, self.near_recv = near_send, near_recv

    def devices(self):
        return [(self.c, p) for p in self.peers]

    def half(self, source, core):
        rows = source.shape[0] // 2
        return pl.ds(pl.multiple_of(core * rows, 16), rows)

    def push(self, i, s):
        source, target = self.pairs[s]
        part = self.half(source, self.core)
        return remote(
            source.at[part], target.at[self.w, part], self.send.at[s, i], self.recv.at[s, i], (self.c, self.peers[i])
        )

    def arrival(self, i, s):
        source, target = self.pairs[s]
        spot = target.at[self.peers[i], self.half(source, self.core)]
        return remote(spot, spot, self.send.at[s, i], self.recv.at[s, i], (self.c, self.peers[i]))

    def hand(self, i, s, core):
        source, target = self.pairs[s]
        spot = target.at[self.peers[i], self.half(source, core)]
        return remote(spot, spot, self.near_send.at[s, i], self.near_recv.at[s, i], self.near)

    def load(self, s):
        return pltpu.make_async_copy(self.pairs[s][0], self.stages[s], self.here.at[s])

    def keep(self, s):
        return pltpu.make_async_copy(self.stages[s], self.pairs[s][1].at[self.w], self.there.at[s])

    def every(self):
        return [(i, s) for s in range(len(self.pairs)) for i in range(len(self.peers))]

    def start(self):
        for i, s in self.every():
            self.push(i, s).start()
        for s in range(len(self.pairs)):
            self.load(s).start()

    def relay(self):
        for s in range(len(self.pairs)):
            self.load(s).wait()
            self.keep(s).start()
        for i, s in self.every():
            self.arrival(i, s).wait_recv()
            self.hand(i, s, self.core).start()

    def finish(self):
        for i, s in self.every():
            self.hand(i, s, 1 - self.core).wait_recv()
            self.hand(i, s, self.core).wait_send()
            self.push(i, s).wait_send()
        for s in range(len(self.pairs)):
            self.keep(s).wait()

    @staticmethod
    def scratch(slabs, count):
        dma = pltpu.SemaphoreType.DMA
        number = len(slabs)
        return (
            [dma((number,))] * 2
            + [dma((number, count - 1))] * 4
            + [pltpu.VMEM(s.shape, s.dtype) for s in slabs]
        )

    @staticmethod
    def shapes(slabs, count):
        return tuple(jax.ShapeDtypeStruct((count,) + s.shape, s.dtype) for s in slabs)


def weights_kernel(count, slabs, swaps, *refs):
    refs = list(refs)

    def take(number):
        taken = refs[:number]
        del refs[:number]
        return taken

    sources, given = take(slabs), take(swaps)
    targets, paired, (zero_ref,) = take(slabs), take(swaps), take(1)
    stages = take(swaps)
    load_sem, keep_sem, swap_send, swap_recv = take(4)
    plan = Slabs(count, sources, targets, *refs)
    c, w = lax.axis_index("ctx"), lax.axis_index("wt")
    side = lax.rem(w, 2)
    partner = (c, flip(w, 1))
    greet(plan.devices() + [plan.near])

    def swap(i):
        return remote(given[i], paired[i].at[side], swap_send.at[i], swap_recv.at[i], partner)

    def load(i):
        return pltpu.make_async_copy(given[i], stages[i], load_sem.at[i])

    def keep(i):
        return pltpu.make_async_copy(stages[i], paired[i].at[side], keep_sem.at[i])

    plan.start()
    for i in range(swaps):
        swap(i).start()
        load(i).start()
    zero_ref[...] = jnp.zeros_like(zero_ref)
    for i in range(swaps):
        load(i).wait()
        keep(i).start()
    plan.relay()
    plan.finish()
    for i in range(swaps):
        keep(i).wait()
        swap(i).wait()


def gather_weights(slabs, swaps):
    count = lax.axis_size("wt")
    dma = pltpu.SemaphoreType.DMA((len(swaps),))
    pairs = tuple(jax.ShapeDtypeStruct((2,) + s.shape, s.dtype) for s in swaps)
    shapes = Slabs.shapes(slabs, count) + pairs
    return pl.pallas_call(
        functools.partial(weights_kernel, count, len(slabs), len(swaps)),
        out_shape=shapes + (jax.ShapeDtypeStruct((8, 128), jnp.int32),),
        in_specs=[pl.BlockSpec(memory_space=pl.ANY)] * (len(slabs) + len(swaps)),
        out_specs=(pl.BlockSpec(memory_space=pl.ANY),) * len(shapes)
        + (pl.BlockSpec(memory_space=pltpu.VMEM),),
        scratch_shapes=[pltpu.VMEM(s.shape, s.dtype) for s in swaps]
        + [dma] * 4
        + Slabs.scratch(slabs, count),
        compiler_params=pltpu.CompilerParams(
            collective_id=1, has_side_effects=True, vmem_limit_bytes=WIDE
        ),
        cost_estimate=LONG,
        name="gather_weights",
    )(*slabs, *swaps)


def gather_kernel(chips, downward, paired, count, slabs, passed, rows_ref, *refs):
    refs = list(refs)

    def take(number):
        taken = refs[:number]
        del refs[:number]
        return taken

    hops = count // 2 - 1
    sources, moved = take(slabs), take(passed)
    (out_ref,), targets, landed, (zero_ref,) = take(1), take(slabs), take(passed * hops), take(1)
    (stage,) = take(1)
    here, up_send, up_recv, down_send, down_recv, pair_send, pair_recv, near_send, near_recv = take(9)
    plan = Slabs(count, sources, targets, *take(6 + slabs)) if slabs else None
    pass_send, pass_recv = take(2) if passed else (None, None)
    zero_ref[...] = jnp.zeros_like(zero_ref)
    c, w = lax.axis_index("ctx"), lax.axis_index("wt")
    z = c // 2
    core = lax.rem(c, 2)
    side = lax.rem(w, 2) if paired else 0
    near, partner = (flip(c, 1), w), (c, flip(w, 1))
    above = (lax.rem(c + 2, 2 * chips), w)
    below = (lax.rem(c + 2 * chips - 2, 2 * chips), w)
    far = [(c, flip(w, 2 * d + 2)) for d in range(hops)]
    greet([near, above, below] + ([partner] if paired else []) + (plan.devices() if plan else []) + (far if passed else []))

    def onward(i, d):
        return remote(
            moved[i], landed[i * hops + d], pass_send.at[i, d], pass_recv.at[i, d], far[d]
        )

    def spot(chip, which, parity):
        return out_ref.at[chip, which, parity]

    def lift(chip, source):
        return remote(source, spot(chip, side, core), up_send.at[chip], up_recv.at[chip], above)

    def drop(chip, source):
        return remote(source, spot(chip, side, core), down_send.at[chip], down_recv.at[chip], below)

    def give(chip, source):
        return remote(source, spot(chip, side, core), pair_send.at[chip], pair_recv.at[chip], partner)

    def taken(chip):
        return remote(
            spot(chip, 1 - side, core), spot(chip, 1 - side, core), pair_send.at[chip], pair_recv.at[chip], partner
        )

    def hand(chip, which, source):
        return remote(source, spot(chip, which, core), near_send.at[chip, which], near_recv.at[chip, which], near)

    def handed(chip, which):
        there = spot(chip, which, 1 - core)
        return remote(there, there, near_send.at[chip, which], near_recv.at[chip, which], near)

    def settle_pair(chip):
        taken(chip).wait_recv()
        hand(chip, 1 - side, spot(chip, 1 - side, core)).start()

    load = pltpu.make_async_copy(rows_ref, stage, here.at[0])
    keep = pltpu.make_async_copy(stage, spot(z, side, core), here.at[1])
    load.start()
    pl.when(z < chips - 1)(lambda: lift(z, rows_ref).start())
    if downward:
        pl.when(z > 0)(lambda: drop(z, rows_ref).start())
    if paired:
        give(z, rows_ref).start()
    hand(z, side, rows_ref).start()
    if plan:
        plan.start()
    for d in range(hops):
        for i in range(passed):
            onward(i, d).start()
    load.wait()
    keep.start()
    for step in range(1, chips):
        low, high = z - step, z + step

        @pl.when(low >= 0)
        def _():
            lift(low, spot(low, side, core)).wait_recv()
            pl.when(z < chips - 1)(lambda: lift(low, spot(low, side, core)).start())
            if paired:
                give(low, spot(low, side, core)).start()
            hand(low, side, spot(low, side, core)).start()

        if downward:

            @pl.when(high < chips)
            def _():
                drop(high, spot(high, side, core)).wait_recv()
                pl.when(z > 0)(lambda: drop(high, spot(high, side, core)).start())
                if paired:
                    give(high, spot(high, side, core)).start()
                hand(high, side, spot(high, side, core)).start()

        if paired:
            if step == 1:
                settle_pair(z)
            else:
                pl.when(z - step + 1 >= 0)(lambda: settle_pair(z - step + 1))
                pl.when(z + step - 1 < chips)(lambda: settle_pair(z + step - 1))
    if paired:
        pl.when(z - chips + 1 >= 0)(lambda: settle_pair(z - chips + 1))
        pl.when(z + chips - 1 < chips)(lambda: settle_pair(z + chips - 1))
    keep.wait()
    if plan:
        plan.relay()
        plan.finish()

    def finish(chip):
        here_now = spot(chip, side, core)
        pl.when((z < chips - 1) & (chip <= z))(lambda: lift(chip, here_now).wait_send())
        if downward:
            pl.when((z > 0) & (chip >= z))(lambda: drop(chip, here_now).wait_send())
        if paired:
            give(chip, here_now).wait_send()
            for which in range(2):
                hand(chip, which, spot(chip, which, core)).wait_send()
                handed(chip, which).wait_recv()
        else:
            hand(chip, side, here_now).wait_send()
            handed(chip, side).wait_recv()

    for chip in range(chips):
        if downward:
            finish(chip)
        else:
            pl.when(chip <= z)(lambda: finish(chip))
    for d in range(hops):
        for i in range(passed):
            onward(i, d).wait()


def gather_rows(rows, collective_id, downward, paired, name, slabs=(), moved=()):
    chips = lax.axis_size("ctx") // 2
    count = lax.axis_size("wt")
    hops = count // 2 - 1
    line = pltpu.SemaphoreType.DMA((chips,))
    both = pltpu.SemaphoreType.DMA((chips, 2))
    shape = jax.ShapeDtypeStruct((chips, 2 if paired else 1, 2) + rows.shape, rows.dtype)
    landed = tuple(jax.ShapeDtypeStruct(m.shape, m.dtype) for m in moved for _ in range(hops))
    shapes = (shape,) + Slabs.shapes(slabs, count) + landed
    *results, zero = pl.pallas_call(
        functools.partial(gather_kernel, chips, downward, paired, count, len(slabs), len(moved)),
        out_shape=shapes + (jax.ShapeDtypeStruct((8, 128), jnp.int32),),
        in_specs=[pl.BlockSpec(memory_space=pl.ANY)] * (1 + len(slabs) + len(moved)),
        out_specs=(pl.BlockSpec(memory_space=pl.ANY),) * len(shapes)
        + (pl.BlockSpec(memory_space=pltpu.VMEM),),
        scratch_shapes=[pltpu.VMEM(rows.shape, rows.dtype), pltpu.SemaphoreType.DMA((2,))]
        + [line] * 6
        + [both] * 2
        + (Slabs.scratch(slabs, count) if slabs else [])
        + ([pltpu.SemaphoreType.DMA((len(moved), hops))] * 2 if moved else []),
        compiler_params=pltpu.CompilerParams(
            collective_id=collective_id, has_side_effects=True, vmem_limit_bytes=WIDE
        ),
        cost_estimate=LONG,
        name=name,
    )(rows, *slabs, *moved)
    return results + [zero[0, 0]]


def scatter_kernel(chips, upward, paired, pieces, partial_ref, out_ref, own, sib, mate, low_in, high_in, load, near_send, near_recv, pair_send, pair_recv, up_send, up_recv, down_send, down_recv):
    c, w = lax.axis_index("ctx"), lax.axis_index("wt")
    z = c // 2
    core = lax.rem(c, 2)
    side = lax.rem(w, 2) if paired else 0
    sides = 2 if paired else 1
    near, partner = (flip(c, 1), w), (c, flip(w, 1))
    above = (lax.rem(c + 2, 2 * chips), w)
    below = (lax.rem(c + 2 * chips - 2, 2 * chips), w)
    rows = own.shape[2] // pieces
    greet([near, above, below] + ([partner] if paired else []))
    order = []
    for i in range(chips // 2):
        order += [chips - 1 - i, i]
    if chips % 2:
        order.append(chips // 2)
    if not upward:
        order = list(range(chips))

    def wanted(chip, action):
        if upward:
            action()
        else:
            pl.when(chip <= z)(action)

    def fetch(chip, which):
        return pltpu.make_async_copy(
            partial_ref.at[chip, which, core], own.at[chip, which], load.at[chip, which]
        )

    def hand(chip, which):
        return remote(
            partial_ref.at[chip, which, 1 - core],
            sib.at[chip, which],
            near_send.at[chip, which],
            near_recv.at[chip, which],
            near,
        )

    def cut(piece):
        return pl.ds(piece * rows, rows)

    def give(chip, piece):
        return remote(
            own.at[chip, 1 - side, cut(piece)],
            mate.at[chip, cut(piece)],
            pair_send.at[chip, piece],
            pair_recv.at[chip, piece],
            partner,
        )

    def lift(chip, piece):
        return remote(
            own.at[chip, side, cut(piece)],
            low_in.at[chip, cut(piece)],
            up_send.at[chip, piece],
            up_recv.at[chip, piece],
            above,
        )

    def drop(chip, piece):
        return remote(
            own.at[chip, side, cut(piece)],
            high_in.at[chip, cut(piece)],
            down_send.at[chip, piece],
            down_recv.at[chip, piece],
            below,
        )

    def add_into(chip, which, piece, other):
        spot = own.at[chip, which, cut(piece)]
        spot[...] = spot[...] + other[...]

    for chip in order:

        def begin(chip=chip):
            for which in range(sides):
                hand(chip, which).start()
                fetch(chip, which).start()

        wanted(chip, begin)

    def meet(chip):
        for which in range(sides):
            fetch(chip, which).wait()
            hand(chip, which).wait_recv()
        for piece in range(pieces):
            if paired:
                add_into(chip, 1 - side, piece, sib.at[chip, 1 - side, cut(piece)])
                give(chip, piece).start()
            add_into(chip, side, piece, sib.at[chip, side, cut(piece)])

    def travel(chip):
        for piece in range(pieces):
            if paired:
                give(chip, piece).wait_recv()
                add_into(chip, side, piece, mate.at[chip, cut(piece)])
            if upward:

                @pl.when(z < chip)
                def _():
                    @pl.when(z > 0)
                    def _():
                        lift(chip, piece).wait_recv()
                        add_into(chip, side, piece, low_in.at[chip, cut(piece)])

                    lift(chip, piece).start()

            @pl.when(z > chip)
            def _():
                @pl.when(z < chips - 1)
                def _():
                    drop(chip, piece).wait_recv()
                    add_into(chip, side, piece, high_in.at[chip, cut(piece)])

                drop(chip, piece).start()

    for i, chip in enumerate(order):
        wanted(chip, lambda: meet(chip))
        if i >= 1:
            wanted(order[i - 1], lambda: travel(order[i - 1]))
    wanted(order[-1], lambda: travel(order[-1]))
    for piece in range(pieces):
        out_ref[cut(piece), :] = own.at[z, side, cut(piece)][...].astype(jnp.float32)
    for piece in range(pieces):
        if upward:

            @pl.when(z > 0)
            def _():
                lift(z, piece).wait_recv()
                out_ref[cut(piece), :] += low_in.at[z, cut(piece)][...].astype(jnp.float32)

        @pl.when(z < chips - 1)
        def _():
            drop(z, piece).wait_recv()
            out_ref[cut(piece), :] += high_in.at[z, cut(piece)][...].astype(jnp.float32)

    def finish(chip):
        for which in range(sides):
            hand(chip, which).wait_send()
        for piece in range(pieces):
            if paired:
                give(chip, piece).wait_send()
            if upward:
                pl.when(z < chip)(lambda: lift(chip, piece).wait_send())
            pl.when(z > chip)(lambda: drop(chip, piece).wait_send())

    for chip in order:
        wanted(chip, lambda: finish(chip))


def scatter_rows(partial, collective_id, upward, paired, name):
    chips, sides, _, tokens, width = partial.shape
    pieces = 2
    dma = pltpu.SemaphoreType.DMA
    block = (tokens, width)
    return pl.pallas_call(
        functools.partial(scatter_kernel, chips, upward, paired, pieces),
        out_shape=jax.ShapeDtypeStruct(block, jnp.float32),
        in_specs=[pl.BlockSpec(memory_space=pl.ANY)],
        out_specs=pl.BlockSpec(memory_space=pltpu.VMEM),
        scratch_shapes=[
            pltpu.VMEM((chips, sides) + block, jnp.bfloat16),
            pltpu.VMEM((chips, sides) + block, jnp.bfloat16),
            pltpu.VMEM((chips if paired else 1,) + block, jnp.bfloat16),
            pltpu.VMEM((chips if upward else 1,) + block, jnp.bfloat16),
            pltpu.VMEM((chips,) + block, jnp.bfloat16),
            dma((chips, 2)),
            dma((chips, 2)),
            dma((chips, 2)),
        ]
        + [dma((chips, pieces))] * 6,
        compiler_params=pltpu.CompilerParams(
            collective_id=collective_id, has_side_effects=True, vmem_limit_bytes=WIDE
        ),
        cost_estimate=LONG,
        name=name,
    )(partial)


def dense_kernel(chips, count, matrices, pieces, *refs):
    refs = list(refs)

    def take(number):
        taken = refs[:number]
        del refs[:number]
        return taken

    grads, outs = take(matrices), take(matrices)
    own, sib, mates, low, final = (take(matrices) for _ in range(5))
    (load, near_send, near_recv, send, recv, low_send, low_recv, back_send, back_recv, last_send, last_recv, keep) = refs
    c, w = lax.axis_index("ctx"), lax.axis_index("wt")
    z = c // 2
    core = lax.rem(c, 2)
    near = (flip(c, 1), w)
    above = (lax.rem(c + 2, 2 * chips), w)
    below = (lax.rem(c + 2 * chips - 2, 2 * chips), w)
    peers = [flip(w, d) for d in range(1, count)]
    greet([near, above, below] + [(c, p) for p in peers])

    def span(j, parity=None):
        m, first, rows = pieces[j]
        if parity is None:
            return pl.ds(first, rows)
        half = grads[m].shape[1] // 2
        return pl.ds(pl.multiple_of(parity * half + first, 16), rows)

    def fetch(j):
        m = pieces[j][0]
        return pltpu.make_async_copy(grads[m].at[:, span(j, core)], own[m].at[:, span(j)], load.at[j])

    def hand(j):
        m = pieces[j][0]
        return remote(
            grads[m].at[:, span(j, 1 - core)], sib[m].at[:, span(j)], near_send.at[j], near_recv.at[j], near
        )

    def give(j, d):
        m = pieces[j][0]
        return remote(
            own[m].at[peers[d], span(j)], mates[m].at[d, span(j)], send.at[j, d], recv.at[j, d], (c, peers[d])
        )

    def total(j):
        return own[pieces[j][0]].at[w, span(j)]

    def add(spot, other):
        spot[...] = spot[...] + other[...]

    def start(j):
        hand(j).start()
        fetch(j).start()

    def share(j):
        m = pieces[j][0]
        fetch(j).wait()
        hand(j).wait_recv()
        for d in range(count - 1):
            add(own[m].at[peers[d], span(j)], sib[m].at[peers[d], span(j)])
            give(j, d).start()
        add(total(j), sib[m].at[w, span(j)])

    def collect(j):
        m = pieces[j][0]
        value = total(j)[...].astype(jnp.float32)
        for d in range(count - 1):
            give(j, d).wait_recv()
            value = value + mates[m][d, span(j), :].astype(jnp.float32)
        total(j)[...] = value.astype(jnp.bfloat16)

    def line(j):
        return (z, above, below) if j % 2 == 0 else (chips - 1 - z, below, above)

    def onward(j):
        m = pieces[j][0]
        return remote(total(j), low[m].at[span(j)], low_send.at[j], low_recv.at[j], line(j)[1])

    def backward(j):
        spot = final[pieces[j][0]].at[span(j)]
        return remote(spot, spot, back_send.at[j], back_recv.at[j], line(j)[2])

    def across(j, parity):
        m = pieces[j][0]
        return remote(
            final[m].at[span(j)], outs[m].at[span(j, parity)], last_send.at[j], last_recv.at[j], near
        )

    def store(j):
        m = pieces[j][0]
        return pltpu.make_async_copy(final[m].at[span(j)], outs[m].at[span(j, core)], keep.at[j])

    def accumulate(j):
        place = line(j)[0]
        m = pieces[j][0]

        @pl.when(place > 0)
        def _():
            onward(j).wait_recv()
            add(total(j), low[m].at[span(j)])

        @pl.when(place < chips - 1)
        def _():
            onward(j).start()

        @pl.when(place == chips - 1)
        def _():
            final[m][span(j), :] = total(j)[...]
            backward(j).start()
            across(j, core).start()
            store(j).start()

    def spread(j):
        place = line(j)[0]

        @pl.when(place < chips - 1)
        def _():
            backward(j).wait_recv()
            pl.when(place > 0)(lambda: backward(j).start())
            across(j, core).start()
            store(j).start()

    number = len(pieces)
    for j in range(number):
        start(j)
    for j in range(number):
        share(j)
    last = chips - 1
    for t in range(number + 2 * last):
        if t < number:
            collect(t)
        for hop in range(2 * last, -1, -1):
            j = t - hop
            if not 0 <= j < number:
                continue
            if hop <= last:
                pl.when(line(j)[0] == hop)(lambda: accumulate(j))
            if hop > last:
                pl.when(line(j)[0] == 2 * last - hop)(lambda: spread(j))
    for j in range(number):
        place = line(j)[0]
        hand(j).wait_send()
        for d in range(count - 1):
            give(j, d).wait_send()
        pl.when(place < chips - 1)(lambda: onward(j).wait_send())
        pl.when(place > 0)(lambda: backward(j).wait_send())
        across(j, core).wait_send()
        across(j, 1 - core).wait_recv()
        store(j).wait()


def reduce_dense(grads):
    count = lax.axis_size("wt")
    chips = lax.axis_size("ctx") // 2
    shapes = [(g.shape[0] // count, g.shape[1]) for g in grads]
    pieces = []
    for m, (rows, _) in enumerate(shapes):
        half, width = rows // 2, shapes[m][1]
        cuts = max(n for n in range(1, 5) if half % (16 * n) == 0 and (n == 1 or half * width > 120000 * (n - 1)))
        for i in range(cuts):
            pieces.append((m, i * (rows // 2 // cuts), rows // 2 // cuts))
    halves = [(rows // 2, width) for rows, width in shapes]
    dma = pltpu.SemaphoreType.DMA
    one, many = dma((len(pieces),)), dma((len(pieces), count - 1))
    return pl.pallas_call(
        functools.partial(dense_kernel, chips, count, len(grads), tuple(pieces)),
        out_shape=[jax.ShapeDtypeStruct(s, jnp.bfloat16) for s in shapes],
        in_specs=[pl.BlockSpec(memory_space=pl.ANY)] * len(grads),
        out_specs=[pl.BlockSpec(memory_space=pl.ANY)] * len(grads),
        scratch_shapes=[pltpu.VMEM((count,) + h, jnp.bfloat16) for h in halves]
        + [pltpu.VMEM((count,) + h, jnp.bfloat16) for h in halves]
        + [pltpu.VMEM((count - 1,) + h, jnp.bfloat16) for h in halves]
        + [pltpu.VMEM(h, jnp.bfloat16) for h in halves]
        + [pltpu.VMEM(h, jnp.bfloat16) for h in halves]
        + [one, one, one, many, many, one, one, one, one, one, one, one],
        compiler_params=pltpu.CompilerParams(
            collective_id=7, has_side_effects=True, vmem_limit_bytes=WIDE
        ),
        cost_estimate=LONG,
        name="reduce_dense",
    )(*[g.reshape((count,) + s) for g, s in zip(grads, shapes)])


def dot_of(a, b, left, right):
    return lax.dot_general(
        a, b, (((left,), (right,)), ((), ())), preferred_element_type=jnp.float32
    )


def stacked_heads(ref):
    return jnp.concatenate(
        [ref[:, h * HEAD_DIM : (h + 1) * HEAD_DIM] for h in range(ref.shape[1] // HEAD_DIM)], axis=0
    )


exponent_scale = HEAD_DIM ** (-0.5) * math.log2(math.e)


def attend_kernel(place_ref, query_ref, both_ref, row_ref, column_ref, out_ref, log_ref, best, total, accum):
    tokens = query_ref.shape[0]
    group = query_ref.shape[1] // HEAD_DIM
    width = 2 * tokens
    place = place_ref[0]
    queries = stacked_heads(query_ref)
    best[...] = jnp.full_like(best, masked_value)
    total[...] = jnp.zeros_like(total)
    accum[...] = jnp.zeros_like(accum)
    query_pos = place * tokens + lax.broadcasted_iota(jnp.int32, (tokens, width), 0)
    key_pos = lax.broadcasted_iota(jnp.int32, (tokens, width), 1)

    def step(j, carry):
        span = pl.ds(pl.multiple_of(j * width, width), width)
        allowed = (key_pos + j * width <= query_pos) & (row_ref[0:1, span] == column_ref[:, 0:1])
        bias = jnp.where(allowed, 0.0, masked_value)
        scores = dot_of(queries, both_ref[span, :HEAD_DIM], 1, 1)
        scores = (scores.reshape(group, tokens, width) + bias[None]).reshape(group * tokens, width)
        newest = jnp.maximum(best[...], jnp.max(scores, axis=1, keepdims=True))
        factor = jnp.exp2((best[...] - newest) * exponent_scale)
        weights = jnp.exp2((scores - newest[:, :1]) * exponent_scale)
        total[...] = total[...] * factor + jnp.sum(weights, axis=1, keepdims=True)
        accum[...] = accum[...] * factor + dot_of(
            weights.astype(jnp.bfloat16), both_ref[span, HEAD_DIM:], 1, 0
        )
        best[...] = newest
        return carry

    lax.fori_loop(0, place // 2 + 1, step, 0)
    heads = accum[...] / total[...]
    for h in range(group):
        out_ref[:, h * HEAD_DIM : (h + 1) * HEAD_DIM] = heads[h * tokens : (h + 1) * tokens]
    logs = best[...] * exponent_scale + jnp.log2(total[...])
    log_ref[0] = jnp.transpose(logs)[:8]


def attend(place, projected, both, seg_row, seg_column):
    tokens = projected.shape[0]
    group = HEADS // KV_HEADS
    rows, span = group * tokens, both.shape[0]
    stat = pltpu.VMEM((rows, HEAD_DIM), jnp.float32)
    return pl.pallas_call(
        attend_kernel,
        grid=(KV_HEADS,),
        out_shape=(
            jax.ShapeDtypeStruct((tokens, HEADS * HEAD_DIM), jnp.float32),
            jax.ShapeDtypeStruct((KV_HEADS, 8, rows), jnp.float32),
        ),
        in_specs=[
            pl.BlockSpec(memory_space=pltpu.SMEM),
            pl.BlockSpec((tokens, group * HEAD_DIM), lambda g: (0, g)),
            pl.BlockSpec((span, 2 * HEAD_DIM), lambda g: (0, g)),
            pl.BlockSpec((1, span), lambda g: (0, 0)),
            pl.BlockSpec((tokens, 1), lambda g: (0, 0)),
        ],
        out_specs=(
            pl.BlockSpec((tokens, group * HEAD_DIM), lambda g: (0, g)),
            pl.BlockSpec((1, 8, rows), lambda g: (g, 0, 0)),
        ),
        scratch_shapes=[stat, stat, stat],
        compiler_params=pltpu.CompilerParams(vmem_limit_bytes=WIDE),
        cost_estimate=CHEAP,
        name="attend",
    )(place, projected, both, seg_row, seg_column)


def attend_back_kernel(place_ref, query_ref, both_ref, row_ref, column_ref, heads_ref, grad_ref, log_ref, grad_query_ref, grad_both_ref, accum):
    tokens = query_ref.shape[0]
    group = query_ref.shape[1] // HEAD_DIM
    width = 2 * tokens
    rows = group * tokens
    scale = HEAD_DIM ** (-0.5)
    place = place_ref[0]
    queries, grads = stacked_heads(query_ref), stacked_heads(grad_ref)
    product = grads.astype(jnp.float32) * stacked_heads(heads_ref)
    delta = jnp.sum(product, axis=1, keepdims=True)
    delta = jnp.transpose(jnp.broadcast_to(delta, (rows, HEAD_DIM)))[0:1]
    logs = log_ref[0, 0:1, :]
    accum[...] = jnp.zeros_like(accum)
    grad_both_ref[...] = jnp.zeros_like(grad_both_ref)
    query_pos = place * tokens + lax.broadcasted_iota(jnp.int32, (width, tokens), 1)
    key_pos = lax.broadcasted_iota(jnp.int32, (width, tokens), 0)

    def step(j, carry):
        span = pl.ds(pl.multiple_of(j * width, width), width)
        allowed = (key_pos + j * width <= query_pos) & (column_ref[span, 0:1] == row_ref[0:1, :])
        bias = jnp.where(allowed, 0.0, masked_value)
        bias = jnp.concatenate([bias] * group, axis=1)
        keys, values = both_ref[span, :HEAD_DIM], both_ref[span, HEAD_DIM:]
        scores = dot_of(keys, queries, 1, 1)
        probs = jnp.exp2(scores * exponent_scale + bias - logs)
        grad_probs = dot_of(values, grads, 1, 1)
        grad_scores = (probs * (grad_probs - delta)).astype(jnp.bfloat16)
        accum[...] += dot_of(grad_scores, keys, 0, 0)
        grad_both_ref[span, :HEAD_DIM] = (dot_of(grad_scores, queries, 1, 0) * scale).astype(jnp.bfloat16)
        grad_both_ref[span, HEAD_DIM:] = dot_of(probs.astype(jnp.bfloat16), grads, 1, 0).astype(jnp.bfloat16)
        return carry

    lax.fori_loop(0, place // 2 + 1, step, 0)
    grad_queries = (accum[...] * scale).astype(jnp.bfloat16)
    for h in range(group):
        grad_query_ref[:, h * HEAD_DIM : (h + 1) * HEAD_DIM] = grad_queries[h * tokens : (h + 1) * tokens]


def attend_back(place, projected, both, query_seg_row, seg_column, heads_out, grad_attended, logs):
    tokens = projected.shape[0]
    group = HEADS // KV_HEADS
    rows, span = group * tokens, both.shape[0]
    per_group = pl.BlockSpec((tokens, group * HEAD_DIM), lambda g: (0, g))
    return pl.pallas_call(
        attend_back_kernel,
        grid=(KV_HEADS,),
        out_shape=(
            jax.ShapeDtypeStruct((tokens, HEADS * HEAD_DIM), jnp.bfloat16),
            jax.ShapeDtypeStruct(both.shape, jnp.bfloat16),
        ),
        in_specs=[
            pl.BlockSpec(memory_space=pltpu.SMEM),
            per_group,
            pl.BlockSpec((span, 2 * HEAD_DIM), lambda g: (0, g)),
            pl.BlockSpec((1, tokens), lambda g: (0, 0)),
            pl.BlockSpec((span, 1), lambda g: (0, 0)),
            per_group,
            per_group,
            pl.BlockSpec((1, 8, rows), lambda g: (g, 0, 0)),
        ],
        out_specs=(per_group, pl.BlockSpec((span, 2 * HEAD_DIM), lambda g: (0, g))),
        scratch_shapes=[pltpu.VMEM((rows, HEAD_DIM), jnp.float32)],
        compiler_params=pltpu.CompilerParams(vmem_limit_bytes=WIDE),
        cost_estimate=CHEAP,
        name="attend_back",
    )(place, projected, both, query_seg_row, seg_column, heads_out, grad_attended, logs)


def pick_kernel(scaled, slot_ref, gate_ref, rows_ref, out_ref, scale_ref=None):
    local, depth = out_ref.shape[2], out_ref.shape[3]
    tokens = rows_ref.shape[3]
    place = lax.broadcasted_iota(jnp.int32, (depth, tokens), 0)
    total, weight = None, None
    for core in range(2):
        span = slice(core * tokens, (core + 1) * tokens)
        chosen = [slot_ref[0, 0, e : e + 1, span] == place for e in range(local)]
        ones = jnp.concatenate([c.astype(jnp.float32) for c in chosen], axis=0).astype(jnp.bfloat16)
        rows = rows_ref[0, core, 0] if scaled else rows_ref[0, 0, core]
        term = jnp.dot(ones, rows, preferred_element_type=jnp.float32)
        total = term if total is None else total + term
        if scaled:
            gates = jnp.concatenate(
                [
                    jnp.sum(jnp.where(c, gate_ref[0, 0, e : e + 1, span], 0.0), axis=1, keepdims=True)
                    for e, c in enumerate(chosen)
                ],
                axis=0,
            )
            weight = gates if weight is None else weight + gates
    if scaled:
        total = total * weight
        scale_ref[0, 0] = jnp.broadcast_to(weight, (local * depth, 128)).reshape(local, depth, 128)
    out_ref[0, 0] = total.astype(jnp.bfloat16).reshape(local, depth, total.shape[1])


def pick_rows(rows, slots, gates, scaled):
    chips, sides, local, both = slots.shape
    tokens, width = both // 2, rows.shape[4]
    depth = 2 * CAP
    table = pl.BlockSpec((1, 1, local, both), lambda z, s: (z, s, 0, 0))
    shapes = [jax.ShapeDtypeStruct((chips, sides, local, depth, width), jnp.bfloat16)]
    specs = [pl.BlockSpec((1, 1, local, depth, width), lambda z, s: (z, s, 0, 0, 0))]
    if scaled:
        shapes.append(jax.ShapeDtypeStruct((chips, sides, local, depth, 128), jnp.float32))
        specs.append(pl.BlockSpec((1, 1, local, depth, 128), lambda z, s: (z, s, 0, 0, 0)))
        source = pl.BlockSpec((1, 2, 1, tokens, width), lambda z, s: (z, 0, s, 0, 0))
    else:
        source = pl.BlockSpec((1, 1, 2, tokens, width), lambda z, s: (z, s, 0, 0, 0))
    return pl.pallas_call(
        functools.partial(pick_kernel, scaled),
        grid=(chips, sides),
        out_shape=shapes,
        in_specs=[table, table, source],
        out_specs=specs,
        compiler_params=pltpu.CompilerParams(vmem_limit_bytes=WIDE),
        cost_estimate=CHEAP,
        name="pick_grads" if scaled else "pick_tokens",
    )(slots, gates, rows)


def spread_kernel(slot_ref, rows_ref, out_ref):
    local, depth, width = rows_ref.shape[2:]
    tokens = out_ref.shape[3]
    place = lax.broadcasted_iota(jnp.int32, (depth, tokens), 0)
    rows = rows_ref[0, 0].reshape(local * depth, width)
    for core in range(2):
        span = slice(core * tokens, (core + 1) * tokens)
        ones = jnp.concatenate(
            [(slot_ref[0, 0, e : e + 1, span] == place).astype(jnp.float32) for e in range(local)], axis=0
        ).astype(jnp.bfloat16)
        out_ref[0, 0, core] = lax.dot_general(
            ones, rows, (((0,), (0,)), ((), ())), preferred_element_type=jnp.float32
        ).astype(jnp.bfloat16)


def spread_rows(rows, slots, name):
    chips, sides, local, both = slots.shape
    depth, width = rows.shape[3:]
    tokens = both // 2
    return pl.pallas_call(
        spread_kernel,
        grid=(chips, sides),
        out_shape=jax.ShapeDtypeStruct((chips, sides, 2, tokens, width), jnp.bfloat16),
        in_specs=[
            pl.BlockSpec((1, 1, local, both), lambda z, s: (z, s, 0, 0)),
            pl.BlockSpec((1, 1, local, depth, width), lambda z, s: (z, s, 0, 0, 0)),
        ],
        out_specs=pl.BlockSpec((1, 1, 2, tokens, width), lambda z, s: (z, s, 0, 0, 0)),
        compiler_params=pltpu.CompilerParams(vmem_limit_bytes=WIDE),
        cost_estimate=CHEAP,
        name=name,
    )(slots, rows)


def expert_kernel(blocks, x_ref, g_ref, scale_ref, *refs):
    tall_refs, down_refs = refs[:blocks], refs[blocks : 2 * blocks]
    result_ref, back_ref, grad_tall_ref, grad_down_ref = refs[2 * blocks :]
    w = lax.axis_index("wt")
    chips, sides, _, depth, width = x_ref.shape
    rows = chips * sides * depth
    part = tall_refs[0].shape[2]
    nn, nt, tn = (((1,), (0,)), ((), ())), (((1,), (1,)), ((), ())), (((0,), (0,)), ((), ()))

    def dot(a, b, dims):
        return lax.dot_general(a, b, dims, preferred_element_type=jnp.float32)

    def columns(ref, q):
        if blocks == 1:
            return ref.at[:, :, 0]
        span = pl.ds(pl.multiple_of(flip(w, q) * part, 128), part)
        return ref.at[:, :, 0, :, span]

    def piece(ref, q):
        return columns(ref, q)[...].reshape(rows, part)

    gate, up, grad_inner = None, None, None
    for q in range(blocks):
        x = piece(x_ref, q)
        more_gate, more_up = dot(x, tall_refs[q][0, 0], nn), dot(x, tall_refs[q][0, 1], nn)
        gate, up = (more_gate, more_up) if q == 0 else (gate + more_gate, up + more_up)
    for q in range(blocks):
        more = dot(piece(g_ref, q), down_refs[q][0], nt)
        grad_inner = more if q == 0 else grad_inner + more
    sigmoid = jax.nn.sigmoid(gate)
    activated = gate * sigmoid
    inner = (activated * up).astype(jnp.bfloat16)
    grad_gate = (grad_inner * up * (sigmoid * (1.0 + gate * (1.0 - sigmoid)))).astype(jnp.bfloat16)
    grad_up = (grad_inner * activated).astype(jnp.bfloat16)
    scale = scale_ref[...].reshape(rows, 128)[:, :1]
    for q in range(blocks):
        result = dot(inner, down_refs[q][0], nn) * scale
        columns(result_ref, q)[...] = result.astype(jnp.bfloat16).reshape(chips, sides, depth, part)
        back = dot(grad_gate, tall_refs[q][0, 0], nt) + dot(grad_up, tall_refs[q][0, 1], nt)
        columns(back_ref, q)[...] = back.astype(jnp.bfloat16).reshape(chips, sides, depth, part)
        grad_down_ref[q, 0] = dot(inner, piece(g_ref, q), tn).astype(jnp.bfloat16)
        x = piece(x_ref, q)
        grad_tall_ref[q, 0, 0] = dot(x, grad_gate, tn).astype(jnp.bfloat16)
        grad_tall_ref[q, 0, 1] = dot(x, grad_up, tn).astype(jnp.bfloat16)


def run_experts(x, g, scale, talls, downs):
    chips, sides, local, depth, width = x.shape
    blocks = len(talls)
    part, inner = talls[0].shape[2:]
    large = chips * sides * depth > 1024
    rows = pl.BlockSpec((chips, sides, 1, depth, width), lambda e: (0, 0, e, 0, 0))
    sources = pl.BlockSpec(
        (chips, sides, 1, depth, width),
        lambda e: (0, 0, e, 0, 0),
        pipeline_mode=pl.Buffered(1 if large else 2),
    )
    scales = pl.BlockSpec((chips, sides, 1, depth, 128), lambda e: (0, 0, e, 0, 0))
    tall = pl.BlockSpec((1, 2, part, inner), lambda e: (e, 0, 0, 0))
    flat = pl.BlockSpec((1, inner, part), lambda e: (e, 0, 0))
    tall_out = pl.BlockSpec((blocks, 1, 2, part, inner), lambda e: (0, e, 0, 0, 0))
    flat_out = pl.BlockSpec((blocks, 1, inner, part), lambda e: (0, e, 0, 0))
    total = chips * sides * local * depth
    return pl.pallas_call(
        functools.partial(expert_kernel, blocks),
        grid=(local,),
        out_shape=(
            jax.ShapeDtypeStruct(x.shape, jnp.bfloat16),
            jax.ShapeDtypeStruct(x.shape, jnp.bfloat16),
            jax.ShapeDtypeStruct((blocks, local, 2, part, inner), jnp.bfloat16),
            jax.ShapeDtypeStruct((blocks, local, inner, part), jnp.bfloat16),
        ),
        in_specs=[sources, sources, scales] + [tall] * blocks + [flat] * blocks,
        out_specs=(rows, rows, tall_out, flat_out),
        compiler_params=pltpu.CompilerParams(vmem_limit_bytes=60 * 2**20),
        cost_estimate=CHEAP,
        name="experts",
    )(x, g, scale, *talls, *downs)


def swap_pairs(value, axis, distance):
    count = lax.axis_size(axis)
    return lax.ppermute(value, axis, [(i, i ^ distance) for i in range(count)])


def own_and_other(stacked, mine):
    return (
        lax.dynamic_index_in_dim(stacked, mine, 0, keepdims=False),
        lax.dynamic_index_in_dim(stacked, 1 - mine, 0, keepdims=False),
    )


def in_order(own, other, mine):
    first = jnp.where(mine == 0, own, other)
    second = jnp.where(mine == 0, other, own)
    return jnp.stack([first, second])


def collect_expert(shard, side, pairs):
    local = shard.shape[0]
    kept, given = own_and_other(shard.reshape((2, local // 2) + shard.shape[1:]), side)
    return kept, swap_pairs(given, "wt", 1), [swap_pairs(kept, "wt", 2 * d) for d in range(1, pairs)]


def settle_blocks(blocks, index, axis):
    stacked = jnp.stack(blocks)
    return jnp.concatenate(
        [
            lax.dynamic_index_in_dim(stacked, jnp.bitwise_xor(j, index), 0, False)
            for j in range(len(blocks))
        ],
        axis=axis,
    )


def split_blocks(whole, index, count, axis):
    parts = jnp.stack(jnp.split(whole, count, axis=axis))
    return jnp.stack(
        [
            lax.dynamic_index_in_dim(parts, jnp.bitwise_xor(q, index), 0, False)
            for q in range(count)
        ]
    )


def scatter_expert(grads, arrived, side):
    total = grads[:2].astype(jnp.float32)
    for more in arrived:
        total = total + more.astype(jnp.float32)
    other = swap_pairs(total[1].astype(jnp.bfloat16), "wt", 1).astype(jnp.float32)
    both = in_order(total[0], other, side)
    return both.reshape((-1,) + both.shape[2:])


def body(
    hidden,
    segment_ids,
    routes,
    gates,
    cotangent,
    norm_one_gain,
    w_query,
    w_key,
    w_value,
    w_out,
    norm_two_gain,
    shared_gate,
    shared_up,
    shared_down,
    expert_gate,
    expert_up,
    expert_down,
):
    wt_index = lax.axis_index("wt")
    wt_count = lax.axis_size("wt")
    ctx_count = lax.axis_size("ctx")
    chips = ctx_count // 2
    pairs = wt_count // 2
    tokens, width_model = hidden.shape[1:]
    wide, kv_width = w_query.shape[1], w_key.shape[1]
    shared_width = shared_gate.shape[1]
    tables = jnp.concatenate(
        [
            jnp.swapaxes(routes[0], 0, 1).astype(jnp.float32),
            jnp.zeros((8 - TOPK, tokens), jnp.float32),
            jnp.swapaxes(gates[0], 0, 1),
            jnp.zeros((8 - TOPK, tokens), jnp.float32),
        ],
        axis=0,
    )
    grad_rows = cotangent[0]
    key_parts = jnp.stack(
        [w_key.reshape(-1, KV_HEADS, HEAD_DIM), w_value.reshape(-1, KV_HEADS, HEAD_DIM)], axis=2
    ).reshape(-1, 2 * kv_width)
    slab, gains, table_pair, grad_pair, zero = gather_weights(
        (
            jnp.concatenate([w_query, key_parts], axis=1),
            jnp.concatenate(
                [
                    norm_one_gain[None],
                    norm_two_gain[None],
                    jnp.zeros((30, norm_one_gain.shape[0]), jnp.bfloat16),
                ]
            ),
        ),
        (tables, grad_rows),
    )
    all_tables = lax.all_gather(table_pair, "ctx", axis=0)
    all_grads = lax.all_gather(grad_pair, "ctx", axis=0).reshape(chips, 2, 2, tokens, width_model)
    zero = zero[0, 0]
    side = lax.rem(wt_index, 2)
    slab = slab.reshape(-1, slab.shape[2])
    gain_one, gain_two = gains[:, 0].reshape(-1), gains[:, 1].reshape(-1)
    local = expert_gate.shape[0] // 2
    first_expert = (lax.axis_index("ctx") * 2 + side) * local

    inputs = hidden[0].astype(jnp.float32)
    offset = lax.axis_index("ctx") * tokens
    seg_all = segment_ids[0]
    query_seg = lax.dynamic_slice_in_dim(seg_all, offset, tokens)
    scale_one = inverse_rms(inputs)
    gain_one_full = gain_one.astype(jnp.float32)
    normed = (inputs * scale_one * gain_one_full).astype(jnp.bfloat16)
    projected = jnp.dot(normed, slab, preferred_element_type=jnp.float32).astype(jnp.bfloat16)
    both, out_weight, both_weight, down_weight, zero = gather_rows(
        projected[:, wide:],
        2,
        False,
        False,
        "gather_keys",
        (w_out, jnp.concatenate([shared_gate, shared_up], axis=1), shared_down),
    )
    out_weight = out_weight.reshape(-1, out_weight.shape[2])
    both_weight = both_weight.reshape(-1, both_weight.shape[2])
    down_weight = down_weight.reshape(-1, down_weight.shape[2])
    both = both.reshape(-1, 2 * kv_width)
    later = side + zero
    collected = [
        collect_expert(jnp.stack([expert_gate, expert_up], axis=1), later, pairs),
        collect_expert(expert_down, later, pairs),
    ]

    table_shape = (chips, 2, 2, 16, tokens)
    ordered_tables = jnp.transpose(all_tables.reshape(table_shape), (0, 2, 3, 1, 4)).reshape(
        chips, 2, 16, 2 * tokens
    )
    experts_here = (first_expert + jnp.arange(local, dtype=jnp.int32)).astype(jnp.float32)
    named = ordered_tables[:, :, None, :TOPK] == experts_here[None, None, :, None, None]
    member = jnp.any(named, axis=3)
    slot_gates = jnp.sum(jnp.where(named, ordered_tables[:, :, None, 8 : 8 + TOPK], 0.0), axis=3)
    earlier = (
        jnp.arange(2 * tokens)[:, None] < jnp.arange(2 * tokens)[None, :]
    ).astype(jnp.bfloat16)
    rank = jnp.dot(member.astype(jnp.bfloat16), earlier, preferred_element_type=jnp.float32)
    slots = jnp.where(member, rank.astype(jnp.int32), -1)

    place = lax.axis_index("ctx").astype(jnp.int32).reshape(1)
    seg_row, seg_column = seg_all[None, :], seg_all[:, None]
    attended_full, logs = attend(place, projected, both, seg_row, query_seg[:, None])
    attended = attended_full.astype(jnp.bfloat16)
    attended, collected = lax.optimization_barrier((attended, collected))
    middle = inputs + jnp.dot(attended, out_weight, preferred_element_type=jnp.float32)
    scale_two = inverse_rms(middle)
    gain_two_full = gain_two.astype(jnp.float32)
    normed_two = (middle * scale_two * gain_two_full).astype(jnp.bfloat16)

    all_rows, *landed, zero = gather_rows(
        normed_two, 3, True, True, "gather_tokens", (), [c[1] for c in collected]
    )

    def blocks_of(i):
        kept, paired, straight = collected[i]
        blocks = [kept, paired]
        for d in range(pairs - 1):
            blocks += [straight[d], landed[i * (pairs - 1) + d]]
        return blocks

    tall_blocks, down_blocks = blocks_of(0), blocks_of(1)
    (received_rows,) = pick_rows(all_rows, slots, slot_gates, False)
    grad_received, row_gates = pick_rows(all_grads, slots, slot_gates, True)
    if down_blocks[0].shape[2] % 128:
        results, backs, grads_tall, grads_down = run_experts(
            received_rows,
            grad_received,
            row_gates,
            [settle_blocks(tall_blocks, wt_index, 2)],
            [settle_blocks(down_blocks, wt_index, 2)],
        )
        grads_tall = split_blocks(grads_tall[0], wt_index, wt_count, 2)
        grads_down = split_blocks(grads_down[0], wt_index, wt_count, 2)
    else:
        results, backs, grads_tall, grads_down = run_experts(
            received_rows, grad_received, row_gates, tall_blocks, down_blocks
        )
    expert_grads = (grads_tall, grads_down)
    arrived = [
        [swap_pairs(g[2 * d : 2 * d + 2], "wt", 2 * d) for d in range(1, pairs)] for g in expert_grads
    ]
    routed_grad = scatter_rows(
        spread_rows(backs, slots, "spread_grads"), 5, True, True, "scatter_grads"
    )
    spread = spread_rows(results, slots, "spread_results")
    partial = lax.psum_scatter(
        jnp.swapaxes(spread, 1, 2).reshape(ctx_count, 2, tokens, width_model),
        "ctx",
        scatter_dimension=0,
        tiled=True,
    )[0]
    kept, given = own_and_other(partial, side)
    routed = kept.astype(jnp.float32) + swap_pairs(given, "wt", 1).astype(jnp.float32)

    shared_parts = jnp.dot(normed_two, both_weight, preferred_element_type=jnp.float32)
    shared_gate_part, shared_up_part = shared_parts[:, :shared_width], shared_parts[:, shared_width:]
    shared_inner = (jax.nn.silu(shared_gate_part) * shared_up_part).astype(jnp.bfloat16)
    shared_result = jnp.dot(shared_inner, down_weight, preferred_element_type=jnp.float32)
    output = (middle + shared_result + routed).astype(jnp.bfloat16)
    grad_out = grad_rows.astype(jnp.float32)
    grad_shared_down = jnp.einsum(
        "tf,td->fd", shared_inner, grad_rows, preferred_element_type=jnp.float32
    )
    grad_shared_inner = jnp.einsum(
        "td,fd->tf", grad_rows, down_weight, preferred_element_type=jnp.float32
    )
    grad_shared_gate_part = (
        grad_shared_inner * shared_up_part * silu_slope(shared_gate_part)
    ).astype(jnp.bfloat16)
    grad_shared_up_part = (grad_shared_inner * jax.nn.silu(shared_gate_part)).astype(jnp.bfloat16)
    grad_shared_parts = jnp.concatenate([grad_shared_gate_part, grad_shared_up_part], axis=1)
    grad_shared_both = jnp.einsum(
        "td,tf->df", normed_two, grad_shared_parts, preferred_element_type=jnp.float32
    )
    grad_normed_two = (
        jnp.einsum("tf,df->td", grad_shared_parts, both_weight, preferred_element_type=jnp.float32)
        + routed_grad
    )
    grad_gain_two = jnp.sum(grad_normed_two * middle * scale_two, axis=0)
    scaled_two = grad_normed_two * gain_two_full
    grad_middle = (
        grad_out
        + scale_two * scaled_two
        - middle * scale_two**3 * jnp.mean(scaled_two * middle, axis=-1, keepdims=True)
    )
    grad_branch = grad_middle.astype(jnp.bfloat16)
    grad_out_weight = jnp.einsum(
        "tq,td->qd", attended, grad_branch, preferred_element_type=jnp.float32
    )
    grad_attended = jnp.einsum(
        "td,qd->tq", grad_branch, out_weight, preferred_element_type=jnp.float32
    ).astype(jnp.bfloat16)
    grad_queries, grad_parts = attend_back(
        place, projected, both, query_seg[None, :], seg_column, attended_full, grad_attended, logs
    )
    grad_both = scatter_rows(
        grad_parts.reshape(chips, 1, 2, tokens, 2 * kv_width),
        6,
        False,
        False,
        "scatter_keys",
    ).astype(jnp.bfloat16)
    grad_both, arrived = lax.optimization_barrier((grad_both, arrived))
    sum_tall, sum_experts_down = [
        scatter_expert(g, a, side) for g, a in zip(expert_grads, arrived)
    ]
    sum_experts_gate, sum_experts_up = sum_tall[:, 0], sum_tall[:, 1]
    grad_projected = jnp.concatenate([grad_queries, grad_both], axis=1)
    grad_slab = jnp.einsum("tc,tq->cq", normed, grad_projected, preferred_element_type=jnp.float32)
    grad_normed = jnp.einsum(
        "tq,cq->tc", grad_projected, slab, preferred_element_type=jnp.float32
    )
    grad_gain_one = jnp.sum(grad_normed * inputs * scale_one, axis=0)
    scaled_one = grad_normed * gain_one_full
    grad_inputs = (
        grad_middle
        + scale_one * scaled_one
        - inputs * scale_one**3 * jnp.mean(scaled_one * inputs, axis=-1, keepdims=True)
    )

    depth = norm_one_gain.shape[0]
    gain_grads = jnp.stack([grad_gain_one, grad_gain_two]).reshape(2, wt_count, 1, depth)
    gain_grads = jnp.pad(gain_grads.astype(jnp.bfloat16), ((0, 0), (0, 0), (0, 15), (0, 0)))
    gain_grads = jnp.swapaxes(gain_grads, 0, 1).reshape(wt_count * 32, depth)
    final_slab, final_shared, final_out, final_down, final_gains = [
        total.astype(jnp.float32)
        for total in reduce_dense(
            [
                grad_slab.astype(jnp.bfloat16),
                grad_shared_both.astype(jnp.bfloat16),
                grad_out_weight.astype(jnp.bfloat16),
                grad_shared_down.astype(jnp.bfloat16),
                gain_grads,
            ]
        )
    ]
    final_gate, final_up = final_shared[:, :shared_width], final_shared[:, shared_width:]
    final_query = final_slab[:, :wide]
    final_parts = final_slab[:, wide:].reshape(-1, KV_HEADS, 2, HEAD_DIM)
    final_key = final_parts[:, :, 0].reshape(-1, kv_width)
    final_value = final_parts[:, :, 1].reshape(-1, kv_width)
    final_gain_one, final_gain_two = final_gains[0], final_gains[16]
    return (
        output[None],
        grad_inputs[None],
        final_gain_one,
        final_query,
        final_key,
        final_value,
        final_out,
        final_gain_two,
        final_gate,
        final_up,
        final_down,
        sum_experts_gate,
        sum_experts_up,
        sum_experts_down,
    )


def solution(mesh):
    placed = (
        P("wt", "ctx", None),
        P("wt", None),
        P("wt", "ctx", None),
        P("wt", "ctx", None),
        P("wt", "ctx", None),
        P("wt"),
        P("wt", None),
        P("wt", None),
        P("wt", None),
        P("wt", None),
        P("wt"),
        P("wt", None),
        P("wt", None),
        P("wt", None),
        P("ctx", "wt", None),
        P("ctx", "wt", None),
        P("ctx", None, "wt"),
    )
    return jax.shard_map(
        body,
        mesh=mesh,
        in_specs=placed,
        out_specs=(
            P("wt", "ctx", None),
            P("wt", "ctx", None),
            P("wt"),
            P("wt", None),
            P("wt", None),
            P("wt", None),
            P("wt", None),
            P("wt"),
            P("wt", None),
            P("wt", None),
            P("wt", None),
            P("ctx", "wt", None),
            P("ctx", "wt", None),
            P("ctx", None, "wt"),
        ),
        check_vma=False,
    )
```

```python
import functools
import math

import jax
import jax.numpy as jnp
from jax import lax
from jax.experimental import pallas as pl
from jax.experimental.pallas import tpu as pltpu
from jax.sharding import PartitionSpec as P

HEADS = 12
KV_HEADS = 4
HEAD_DIM = 128
EXPERTS = 64
TOPK = 6
CAP = 40


epsilon = 1e-05
masked_value = -1e30


def inverse_rms(rows):
    return lax.rsqrt(jnp.mean(rows * rows, axis=-1, keepdims=True) + epsilon)


def silu_slope(gate_part):
    sigmoid = jax.nn.sigmoid(gate_part)
    return sigmoid * (1.0 + gate_part * (1.0 - sigmoid))


MESH = pl.DeviceIdType.MESH
WIDE = 56 * 2**20
LONG = pl.CostEstimate(flops=0, bytes_accessed=2_000_000_000, transcendentals=0)
CHEAP = pl.CostEstimate(flops=0, bytes_accessed=4096, transcendentals=0)


def flip(index, distance):
    result = index
    bit = 1
    while bit <= distance:
        if distance // bit % 2:
            result = result + bit - 2 * bit * (index // bit % 2)
        bit *= 2
    return result


def remote(src, dst, send_sem, recv_sem, device):
    return pltpu.make_async_remote_copy(
        src_ref=src,
        dst_ref=dst,
        send_sem=send_sem,
        recv_sem=recv_sem,
        device_id=device,
        device_id_type=MESH,
    )


def greet(devices):
    barrier = pltpu.get_barrier_semaphore()
    for device in devices:
        pl.semaphore_signal(barrier, inc=1, device_id=device, device_id_type=MESH)
    pl.semaphore_wait(barrier, len(devices))


class Slabs:
    def __init__(self, count, sources, targets, here, there, send, recv, near_send, near_recv, *stages):
        self.c, self.w = lax.axis_index("ctx"), lax.axis_index("wt")
        self.core = lax.rem(self.c, 2)
        self.near = (flip(self.c, 1), self.w)
        self.peers = [flip(self.w, d) for d in range(1, count)]
        self.pairs = list(zip(sources, targets))
        self.here, self.there, self.send, self.recv = here, there, send, recv
        self.stages = stages
        self.near_send, self.near_recv = near_send, near_recv

    def devices(self):
        return [(self.c, p) for p in self.peers]

    def half(self, source, core):
        rows = source.shape[0] // 2
        return pl.ds(pl.multiple_of(core * rows, 16), rows)

    def push(self, i, s):
        source, target = self.pairs[s]
        part = self.half(source, self.core)
        return remote(
            source.at[part], target.at[self.w, part], self.send.at[s, i], self.recv.at[s, i], (self.c, self.peers[i])
        )

    def arrival(self, i, s):
        source, target = self.pairs[s]
        spot = target.at[self.peers[i], self.half(source, self.core)]
        return remote(spot, spot, self.send.at[s, i], self.recv.at[s, i], (self.c, self.peers[i]))

    def hand(self, i, s, core):
        source, target = self.pairs[s]
        spot = target.at[self.peers[i], self.half(source, core)]
        return remote(spot, spot, self.near_send.at[s, i], self.near_recv.at[s, i], self.near)

    def load(self, s):
        return pltpu.make_async_copy(self.pairs[s][0], self.stages[s], self.here.at[s])

    def keep(self, s):
        return pltpu.make_async_copy(self.stages[s], self.pairs[s][1].at[self.w], self.there.at[s])

    def every(self):
        return [(i, s) for s in range(len(self.pairs)) for i in range(len(self.peers))]

    def start(self):
        for i, s in self.every():
            self.push(i, s).start()
        for s in range(len(self.pairs)):
            self.load(s).start()

    def relay(self):
        for s in range(len(self.pairs)):
            self.load(s).wait()
            self.keep(s).start()
        for i, s in self.every():
            self.arrival(i, s).wait_recv()
            self.hand(i, s, self.core).start()

    def finish(self):
        for i, s in self.every():
            self.hand(i, s, 1 - self.core).wait_recv()
            self.hand(i, s, self.core).wait_send()
            self.push(i, s).wait_send()
        for s in range(len(self.pairs)):
            self.keep(s).wait()

    @staticmethod
    def scratch(slabs, count):
        dma = pltpu.SemaphoreType.DMA
        number = len(slabs)
        return (
            [dma((number,))] * 2
            + [dma((number, count - 1))] * 4
            + [pltpu.VMEM(s.shape, s.dtype) for s in slabs]
        )

    @staticmethod
    def shapes(slabs, count):
        return tuple(jax.ShapeDtypeStruct((count,) + s.shape, s.dtype) for s in slabs)


def weights_kernel(count, slabs, swaps, *refs):
    refs = list(refs)

    def take(number):
        taken = refs[:number]
        del refs[:number]
        return taken

    sources, given = take(slabs), take(swaps)
    targets, paired, (zero_ref,) = take(slabs), take(swaps), take(1)
    stages = take(swaps)
    load_sem, keep_sem, swap_send, swap_recv = take(4)
    plan = Slabs(count, sources, targets, *refs)
    c, w = lax.axis_index("ctx"), lax.axis_index("wt")
    side = lax.rem(w, 2)
    partner = (c, flip(w, 1))
    greet(plan.devices() + [plan.near])

    def swap(i):
        return remote(given[i], paired[i].at[side], swap_send.at[i], swap_recv.at[i], partner)

    def load(i):
        return pltpu.make_async_copy(given[i], stages[i], load_sem.at[i])

    def keep(i):
        return pltpu.make_async_copy(stages[i], paired[i].at[side], keep_sem.at[i])

    plan.start()
    for i in range(swaps):
        swap(i).start()
        load(i).start()
    zero_ref[...] = jnp.zeros_like(zero_ref)
    for i in range(swaps):
        load(i).wait()
        keep(i).start()
    plan.relay()
    plan.finish()
    for i in range(swaps):
        keep(i).wait()
        swap(i).wait()


def gather_weights(slabs, swaps):
    count = lax.axis_size("wt")
    dma = pltpu.SemaphoreType.DMA((len(swaps),))
    pairs = tuple(jax.ShapeDtypeStruct((2,) + s.shape, s.dtype) for s in swaps)
    shapes = Slabs.shapes(slabs, count) + pairs
    return pl.pallas_call(
        functools.partial(weights_kernel, count, len(slabs), len(swaps)),
        out_shape=shapes + (jax.ShapeDtypeStruct((8, 128), jnp.int32),),
        in_specs=[pl.BlockSpec(memory_space=pl.ANY)] * (len(slabs) + len(swaps)),
        out_specs=(pl.BlockSpec(memory_space=pl.ANY),) * len(shapes)
        + (pl.BlockSpec(memory_space=pltpu.VMEM),),
        scratch_shapes=[pltpu.VMEM(s.shape, s.dtype) for s in swaps]
        + [dma] * 4
        + Slabs.scratch(slabs, count),
        compiler_params=pltpu.CompilerParams(
            collective_id=1, has_side_effects=True, vmem_limit_bytes=WIDE
        ),
        cost_estimate=LONG,
        name="gather_weights",
    )(*slabs, *swaps)


def gather_kernel(chips, downward, paired, count, slabs, passed, rows_ref, *refs):
    refs = list(refs)

    def take(number):
        taken = refs[:number]
        del refs[:number]
        return taken

    hops = count // 2 - 1
    sources, moved = take(slabs), take(passed)
    (out_ref,), targets, landed, (zero_ref,) = take(1), take(slabs), take(passed * hops), take(1)
    (stage,) = take(1)
    here, up_send, up_recv, down_send, down_recv, pair_send, pair_recv, near_send, near_recv = take(9)
    plan = Slabs(count, sources, targets, *take(6 + slabs)) if slabs else None
    pass_send, pass_recv = take(2) if passed else (None, None)
    zero_ref[...] = jnp.zeros_like(zero_ref)
    c, w = lax.axis_index("ctx"), lax.axis_index("wt")
    z = c // 2
    core = lax.rem(c, 2)
    side = lax.rem(w, 2) if paired else 0
    near, partner = (flip(c, 1), w), (c, flip(w, 1))
    above = (lax.rem(c + 2, 2 * chips), w)
    below = (lax.rem(c + 2 * chips - 2, 2 * chips), w)
    far = [(c, flip(w, 2 * d + 2)) for d in range(hops)]
    greet([near, above, below] + ([partner] if paired else []) + (plan.devices() if plan else []) + (far if passed else []))

    def onward(i, d):
        return remote(
            moved[i], landed[i * hops + d], pass_send.at[i, d], pass_recv.at[i, d], far[d]
        )

    def spot(chip, which, parity):
        return out_ref.at[chip, which, parity]

    def lift(chip, source):
        return remote(source, spot(chip, side, core), up_send.at[chip], up_recv.at[chip], above)

    def drop(chip, source):
        return remote(source, spot(chip, side, core), down_send.at[chip], down_recv.at[chip], below)

    def give(chip, source):
        return remote(source, spot(chip, side, core), pair_send.at[chip], pair_recv.at[chip], partner)

    def taken(chip):
        return remote(
            spot(chip, 1 - side, core), spot(chip, 1 - side, core), pair_send.at[chip], pair_recv.at[chip], partner
        )

    def hand(chip, which, source):
        return remote(source, spot(chip, which, core), near_send.at[chip, which], near_recv.at[chip, which], near)

    def handed(chip, which):
        there = spot(chip, which, 1 - core)
        return remote(there, there, near_send.at[chip, which], near_recv.at[chip, which], near)

    def settle_pair(chip):
        taken(chip).wait_recv()
        hand(chip, 1 - side, spot(chip, 1 - side, core)).start()

    load = pltpu.make_async_copy(rows_ref, stage, here.at[0])
    keep = pltpu.make_async_copy(stage, spot(z, side, core), here.at[1])
    load.start()
    pl.when(z < chips - 1)(lambda: lift(z, rows_ref).start())
    if downward:
        pl.when(z > 0)(lambda: drop(z, rows_ref).start())
    if paired:
        give(z, rows_ref).start()
    hand(z, side, rows_ref).start()
    if plan:
        plan.start()
    for d in range(hops):
        for i in range(passed):
            onward(i, d).start()
    load.wait()
    keep.start()
    for step in range(1, chips):
        low, high = z - step, z + step

        @pl.when(low >= 0)
        def _():
            lift(low, spot(low, side, core)).wait_recv()
            pl.when(z < chips - 1)(lambda: lift(low, spot(low, side, core)).start())
            if paired:
                give(low, spot(low, side, core)).start()
            hand(low, side, spot(low, side, core)).start()

        if downward:

            @pl.when(high < chips)
            def _():
                drop(high, spot(high, side, core)).wait_recv()
                pl.when(z > 0)(lambda: drop(high, spot(high, side, core)).start())
                if paired:
                    give(high, spot(high, side, core)).start()
                hand(high, side, spot(high, side, core)).start()

        if paired:
            if step == 1:
                settle_pair(z)
            else:
                pl.when(z - step + 1 >= 0)(lambda: settle_pair(z - step + 1))
                pl.when(z + step - 1 < chips)(lambda: settle_pair(z + step - 1))
    if paired:
        pl.when(z - chips + 1 >= 0)(lambda: settle_pair(z - chips + 1))
        pl.when(z + chips - 1 < chips)(lambda: settle_pair(z + chips - 1))
    keep.wait()
    if plan:
        plan.relay()
        plan.finish()

    def finish(chip):
        here_now = spot(chip, side, core)
        pl.when((z < chips - 1) & (chip <= z))(lambda: lift(chip, here_now).wait_send())
        if downward:
            pl.when((z > 0) & (chip >= z))(lambda: drop(chip, here_now).wait_send())
        if paired:
            give(chip, here_now).wait_send()
            for which in range(2):
                hand(chip, which, spot(chip, which, core)).wait_send()
                handed(chip, which).wait_recv()
        else:
            hand(chip, side, here_now).wait_send()
            handed(chip, side).wait_recv()

    for chip in range(chips):
        if downward:
            finish(chip)
        else:
            pl.when(chip <= z)(lambda: finish(chip))
    for d in range(hops):
        for i in range(passed):
            onward(i, d).wait()


def gather_rows(rows, collective_id, downward, paired, name, slabs=(), moved=()):
    chips = lax.axis_size("ctx") // 2
    count = lax.axis_size("wt")
    hops = count // 2 - 1
    line = pltpu.SemaphoreType.DMA((chips,))
    both = pltpu.SemaphoreType.DMA((chips, 2))
    shape = jax.ShapeDtypeStruct((chips, 2 if paired else 1, 2) + rows.shape, rows.dtype)
    landed = tuple(jax.ShapeDtypeStruct(m.shape, m.dtype) for m in moved for _ in range(hops))
    shapes = (shape,) + Slabs.shapes(slabs, count) + landed
    *results, zero = pl.pallas_call(
        functools.partial(gather_kernel, chips, downward, paired, count, len(slabs), len(moved)),
        out_shape=shapes + (jax.ShapeDtypeStruct((8, 128), jnp.int32),),
        in_specs=[pl.BlockSpec(memory_space=pl.ANY)] * (1 + len(slabs) + len(moved)),
        out_specs=(pl.BlockSpec(memory_space=pl.ANY),) * len(shapes)
        + (pl.BlockSpec(memory_space=pltpu.VMEM),),
        scratch_shapes=[pltpu.VMEM(rows.shape, rows.dtype), pltpu.SemaphoreType.DMA((2,))]
        + [line] * 6
        + [both] * 2
        + (Slabs.scratch(slabs, count) if slabs else [])
        + ([pltpu.SemaphoreType.DMA((len(moved), hops))] * 2 if moved else []),
        compiler_params=pltpu.CompilerParams(
            collective_id=collective_id, has_side_effects=True, vmem_limit_bytes=WIDE
        ),
        cost_estimate=LONG,
        name=name,
    )(rows, *slabs, *moved)
    return results + [zero[0, 0]]


def scatter_kernel(chips, upward, paired, pieces, partial_ref, out_ref, own, sib, mate, low_in, high_in, load, near_send, near_recv, pair_send, pair_recv, up_send, up_recv, down_send, down_recv):
    c, w = lax.axis_index("ctx"), lax.axis_index("wt")
    z = c // 2
    core = lax.rem(c, 2)
    side = lax.rem(w, 2) if paired else 0
    sides = 2 if paired else 1
    near, partner = (flip(c, 1), w), (c, flip(w, 1))
    above = (lax.rem(c + 2, 2 * chips), w)
    below = (lax.rem(c + 2 * chips - 2, 2 * chips), w)
    rows = own.shape[2] // pieces
    greet([near, above, below] + ([partner] if paired else []))
    order = []
    for i in range(chips // 2):
        order += [chips - 1 - i, i]
    if chips % 2:
        order.append(chips // 2)
    if not upward:
        order = list(range(chips))

    def wanted(chip, action):
        if upward:
            action()
        else:
            pl.when(chip <= z)(action)

    def fetch(chip, which):
        return pltpu.make_async_copy(
            partial_ref.at[chip, which, core], own.at[chip, which], load.at[chip, which]
        )

    def hand(chip, which):
        return remote(
            partial_ref.at[chip, which, 1 - core],
            sib.at[chip, which],
            near_send.at[chip, which],
            near_recv.at[chip, which],
            near,
        )

    def cut(piece):
        return pl.ds(piece * rows, rows)

    def give(chip, piece):
        return remote(
            own.at[chip, 1 - side, cut(piece)],
            mate.at[chip, cut(piece)],
            pair_send.at[chip, piece],
            pair_recv.at[chip, piece],
            partner,
        )

    def lift(chip, piece):
        return remote(
            own.at[chip, side, cut(piece)],
            low_in.at[chip, cut(piece)],
            up_send.at[chip, piece],
            up_recv.at[chip, piece],
            above,
        )

    def drop(chip, piece):
        return remote(
            own.at[chip, side, cut(piece)],
            high_in.at[chip, cut(piece)],
            down_send.at[chip, piece],
            down_recv.at[chip, piece],
            below,
        )

    def add_into(chip, which, piece, other):
        spot = own.at[chip, which, cut(piece)]
        spot[...] = spot[...] + other[...]

    for chip in order:

        def begin(chip=chip):
            for which in range(sides):
                hand(chip, which).start()
                fetch(chip, which).start()

        wanted(chip, begin)

    def meet(chip):
        for which in range(sides):
            fetch(chip, which).wait()
            hand(chip, which).wait_recv()
        for piece in range(pieces):
            if paired:
                add_into(chip, 1 - side, piece, sib.at[chip, 1 - side, cut(piece)])
                give(chip, piece).start()
            add_into(chip, side, piece, sib.at[chip, side, cut(piece)])

    def travel(chip):
        for piece in range(pieces):
            if paired:
                give(chip, piece).wait_recv()
                add_into(chip, side, piece, mate.at[chip, cut(piece)])
            if upward:

                @pl.when(z < chip)
                def _():
                    @pl.when(z > 0)
                    def _():
                        lift(chip, piece).wait_recv()
                        add_into(chip, side, piece, low_in.at[chip, cut(piece)])

                    lift(chip, piece).start()

            @pl.when(z > chip)
            def _():
                @pl.when(z < chips - 1)
                def _():
                    drop(chip, piece).wait_recv()
                    add_into(chip, side, piece, high_in.at[chip, cut(piece)])

                drop(chip, piece).start()

    for i, chip in enumerate(order):
        wanted(chip, lambda: meet(chip))
        if i >= 1:
            wanted(order[i - 1], lambda: travel(order[i - 1]))
    wanted(order[-1], lambda: travel(order[-1]))
    for piece in range(pieces):
        out_ref[cut(piece), :] = own.at[z, side, cut(piece)][...].astype(jnp.float32)
    for piece in range(pieces):
        if upward:

            @pl.when(z > 0)
            def _():
                lift(z, piece).wait_recv()
                out_ref[cut(piece), :] += low_in.at[z, cut(piece)][...].astype(jnp.float32)

        @pl.when(z < chips - 1)
        def _():
            drop(z, piece).wait_recv()
            out_ref[cut(piece), :] += high_in.at[z, cut(piece)][...].astype(jnp.float32)

    def finish(chip):
        for which in range(sides):
            hand(chip, which).wait_send()
        for piece in range(pieces):
            if paired:
                give(chip, piece).wait_send()
            if upward:
                pl.when(z < chip)(lambda: lift(chip, piece).wait_send())
            pl.when(z > chip)(lambda: drop(chip, piece).wait_send())

    for chip in order:
        wanted(chip, lambda: finish(chip))


def scatter_rows(partial, collective_id, upward, paired, name):
    chips, sides, _, tokens, width = partial.shape
    pieces = 2
    dma = pltpu.SemaphoreType.DMA
    block = (tokens, width)
    return pl.pallas_call(
        functools.partial(scatter_kernel, chips, upward, paired, pieces),
        out_shape=jax.ShapeDtypeStruct(block, jnp.float32),
        in_specs=[pl.BlockSpec(memory_space=pl.ANY)],
        out_specs=pl.BlockSpec(memory_space=pltpu.VMEM),
        scratch_shapes=[
            pltpu.VMEM((chips, sides) + block, jnp.bfloat16),
            pltpu.VMEM((chips, sides) + block, jnp.bfloat16),
            pltpu.VMEM((chips if paired else 1,) + block, jnp.bfloat16),
            pltpu.VMEM((chips if upward else 1,) + block, jnp.bfloat16),
            pltpu.VMEM((chips,) + block, jnp.bfloat16),
            dma((chips, 2)),
            dma((chips, 2)),
            dma((chips, 2)),
        ]
        + [dma((chips, pieces))] * 6,
        compiler_params=pltpu.CompilerParams(
            collective_id=collective_id, has_side_effects=True, vmem_limit_bytes=WIDE
        ),
        cost_estimate=LONG if paired else CHEAP,
        name=name,
    )(partial)


def dense_kernel(chips, count, matrices, pieces, *refs):
    refs = list(refs)

    def take(number):
        taken = refs[:number]
        del refs[:number]
        return taken

    grads, outs = take(matrices), take(matrices)
    own, sib, mates, low, final = (take(matrices) for _ in range(5))
    (load, near_send, near_recv, send, recv, low_send, low_recv, back_send, back_recv, last_send, last_recv, keep) = refs
    c, w = lax.axis_index("ctx"), lax.axis_index("wt")
    z = c // 2
    core = lax.rem(c, 2)
    near = (flip(c, 1), w)
    above = (lax.rem(c + 2, 2 * chips), w)
    below = (lax.rem(c + 2 * chips - 2, 2 * chips), w)
    peers = [flip(w, d) for d in range(1, count)]
    greet([near, above, below] + [(c, p) for p in peers])

    def span(j, parity=None):
        m, first, rows = pieces[j]
        if parity is None:
            return pl.ds(first, rows)
        half = grads[m].shape[1] // 2
        return pl.ds(pl.multiple_of(parity * half + first, 16), rows)

    def fetch(j):
        m = pieces[j][0]
        return pltpu.make_async_copy(grads[m].at[:, span(j, core)], own[m].at[:, span(j)], load.at[j])

    def hand(j):
        m = pieces[j][0]
        return remote(
            grads[m].at[:, span(j, 1 - core)], sib[m].at[:, span(j)], near_send.at[j], near_recv.at[j], near
        )

    def give(j, d):
        m = pieces[j][0]
        return remote(
            own[m].at[peers[d], span(j)], mates[m].at[d, span(j)], send.at[j, d], recv.at[j, d], (c, peers[d])
        )

    def total(j):
        return own[pieces[j][0]].at[w, span(j)]

    def add(spot, other):
        spot[...] = spot[...] + other[...]

    def start(j):
        hand(j).start()
        fetch(j).start()

    def share(j):
        m = pieces[j][0]
        fetch(j).wait()
        hand(j).wait_recv()
        for d in range(count - 1):
            add(own[m].at[peers[d], span(j)], sib[m].at[peers[d], span(j)])
            give(j, d).start()
        add(total(j), sib[m].at[w, span(j)])

    def collect(j):
        m = pieces[j][0]
        value = total(j)[...].astype(jnp.float32)
        for d in range(count - 1):
            give(j, d).wait_recv()
            value = value + mates[m][d, span(j), :].astype(jnp.float32)
        total(j)[...] = value.astype(jnp.bfloat16)

    def line(j):
        return (z, above, below) if j % 2 == 0 else (chips - 1 - z, below, above)

    def onward(j):
        m = pieces[j][0]
        return remote(total(j), low[m].at[span(j)], low_send.at[j], low_recv.at[j], line(j)[1])

    def backward(j):
        spot = final[pieces[j][0]].at[span(j)]
        return remote(spot, spot, back_send.at[j], back_recv.at[j], line(j)[2])

    def across(j, parity):
        m = pieces[j][0]
        return remote(
            final[m].at[span(j)], outs[m].at[span(j, parity)], last_send.at[j], last_recv.at[j], near
        )

    def store(j):
        m = pieces[j][0]
        return pltpu.make_async_copy(final[m].at[span(j)], outs[m].at[span(j, core)], keep.at[j])

    def accumulate(j):
        place = line(j)[0]
        m = pieces[j][0]

        @pl.when(place > 0)
        def _():
            onward(j).wait_recv()
            add(total(j), low[m].at[span(j)])

        @pl.when(place < chips - 1)
        def _():
            onward(j).start()

        @pl.when(place == chips - 1)
        def _():
            final[m][span(j), :] = total(j)[...]
            backward(j).start()
            across(j, core).start()
            store(j).start()

    def spread(j):
        place = line(j)[0]

        @pl.when(place < chips - 1)
        def _():
            backward(j).wait_recv()
            pl.when(place > 0)(lambda: backward(j).start())
            across(j, core).start()
            store(j).start()

    number = len(pieces)
    for j in range(number):
        start(j)
    for j in range(number):
        share(j)
    last = chips - 1
    for t in range(number + 2 * last):
        if t < number:
            collect(t)
        for hop in range(2 * last, -1, -1):
            j = t - hop
            if not 0 <= j < number:
                continue
            if hop <= last:
                pl.when(line(j)[0] == hop)(lambda: accumulate(j))
            if hop > last:
                pl.when(line(j)[0] == 2 * last - hop)(lambda: spread(j))
    for j in range(number):
        place = line(j)[0]
        hand(j).wait_send()
        for d in range(count - 1):
            give(j, d).wait_send()
        pl.when(place < chips - 1)(lambda: onward(j).wait_send())
        pl.when(place > 0)(lambda: backward(j).wait_send())
        across(j, core).wait_send()
        across(j, 1 - core).wait_recv()
        store(j).wait()


def reduce_dense(grads):
    count = lax.axis_size("wt")
    chips = lax.axis_size("ctx") // 2
    shapes = [(g.shape[0] // count, g.shape[1]) for g in grads]
    pieces = []
    for m, (rows, _) in enumerate(shapes):
        half, width = rows // 2, shapes[m][1]
        cuts = max(n for n in range(1, 5) if half % (16 * n) == 0 and (n == 1 or half * width > 120000 * (n - 1)))
        for i in range(cuts):
            pieces.append((m, i * (rows // 2 // cuts), rows // 2 // cuts))
    halves = [(rows // 2, width) for rows, width in shapes]
    dma = pltpu.SemaphoreType.DMA
    one, many = dma((len(pieces),)), dma((len(pieces), count - 1))
    return pl.pallas_call(
        functools.partial(dense_kernel, chips, count, len(grads), tuple(pieces)),
        out_shape=[jax.ShapeDtypeStruct(s, jnp.bfloat16) for s in shapes],
        in_specs=[pl.BlockSpec(memory_space=pl.ANY)] * len(grads),
        out_specs=[pl.BlockSpec(memory_space=pl.ANY)] * len(grads),
        scratch_shapes=[pltpu.VMEM((count,) + h, jnp.bfloat16) for h in halves]
        + [pltpu.VMEM((count,) + h, jnp.bfloat16) for h in halves]
        + [pltpu.VMEM((count - 1,) + h, jnp.bfloat16) for h in halves]
        + [pltpu.VMEM(h, jnp.bfloat16) for h in halves]
        + [pltpu.VMEM(h, jnp.bfloat16) for h in halves]
        + [one, one, one, many, many, one, one, one, one, one, one, one],
        compiler_params=pltpu.CompilerParams(
            collective_id=7, has_side_effects=True, vmem_limit_bytes=WIDE
        ),
        cost_estimate=LONG,
        name="reduce_dense",
    )(*[g.reshape((count,) + s) for g, s in zip(grads, shapes)])


def dot_of(a, b, left, right):
    return lax.dot_general(
        a, b, (((left,), (right,)), ((), ())), preferred_element_type=jnp.float32
    )


def stacked_heads(ref):
    return jnp.concatenate(
        [ref[:, h * HEAD_DIM : (h + 1) * HEAD_DIM] for h in range(ref.shape[1] // HEAD_DIM)], axis=0
    )


exponent_scale = HEAD_DIM ** (-0.5) * math.log2(math.e)


def attend_kernel(place_ref, query_ref, both_ref, row_ref, column_ref, out_ref, log_ref, best, total, accum):
    tokens = query_ref.shape[0]
    group = query_ref.shape[1] // HEAD_DIM
    width = 2 * tokens
    place = place_ref[0]
    queries = stacked_heads(query_ref)
    best[...] = jnp.full_like(best, masked_value)
    total[...] = jnp.zeros_like(total)
    accum[...] = jnp.zeros_like(accum)
    query_pos = place * tokens + lax.broadcasted_iota(jnp.int32, (tokens, width), 0)
    key_pos = lax.broadcasted_iota(jnp.int32, (tokens, width), 1)

    def step(j, carry):
        span = pl.ds(pl.multiple_of(j * width, width), width)
        allowed = (key_pos + j * width <= query_pos) & (row_ref[0:1, span] == column_ref[:, 0:1])
        bias = jnp.where(allowed, 0.0, masked_value)
        scores = dot_of(queries, both_ref[span, :HEAD_DIM], 1, 1)
        scores = (scores.reshape(group, tokens, width) + bias[None]).reshape(group * tokens, width)
        newest = jnp.maximum(best[...], jnp.max(scores, axis=1, keepdims=True))
        factor = jnp.exp2((best[...] - newest) * exponent_scale)
        weights = jnp.exp2((scores - newest[:, :1]) * exponent_scale)
        total[...] = total[...] * factor + jnp.sum(weights, axis=1, keepdims=True)
        accum[...] = accum[...] * factor + dot_of(
            weights.astype(jnp.bfloat16), both_ref[span, HEAD_DIM:], 1, 0
        )
        best[...] = newest
        return carry

    lax.fori_loop(0, place // 2 + 1, step, 0)
    heads = accum[...] / total[...]
    for h in range(group):
        out_ref[:, h * HEAD_DIM : (h + 1) * HEAD_DIM] = heads[h * tokens : (h + 1) * tokens]
    logs = best[...] * exponent_scale + jnp.log2(total[...])
    log_ref[0] = jnp.transpose(logs)[:8]


def attend(place, projected, both, seg_row, seg_column):
    tokens = projected.shape[0]
    group = HEADS // KV_HEADS
    rows, span = group * tokens, both.shape[0]
    stat = pltpu.VMEM((rows, HEAD_DIM), jnp.float32)
    return pl.pallas_call(
        attend_kernel,
        grid=(KV_HEADS,),
        out_shape=(
            jax.ShapeDtypeStruct((tokens, HEADS * HEAD_DIM), jnp.float32),
            jax.ShapeDtypeStruct((KV_HEADS, 8, rows), jnp.float32),
        ),
        in_specs=[
            pl.BlockSpec(memory_space=pltpu.SMEM),
            pl.BlockSpec((tokens, group * HEAD_DIM), lambda g: (0, g)),
            pl.BlockSpec((span, 2 * HEAD_DIM), lambda g: (0, g)),
            pl.BlockSpec((1, span), lambda g: (0, 0)),
            pl.BlockSpec((tokens, 1), lambda g: (0, 0)),
        ],
        out_specs=(
            pl.BlockSpec((tokens, group * HEAD_DIM), lambda g: (0, g)),
            pl.BlockSpec((1, 8, rows), lambda g: (g, 0, 0)),
        ),
        scratch_shapes=[stat, stat, stat],
        compiler_params=pltpu.CompilerParams(vmem_limit_bytes=WIDE),
        cost_estimate=CHEAP,
        name="attend",
    )(place, projected, both, seg_row, seg_column)


def attend_back_kernel(place_ref, query_ref, both_ref, row_ref, column_ref, heads_ref, grad_ref, log_ref, grad_query_ref, grad_both_ref, accum):
    tokens = query_ref.shape[0]
    group = query_ref.shape[1] // HEAD_DIM
    width = 2 * tokens
    rows = group * tokens
    scale = HEAD_DIM ** (-0.5)
    place = place_ref[0]
    queries, grads = stacked_heads(query_ref), stacked_heads(grad_ref)
    product = grads.astype(jnp.float32) * stacked_heads(heads_ref)
    delta = jnp.sum(product, axis=1, keepdims=True)
    delta = jnp.transpose(jnp.broadcast_to(delta, (rows, HEAD_DIM)))[0:1]
    logs = log_ref[0, 0:1, :]
    accum[...] = jnp.zeros_like(accum)
    grad_both_ref[...] = jnp.zeros_like(grad_both_ref)
    query_pos = place * tokens + lax.broadcasted_iota(jnp.int32, (width, tokens), 1)
    key_pos = lax.broadcasted_iota(jnp.int32, (width, tokens), 0)

    def step(j, carry):
        span = pl.ds(pl.multiple_of(j * width, width), width)
        allowed = (key_pos + j * width <= query_pos) & (column_ref[span, 0:1] == row_ref[0:1, :])
        bias = jnp.where(allowed, 0.0, masked_value)
        bias = jnp.concatenate([bias] * group, axis=1)
        keys, values = both_ref[span, :HEAD_DIM], both_ref[span, HEAD_DIM:]
        scores = dot_of(keys, queries, 1, 1)
        probs = jnp.exp2(scores * exponent_scale + bias - logs)
        grad_probs = dot_of(values, grads, 1, 1)
        grad_scores = (probs * (grad_probs - delta)).astype(jnp.bfloat16)
        accum[...] += dot_of(grad_scores, keys, 0, 0)
        grad_both_ref[span, :HEAD_DIM] = (dot_of(grad_scores, queries, 1, 0) * scale).astype(jnp.bfloat16)
        grad_both_ref[span, HEAD_DIM:] = dot_of(probs.astype(jnp.bfloat16), grads, 1, 0).astype(jnp.bfloat16)
        return carry

    lax.fori_loop(0, place // 2 + 1, step, 0)
    grad_queries = (accum[...] * scale).astype(jnp.bfloat16)
    for h in range(group):
        grad_query_ref[:, h * HEAD_DIM : (h + 1) * HEAD_DIM] = grad_queries[h * tokens : (h + 1) * tokens]


def attend_back(place, projected, both, query_seg_row, seg_column, heads_out, grad_attended, logs):
    tokens = projected.shape[0]
    group = HEADS // KV_HEADS
    rows, span = group * tokens, both.shape[0]
    per_group = pl.BlockSpec((tokens, group * HEAD_DIM), lambda g: (0, g))
    return pl.pallas_call(
        attend_back_kernel,
        grid=(KV_HEADS,),
        out_shape=(
            jax.ShapeDtypeStruct((tokens, HEADS * HEAD_DIM), jnp.bfloat16),
            jax.ShapeDtypeStruct(both.shape, jnp.bfloat16),
        ),
        in_specs=[
            pl.BlockSpec(memory_space=pltpu.SMEM),
            per_group,
            pl.BlockSpec((span, 2 * HEAD_DIM), lambda g: (0, g)),
            pl.BlockSpec((1, tokens), lambda g: (0, 0)),
            pl.BlockSpec((span, 1), lambda g: (0, 0)),
            per_group,
            per_group,
            pl.BlockSpec((1, 8, rows), lambda g: (g, 0, 0)),
        ],
        out_specs=(per_group, pl.BlockSpec((span, 2 * HEAD_DIM), lambda g: (0, g))),
        scratch_shapes=[pltpu.VMEM((rows, HEAD_DIM), jnp.float32)],
        compiler_params=pltpu.CompilerParams(vmem_limit_bytes=WIDE),
        cost_estimate=CHEAP,
        name="attend_back",
    )(place, projected, both, query_seg_row, seg_column, heads_out, grad_attended, logs)


def pick_kernel(scaled, slot_ref, gate_ref, rows_ref, out_ref, scale_ref=None):
    local, depth = out_ref.shape[2], out_ref.shape[3]
    tokens = slot_ref.shape[3] // 2
    place = lax.broadcasted_iota(jnp.int32, (depth, tokens), 0)
    total, weight = None, None
    for core in range(2):
        span = slice(core * tokens, (core + 1) * tokens)
        chosen = [slot_ref[0, 0, e : e + 1, span] == place for e in range(local)]
        ones = jnp.concatenate([c.astype(jnp.float32) for c in chosen], axis=0).astype(jnp.bfloat16)
        rows = rows_ref[0, core, 0] if scaled else rows_ref[0, 0, core]
        term = jnp.dot(ones, rows, preferred_element_type=jnp.float32)
        total = term if total is None else total + term
        if scaled:
            gates = jnp.concatenate(
                [
                    jnp.sum(jnp.where(c, gate_ref[0, 0, e : e + 1, span], 0.0), axis=1, keepdims=True)
                    for e, c in enumerate(chosen)
                ],
                axis=0,
            )
            weight = gates if weight is None else weight + gates
    if scaled:
        total = total * weight
        scale_ref[0, 0] = jnp.broadcast_to(weight, (local * depth, 128)).reshape(local, depth, 128)
    out_ref[0, 0] = total.astype(jnp.bfloat16).reshape(local, depth, total.shape[1])


def pick_rows(rows, slots, gates, scaled):
    chips, sides, local, both = slots.shape
    tokens, width = both // 2, rows.shape[4]
    depth = 2 * CAP
    table = pl.BlockSpec((1, 1, local, both), lambda z, s: (z, s, 0, 0))
    shapes = [jax.ShapeDtypeStruct((chips, sides, local, depth, width), jnp.bfloat16)]
    specs = [pl.BlockSpec((1, 1, local, depth, width), lambda z, s: (z, s, 0, 0, 0))]
    if scaled:
        shapes.append(jax.ShapeDtypeStruct((chips, sides, local, depth, 128), jnp.float32))
        specs.append(pl.BlockSpec((1, 1, local, depth, 128), lambda z, s: (z, s, 0, 0, 0)))
        source = pl.BlockSpec((1, 2, 1, tokens, width), lambda z, s: (z, 0, s, 0, 0))
    else:
        source = pl.BlockSpec((1, 1, 2, tokens, width), lambda z, s: (z, s, 0, 0, 0))
    return pl.pallas_call(
        functools.partial(pick_kernel, scaled),
        grid=(chips, sides),
        out_shape=shapes,
        in_specs=[table, table, source],
        out_specs=specs,
        compiler_params=pltpu.CompilerParams(vmem_limit_bytes=WIDE),
        cost_estimate=CHEAP,
        name="pick_grads" if scaled else "pick_tokens",
    )(slots, gates, rows)


def spread_kernel(apart, slot_ref, rows_ref, out_ref):
    local, depth, width = rows_ref.shape[2:]
    tokens = out_ref.shape[3]
    place = lax.broadcasted_iota(jnp.int32, (depth, tokens), 0)
    rows = rows_ref[0, 0].reshape(local * depth, width)
    for core in range(2):
        span = slice(core * tokens, (core + 1) * tokens)
        ones = jnp.concatenate(
            [(slot_ref[0, 0, e : e + 1, span] == place).astype(jnp.float32) for e in range(local)], axis=0
        ).astype(jnp.bfloat16)
        spot = out_ref.at[0, core, 0] if apart else out_ref.at[0, 0, core]
        spot[...] = lax.dot_general(
            ones, rows, (((0,), (0,)), ((), ())), preferred_element_type=jnp.float32
        ).astype(jnp.bfloat16)


def spread_rows(rows, slots, name, apart):
    chips, sides, local, both = slots.shape
    depth, width = rows.shape[3:]
    tokens = both // 2
    return pl.pallas_call(
        functools.partial(spread_kernel, apart),
        grid=(chips, sides),
        out_shape=jax.ShapeDtypeStruct(
            (chips, 2, sides, tokens, width) if apart else (chips, sides, 2, tokens, width), jnp.bfloat16
        ),
        in_specs=[
            pl.BlockSpec((1, 1, local, both), lambda z, s: (z, s, 0, 0)),
            pl.BlockSpec((1, 1, local, depth, width), lambda z, s: (z, s, 0, 0, 0)),
        ],
        out_specs=pl.BlockSpec((1, 2, 1, tokens, width), lambda z, s: (z, 0, s, 0, 0))
        if apart
        else pl.BlockSpec((1, 1, 2, tokens, width), lambda z, s: (z, s, 0, 0, 0)),
        compiler_params=pltpu.CompilerParams(vmem_limit_bytes=WIDE),
        cost_estimate=CHEAP,
        name=name,
    )(slots, rows)


def expert_kernel(blocks, x_ref, g_ref, scale_ref, *refs):
    tall_refs, down_refs = refs[:blocks], refs[blocks : 2 * blocks]
    result_ref, back_ref, *grad_refs = refs[2 * blocks :]
    hops = len(grad_refs) // 3
    grad_gate_refs, grad_up_refs = grad_refs[:hops], grad_refs[hops : 2 * hops]
    grad_down_refs = grad_refs[2 * hops :]
    w = lax.axis_index("wt")
    chips, sides, _, depth, width = x_ref.shape
    rows = chips * sides * depth
    part = tall_refs[0].shape[2]
    nn, nt, tn = (((1,), (0,)), ((), ())), (((1,), (1,)), ((), ())), (((0,), (0,)), ((), ()))

    def dot(a, b, dims):
        return lax.dot_general(a, b, dims, preferred_element_type=jnp.float32)

    def columns(ref, q):
        if blocks == 1:
            return ref.at[:, :, 0]
        span = pl.ds(pl.multiple_of(flip(w, q) * part, 128), part)
        return ref.at[:, :, 0, :, span]

    def piece(ref, q):
        return columns(ref, q)[...].reshape(rows, part)

    gate, up, grad_inner = None, None, None
    for q in range(blocks):
        x = piece(x_ref, q)
        more_gate, more_up = dot(x, tall_refs[q][0, 0], nn), dot(x, tall_refs[q][0, 1], nn)
        gate, up = (more_gate, more_up) if q == 0 else (gate + more_gate, up + more_up)
    for q in range(blocks):
        more = dot(piece(g_ref, q), down_refs[q][0], nt)
        grad_inner = more if q == 0 else grad_inner + more
    sigmoid = jax.nn.sigmoid(gate)
    activated = gate * sigmoid
    inner = (activated * up).astype(jnp.bfloat16)
    grad_gate = (grad_inner * up * (sigmoid * (1.0 + gate * (1.0 - sigmoid)))).astype(jnp.bfloat16)
    grad_up = (grad_inner * activated).astype(jnp.bfloat16)
    scale = scale_ref[...].reshape(rows, 128)[:, :1]
    for q in range(blocks):
        result = dot(inner, down_refs[q][0], nn) * scale
        columns(result_ref, q)[...] = result.astype(jnp.bfloat16).reshape(chips, sides, depth, part)
        back = dot(grad_gate, tall_refs[q][0, 0], nt) + dot(grad_up, tall_refs[q][0, 1], nt)
        columns(back_ref, q)[...] = back.astype(jnp.bfloat16).reshape(chips, sides, depth, part)
        grad_down_refs[q // 2][q % 2, 0] = dot(inner, piece(g_ref, q), tn).astype(jnp.bfloat16)
        x = piece(x_ref, q)
        grad_gate_refs[q // 2][q % 2, 0] = dot(x, grad_gate, tn).astype(jnp.bfloat16)
        grad_up_refs[q // 2][q % 2, 0] = dot(x, grad_up, tn).astype(jnp.bfloat16)


def run_experts(x, g, scale, talls, downs):
    chips, sides, local, depth, width = x.shape
    blocks = len(talls)
    part, inner = talls[0].shape[2:]
    large = chips * sides * depth > 1024
    rows = pl.BlockSpec((chips, sides, 1, depth, width), lambda e: (0, 0, e, 0, 0))
    sources = pl.BlockSpec(
        (chips, sides, 1, depth, width),
        lambda e: (0, 0, e, 0, 0),
        pipeline_mode=pl.Buffered(1 if large else 2),
    )
    scales = pl.BlockSpec((chips, sides, 1, depth, 128), lambda e: (0, 0, e, 0, 0))
    tall = pl.BlockSpec((1, 2, part, inner), lambda e: (e, 0, 0, 0))
    flat = pl.BlockSpec((1, inner, part), lambda e: (e, 0, 0))
    hops, each = max(blocks // 2, 1), min(blocks, 2)
    tall_out = pl.BlockSpec((each, 1, part, inner), lambda e: (0, e, 0, 0))
    flat_out = pl.BlockSpec((each, 1, inner, part), lambda e: (0, e, 0, 0))
    return pl.pallas_call(
        functools.partial(expert_kernel, blocks),
        grid=(local,),
        out_shape=(
            jax.ShapeDtypeStruct(x.shape, jnp.bfloat16),
            jax.ShapeDtypeStruct(x.shape, jnp.bfloat16),
            *[jax.ShapeDtypeStruct((each, local, part, inner), jnp.bfloat16)] * (2 * hops),
            *[jax.ShapeDtypeStruct((each, local, inner, part), jnp.bfloat16)] * hops,
        ),
        in_specs=[sources, sources, scales] + [tall] * blocks + [flat] * blocks,
        out_specs=(rows, rows) + (tall_out,) * (2 * hops) + (flat_out,) * hops,
        compiler_params=pltpu.CompilerParams(vmem_limit_bytes=60 * 2**20),
        cost_estimate=CHEAP,
        name="experts",
    )(x, g, scale, *talls, *downs)


def place_kernel(arrivals, side_ref, *refs):
    own, other, more, outs = refs[:3], refs[3:6], refs[6 : 6 + 3 * arrivals], refs[6 + 3 * arrivals :]
    mine = pl.program_id(0) == side_ref[0]

    @pl.when(mine)
    def _():
        for i in range(3):
            value = own[i][0, 0].astype(jnp.float32)
            for m in more[i * arrivals : (i + 1) * arrivals]:
                value = value + m[0, 0].astype(jnp.float32)
            outs[i][0] = value

    @pl.when(jnp.logical_not(mine))
    def _():
        for i in range(3):
            outs[i][0] = other[i][0].astype(jnp.float32)


def place_experts(side, own, more, other):
    local = other[0].shape[0]
    arrivals = len(more[0])
    shapes = [o.shape[1:] for o in other]
    paired = [pl.BlockSpec((1, 1) + s, lambda h, e: (0, e, 0, 0)) for s in shapes]
    single = [pl.BlockSpec((1,) + s, lambda h, e: (e, 0, 0)) for s in shapes]
    return pl.pallas_call(
        functools.partial(place_kernel, arrivals),
        grid=(2, local),
        out_shape=[jax.ShapeDtypeStruct((2 * local,) + s, jnp.float32) for s in shapes],
        in_specs=[pl.BlockSpec(memory_space=pltpu.SMEM)]
        + paired
        + single
        + [p for p in paired for _ in range(arrivals)],
        out_specs=[pl.BlockSpec((1,) + s, lambda h, e: (h * local + e, 0, 0)) for s in shapes],
        compiler_params=pltpu.CompilerParams(vmem_limit_bytes=WIDE),
        cost_estimate=CHEAP,
        name="place_experts",
    )(side, *own, *other, *[m for group in more for m in group])


def swap_pairs(value, axis, distance):
    count = lax.axis_size(axis)
    return lax.ppermute(value, axis, [(i, i ^ distance) for i in range(count)])


def own_and_other(stacked, mine):
    return (
        lax.dynamic_index_in_dim(stacked, mine, 0, keepdims=False),
        lax.dynamic_index_in_dim(stacked, 1 - mine, 0, keepdims=False),
    )


def collect_expert(shard, side, pairs):
    local = shard.shape[0]
    kept, given = own_and_other(shard.reshape((2, local // 2) + shard.shape[1:]), side)
    return kept, swap_pairs(given, "wt", 1), [swap_pairs(kept, "wt", 2 * d) for d in range(1, pairs)]


def settle_blocks(blocks, index, axis):
    stacked = jnp.stack(blocks)
    return jnp.concatenate(
        [
            lax.dynamic_index_in_dim(stacked, jnp.bitwise_xor(j, index), 0, False)
            for j in range(len(blocks))
        ],
        axis=axis,
    )


def split_blocks(whole, index, count, axis):
    parts = jnp.stack(jnp.split(whole, count, axis=axis))
    return jnp.stack(
        [
            lax.dynamic_index_in_dim(parts, jnp.bitwise_xor(q, index), 0, False)
            for q in range(count)
        ]
    )


def body(
    hidden,
    segment_ids,
    routes,
    gates,
    cotangent,
    norm_one_gain,
    w_query,
    w_key,
    w_value,
    w_out,
    norm_two_gain,
    shared_gate,
    shared_up,
    shared_down,
    expert_gate,
    expert_up,
    expert_down,
):
    wt_index = lax.axis_index("wt")
    wt_count = lax.axis_size("wt")
    ctx_count = lax.axis_size("ctx")
    chips = ctx_count // 2
    pairs = wt_count // 2
    tokens, width_model = hidden.shape[1:]
    wide, kv_width = w_query.shape[1], w_key.shape[1]
    shared_width = shared_gate.shape[1]
    gates_here = gates[0]
    gate_high = gates_here.astype(jnp.bfloat16)
    gate_rest = gates_here - gate_high.astype(jnp.float32)
    gate_middle = gate_rest.astype(jnp.bfloat16)
    gate_low = (gate_rest - gate_middle.astype(jnp.float32)).astype(jnp.bfloat16)
    table = jnp.concatenate(
        [routes[0].astype(jnp.bfloat16), gate_high, gate_middle, gate_low], axis=1
    )
    grad_rows = cotangent[0]
    depth = norm_one_gain.shape[0]
    extra_rows = 16
    table_rows = extra_rows * width_model // tokens
    packed = jnp.pad(jnp.swapaxes(table, 0, 1), ((0, table_rows - 4 * TOPK), (0, 0)))
    extended = jnp.concatenate([grad_rows, packed.reshape(extra_rows, width_model)], axis=0)
    gain_pair = jnp.concatenate(
        [norm_one_gain[None], norm_two_gain[None], jnp.zeros((30, depth), jnp.bfloat16)]
    )
    query_weight, key_weight, value_weight, gains, grad_pair, zero = gather_weights(
        (w_query, w_key, w_value, gain_pair), (extended,)
    )
    query_weight = query_weight.reshape(-1, wide)
    key_weight = key_weight.reshape(-1, kv_width)
    value_weight = value_weight.reshape(-1, kv_width)
    zero = zero[0, 0]
    side = lax.rem(wt_index, 2)
    later = side + zero
    collected = [
        collect_expert(jnp.stack([expert_gate, expert_up], axis=1), later, pairs),
        collect_expert(expert_down, later, pairs),
    ]
    gain_one, gain_two = gains[:, 0].reshape(-1), gains[:, 1].reshape(-1)
    local = expert_gate.shape[0] // 2
    first_expert = (lax.axis_index("ctx") * 2 + side) * local

    inputs = hidden[0].astype(jnp.float32)
    offset = lax.axis_index("ctx") * tokens
    seg_all = segment_ids[0]
    query_seg = lax.dynamic_slice_in_dim(seg_all, offset, tokens)
    scale_one = inverse_rms(inputs)
    gain_one_full = gain_one.astype(jnp.float32)
    normed = (inputs * scale_one * gain_one_full).astype(jnp.bfloat16)

    def project(weight):
        return jnp.dot(normed, weight, preferred_element_type=jnp.float32).astype(jnp.bfloat16)

    queries = project(query_weight)
    fresh = jnp.stack(
        [
            project(key_weight).reshape(tokens, KV_HEADS, HEAD_DIM),
            project(value_weight).reshape(tokens, KV_HEADS, HEAD_DIM),
        ],
        axis=2,
    ).reshape(tokens, 2 * kv_width)
    both, out_weight, both_weight, down_weight, zero = gather_rows(
        fresh,
        2,
        False,
        False,
        "gather_keys",
        (w_out, jnp.concatenate([shared_gate, shared_up], axis=1), shared_down),
    )
    out_weight = out_weight.reshape(-1, out_weight.shape[2])
    both_weight = both_weight.reshape(-1, both_weight.shape[2])
    down_weight = down_weight.reshape(-1, down_weight.shape[2])
    both = both.reshape(-1, 2 * kv_width)

    grad_pair = lax.dynamic_index_in_dim(jnp.stack([grad_pair, grad_pair]), zero, 0, False)
    all_grads = lax.all_gather(grad_pair, "ctx", axis=0).reshape(
        chips, 2, 2, tokens + extra_rows, width_model
    )
    tables = all_grads[:, :, :, tokens:].reshape(chips, 2, 2, table_rows, tokens)[:, :, :, : 4 * TOPK]
    tables = jnp.transpose(tables.astype(jnp.float32), (0, 2, 3, 1, 4)).reshape(
        chips, 2, 4 * TOPK, 2 * tokens
    )
    table_routes, gate_parts = tables[:, :, :TOPK], tables[:, :, TOPK:]
    table_gates = (
        gate_parts[:, :, :TOPK] + gate_parts[:, :, TOPK : 2 * TOPK] + gate_parts[:, :, 2 * TOPK :]
    )
    experts_here = (first_expert + jnp.arange(local, dtype=jnp.int32)).astype(jnp.float32)
    named = table_routes[:, :, None] == experts_here[None, None, :, None, None]
    member = jnp.any(named, axis=3)
    slot_gates = jnp.sum(jnp.where(named, table_gates[:, :, None], 0.0), axis=3)
    earlier = (
        jnp.arange(2 * tokens)[:, None] < jnp.arange(2 * tokens)[None, :]
    ).astype(jnp.bfloat16)
    rank = jnp.dot(member.astype(jnp.bfloat16), earlier, preferred_element_type=jnp.float32)
    slots = jnp.where(member, rank.astype(jnp.int32), -1)

    place = lax.axis_index("ctx").astype(jnp.int32).reshape(1)
    seg_row, seg_column = seg_all[None, :], seg_all[:, None]
    attended_full, logs = attend(place, queries, both, seg_row, query_seg[:, None])
    attended = attended_full.astype(jnp.bfloat16)
    attended, collected = lax.optimization_barrier((attended, collected))
    middle = inputs + jnp.dot(attended, out_weight, preferred_element_type=jnp.float32)
    scale_two = inverse_rms(middle)
    gain_two_full = gain_two.astype(jnp.float32)
    normed_two = (middle * scale_two * gain_two_full).astype(jnp.bfloat16)

    all_rows, *landed, zero = gather_rows(
        normed_two, 3, True, True, "gather_tokens", (), [c[1] for c in collected]
    )

    def blocks_of(i):
        kept, paired, straight = collected[i]
        blocks = [kept, paired]
        for d in range(pairs - 1):
            blocks += [straight[d], landed[i * (pairs - 1) + d]]
        return blocks

    tall_blocks, down_blocks = blocks_of(0), blocks_of(1)
    (received_rows,) = pick_rows(all_rows, slots, slot_gates, False)
    grad_received, row_gates = pick_rows(all_grads, slots, slot_gates, True)
    if down_blocks[0].shape[2] % 128:
        results, backs, grads_gate, grads_up, grads_down = run_experts(
            received_rows,
            grad_received,
            row_gates,
            [settle_blocks(tall_blocks, wt_index, 2)],
            [settle_blocks(down_blocks, wt_index, 2)],
        )
        wholes = [
            split_blocks(grads_gate[0], wt_index, wt_count, 1),
            split_blocks(grads_up[0], wt_index, wt_count, 1),
            split_blocks(grads_down[0], wt_index, wt_count, 2),
        ]
        hop_grads = [[g[2 * d : 2 * d + 2] for d in range(pairs)] for g in wholes]
    else:
        results, backs, *rest = run_experts(
            received_rows, grad_received, row_gates, tall_blocks, down_blocks
        )
        hop_grads = [rest[i * pairs : (i + 1) * pairs] for i in range(3)]
    arrived = [[swap_pairs(g[d], "wt", 2 * d) for d in range(1, pairs)] for g in hop_grads]
    first_arrived, later_arrived = arrived[:1], arrived[1:]
    routed_grad = scatter_rows(
        spread_rows(backs, slots, "spread_grads", False), 5, True, True, "scatter_grads"
    )
    routed_grad, results, first_arrived = lax.optimization_barrier(
        (routed_grad, results, first_arrived)
    )
    spread = spread_rows(results, slots, "spread_results", True)
    partial = lax.psum_scatter(
        spread.reshape(ctx_count, 2, tokens, width_model), "ctx", scatter_dimension=0, tiled=True
    )[0]

    shared_parts = jnp.dot(normed_two, both_weight, preferred_element_type=jnp.float32)
    shared_gate_part, shared_up_part = shared_parts[:, :shared_width], shared_parts[:, shared_width:]
    shared_inner = (jax.nn.silu(shared_gate_part) * shared_up_part).astype(jnp.bfloat16)
    shared_result = jnp.dot(shared_inner, down_weight, preferred_element_type=jnp.float32)
    grad_out = grad_rows.astype(jnp.float32)
    grad_shared_down = jnp.einsum(
        "tf,td->fd", shared_inner, grad_rows, preferred_element_type=jnp.float32
    )
    grad_shared_inner = jnp.einsum(
        "td,fd->tf", grad_rows, down_weight, preferred_element_type=jnp.float32
    )
    grad_shared_gate_part = (
        grad_shared_inner * shared_up_part * silu_slope(shared_gate_part)
    ).astype(jnp.bfloat16)
    grad_shared_up_part = (grad_shared_inner * jax.nn.silu(shared_gate_part)).astype(jnp.bfloat16)
    grad_shared_parts = jnp.concatenate([grad_shared_gate_part, grad_shared_up_part], axis=1)
    grad_shared_both = jnp.einsum(
        "td,tf->df", normed_two, grad_shared_parts, preferred_element_type=jnp.float32
    )
    grad_normed_two = (
        jnp.einsum("tf,df->td", grad_shared_parts, both_weight, preferred_element_type=jnp.float32)
        + routed_grad
    )
    grad_gain_two = jnp.sum(grad_normed_two * middle * scale_two, axis=0)
    scaled_two = grad_normed_two * gain_two_full
    grad_middle = (
        grad_out
        + scale_two * scaled_two
        - middle * scale_two**3 * jnp.mean(scaled_two * middle, axis=-1, keepdims=True)
    )
    grad_branch = grad_middle.astype(jnp.bfloat16)
    grad_out_weight = jnp.einsum(
        "tq,td->qd", attended, grad_branch, preferred_element_type=jnp.float32
    )
    grad_attended = jnp.einsum(
        "td,qd->tq", grad_branch, out_weight, preferred_element_type=jnp.float32
    ).astype(jnp.bfloat16)
    grad_queries, grad_parts = attend_back(
        place, queries, both, query_seg[None, :], seg_column, attended_full, grad_attended, logs
    )
    grad_both = scatter_rows(
        grad_parts.reshape(chips, 1, 2, tokens, 2 * kv_width),
        6,
        False,
        False,
        "scatter_keys",
    ).astype(jnp.bfloat16)
    grad_both, later_arrived = lax.optimization_barrier((grad_both, later_arrived))
    arrived = first_arrived + later_arrived

    def crossed(own, more):
        total = own[1].astype(jnp.float32)
        for m in more:
            total = total + m[1].astype(jnp.float32)
        return swap_pairs(total.astype(jnp.bfloat16), "wt", 1)

    others = [crossed(g[0], a) for g, a in zip(hop_grads, arrived)]
    grad_both = grad_both.reshape(tokens, KV_HEADS, 2, HEAD_DIM)
    grad_keys = grad_both[:, :, 0].reshape(tokens, kv_width)
    grad_values = grad_both[:, :, 1].reshape(tokens, kv_width)

    def weight_grad(grad):
        return jnp.einsum("tc,tq->cq", normed, grad, preferred_element_type=jnp.float32).astype(
            jnp.bfloat16
        )

    def input_grad(grad, weight):
        return jnp.einsum("tq,cq->tc", grad, weight, preferred_element_type=jnp.float32)

    grad_normed = (
        input_grad(grad_queries, query_weight)
        + input_grad(grad_keys, key_weight)
        + input_grad(grad_values, value_weight)
    )
    grad_gain_one = jnp.sum(grad_normed * inputs * scale_one, axis=0)
    scaled_one = grad_normed * gain_one_full
    grad_inputs = (
        grad_middle
        + scale_one * scaled_one
        - inputs * scale_one**3 * jnp.mean(scaled_one * inputs, axis=-1, keepdims=True)
    )

    gain_grads = jnp.stack([grad_gain_one, grad_gain_two]).reshape(2, wt_count, 1, depth)
    gain_grads = jnp.pad(gain_grads.astype(jnp.bfloat16), ((0, 0), (0, 0), (0, 15), (0, 0)))
    gain_grads = jnp.swapaxes(gain_grads, 0, 1).reshape(wt_count * 32, depth)
    dense_grads = [
        weight_grad(grad_queries),
        grad_shared_both.astype(jnp.bfloat16),
        grad_out_weight.astype(jnp.bfloat16),
        grad_shared_down.astype(jnp.bfloat16),
        weight_grad(grad_keys),
        weight_grad(grad_values),
        gain_grads,
    ]
    dense_grads, partial = lax.optimization_barrier((dense_grads, partial))
    kept, given = own_and_other(partial, side)
    crossing = swap_pairs(given, "wt", 1)
    totals = reduce_dense(dense_grads)
    totals, others, crossing = lax.optimization_barrier((totals, others, crossing))
    routed = kept.astype(jnp.float32) + crossing.astype(jnp.float32)
    output = (middle + shared_result + routed).astype(jnp.bfloat16)
    sum_experts_gate, sum_experts_up, sum_experts_down = place_experts(
        side.astype(jnp.int32).reshape(1), [g[0] for g in hop_grads], arrived, others
    )
    final_query, final_shared, final_out, final_down, final_key, final_value, final_gains = [
        total.astype(jnp.float32) for total in totals
    ]
    final_gate, final_up = final_shared[:, :shared_width], final_shared[:, shared_width:]
    final_gain_one, final_gain_two = final_gains[0], final_gains[16]
    return (
        output[None],
        grad_inputs[None],
        final_gain_one,
        final_query,
        final_key,
        final_value,
        final_out,
        final_gain_two,
        final_gate,
        final_up,
        final_down,
        sum_experts_gate,
        sum_experts_up,
        sum_experts_down,
    )


def solution(mesh):
    placed = (
        P("wt", "ctx", None),
        P("wt", None),
        P("wt", "ctx", None),
        P("wt", "ctx", None),
        P("wt", "ctx", None),
        P("wt"),
        P("wt", None),
        P("wt", None),
        P("wt", None),
        P("wt", None),
        P("wt"),
        P("wt", None),
        P("wt", None),
        P("wt", None),
        P("ctx", "wt", None),
        P("ctx", "wt", None),
        P("ctx", None, "wt"),
    )
    return jax.shard_map(
        body,
        mesh=mesh,
        in_specs=placed,
        out_specs=(
            P("wt", "ctx", None),
            P("wt", "ctx", None),
            P("wt"),
            P("wt", None),
            P("wt", None),
            P("wt", None),
            P("wt", None),
            P("wt"),
            P("wt", None),
            P("wt", None),
            P("wt", None),
            P("ctx", "wt", None),
            P("ctx", "wt", None),
            P("ctx", None, "wt"),
        ),
        check_vma=False,
    )
```

```python
import functools
import math

import jax
import jax.numpy as jnp
from jax import lax
from jax.experimental import pallas as pl
from jax.experimental.pallas import tpu as pltpu
from jax.sharding import PartitionSpec as P

HEADS = 12
KV_HEADS = 4
HEAD_DIM = 128
EXPERTS = 64
TOPK = 6
CAP = 40


epsilon = 1e-05
masked_value = -1e30


def inverse_rms(rows):
    return lax.rsqrt(jnp.mean(rows * rows, axis=-1, keepdims=True) + epsilon)


def silu_slope(gate_part):
    sigmoid = jax.nn.sigmoid(gate_part)
    return sigmoid * (1.0 + gate_part * (1.0 - sigmoid))


MESH = pl.DeviceIdType.MESH
WIDE = 56 * 2**20
LONG = pl.CostEstimate(flops=0, bytes_accessed=2_000_000_000, transcendentals=0)
CHEAP = pl.CostEstimate(flops=0, bytes_accessed=4096, transcendentals=0)


def flip(index, distance):
    result = index
    bit = 1
    while bit <= distance:
        if distance // bit % 2:
            result = result + bit - 2 * bit * (index // bit % 2)
        bit *= 2
    return result


def remote(src, dst, send_sem, recv_sem, device):
    return pltpu.make_async_remote_copy(
        src_ref=src,
        dst_ref=dst,
        send_sem=send_sem,
        recv_sem=recv_sem,
        device_id=device,
        device_id_type=MESH,
    )


def greet(devices):
    barrier = pltpu.get_barrier_semaphore()
    for device in devices:
        pl.semaphore_signal(barrier, inc=1, device_id=device, device_id_type=MESH)
    pl.semaphore_wait(barrier, len(devices))


class Slabs:
    def __init__(self, count, sources, targets, here, there, send, recv, near_send, near_recv, *stages):
        self.c, self.w = lax.axis_index("ctx"), lax.axis_index("wt")
        self.core = lax.rem(self.c, 2)
        self.near = (flip(self.c, 1), self.w)
        self.peers = [flip(self.w, d) for d in range(1, count)]
        self.pairs = list(zip(sources, targets))
        self.here, self.there, self.send, self.recv = here, there, send, recv
        self.stages = stages
        self.near_send, self.near_recv = near_send, near_recv

    def devices(self):
        return [(self.c, p) for p in self.peers]

    def half(self, source, core):
        rows = source.shape[0] // 2
        return pl.ds(pl.multiple_of(core * rows, 16), rows)

    def push(self, i, s):
        source, target = self.pairs[s]
        part = self.half(source, self.core)
        return remote(
            source.at[part], target.at[self.w, part], self.send.at[s, i], self.recv.at[s, i], (self.c, self.peers[i])
        )

    def arrival(self, i, s):
        source, target = self.pairs[s]
        spot = target.at[self.peers[i], self.half(source, self.core)]
        return remote(spot, spot, self.send.at[s, i], self.recv.at[s, i], (self.c, self.peers[i]))

    def hand(self, i, s, core):
        source, target = self.pairs[s]
        spot = target.at[self.peers[i], self.half(source, core)]
        return remote(spot, spot, self.near_send.at[s, i], self.near_recv.at[s, i], self.near)

    def load(self, s):
        return pltpu.make_async_copy(self.pairs[s][0], self.stages[s], self.here.at[s])

    def keep(self, s):
        return pltpu.make_async_copy(self.stages[s], self.pairs[s][1].at[self.w], self.there.at[s])

    def every(self):
        return [(i, s) for s in range(len(self.pairs)) for i in range(len(self.peers))]

    def start(self):
        for i, s in self.every():
            self.push(i, s).start()
        for s in range(len(self.pairs)):
            self.load(s).start()

    def relay(self):
        for s in range(len(self.pairs)):
            self.load(s).wait()
            self.keep(s).start()
        for i, s in self.every():
            self.arrival(i, s).wait_recv()
            self.hand(i, s, self.core).start()

    def finish(self):
        for i, s in self.every():
            self.hand(i, s, 1 - self.core).wait_recv()
            self.hand(i, s, self.core).wait_send()
            self.push(i, s).wait_send()
        for s in range(len(self.pairs)):
            self.keep(s).wait()

    @staticmethod
    def scratch(slabs, count):
        dma = pltpu.SemaphoreType.DMA
        number = len(slabs)
        return (
            [dma((number,))] * 2
            + [dma((number, count - 1))] * 4
            + [pltpu.VMEM(s.shape, s.dtype) for s in slabs]
        )

    @staticmethod
    def shapes(slabs, count):
        return tuple(jax.ShapeDtypeStruct((count,) + s.shape, s.dtype) for s in slabs)


def weights_kernel(count, slabs, swaps, *refs):
    refs = list(refs)

    def take(number):
        taken = refs[:number]
        del refs[:number]
        return taken

    sources, given = take(slabs), take(swaps)
    targets, paired, (zero_ref,) = take(slabs), take(swaps), take(1)
    stages = take(swaps)
    load_sem, keep_sem, swap_send, swap_recv = take(4)
    plan = Slabs(count, sources, targets, *refs)
    c, w = lax.axis_index("ctx"), lax.axis_index("wt")
    side = lax.rem(w, 2)
    partner = (c, flip(w, 1))
    greet(plan.devices() + [plan.near])

    def swap(i):
        return remote(given[i], paired[i].at[side], swap_send.at[i], swap_recv.at[i], partner)

    def load(i):
        return pltpu.make_async_copy(given[i], stages[i], load_sem.at[i])

    def keep(i):
        return pltpu.make_async_copy(stages[i], paired[i].at[side], keep_sem.at[i])

    plan.start()
    for i in range(swaps):
        swap(i).start()
        load(i).start()
    zero_ref[...] = jnp.zeros_like(zero_ref)
    for i in range(swaps):
        load(i).wait()
        keep(i).start()
    plan.relay()
    plan.finish()
    for i in range(swaps):
        keep(i).wait()
        swap(i).wait()


def gather_weights(slabs, swaps):
    count = lax.axis_size("wt")
    dma = pltpu.SemaphoreType.DMA((len(swaps),))
    pairs = tuple(jax.ShapeDtypeStruct((2,) + s.shape, s.dtype) for s in swaps)
    shapes = Slabs.shapes(slabs, count) + pairs
    return pl.pallas_call(
        functools.partial(weights_kernel, count, len(slabs), len(swaps)),
        out_shape=shapes + (jax.ShapeDtypeStruct((8, 128), jnp.int32),),
        in_specs=[pl.BlockSpec(memory_space=pl.ANY)] * (len(slabs) + len(swaps)),
        out_specs=(pl.BlockSpec(memory_space=pl.ANY),) * len(shapes)
        + (pl.BlockSpec(memory_space=pltpu.VMEM),),
        scratch_shapes=[pltpu.VMEM(s.shape, s.dtype) for s in swaps]
        + [dma] * 4
        + Slabs.scratch(slabs, count),
        compiler_params=pltpu.CompilerParams(
            collective_id=1, has_side_effects=True, vmem_limit_bytes=WIDE
        ),
        cost_estimate=LONG,
        name="gather_weights",
    )(*slabs, *swaps)


def gather_kernel(chips, downward, paired, count, slabs, passed, rows_ref, *refs):
    refs = list(refs)

    def take(number):
        taken = refs[:number]
        del refs[:number]
        return taken

    hops = count // 2 - 1
    sources, moved = take(slabs), take(passed)
    (out_ref,), targets, landed, (zero_ref,) = take(1), take(slabs), take(passed * hops), take(1)
    (stage,) = take(1)
    here, up_send, up_recv, down_send, down_recv, pair_send, pair_recv, near_send, near_recv = take(9)
    plan = Slabs(count, sources, targets, *take(6 + slabs)) if slabs else None
    pass_send, pass_recv = take(2) if passed else (None, None)
    zero_ref[...] = jnp.zeros_like(zero_ref)
    c, w = lax.axis_index("ctx"), lax.axis_index("wt")
    z = c // 2
    core = lax.rem(c, 2)
    side = lax.rem(w, 2) if paired else 0
    near, partner = (flip(c, 1), w), (c, flip(w, 1))
    above = (lax.rem(c + 2, 2 * chips), w)
    below = (lax.rem(c + 2 * chips - 2, 2 * chips), w)
    far = [(c, flip(w, 2 * d + 2)) for d in range(hops)]
    greet([near, above, below] + ([partner] if paired else []) + (plan.devices() if plan else []) + (far if passed else []))

    def onward(i, d):
        return remote(
            moved[i], landed[i * hops + d], pass_send.at[i, d], pass_recv.at[i, d], far[d]
        )

    def spot(chip, which, parity):
        return out_ref.at[chip, which, parity]

    def lift(chip, source):
        return remote(source, spot(chip, side, core), up_send.at[chip], up_recv.at[chip], above)

    def drop(chip, source):
        return remote(source, spot(chip, side, core), down_send.at[chip], down_recv.at[chip], below)

    def give(chip, source):
        return remote(source, spot(chip, side, core), pair_send.at[chip], pair_recv.at[chip], partner)

    def taken(chip):
        return remote(
            spot(chip, 1 - side, core), spot(chip, 1 - side, core), pair_send.at[chip], pair_recv.at[chip], partner
        )

    def hand(chip, which, source):
        return remote(source, spot(chip, which, core), near_send.at[chip, which], near_recv.at[chip, which], near)

    def handed(chip, which):
        there = spot(chip, which, 1 - core)
        return remote(there, there, near_send.at[chip, which], near_recv.at[chip, which], near)

    def settle_pair(chip):
        taken(chip).wait_recv()
        hand(chip, 1 - side, spot(chip, 1 - side, core)).start()

    load = pltpu.make_async_copy(rows_ref, stage, here.at[0])
    keep = pltpu.make_async_copy(stage, spot(z, side, core), here.at[1])
    load.start()
    pl.when(z < chips - 1)(lambda: lift(z, rows_ref).start())
    if downward:
        pl.when(z > 0)(lambda: drop(z, rows_ref).start())
    if paired:
        give(z, rows_ref).start()
    hand(z, side, rows_ref).start()
    if plan:
        plan.start()
    for d in range(hops):
        for i in range(passed):
            onward(i, d).start()
    load.wait()
    keep.start()
    for step in range(1, chips):
        low, high = z - step, z + step

        @pl.when(low >= 0)
        def _():
            lift(low, spot(low, side, core)).wait_recv()
            pl.when(z < chips - 1)(lambda: lift(low, spot(low, side, core)).start())
            if paired:
                give(low, spot(low, side, core)).start()
            hand(low, side, spot(low, side, core)).start()

        if downward:

            @pl.when(high < chips)
            def _():
                drop(high, spot(high, side, core)).wait_recv()
                pl.when(z > 0)(lambda: drop(high, spot(high, side, core)).start())
                if paired:
                    give(high, spot(high, side, core)).start()
                hand(high, side, spot(high, side, core)).start()

        if paired:
            if step == 1:
                settle_pair(z)
            else:
                pl.when(z - step + 1 >= 0)(lambda: settle_pair(z - step + 1))
                pl.when(z + step - 1 < chips)(lambda: settle_pair(z + step - 1))
    if paired:
        pl.when(z - chips + 1 >= 0)(lambda: settle_pair(z - chips + 1))
        pl.when(z + chips - 1 < chips)(lambda: settle_pair(z + chips - 1))
    keep.wait()
    if plan:
        plan.relay()
        plan.finish()

    def finish(chip):
        here_now = spot(chip, side, core)
        pl.when((z < chips - 1) & (chip <= z))(lambda: lift(chip, here_now).wait_send())
        if downward:
            pl.when((z > 0) & (chip >= z))(lambda: drop(chip, here_now).wait_send())
        if paired:
            give(chip, here_now).wait_send()
            for which in range(2):
                hand(chip, which, spot(chip, which, core)).wait_send()
                handed(chip, which).wait_recv()
        else:
            hand(chip, side, here_now).wait_send()
            handed(chip, side).wait_recv()

    for chip in range(chips):
        if downward:
            finish(chip)
        else:
            pl.when(chip <= z)(lambda: finish(chip))
    for d in range(hops):
        for i in range(passed):
            onward(i, d).wait()


def gather_rows(rows, collective_id, downward, paired, name, slabs=(), moved=()):
    chips = lax.axis_size("ctx") // 2
    count = lax.axis_size("wt")
    hops = count // 2 - 1
    line = pltpu.SemaphoreType.DMA((chips,))
    both = pltpu.SemaphoreType.DMA((chips, 2))
    shape = jax.ShapeDtypeStruct((chips, 2 if paired else 1, 2) + rows.shape, rows.dtype)
    landed = tuple(jax.ShapeDtypeStruct(m.shape, m.dtype) for m in moved for _ in range(hops))
    shapes = (shape,) + Slabs.shapes(slabs, count) + landed
    *results, zero = pl.pallas_call(
        functools.partial(gather_kernel, chips, downward, paired, count, len(slabs), len(moved)),
        out_shape=shapes + (jax.ShapeDtypeStruct((8, 128), jnp.int32),),
        in_specs=[pl.BlockSpec(memory_space=pl.ANY)] * (1 + len(slabs) + len(moved)),
        out_specs=(pl.BlockSpec(memory_space=pl.ANY),) * len(shapes)
        + (pl.BlockSpec(memory_space=pltpu.VMEM),),
        scratch_shapes=[pltpu.VMEM(rows.shape, rows.dtype), pltpu.SemaphoreType.DMA((2,))]
        + [line] * 6
        + [both] * 2
        + (Slabs.scratch(slabs, count) if slabs else [])
        + ([pltpu.SemaphoreType.DMA((len(moved), hops))] * 2 if moved else []),
        compiler_params=pltpu.CompilerParams(
            collective_id=collective_id, has_side_effects=True, vmem_limit_bytes=WIDE
        ),
        cost_estimate=LONG,
        name=name,
    )(rows, *slabs, *moved)
    return results + [zero[0, 0]]


def scatter_kernel(chips, upward, paired, pieces, partial_ref, out_ref, own, sib, mate, low_in, high_in, load, near_send, near_recv, pair_send, pair_recv, up_send, up_recv, down_send, down_recv):
    c, w = lax.axis_index("ctx"), lax.axis_index("wt")
    z = c // 2
    core = lax.rem(c, 2)
    side = lax.rem(w, 2) if paired else 0
    sides = 2 if paired else 1
    near, partner = (flip(c, 1), w), (c, flip(w, 1))
    above = (lax.rem(c + 2, 2 * chips), w)
    below = (lax.rem(c + 2 * chips - 2, 2 * chips), w)
    rows = own.shape[2] // pieces
    greet([near, above, below] + ([partner] if paired else []))
    order = []
    for i in range(chips // 2):
        order += [chips - 1 - i, i]
    if chips % 2:
        order.append(chips // 2)
    if not upward:
        order = list(range(chips))

    def wanted(chip, action):
        if upward:
            action()
        else:
            pl.when(chip <= z)(action)

    def fetch(chip, which):
        return pltpu.make_async_copy(
            partial_ref.at[chip, which, core], own.at[chip, which], load.at[chip, which]
        )

    def hand(chip, which):
        return remote(
            partial_ref.at[chip, which, 1 - core],
            sib.at[chip, which],
            near_send.at[chip, which],
            near_recv.at[chip, which],
            near,
        )

    def cut(piece):
        return pl.ds(piece * rows, rows)

    def give(chip, piece):
        return remote(
            own.at[chip, 1 - side, cut(piece)],
            mate.at[chip, cut(piece)],
            pair_send.at[chip, piece],
            pair_recv.at[chip, piece],
            partner,
        )

    def lift(chip, piece):
        return remote(
            own.at[chip, side, cut(piece)],
            low_in.at[chip, cut(piece)],
            up_send.at[chip, piece],
            up_recv.at[chip, piece],
            above,
        )

    def drop(chip, piece):
        return remote(
            own.at[chip, side, cut(piece)],
            high_in.at[chip, cut(piece)],
            down_send.at[chip, piece],
            down_recv.at[chip, piece],
            below,
        )

    def add_into(chip, which, piece, other):
        spot = own.at[chip, which, cut(piece)]
        spot[...] = spot[...] + other[...]

    for chip in order:

        def begin(chip=chip):
            for which in range(sides):
                hand(chip, which).start()
                fetch(chip, which).start()

        wanted(chip, begin)

    def meet(chip):
        for which in range(sides):
            fetch(chip, which).wait()
            hand(chip, which).wait_recv()
        for piece in range(pieces):
            if paired:
                add_into(chip, 1 - side, piece, sib.at[chip, 1 - side, cut(piece)])
                give(chip, piece).start()
            add_into(chip, side, piece, sib.at[chip, side, cut(piece)])

    def travel(chip):
        for piece in range(pieces):
            if paired:
                give(chip, piece).wait_recv()
                add_into(chip, side, piece, mate.at[chip, cut(piece)])
            if upward:

                @pl.when(z < chip)
                def _():
                    @pl.when(z > 0)
                    def _():
                        lift(chip, piece).wait_recv()
                        add_into(chip, side, piece, low_in.at[chip, cut(piece)])

                    lift(chip, piece).start()

            @pl.when(z > chip)
            def _():
                @pl.when(z < chips - 1)
                def _():
                    drop(chip, piece).wait_recv()
                    add_into(chip, side, piece, high_in.at[chip, cut(piece)])

                drop(chip, piece).start()

    for i, chip in enumerate(order):
        wanted(chip, lambda: meet(chip))
        if i >= 1:
            wanted(order[i - 1], lambda: travel(order[i - 1]))
    wanted(order[-1], lambda: travel(order[-1]))
    for piece in range(pieces):
        out_ref[cut(piece), :] = own.at[z, side, cut(piece)][...].astype(jnp.float32)
    for piece in range(pieces):
        if upward:

            @pl.when(z > 0)
            def _():
                lift(z, piece).wait_recv()
                out_ref[cut(piece), :] += low_in.at[z, cut(piece)][...].astype(jnp.float32)

        @pl.when(z < chips - 1)
        def _():
            drop(z, piece).wait_recv()
            out_ref[cut(piece), :] += high_in.at[z, cut(piece)][...].astype(jnp.float32)

    def finish(chip):
        for which in range(sides):
            hand(chip, which).wait_send()
        for piece in range(pieces):
            if paired:
                give(chip, piece).wait_send()
            if upward:
                pl.when(z < chip)(lambda: lift(chip, piece).wait_send())
            pl.when(z > chip)(lambda: drop(chip, piece).wait_send())

    for chip in order:
        wanted(chip, lambda: finish(chip))


def scatter_rows(partial, collective_id, upward, paired, name):
    chips, sides, _, tokens, width = partial.shape
    pieces = 2
    dma = pltpu.SemaphoreType.DMA
    block = (tokens, width)
    return pl.pallas_call(
        functools.partial(scatter_kernel, chips, upward, paired, pieces),
        out_shape=jax.ShapeDtypeStruct(block, jnp.float32),
        in_specs=[pl.BlockSpec(memory_space=pl.ANY)],
        out_specs=pl.BlockSpec(memory_space=pltpu.VMEM),
        scratch_shapes=[
            pltpu.VMEM((chips, sides) + block, jnp.bfloat16),
            pltpu.VMEM((chips, sides) + block, jnp.bfloat16),
            pltpu.VMEM((chips if paired else 1,) + block, jnp.bfloat16),
            pltpu.VMEM((chips if upward else 1,) + block, jnp.bfloat16),
            pltpu.VMEM((chips,) + block, jnp.bfloat16),
            dma((chips, 2)),
            dma((chips, 2)),
            dma((chips, 2)),
        ]
        + [dma((chips, pieces))] * 6,
        compiler_params=pltpu.CompilerParams(
            collective_id=collective_id, has_side_effects=True, vmem_limit_bytes=WIDE
        ),
        cost_estimate=LONG if paired else CHEAP,
        name=name,
    )(partial)


def dense_kernel(chips, count, matrices, pieces, *refs):
    refs = list(refs)

    def take(number):
        taken = refs[:number]
        del refs[:number]
        return taken

    grads, outs = take(matrices), take(matrices)
    own, sib, mates, low, final = (take(matrices) for _ in range(5))
    (load, near_send, near_recv, send, recv, low_send, low_recv, back_send, back_recv, last_send, last_recv, keep) = refs
    c, w = lax.axis_index("ctx"), lax.axis_index("wt")
    z = c // 2
    core = lax.rem(c, 2)
    near = (flip(c, 1), w)
    above = (lax.rem(c + 2, 2 * chips), w)
    below = (lax.rem(c + 2 * chips - 2, 2 * chips), w)
    peers = [flip(w, d) for d in range(1, count)]
    greet([near, above, below] + [(c, p) for p in peers])

    def span(j, parity=None):
        m, first, rows = pieces[j]
        if parity is None:
            return pl.ds(first, rows)
        half = grads[m].shape[1] // 2
        return pl.ds(pl.multiple_of(parity * half + first, 16), rows)

    def fetch(j):
        m = pieces[j][0]
        return pltpu.make_async_copy(grads[m].at[:, span(j, core)], own[m].at[:, span(j)], load.at[j])

    def hand(j):
        m = pieces[j][0]
        return remote(
            grads[m].at[:, span(j, 1 - core)], sib[m].at[:, span(j)], near_send.at[j], near_recv.at[j], near
        )

    def give(j, d):
        m = pieces[j][0]
        return remote(
            own[m].at[peers[d], span(j)], mates[m].at[d, span(j)], send.at[j, d], recv.at[j, d], (c, peers[d])
        )

    def total(j):
        return own[pieces[j][0]].at[w, span(j)]

    def add(spot, other):
        spot[...] = spot[...] + other[...]

    def start(j):
        hand(j).start()
        fetch(j).start()

    def share(j):
        m = pieces[j][0]
        fetch(j).wait()
        hand(j).wait_recv()
        for d in range(count - 1):
            add(own[m].at[peers[d], span(j)], sib[m].at[peers[d], span(j)])
            give(j, d).start()
        add(total(j), sib[m].at[w, span(j)])

    def collect(j):
        m = pieces[j][0]
        value = total(j)[...].astype(jnp.float32)
        for d in range(count - 1):
            give(j, d).wait_recv()
            value = value + mates[m][d, span(j), :].astype(jnp.float32)
        total(j)[...] = value.astype(jnp.bfloat16)

    def line(j):
        return (z, above, below) if j % 2 == 0 else (chips - 1 - z, below, above)

    def onward(j):
        m = pieces[j][0]
        return remote(total(j), low[m].at[span(j)], low_send.at[j], low_recv.at[j], line(j)[1])

    def backward(j):
        spot = final[pieces[j][0]].at[span(j)]
        return remote(spot, spot, back_send.at[j], back_recv.at[j], line(j)[2])

    def across(j, parity):
        m = pieces[j][0]
        return remote(
            final[m].at[span(j)], outs[m].at[span(j, parity)], last_send.at[j], last_recv.at[j], near
        )

    def store(j):
        m = pieces[j][0]
        return pltpu.make_async_copy(final[m].at[span(j)], outs[m].at[span(j, core)], keep.at[j])

    def accumulate(j):
        place = line(j)[0]
        m = pieces[j][0]

        @pl.when(place > 0)
        def _():
            onward(j).wait_recv()
            add(total(j), low[m].at[span(j)])

        @pl.when(place < chips - 1)
        def _():
            onward(j).start()

        @pl.when(place == chips - 1)
        def _():
            final[m][span(j), :] = total(j)[...]
            backward(j).start()
            across(j, core).start()
            store(j).start()

    def spread(j):
        place = line(j)[0]

        @pl.when(place < chips - 1)
        def _():
            backward(j).wait_recv()
            pl.when(place > 0)(lambda: backward(j).start())
            across(j, core).start()
            store(j).start()

    number = len(pieces)
    for j in range(number):
        start(j)
    for j in range(number):
        share(j)
    last = chips - 1
    for t in range(number + 2 * last):
        if t < number:
            collect(t)
        for hop in range(2 * last, -1, -1):
            j = t - hop
            if not 0 <= j < number:
                continue
            if hop <= last:
                pl.when(line(j)[0] == hop)(lambda: accumulate(j))
            if hop > last:
                pl.when(line(j)[0] == 2 * last - hop)(lambda: spread(j))
    for j in range(number):
        place = line(j)[0]
        hand(j).wait_send()
        for d in range(count - 1):
            give(j, d).wait_send()
        pl.when(place < chips - 1)(lambda: onward(j).wait_send())
        pl.when(place > 0)(lambda: backward(j).wait_send())
        across(j, core).wait_send()
        across(j, 1 - core).wait_recv()
        store(j).wait()


def reduce_dense(grads):
    count = lax.axis_size("wt")
    chips = lax.axis_size("ctx") // 2
    shapes = [(g.shape[0] // count, g.shape[1]) for g in grads]
    pieces = []
    for m, (rows, _) in enumerate(shapes):
        half, width = rows // 2, shapes[m][1]
        cuts = max(n for n in range(1, 5) if half % (16 * n) == 0 and (n == 1 or half * width > 120000 * (n - 1)))
        for i in range(cuts):
            pieces.append((m, i * (rows // 2 // cuts), rows // 2 // cuts))
    halves = [(rows // 2, width) for rows, width in shapes]
    dma = pltpu.SemaphoreType.DMA
    one, many = dma((len(pieces),)), dma((len(pieces), count - 1))
    return pl.pallas_call(
        functools.partial(dense_kernel, chips, count, len(grads), tuple(pieces)),
        out_shape=[jax.ShapeDtypeStruct(s, jnp.bfloat16) for s in shapes],
        in_specs=[pl.BlockSpec(memory_space=pl.ANY)] * len(grads),
        out_specs=[pl.BlockSpec(memory_space=pl.ANY)] * len(grads),
        scratch_shapes=[pltpu.VMEM((count,) + h, jnp.bfloat16) for h in halves]
        + [pltpu.VMEM((count,) + h, jnp.bfloat16) for h in halves]
        + [pltpu.VMEM((count - 1,) + h, jnp.bfloat16) for h in halves]
        + [pltpu.VMEM(h, jnp.bfloat16) for h in halves]
        + [pltpu.VMEM(h, jnp.bfloat16) for h in halves]
        + [one, one, one, many, many, one, one, one, one, one, one, one],
        compiler_params=pltpu.CompilerParams(
            collective_id=7, has_side_effects=True, vmem_limit_bytes=WIDE
        ),
        cost_estimate=LONG,
        name="reduce_dense",
    )(*[g.reshape((count,) + s) for g, s in zip(grads, shapes)])


def dot_of(a, b, left, right):
    return lax.dot_general(
        a, b, (((left,), (right,)), ((), ())), preferred_element_type=jnp.float32
    )


def stacked_heads(ref):
    return jnp.concatenate(
        [ref[:, h * HEAD_DIM : (h + 1) * HEAD_DIM] for h in range(ref.shape[1] // HEAD_DIM)], axis=0
    )


exponent_scale = HEAD_DIM ** (-0.5) * math.log2(math.e)


def attend_kernel(place_ref, query_ref, both_ref, row_ref, column_ref, out_ref, log_ref, best, total, accum):
    tokens = query_ref.shape[0]
    group = query_ref.shape[1] // HEAD_DIM
    width = 2 * tokens
    place = place_ref[0]
    queries = stacked_heads(query_ref)
    best[...] = jnp.full_like(best, masked_value)
    total[...] = jnp.zeros_like(total)
    accum[...] = jnp.zeros_like(accum)
    query_pos = place * tokens + lax.broadcasted_iota(jnp.int32, (tokens, width), 0)
    key_pos = lax.broadcasted_iota(jnp.int32, (tokens, width), 1)

    def step(j, carry):
        span = pl.ds(pl.multiple_of(j * width, width), width)
        allowed = (key_pos + j * width <= query_pos) & (row_ref[0:1, span] == column_ref[:, 0:1])
        bias = jnp.where(allowed, 0.0, masked_value)
        scores = dot_of(queries, both_ref[span, :HEAD_DIM], 1, 1)
        scores = (scores.reshape(group, tokens, width) + bias[None]).reshape(group * tokens, width)
        newest = jnp.maximum(best[...], jnp.max(scores, axis=1, keepdims=True))
        factor = jnp.exp2((best[...] - newest) * exponent_scale)
        weights = jnp.exp2((scores - newest[:, :1]) * exponent_scale)
        total[...] = total[...] * factor + jnp.sum(weights, axis=1, keepdims=True)
        accum[...] = accum[...] * factor + dot_of(
            weights.astype(jnp.bfloat16), both_ref[span, HEAD_DIM:], 1, 0
        )
        best[...] = newest
        return carry

    lax.fori_loop(0, place // 2 + 1, step, 0)
    heads = accum[...] / total[...]
    for h in range(group):
        out_ref[:, h * HEAD_DIM : (h + 1) * HEAD_DIM] = heads[h * tokens : (h + 1) * tokens]
    logs = best[...] * exponent_scale + jnp.log2(total[...])
    log_ref[0] = jnp.transpose(logs)[:8]


def attend(place, projected, both, seg_row, seg_column):
    tokens = projected.shape[0]
    group = HEADS // KV_HEADS
    rows, span = group * tokens, both.shape[0]
    stat = pltpu.VMEM((rows, HEAD_DIM), jnp.float32)
    return pl.pallas_call(
        attend_kernel,
        grid=(KV_HEADS,),
        out_shape=(
            jax.ShapeDtypeStruct((tokens, HEADS * HEAD_DIM), jnp.float32),
            jax.ShapeDtypeStruct((KV_HEADS, 8, rows), jnp.float32),
        ),
        in_specs=[
            pl.BlockSpec(memory_space=pltpu.SMEM),
            pl.BlockSpec((tokens, group * HEAD_DIM), lambda g: (0, g)),
            pl.BlockSpec((span, 2 * HEAD_DIM), lambda g: (0, g)),
            pl.BlockSpec((1, span), lambda g: (0, 0)),
            pl.BlockSpec((tokens, 1), lambda g: (0, 0)),
        ],
        out_specs=(
            pl.BlockSpec((tokens, group * HEAD_DIM), lambda g: (0, g)),
            pl.BlockSpec((1, 8, rows), lambda g: (g, 0, 0)),
        ),
        scratch_shapes=[stat, stat, stat],
        compiler_params=pltpu.CompilerParams(vmem_limit_bytes=WIDE),
        cost_estimate=CHEAP,
        name="attend",
    )(place, projected, both, seg_row, seg_column)


def attend_back_kernel(place_ref, query_ref, both_ref, row_ref, column_ref, heads_ref, grad_ref, log_ref, grad_query_ref, grad_both_ref, accum):
    tokens = query_ref.shape[0]
    group = query_ref.shape[1] // HEAD_DIM
    width = 2 * tokens
    rows = group * tokens
    scale = HEAD_DIM ** (-0.5)
    place = place_ref[0]
    queries, grads = stacked_heads(query_ref), stacked_heads(grad_ref)
    product = grads.astype(jnp.float32) * stacked_heads(heads_ref)
    delta = jnp.sum(product, axis=1, keepdims=True)
    delta = jnp.transpose(jnp.broadcast_to(delta, (rows, HEAD_DIM)))[0:1]
    logs = log_ref[0, 0:1, :]
    accum[...] = jnp.zeros_like(accum)
    grad_both_ref[...] = jnp.zeros_like(grad_both_ref)
    query_pos = place * tokens + lax.broadcasted_iota(jnp.int32, (width, tokens), 1)
    key_pos = lax.broadcasted_iota(jnp.int32, (width, tokens), 0)

    def step(j, carry):
        span = pl.ds(pl.multiple_of(j * width, width), width)
        allowed = (key_pos + j * width <= query_pos) & (column_ref[span, 0:1] == row_ref[0:1, :])
        bias = jnp.where(allowed, 0.0, masked_value)
        bias = jnp.concatenate([bias] * group, axis=1)
        keys, values = both_ref[span, :HEAD_DIM], both_ref[span, HEAD_DIM:]
        scores = dot_of(keys, queries, 1, 1)
        probs = jnp.exp2(scores * exponent_scale + bias - logs)
        grad_probs = dot_of(values, grads, 1, 1)
        grad_scores = (probs * (grad_probs - delta)).astype(jnp.bfloat16)
        accum[...] += dot_of(grad_scores, keys, 0, 0)
        grad_both_ref[span, :HEAD_DIM] = (dot_of(grad_scores, queries, 1, 0) * scale).astype(jnp.bfloat16)
        grad_both_ref[span, HEAD_DIM:] = dot_of(probs.astype(jnp.bfloat16), grads, 1, 0).astype(jnp.bfloat16)
        return carry

    lax.fori_loop(0, place // 2 + 1, step, 0)
    grad_queries = (accum[...] * scale).astype(jnp.bfloat16)
    for h in range(group):
        grad_query_ref[:, h * HEAD_DIM : (h + 1) * HEAD_DIM] = grad_queries[h * tokens : (h + 1) * tokens]


def attend_back(place, projected, both, query_seg_row, seg_column, heads_out, grad_attended, logs):
    tokens = projected.shape[0]
    group = HEADS // KV_HEADS
    rows, span = group * tokens, both.shape[0]
    per_group = pl.BlockSpec((tokens, group * HEAD_DIM), lambda g: (0, g))
    return pl.pallas_call(
        attend_back_kernel,
        grid=(KV_HEADS,),
        out_shape=(
            jax.ShapeDtypeStruct((tokens, HEADS * HEAD_DIM), jnp.bfloat16),
            jax.ShapeDtypeStruct(both.shape, jnp.bfloat16),
        ),
        in_specs=[
            pl.BlockSpec(memory_space=pltpu.SMEM),
            per_group,
            pl.BlockSpec((span, 2 * HEAD_DIM), lambda g: (0, g)),
            pl.BlockSpec((1, tokens), lambda g: (0, 0)),
            pl.BlockSpec((span, 1), lambda g: (0, 0)),
            per_group,
            per_group,
            pl.BlockSpec((1, 8, rows), lambda g: (g, 0, 0)),
        ],
        out_specs=(per_group, pl.BlockSpec((span, 2 * HEAD_DIM), lambda g: (0, g))),
        scratch_shapes=[pltpu.VMEM((rows, HEAD_DIM), jnp.float32)],
        compiler_params=pltpu.CompilerParams(vmem_limit_bytes=WIDE),
        cost_estimate=CHEAP,
        name="attend_back",
    )(place, projected, both, query_seg_row, seg_column, heads_out, grad_attended, logs)


def pick_kernel(scaled, slot_ref, gate_ref, rows_ref, out_ref, scale_ref=None):
    local, depth = out_ref.shape[2], out_ref.shape[3]
    tokens = slot_ref.shape[3] // 2
    place = lax.broadcasted_iota(jnp.int32, (depth, tokens), 0)
    total, weight = None, None
    for core in range(2):
        span = slice(core * tokens, (core + 1) * tokens)
        chosen = [slot_ref[0, 0, e : e + 1, span] == place for e in range(local)]
        ones = jnp.concatenate([c.astype(jnp.float32) for c in chosen], axis=0).astype(jnp.bfloat16)
        rows = rows_ref[0, core, 0] if scaled else rows_ref[0, 0, core]
        term = jnp.dot(ones, rows, preferred_element_type=jnp.float32)
        total = term if total is None else total + term
        if scaled:
            gates = jnp.concatenate(
                [
                    jnp.sum(jnp.where(c, gate_ref[0, 0, e : e + 1, span], 0.0), axis=1, keepdims=True)
                    for e, c in enumerate(chosen)
                ],
                axis=0,
            )
            weight = gates if weight is None else weight + gates
    if scaled:
        total = total * weight
        scale_ref[0, 0] = jnp.broadcast_to(weight, (local * depth, 128)).reshape(local, depth, 128)
    out_ref[0, 0] = total.astype(jnp.bfloat16).reshape(local, depth, total.shape[1])


def pick_rows(rows, slots, gates, scaled):
    chips, sides, local, both = slots.shape
    tokens, width = both // 2, rows.shape[4]
    depth = 2 * CAP
    table = pl.BlockSpec((1, 1, local, both), lambda z, s: (z, s, 0, 0))
    shapes = [jax.ShapeDtypeStruct((chips, sides, local, depth, width), jnp.bfloat16)]
    specs = [pl.BlockSpec((1, 1, local, depth, width), lambda z, s: (z, s, 0, 0, 0))]
    if scaled:
        shapes.append(jax.ShapeDtypeStruct((chips, sides, local, depth, 128), jnp.float32))
        specs.append(pl.BlockSpec((1, 1, local, depth, 128), lambda z, s: (z, s, 0, 0, 0)))
        source = pl.BlockSpec((1, 2, 1, tokens, width), lambda z, s: (z, 0, s, 0, 0))
    else:
        source = pl.BlockSpec((1, 1, 2, tokens, width), lambda z, s: (z, s, 0, 0, 0))
    return pl.pallas_call(
        functools.partial(pick_kernel, scaled),
        grid=(chips, sides),
        out_shape=shapes,
        in_specs=[table, table, source],
        out_specs=specs,
        compiler_params=pltpu.CompilerParams(vmem_limit_bytes=WIDE),
        cost_estimate=CHEAP,
        name="pick_grads" if scaled else "pick_tokens",
    )(slots, gates, rows)


def spread_kernel(apart, slot_ref, rows_ref, out_ref):
    local, depth, width = rows_ref.shape[2:]
    tokens = out_ref.shape[3]
    place = lax.broadcasted_iota(jnp.int32, (depth, tokens), 0)
    rows = rows_ref[0, 0].reshape(local * depth, width)
    for core in range(2):
        span = slice(core * tokens, (core + 1) * tokens)
        ones = jnp.concatenate(
            [(slot_ref[0, 0, e : e + 1, span] == place).astype(jnp.float32) for e in range(local)], axis=0
        ).astype(jnp.bfloat16)
        spot = out_ref.at[0, core, 0] if apart else out_ref.at[0, 0, core]
        spot[...] = lax.dot_general(
            ones, rows, (((0,), (0,)), ((), ())), preferred_element_type=jnp.float32
        ).astype(jnp.bfloat16)


def spread_rows(rows, slots, name, apart):
    chips, sides, local, both = slots.shape
    depth, width = rows.shape[3:]
    tokens = both // 2
    return pl.pallas_call(
        functools.partial(spread_kernel, apart),
        grid=(chips, sides),
        out_shape=jax.ShapeDtypeStruct(
            (chips, 2, sides, tokens, width) if apart else (chips, sides, 2, tokens, width), jnp.bfloat16
        ),
        in_specs=[
            pl.BlockSpec((1, 1, local, both), lambda z, s: (z, s, 0, 0)),
            pl.BlockSpec((1, 1, local, depth, width), lambda z, s: (z, s, 0, 0, 0)),
        ],
        out_specs=pl.BlockSpec((1, 2, 1, tokens, width), lambda z, s: (z, 0, s, 0, 0))
        if apart
        else pl.BlockSpec((1, 1, 2, tokens, width), lambda z, s: (z, s, 0, 0, 0)),
        compiler_params=pltpu.CompilerParams(vmem_limit_bytes=WIDE),
        cost_estimate=CHEAP,
        name=name,
    )(slots, rows)


def expert_kernel(blocks, x_ref, g_ref, scale_ref, *refs):
    tall_refs, down_refs = refs[:blocks], refs[blocks : 2 * blocks]
    result_ref, back_ref, *grad_refs = refs[2 * blocks :]
    hops = len(grad_refs) // 3
    grad_gate_refs, grad_up_refs = grad_refs[:hops], grad_refs[hops : 2 * hops]
    grad_down_refs = grad_refs[2 * hops :]
    w = lax.axis_index("wt")
    chips, sides, _, depth, width = x_ref.shape
    rows = chips * sides * depth
    part = tall_refs[0].shape[2]
    nn, nt, tn = (((1,), (0,)), ((), ())), (((1,), (1,)), ((), ())), (((0,), (0,)), ((), ()))

    def dot(a, b, dims):
        return lax.dot_general(a, b, dims, preferred_element_type=jnp.float32)

    def columns(ref, q):
        if blocks == 1:
            return ref.at[:, :, 0]
        span = pl.ds(pl.multiple_of(flip(w, q) * part, 128), part)
        return ref.at[:, :, 0, :, span]

    def piece(ref, q):
        return columns(ref, q)[...].reshape(rows, part)

    gate, up, grad_inner = None, None, None
    for q in range(blocks):
        x = piece(x_ref, q)
        more_gate, more_up = dot(x, tall_refs[q][0, 0], nn), dot(x, tall_refs[q][0, 1], nn)
        gate, up = (more_gate, more_up) if q == 0 else (gate + more_gate, up + more_up)
    for q in range(blocks):
        more = dot(piece(g_ref, q), down_refs[q][0], nt)
        grad_inner = more if q == 0 else grad_inner + more
    sigmoid = jax.nn.sigmoid(gate)
    activated = gate * sigmoid
    inner = (activated * up).astype(jnp.bfloat16)
    grad_gate = (grad_inner * up * (sigmoid * (1.0 + gate * (1.0 - sigmoid)))).astype(jnp.bfloat16)
    grad_up = (grad_inner * activated).astype(jnp.bfloat16)
    scale = scale_ref[...].reshape(rows, 128)[:, :1]
    for q in range(blocks):
        result = dot(inner, down_refs[q][0], nn) * scale
        columns(result_ref, q)[...] = result.astype(jnp.bfloat16).reshape(chips, sides, depth, part)
        back = dot(grad_gate, tall_refs[q][0, 0], nt) + dot(grad_up, tall_refs[q][0, 1], nt)
        columns(back_ref, q)[...] = back.astype(jnp.bfloat16).reshape(chips, sides, depth, part)
        grad_down_refs[q // 2][q % 2, 0] = dot(inner, piece(g_ref, q), tn).astype(jnp.bfloat16)
        x = piece(x_ref, q)
        grad_gate_refs[q // 2][q % 2, 0] = dot(x, grad_gate, tn).astype(jnp.bfloat16)
        grad_up_refs[q // 2][q % 2, 0] = dot(x, grad_up, tn).astype(jnp.bfloat16)


def run_experts(x, g, scale, talls, downs):
    chips, sides, local, depth, width = x.shape
    blocks = len(talls)
    part, inner = talls[0].shape[2:]
    large = chips * sides * depth > 1024
    rows = pl.BlockSpec((chips, sides, 1, depth, width), lambda e: (0, 0, e, 0, 0))
    sources = pl.BlockSpec(
        (chips, sides, 1, depth, width),
        lambda e: (0, 0, e, 0, 0),
        pipeline_mode=pl.Buffered(1 if large else 2),
    )
    scales = pl.BlockSpec((chips, sides, 1, depth, 128), lambda e: (0, 0, e, 0, 0))
    tall = pl.BlockSpec((1, 2, part, inner), lambda e: (e, 0, 0, 0))
    flat = pl.BlockSpec((1, inner, part), lambda e: (e, 0, 0))
    hops, each = max(blocks // 2, 1), min(blocks, 2)
    tall_out = pl.BlockSpec((each, 1, part, inner), lambda e: (0, e, 0, 0))
    flat_out = pl.BlockSpec((each, 1, inner, part), lambda e: (0, e, 0, 0))
    return pl.pallas_call(
        functools.partial(expert_kernel, blocks),
        grid=(local,),
        out_shape=(
            jax.ShapeDtypeStruct(x.shape, jnp.bfloat16),
            jax.ShapeDtypeStruct(x.shape, jnp.bfloat16),
            *[jax.ShapeDtypeStruct((each, local, part, inner), jnp.bfloat16)] * (2 * hops),
            *[jax.ShapeDtypeStruct((each, local, inner, part), jnp.bfloat16)] * hops,
        ),
        in_specs=[sources, sources, scales] + [tall] * blocks + [flat] * blocks,
        out_specs=(rows, rows) + (tall_out,) * (2 * hops) + (flat_out,) * hops,
        compiler_params=pltpu.CompilerParams(vmem_limit_bytes=60 * 2**20),
        cost_estimate=CHEAP,
        name="experts",
    )(x, g, scale, *talls, *downs)


def place_kernel(arrivals, side_ref, *refs):
    own, other, more, outs = refs[:3], refs[3:6], refs[6 : 6 + 3 * arrivals], refs[6 + 3 * arrivals :]
    mine = pl.program_id(0) == side_ref[0]

    @pl.when(mine)
    def _():
        for i in range(3):
            value = own[i][0, 0].astype(jnp.float32)
            for m in more[i * arrivals : (i + 1) * arrivals]:
                value = value + m[0, 0].astype(jnp.float32)
            outs[i][0] = value

    @pl.when(jnp.logical_not(mine))
    def _():
        for i in range(3):
            outs[i][0] = other[i][0].astype(jnp.float32)


def place_experts(side, own, more, other):
    local = other[0].shape[0]
    arrivals = len(more[0])
    shapes = [o.shape[1:] for o in other]
    paired = [pl.BlockSpec((1, 1) + s, lambda h, e: (0, e, 0, 0)) for s in shapes]
    single = [pl.BlockSpec((1,) + s, lambda h, e: (e, 0, 0)) for s in shapes]
    return pl.pallas_call(
        functools.partial(place_kernel, arrivals),
        grid=(2, local),
        out_shape=[jax.ShapeDtypeStruct((2 * local,) + s, jnp.float32) for s in shapes],
        in_specs=[pl.BlockSpec(memory_space=pltpu.SMEM)]
        + paired
        + single
        + [p for p in paired for _ in range(arrivals)],
        out_specs=[pl.BlockSpec((1,) + s, lambda h, e: (h * local + e, 0, 0)) for s in shapes],
        compiler_params=pltpu.CompilerParams(vmem_limit_bytes=WIDE),
        cost_estimate=CHEAP,
        name="place_experts",
    )(side, *own, *other, *[m for group in more for m in group])


def swap_pairs(value, axis, distance):
    count = lax.axis_size(axis)
    return lax.ppermute(value, axis, [(i, i ^ distance) for i in range(count)])


def own_and_other(stacked, mine):
    return (
        lax.dynamic_index_in_dim(stacked, mine, 0, keepdims=False),
        lax.dynamic_index_in_dim(stacked, 1 - mine, 0, keepdims=False),
    )


def collect_expert(shard, side, pairs):
    local = shard.shape[0]
    kept, given = own_and_other(shard.reshape((2, local // 2) + shard.shape[1:]), side)
    return kept, swap_pairs(given, "wt", 1), [swap_pairs(kept, "wt", 2 * d) for d in range(1, pairs)]


def settle_blocks(blocks, index, axis):
    stacked = jnp.stack(blocks)
    return jnp.concatenate(
        [
            lax.dynamic_index_in_dim(stacked, jnp.bitwise_xor(j, index), 0, False)
            for j in range(len(blocks))
        ],
        axis=axis,
    )


def split_blocks(whole, index, count, axis):
    parts = jnp.stack(jnp.split(whole, count, axis=axis))
    return jnp.stack(
        [
            lax.dynamic_index_in_dim(parts, jnp.bitwise_xor(q, index), 0, False)
            for q in range(count)
        ]
    )


def body(
    hidden,
    segment_ids,
    routes,
    gates,
    cotangent,
    norm_one_gain,
    w_query,
    w_key,
    w_value,
    w_out,
    norm_two_gain,
    shared_gate,
    shared_up,
    shared_down,
    expert_gate,
    expert_up,
    expert_down,
):
    wt_index = lax.axis_index("wt")
    wt_count = lax.axis_size("wt")
    ctx_count = lax.axis_size("ctx")
    chips = ctx_count // 2
    pairs = wt_count // 2
    tokens, width_model = hidden.shape[1:]
    wide, kv_width = w_query.shape[1], w_key.shape[1]
    shared_width = shared_gate.shape[1]
    gates_here = gates[0]
    gate_high = gates_here.astype(jnp.bfloat16)
    gate_rest = gates_here - gate_high.astype(jnp.float32)
    gate_middle = gate_rest.astype(jnp.bfloat16)
    gate_low = (gate_rest - gate_middle.astype(jnp.float32)).astype(jnp.bfloat16)
    table = jnp.concatenate(
        [routes[0].astype(jnp.bfloat16), gate_high, gate_middle, gate_low], axis=1
    )
    grad_rows = cotangent[0]
    depth = norm_one_gain.shape[0]
    extra_rows = 16
    table_rows = extra_rows * width_model // tokens
    packed = jnp.pad(jnp.swapaxes(table, 0, 1), ((0, table_rows - 4 * TOPK), (0, 0)))
    extended = jnp.concatenate([grad_rows, packed.reshape(extra_rows, width_model)], axis=0)
    gain_pair = jnp.concatenate(
        [norm_one_gain[None], norm_two_gain[None], jnp.zeros((30, depth), jnp.bfloat16)]
    )
    query_weight, key_weight, value_weight, gains, grad_pair, zero = gather_weights(
        (w_query, w_key, w_value, gain_pair), (extended,)
    )
    query_weight = query_weight.reshape(-1, wide)
    key_weight = key_weight.reshape(-1, kv_width)
    value_weight = value_weight.reshape(-1, kv_width)
    zero = zero[0, 0]
    side = lax.rem(wt_index, 2)
    later = side + zero
    collected = [
        collect_expert(jnp.stack([expert_gate, expert_up], axis=1), later, pairs),
        collect_expert(expert_down, later, pairs),
    ]
    gain_one, gain_two = gains[:, 0].reshape(-1), gains[:, 1].reshape(-1)
    local = expert_gate.shape[0] // 2
    first_expert = (lax.axis_index("ctx") * 2 + side) * local

    inputs = hidden[0].astype(jnp.float32)
    offset = lax.axis_index("ctx") * tokens
    seg_all = segment_ids[0]
    query_seg = lax.dynamic_slice_in_dim(seg_all, offset, tokens)
    scale_one = inverse_rms(inputs)
    gain_one_full = gain_one.astype(jnp.float32)
    normed = (inputs * scale_one * gain_one_full).astype(jnp.bfloat16)

    def project(weight):
        return jnp.dot(normed, weight, preferred_element_type=jnp.float32).astype(jnp.bfloat16)

    queries = project(query_weight)
    fresh = jnp.stack(
        [
            project(key_weight).reshape(tokens, KV_HEADS, HEAD_DIM),
            project(value_weight).reshape(tokens, KV_HEADS, HEAD_DIM),
        ],
        axis=2,
    ).reshape(tokens, 2 * kv_width)
    both, out_weight, both_weight, down_weight, zero = gather_rows(
        fresh,
        2,
        False,
        False,
        "gather_keys",
        (w_out, jnp.concatenate([shared_gate, shared_up], axis=1), shared_down),
    )
    out_weight = out_weight.reshape(-1, out_weight.shape[2])
    both_weight = both_weight.reshape(-1, both_weight.shape[2])
    down_weight = down_weight.reshape(-1, down_weight.shape[2])
    both = both.reshape(-1, 2 * kv_width)

    grad_pair = lax.dynamic_index_in_dim(jnp.stack([grad_pair, grad_pair]), zero, 0, False)
    all_grads = lax.all_gather(grad_pair, "ctx", axis=0).reshape(
        chips, 2, 2, tokens + extra_rows, width_model
    )
    tables = all_grads[:, :, :, tokens:].reshape(chips, 2, 2, table_rows, tokens)[:, :, :, : 4 * TOPK]
    tables = jnp.transpose(tables.astype(jnp.float32), (0, 2, 3, 1, 4)).reshape(
        chips, 2, 4 * TOPK, 2 * tokens
    )
    table_routes, gate_parts = tables[:, :, :TOPK], tables[:, :, TOPK:]
    table_gates = (
        gate_parts[:, :, :TOPK] + gate_parts[:, :, TOPK : 2 * TOPK] + gate_parts[:, :, 2 * TOPK :]
    )
    experts_here = (first_expert + jnp.arange(local, dtype=jnp.int32)).astype(jnp.float32)
    named = table_routes[:, :, None] == experts_here[None, None, :, None, None]
    member = jnp.any(named, axis=3)
    slot_gates = jnp.sum(jnp.where(named, table_gates[:, :, None], 0.0), axis=3)
    earlier = (
        jnp.arange(2 * tokens)[:, None] < jnp.arange(2 * tokens)[None, :]
    ).astype(jnp.bfloat16)
    rank = jnp.dot(member.astype(jnp.bfloat16), earlier, preferred_element_type=jnp.float32)
    slots = jnp.where(member, rank.astype(jnp.int32), -1)

    place = lax.axis_index("ctx").astype(jnp.int32).reshape(1)
    seg_row, seg_column = seg_all[None, :], seg_all[:, None]
    attended_full, logs = attend(place, queries, both, seg_row, query_seg[:, None])
    attended = attended_full.astype(jnp.bfloat16)
    middle = inputs + jnp.dot(attended, out_weight, preferred_element_type=jnp.float32)
    scale_two = inverse_rms(middle)
    gain_two_full = gain_two.astype(jnp.float32)
    normed_two = (middle * scale_two * gain_two_full).astype(jnp.bfloat16)

    shared_parts = jnp.dot(normed_two, both_weight, preferred_element_type=jnp.float32)
    shared_gate_part, shared_up_part = shared_parts[:, :shared_width], shared_parts[:, shared_width:]
    shared_inner = (jax.nn.silu(shared_gate_part) * shared_up_part).astype(jnp.bfloat16)
    shared_result = jnp.dot(shared_inner, down_weight, preferred_element_type=jnp.float32)
    grad_out = grad_rows.astype(jnp.float32)
    grad_shared_down = jnp.einsum(
        "tf,td->fd", shared_inner, grad_rows, preferred_element_type=jnp.float32
    )
    grad_shared_inner = jnp.einsum(
        "td,fd->tf", grad_rows, down_weight, preferred_element_type=jnp.float32
    )
    grad_shared_gate_part = (
        grad_shared_inner * shared_up_part * silu_slope(shared_gate_part)
    ).astype(jnp.bfloat16)
    grad_shared_up_part = (grad_shared_inner * jax.nn.silu(shared_gate_part)).astype(jnp.bfloat16)
    grad_shared_parts = jnp.concatenate([grad_shared_gate_part, grad_shared_up_part], axis=1)
    grad_shared_both = jnp.einsum(
        "td,tf->df", normed_two, grad_shared_parts, preferred_element_type=jnp.float32
    )
    grad_shared_rows = jnp.einsum(
        "tf,df->td", grad_shared_parts, both_weight, preferred_element_type=jnp.float32
    )
    grad_shared_both = grad_shared_both.astype(jnp.bfloat16)
    grad_shared_down = grad_shared_down.astype(jnp.bfloat16)
    normed_two, collected, shared_result, grad_shared_both, grad_shared_down, grad_shared_rows = (
        lax.optimization_barrier(
            (normed_two, collected, shared_result, grad_shared_both, grad_shared_down, grad_shared_rows)
        )
    )
    all_rows, *landed, zero = gather_rows(
        normed_two, 3, True, True, "gather_tokens", (), [c[1] for c in collected]
    )

    def blocks_of(i):
        kept, paired, straight = collected[i]
        blocks = [kept, paired]
        for d in range(pairs - 1):
            blocks += [straight[d], landed[i * (pairs - 1) + d]]
        return blocks

    tall_blocks, down_blocks = blocks_of(0), blocks_of(1)
    (received_rows,) = pick_rows(all_rows, slots, slot_gates, False)
    grad_received, row_gates = pick_rows(all_grads, slots, slot_gates, True)
    if down_blocks[0].shape[2] % 128:
        results, backs, grads_gate, grads_up, grads_down = run_experts(
            received_rows,
            grad_received,
            row_gates,
            [settle_blocks(tall_blocks, wt_index, 2)],
            [settle_blocks(down_blocks, wt_index, 2)],
        )
        wholes = [
            split_blocks(grads_gate[0], wt_index, wt_count, 1),
            split_blocks(grads_up[0], wt_index, wt_count, 1),
            split_blocks(grads_down[0], wt_index, wt_count, 2),
        ]
        hop_grads = [[g[2 * d : 2 * d + 2] for d in range(pairs)] for g in wholes]
    else:
        results, backs, *rest = run_experts(
            received_rows, grad_received, row_gates, tall_blocks, down_blocks
        )
        hop_grads = [rest[i * pairs : (i + 1) * pairs] for i in range(3)]
    arrived = [[swap_pairs(g[d], "wt", 2 * d) for d in range(1, pairs)] for g in hop_grads]
    first_arrived, later_arrived = arrived[:1], arrived[1:]
    routed_grad = scatter_rows(
        spread_rows(backs, slots, "spread_grads", False), 5, True, True, "scatter_grads"
    )
    routed_grad, first_arrived = lax.optimization_barrier((routed_grad, first_arrived))

    def crossed(own, more):
        total = own[1].astype(jnp.float32)
        for m in more:
            total = total + m[1].astype(jnp.float32)
        return swap_pairs(total.astype(jnp.bfloat16), "wt", 1)

    gate_other = crossed(hop_grads[0][0], first_arrived[0])
    grad_normed_two = grad_shared_rows + routed_grad
    grad_gain_two = jnp.sum(grad_normed_two * middle * scale_two, axis=0)
    scaled_two = grad_normed_two * gain_two_full
    grad_middle = (
        grad_out
        + scale_two * scaled_two
        - middle * scale_two**3 * jnp.mean(scaled_two * middle, axis=-1, keepdims=True)
    )
    grad_branch = grad_middle.astype(jnp.bfloat16)
    grad_out_weight = jnp.einsum(
        "tq,td->qd", attended, grad_branch, preferred_element_type=jnp.float32
    )
    grad_attended = jnp.einsum(
        "td,qd->tq", grad_branch, out_weight, preferred_element_type=jnp.float32
    ).astype(jnp.bfloat16)
    grad_attended, up_arrived = lax.optimization_barrier((grad_attended, later_arrived[0]))
    up_other = crossed(hop_grads[1][0], up_arrived)
    grad_queries, grad_parts = attend_back(
        place, queries, both, query_seg[None, :], seg_column, attended_full, grad_attended, logs
    )
    grad_both = scatter_rows(
        grad_parts.reshape(chips, 1, 2, tokens, 2 * kv_width),
        6,
        False,
        False,
        "scatter_keys",
    ).astype(jnp.bfloat16)
    grad_both, down_arrived, gate_other, up_other, results = lax.optimization_barrier(
        (grad_both, later_arrived[1], gate_other, up_other, results)
    )
    arrived = [first_arrived[0], up_arrived, down_arrived]
    down_other = crossed(hop_grads[2][0], down_arrived)
    partial = lax.psum_scatter(
        spread_rows(results, slots, "spread_results", True).reshape(ctx_count, 2, tokens, width_model),
        "ctx",
        scatter_dimension=0,
        tiled=True,
    )[0]
    grad_both = grad_both.reshape(tokens, KV_HEADS, 2, HEAD_DIM)
    grad_keys = grad_both[:, :, 0].reshape(tokens, kv_width)
    grad_values = grad_both[:, :, 1].reshape(tokens, kv_width)

    def weight_grad(grad):
        return jnp.einsum("tc,tq->cq", normed, grad, preferred_element_type=jnp.float32).astype(
            jnp.bfloat16
        )

    def input_grad(grad, weight):
        return jnp.einsum("tq,cq->tc", grad, weight, preferred_element_type=jnp.float32)

    grad_normed = (
        input_grad(grad_queries, query_weight)
        + input_grad(grad_keys, key_weight)
        + input_grad(grad_values, value_weight)
    )
    grad_gain_one = jnp.sum(grad_normed * inputs * scale_one, axis=0)
    scaled_one = grad_normed * gain_one_full
    grad_inputs = (
        grad_middle
        + scale_one * scaled_one
        - inputs * scale_one**3 * jnp.mean(scaled_one * inputs, axis=-1, keepdims=True)
    )

    gain_grads = jnp.stack([grad_gain_one, grad_gain_two]).reshape(2, wt_count, 1, depth)
    gain_grads = jnp.pad(gain_grads.astype(jnp.bfloat16), ((0, 0), (0, 0), (0, 15), (0, 0)))
    gain_grads = jnp.swapaxes(gain_grads, 0, 1).reshape(wt_count * 32, depth)
    dense_grads = [
        weight_grad(grad_queries),
        grad_shared_both,
        grad_out_weight.astype(jnp.bfloat16),
        grad_shared_down,
        weight_grad(grad_keys),
        weight_grad(grad_values),
        gain_grads,
    ]
    totals = reduce_dense(dense_grads)
    totals, down_other, partial = lax.optimization_barrier((totals, down_other, partial))
    others = [gate_other, up_other, down_other]
    kept, given = own_and_other(partial, side)
    crossing = swap_pairs(given, "wt", 1)
    routed = kept.astype(jnp.float32) + crossing.astype(jnp.float32)
    output = (middle + shared_result + routed).astype(jnp.bfloat16)
    sum_experts_gate, sum_experts_up, sum_experts_down = place_experts(
        side.astype(jnp.int32).reshape(1), [g[0] for g in hop_grads], arrived, others
    )
    final_query, final_shared, final_out, final_down, final_key, final_value, final_gains = [
        total.astype(jnp.float32) for total in totals
    ]
    final_gate, final_up = final_shared[:, :shared_width], final_shared[:, shared_width:]
    final_gain_one, final_gain_two = final_gains[0], final_gains[16]
    return (
        output[None],
        grad_inputs[None],
        final_gain_one,
        final_query,
        final_key,
        final_value,
        final_out,
        final_gain_two,
        final_gate,
        final_up,
        final_down,
        sum_experts_gate,
        sum_experts_up,
        sum_experts_down,
    )


def solution(mesh):
    placed = (
        P("wt", "ctx", None),
        P("wt", None),
        P("wt", "ctx", None),
        P("wt", "ctx", None),
        P("wt", "ctx", None),
        P("wt"),
        P("wt", None),
        P("wt", None),
        P("wt", None),
        P("wt", None),
        P("wt"),
        P("wt", None),
        P("wt", None),
        P("wt", None),
        P("ctx", "wt", None),
        P("ctx", "wt", None),
        P("ctx", None, "wt"),
    )
    return jax.shard_map(
        body,
        mesh=mesh,
        in_specs=placed,
        out_specs=(
            P("wt", "ctx", None),
            P("wt", "ctx", None),
            P("wt"),
            P("wt", None),
            P("wt", None),
            P("wt", None),
            P("wt", None),
            P("wt"),
            P("wt", None),
            P("wt", None),
            P("wt", None),
            P("ctx", "wt", None),
            P("ctx", "wt", None),
            P("ctx", None, "wt"),
        ),
        check_vma=False,
    )
```

```python
import functools
import math

import jax
import jax.numpy as jnp
from jax import lax
from jax.experimental import pallas as pl
from jax.experimental.pallas import tpu as pltpu
from jax.sharding import PartitionSpec as P

HEADS = 12
KV_HEADS = 4
HEAD_DIM = 128
EXPERTS = 64
TOPK = 6
CAP = 40


epsilon = 1e-05
masked_value = -1e30


def inverse_rms(rows):
    return lax.rsqrt(jnp.mean(rows * rows, axis=-1, keepdims=True) + epsilon)


def silu_slope(gate_part):
    sigmoid = jax.nn.sigmoid(gate_part)
    return sigmoid * (1.0 + gate_part * (1.0 - sigmoid))


MESH = pl.DeviceIdType.MESH
WIDE = 56 * 2**20
LONG = pl.CostEstimate(flops=0, bytes_accessed=2_000_000_000, transcendentals=0)
CHEAP = pl.CostEstimate(flops=0, bytes_accessed=4096, transcendentals=0)


def flip(index, distance):
    result = index
    bit = 1
    while bit <= distance:
        if distance // bit % 2:
            result = result + bit - 2 * bit * (index // bit % 2)
        bit *= 2
    return result


def remote(src, dst, send_sem, recv_sem, device):
    return pltpu.make_async_remote_copy(
        src_ref=src,
        dst_ref=dst,
        send_sem=send_sem,
        recv_sem=recv_sem,
        device_id=device,
        device_id_type=MESH,
    )


def greet(devices):
    barrier = pltpu.get_barrier_semaphore()
    for device in devices:
        pl.semaphore_signal(barrier, inc=1, device_id=device, device_id_type=MESH)
    pl.semaphore_wait(barrier, len(devices))


class Slabs:
    def __init__(self, count, sources, targets, here, there, send, recv, near_send, near_recv, *stages):
        self.c, self.w = lax.axis_index("ctx"), lax.axis_index("wt")
        self.core = lax.rem(self.c, 2)
        self.near = (flip(self.c, 1), self.w)
        self.count = count
        self.pairs = list(zip(sources, targets))
        self.here, self.there, self.send, self.recv = here, there, send, recv
        self.near_send, self.near_recv = near_send, near_recv
        self.stages = stages
        dims = [1 << i for i in range(count.bit_length() - 1)]
        self.orders = [dims, dims[::-1]]

    def devices(self):
        return [(self.c, flip(self.w, d)) for d in self.orders[0]]

    def rows(self, s, p, core):
        rows = self.pairs[s][0].shape[0] // 4
        return pl.ds(pl.multiple_of((core * 2 + p) * rows, 16), rows)

    def block(self, s, p, f, core):
        return self.pairs[s][1].at[flip(self.w, f), self.rows(s, p, core)]

    def push(self, s, p, stage, held):
        step = self.orders[p][stage]
        part = self.rows(s, p, self.core)
        source = self.pairs[s][0].at[part] if held == 0 else self.block(s, p, held, self.core)
        index = (s, p, (step ^ held) - 1)
        return remote(
            source,
            self.block(s, p, held, self.core),
            self.send.at[index],
            self.recv.at[index],
            (self.c, flip(self.w, step)),
        )

    def arrival(self, s, p, f):
        spot = self.block(s, p, f, self.core)
        return remote(spot, spot, self.send.at[s, p, f - 1], self.recv.at[s, p, f - 1], self.near)

    def hand(self, s, p, f, core):
        spot = self.block(s, p, f, core)
        return remote(spot, spot, self.near_send.at[s, p, f - 1], self.near_recv.at[s, p, f - 1], self.near)

    def load(self, s):
        return pltpu.make_async_copy(self.pairs[s][0], self.stages[s], self.here.at[s])

    def keep(self, s):
        return pltpu.make_async_copy(self.stages[s], self.pairs[s][1].at[self.w], self.there.at[s])

    def last_stage(self, p, f):
        return max(i for i, d in enumerate(self.orders[p]) if f & d)

    def every(self):
        return [(s, p) for s in range(len(self.pairs)) for p in range(2)]

    def start(self):
        for stage in range(len(self.orders[0])):
            for s, p in self.every():
                self.push(s, p, stage, 0).start()
        for s in range(len(self.pairs)):
            self.load(s).start()

    def relay(self):
        for s in range(len(self.pairs)):
            self.load(s).wait()
            self.keep(s).start()
        last = len(self.orders[0])
        for stage in range(last):
            for s, p in self.every():
                for f in range(1, self.count):
                    if self.last_stage(p, f) == stage:
                        self.arrival(s, p, f).wait_recv()
                        for onward in range(stage + 1, last):
                            self.push(s, p, onward, f).start()
                        self.hand(s, p, f, self.core).start()

    def finish(self):
        for s, p in self.every():
            for f in range(1, self.count):
                stage = self.last_stage(p, f)
                self.hand(s, p, f, 1 - self.core).wait_recv()
                self.hand(s, p, f, self.core).wait_send()
                self.push(s, p, stage, f ^ self.orders[p][stage]).wait_send()
        for s in range(len(self.pairs)):
            self.keep(s).wait()

    @staticmethod
    def scratch(slabs, count):
        dma = pltpu.SemaphoreType.DMA
        number = len(slabs)
        return (
            [dma((number,))] * 2
            + [dma((number, 2, count - 1))] * 4
            + [pltpu.VMEM(s.shape, s.dtype) for s in slabs]
        )

    @staticmethod
    def shapes(slabs, count):
        return tuple(jax.ShapeDtypeStruct((count,) + s.shape, s.dtype) for s in slabs)


def weights_kernel(count, slabs, swaps, *refs):
    refs = list(refs)

    def take(number):
        taken = refs[:number]
        del refs[:number]
        return taken

    sources, given = take(slabs), take(swaps)
    targets, paired, (zero_ref,) = take(slabs), take(swaps), take(1)
    stages = take(swaps)
    load_sem, keep_sem, swap_send, swap_recv = take(4)
    plan = Slabs(count, sources, targets, *refs)
    c, w = lax.axis_index("ctx"), lax.axis_index("wt")
    side = lax.rem(w, 2)
    partner = (c, flip(w, 1))
    greet(plan.devices() + [plan.near])

    def swap(i):
        return remote(given[i], paired[i].at[side], swap_send.at[i], swap_recv.at[i], partner)

    def load(i):
        return pltpu.make_async_copy(given[i], stages[i], load_sem.at[i])

    def keep(i):
        return pltpu.make_async_copy(stages[i], paired[i].at[side], keep_sem.at[i])

    plan.start()
    for i in range(swaps):
        swap(i).start()
        load(i).start()
    zero_ref[...] = jnp.zeros_like(zero_ref)
    for i in range(swaps):
        load(i).wait()
        keep(i).start()
    plan.relay()
    plan.finish()
    for i in range(swaps):
        keep(i).wait()
        swap(i).wait()


def gather_weights(slabs, swaps):
    count = lax.axis_size("wt")
    dma = pltpu.SemaphoreType.DMA((len(swaps),))
    pairs = tuple(jax.ShapeDtypeStruct((2,) + s.shape, s.dtype) for s in swaps)
    shapes = Slabs.shapes(slabs, count) + pairs
    return pl.pallas_call(
        functools.partial(weights_kernel, count, len(slabs), len(swaps)),
        out_shape=shapes + (jax.ShapeDtypeStruct((8, 128), jnp.int32),),
        in_specs=[pl.BlockSpec(memory_space=pl.ANY)] * (len(slabs) + len(swaps)),
        out_specs=(pl.BlockSpec(memory_space=pl.ANY),) * len(shapes)
        + (pl.BlockSpec(memory_space=pltpu.VMEM),),
        scratch_shapes=[pltpu.VMEM(s.shape, s.dtype) for s in swaps]
        + [dma] * 4
        + Slabs.scratch(slabs, count),
        compiler_params=pltpu.CompilerParams(
            collective_id=1, has_side_effects=True, vmem_limit_bytes=WIDE
        ),
        cost_estimate=LONG,
        name="gather_weights",
    )(*slabs, *swaps)


def gather_kernel(chips, downward, paired, count, slabs, passed, rows_ref, *refs):
    refs = list(refs)

    def take(number):
        taken = refs[:number]
        del refs[:number]
        return taken

    hops = count // 2 - 1
    sources, moved = take(slabs), take(passed)
    (out_ref,), targets, landed, (zero_ref,) = take(1), take(slabs), take(passed * hops), take(1)
    (stage,) = take(1)
    here, up_send, up_recv, down_send, down_recv, pair_send, pair_recv, near_send, near_recv = take(9)
    plan = Slabs(count, sources, targets, *take(6 + slabs)) if slabs else None
    pass_send, pass_recv = take(2) if passed else (None, None)
    zero_ref[...] = jnp.zeros_like(zero_ref)
    c, w = lax.axis_index("ctx"), lax.axis_index("wt")
    z = c // 2
    core = lax.rem(c, 2)
    side = lax.rem(w, 2) if paired else 0
    near, partner = (flip(c, 1), w), (c, flip(w, 1))
    above = (lax.rem(c + 2, 2 * chips), w)
    below = (lax.rem(c + 2 * chips - 2, 2 * chips), w)
    far = [(c, flip(w, 2 * d + 2)) for d in range(hops)]
    greet([near, above, below] + ([partner] if paired else []) + (plan.devices() if plan else []) + (far if passed else []))

    def onward(i, d):
        return remote(
            moved[i], landed[i * hops + d], pass_send.at[i, d], pass_recv.at[i, d], far[d]
        )

    def spot(chip, which, parity):
        return out_ref.at[chip, which, parity]

    def lift(chip, source):
        return remote(source, spot(chip, side, core), up_send.at[chip], up_recv.at[chip], above)

    def drop(chip, source):
        return remote(source, spot(chip, side, core), down_send.at[chip], down_recv.at[chip], below)

    def give(chip, source):
        return remote(source, spot(chip, side, core), pair_send.at[chip], pair_recv.at[chip], partner)

    def taken(chip):
        return remote(
            spot(chip, 1 - side, core), spot(chip, 1 - side, core), pair_send.at[chip], pair_recv.at[chip], partner
        )

    def hand(chip, which, source):
        return remote(source, spot(chip, which, core), near_send.at[chip, which], near_recv.at[chip, which], near)

    def handed(chip, which):
        there = spot(chip, which, 1 - core)
        return remote(there, there, near_send.at[chip, which], near_recv.at[chip, which], near)

    def settle_pair(chip):
        taken(chip).wait_recv()
        hand(chip, 1 - side, spot(chip, 1 - side, core)).start()

    load = pltpu.make_async_copy(rows_ref, stage, here.at[0])
    keep = pltpu.make_async_copy(stage, spot(z, side, core), here.at[1])
    load.start()
    pl.when(z < chips - 1)(lambda: lift(z, rows_ref).start())
    if downward:
        pl.when(z > 0)(lambda: drop(z, rows_ref).start())
    if paired:
        give(z, rows_ref).start()
    hand(z, side, rows_ref).start()
    if plan:
        plan.start()
    for d in range(hops):
        for i in range(passed):
            onward(i, d).start()
    load.wait()
    keep.start()
    for step in range(1, chips):
        low, high = z - step, z + step

        @pl.when(low >= 0)
        def _():
            lift(low, spot(low, side, core)).wait_recv()
            pl.when(z < chips - 1)(lambda: lift(low, spot(low, side, core)).start())
            if paired:
                give(low, spot(low, side, core)).start()
            hand(low, side, spot(low, side, core)).start()

        if downward:

            @pl.when(high < chips)
            def _():
                drop(high, spot(high, side, core)).wait_recv()
                pl.when(z > 0)(lambda: drop(high, spot(high, side, core)).start())
                if paired:
                    give(high, spot(high, side, core)).start()
                hand(high, side, spot(high, side, core)).start()

        if paired:
            if step == 1:
                settle_pair(z)
            else:
                pl.when(z - step + 1 >= 0)(lambda: settle_pair(z - step + 1))
                pl.when(z + step - 1 < chips)(lambda: settle_pair(z + step - 1))
    if paired:
        pl.when(z - chips + 1 >= 0)(lambda: settle_pair(z - chips + 1))
        pl.when(z + chips - 1 < chips)(lambda: settle_pair(z + chips - 1))
    keep.wait()
    if plan:
        plan.relay()
        plan.finish()

    def finish(chip):
        here_now = spot(chip, side, core)
        pl.when((z < chips - 1) & (chip <= z))(lambda: lift(chip, here_now).wait_send())
        if downward:
            pl.when((z > 0) & (chip >= z))(lambda: drop(chip, here_now).wait_send())
        if paired:
            give(chip, here_now).wait_send()
            for which in range(2):
                hand(chip, which, spot(chip, which, core)).wait_send()
                handed(chip, which).wait_recv()
        else:
            hand(chip, side, here_now).wait_send()
            handed(chip, side).wait_recv()

    for chip in range(chips):
        if downward:
            finish(chip)
        else:
            pl.when(chip <= z)(lambda: finish(chip))
    for d in range(hops):
        for i in range(passed):
            onward(i, d).wait()


def gather_rows(rows, collective_id, downward, paired, name, slabs=(), moved=()):
    chips = lax.axis_size("ctx") // 2
    count = lax.axis_size("wt")
    hops = count // 2 - 1
    line = pltpu.SemaphoreType.DMA((chips,))
    both = pltpu.SemaphoreType.DMA((chips, 2))
    shape = jax.ShapeDtypeStruct((chips, 2 if paired else 1, 2) + rows.shape, rows.dtype)
    landed = tuple(jax.ShapeDtypeStruct(m.shape, m.dtype) for m in moved for _ in range(hops))
    shapes = (shape,) + Slabs.shapes(slabs, count) + landed
    *results, zero = pl.pallas_call(
        functools.partial(gather_kernel, chips, downward, paired, count, len(slabs), len(moved)),
        out_shape=shapes + (jax.ShapeDtypeStruct((8, 128), jnp.int32),),
        in_specs=[pl.BlockSpec(memory_space=pl.ANY)] * (1 + len(slabs) + len(moved)),
        out_specs=(pl.BlockSpec(memory_space=pl.ANY),) * len(shapes)
        + (pl.BlockSpec(memory_space=pltpu.VMEM),),
        scratch_shapes=[pltpu.VMEM(rows.shape, rows.dtype), pltpu.SemaphoreType.DMA((2,))]
        + [line] * 6
        + [both] * 2
        + (Slabs.scratch(slabs, count) if slabs else [])
        + ([pltpu.SemaphoreType.DMA((len(moved), hops))] * 2 if moved else []),
        compiler_params=pltpu.CompilerParams(
            collective_id=collective_id, has_side_effects=True, vmem_limit_bytes=WIDE
        ),
        cost_estimate=LONG,
        name=name,
    )(rows, *slabs, *moved)
    return results + [zero[0, 0]]


def scatter_kernel(chips, upward, paired, pieces, partial_ref, out_ref, own, sib, mate, low_in, high_in, load, near_send, near_recv, pair_send, pair_recv, up_send, up_recv, down_send, down_recv):
    c, w = lax.axis_index("ctx"), lax.axis_index("wt")
    z = c // 2
    core = lax.rem(c, 2)
    side = lax.rem(w, 2) if paired else 0
    sides = 2 if paired else 1
    near, partner = (flip(c, 1), w), (c, flip(w, 1))
    above = (lax.rem(c + 2, 2 * chips), w)
    below = (lax.rem(c + 2 * chips - 2, 2 * chips), w)
    rows = own.shape[2] // pieces
    greet([near, above, below] + ([partner] if paired else []))
    order = []
    for i in range(chips // 2):
        order += [chips - 1 - i, i]
    if chips % 2:
        order.append(chips // 2)
    if not upward:
        order = list(range(chips))

    def wanted(chip, action):
        if upward:
            action()
        else:
            pl.when(chip <= z)(action)

    def fetch(chip, which):
        return pltpu.make_async_copy(
            partial_ref.at[chip, which, core], own.at[chip, which], load.at[chip, which]
        )

    def hand(chip, which):
        return remote(
            partial_ref.at[chip, which, 1 - core],
            sib.at[chip, which],
            near_send.at[chip, which],
            near_recv.at[chip, which],
            near,
        )

    def cut(piece):
        return pl.ds(piece * rows, rows)

    def give(chip, piece):
        return remote(
            own.at[chip, 1 - side, cut(piece)],
            mate.at[chip, cut(piece)],
            pair_send.at[chip, piece],
            pair_recv.at[chip, piece],
            partner,
        )

    def lift(chip, piece):
        return remote(
            own.at[chip, side, cut(piece)],
            low_in.at[chip, cut(piece)],
            up_send.at[chip, piece],
            up_recv.at[chip, piece],
            above,
        )

    def drop(chip, piece):
        return remote(
            own.at[chip, side, cut(piece)],
            high_in.at[chip, cut(piece)],
            down_send.at[chip, piece],
            down_recv.at[chip, piece],
            below,
        )

    def add_into(chip, which, piece, other):
        spot = own.at[chip, which, cut(piece)]
        spot[...] = spot[...] + other[...]

    for chip in order:

        def begin(chip=chip):
            for which in range(sides):
                hand(chip, which).start()
                fetch(chip, which).start()

        wanted(chip, begin)

    def meet(chip):
        for which in range(sides):
            fetch(chip, which).wait()
            hand(chip, which).wait_recv()
        for piece in range(pieces):
            if paired:
                add_into(chip, 1 - side, piece, sib.at[chip, 1 - side, cut(piece)])
                give(chip, piece).start()
            add_into(chip, side, piece, sib.at[chip, side, cut(piece)])

    def travel(chip):
        for piece in range(pieces):
            if paired:
                give(chip, piece).wait_recv()
                add_into(chip, side, piece, mate.at[chip, cut(piece)])
            if upward:

                @pl.when(z < chip)
                def _():
                    @pl.when(z > 0)
                    def _():
                        lift(chip, piece).wait_recv()
                        add_into(chip, side, piece, low_in.at[chip, cut(piece)])

                    lift(chip, piece).start()

            @pl.when(z > chip)
            def _():
                @pl.when(z < chips - 1)
                def _():
                    drop(chip, piece).wait_recv()
                    add_into(chip, side, piece, high_in.at[chip, cut(piece)])

                drop(chip, piece).start()

    for i, chip in enumerate(order):
        wanted(chip, lambda: meet(chip))
        if i >= 1:
            wanted(order[i - 1], lambda: travel(order[i - 1]))
    wanted(order[-1], lambda: travel(order[-1]))
    for piece in range(pieces):
        out_ref[cut(piece), :] = own.at[z, side, cut(piece)][...].astype(jnp.float32)
    for piece in range(pieces):
        if upward:

            @pl.when(z > 0)
            def _():
                lift(z, piece).wait_recv()
                out_ref[cut(piece), :] += low_in.at[z, cut(piece)][...].astype(jnp.float32)

        @pl.when(z < chips - 1)
        def _():
            drop(z, piece).wait_recv()
            out_ref[cut(piece), :] += high_in.at[z, cut(piece)][...].astype(jnp.float32)

    def finish(chip):
        for which in range(sides):
            hand(chip, which).wait_send()
        for piece in range(pieces):
            if paired:
                give(chip, piece).wait_send()
            if upward:
                pl.when(z < chip)(lambda: lift(chip, piece).wait_send())
            pl.when(z > chip)(lambda: drop(chip, piece).wait_send())

    for chip in order:
        wanted(chip, lambda: finish(chip))


def scatter_rows(partial, collective_id, upward, paired, name):
    chips, sides, _, tokens, width = partial.shape
    pieces = 2
    dma = pltpu.SemaphoreType.DMA
    block = (tokens, width)
    return pl.pallas_call(
        functools.partial(scatter_kernel, chips, upward, paired, pieces),
        out_shape=jax.ShapeDtypeStruct(block, jnp.float32),
        in_specs=[pl.BlockSpec(memory_space=pl.ANY)],
        out_specs=pl.BlockSpec(memory_space=pltpu.VMEM),
        scratch_shapes=[
            pltpu.VMEM((chips, sides) + block, jnp.bfloat16),
            pltpu.VMEM((chips, sides) + block, jnp.bfloat16),
            pltpu.VMEM((chips if paired else 1,) + block, jnp.bfloat16),
            pltpu.VMEM((chips if upward else 1,) + block, jnp.bfloat16),
            pltpu.VMEM((chips,) + block, jnp.bfloat16),
            dma((chips, 2)),
            dma((chips, 2)),
            dma((chips, 2)),
        ]
        + [dma((chips, pieces))] * 6,
        compiler_params=pltpu.CompilerParams(
            collective_id=collective_id, has_side_effects=True, vmem_limit_bytes=WIDE
        ),
        cost_estimate=LONG if paired else CHEAP,
        name=name,
    )(partial)


def dense_kernel(chips, count, matrices, pieces, *refs):
    refs = list(refs)

    def take(number):
        taken = refs[:number]
        del refs[:number]
        return taken

    grads, outs = take(matrices), take(matrices)
    own, sib, mates, low, final = (take(matrices) for _ in range(5))
    (load, near_send, near_recv, send, recv, low_send, low_recv, back_send, back_recv, last_send, last_recv, keep) = refs
    c, w = lax.axis_index("ctx"), lax.axis_index("wt")
    z = c // 2
    core = lax.rem(c, 2)
    near = (flip(c, 1), w)
    above = (lax.rem(c + 2, 2 * chips), w)
    below = (lax.rem(c + 2 * chips - 2, 2 * chips), w)
    peers = [flip(w, d) for d in range(1, count)]
    greet([near, above, below] + [(c, p) for p in peers])

    def span(j, parity=None):
        m, first, rows = pieces[j]
        if parity is None:
            return pl.ds(first, rows)
        half = grads[m].shape[1] // 2
        return pl.ds(pl.multiple_of(parity * half + first, 16), rows)

    def fetch(j):
        m = pieces[j][0]
        return pltpu.make_async_copy(grads[m].at[:, span(j, core)], own[m].at[:, span(j)], load.at[j])

    def hand(j):
        m = pieces[j][0]
        return remote(
            grads[m].at[:, span(j, 1 - core)], sib[m].at[:, span(j)], near_send.at[j], near_recv.at[j], near
        )

    def give(j, d):
        m = pieces[j][0]
        return remote(
            own[m].at[peers[d], span(j)], mates[m].at[d, span(j)], send.at[j, d], recv.at[j, d], (c, peers[d])
        )

    def total(j):
        return own[pieces[j][0]].at[w, span(j)]

    def add(spot, other):
        spot[...] = spot[...] + other[...]

    def start(j):
        hand(j).start()
        fetch(j).start()

    def share(j):
        m = pieces[j][0]
        fetch(j).wait()
        hand(j).wait_recv()
        for d in range(count - 1):
            add(own[m].at[peers[d], span(j)], sib[m].at[peers[d], span(j)])
            give(j, d).start()
        add(total(j), sib[m].at[w, span(j)])

    def collect(j):
        m = pieces[j][0]
        value = total(j)[...].astype(jnp.float32)
        for d in range(count - 1):
            give(j, d).wait_recv()
            value = value + mates[m][d, span(j), :].astype(jnp.float32)
        total(j)[...] = value.astype(jnp.bfloat16)

    def line(j):
        return (z, above, below) if j % 2 == 0 else (chips - 1 - z, below, above)

    def onward(j):
        m = pieces[j][0]
        return remote(total(j), low[m].at[span(j)], low_send.at[j], low_recv.at[j], line(j)[1])

    def backward(j):
        spot = final[pieces[j][0]].at[span(j)]
        return remote(spot, spot, back_send.at[j], back_recv.at[j], line(j)[2])

    def across(j, parity):
        m = pieces[j][0]
        return remote(
            final[m].at[span(j)], outs[m].at[span(j, parity)], last_send.at[j], last_recv.at[j], near
        )

    def store(j):
        m = pieces[j][0]
        return pltpu.make_async_copy(final[m].at[span(j)], outs[m].at[span(j, core)], keep.at[j])

    def accumulate(j):
        place = line(j)[0]
        m = pieces[j][0]

        @pl.when(place > 0)
        def _():
            onward(j).wait_recv()
            add(total(j), low[m].at[span(j)])

        @pl.when(place < chips - 1)
        def _():
            onward(j).start()

        @pl.when(place == chips - 1)
        def _():
            final[m][span(j), :] = total(j)[...]
            backward(j).start()
            across(j, core).start()
            store(j).start()

    def spread(j):
        place = line(j)[0]

        @pl.when(place < chips - 1)
        def _():
            backward(j).wait_recv()
            pl.when(place > 0)(lambda: backward(j).start())
            across(j, core).start()
            store(j).start()

    number = len(pieces)
    for j in range(number):
        start(j)
    for j in range(number):
        share(j)
    last = chips - 1
    for t in range(number + 2 * last):
        if t < number:
            collect(t)
        for hop in range(2 * last, -1, -1):
            j = t - hop
            if not 0 <= j < number:
                continue
            if hop <= last:
                pl.when(line(j)[0] == hop)(lambda: accumulate(j))
            if hop > last:
                pl.when(line(j)[0] == 2 * last - hop)(lambda: spread(j))
    for j in range(number):
        place = line(j)[0]
        hand(j).wait_send()
        for d in range(count - 1):
            give(j, d).wait_send()
        pl.when(place < chips - 1)(lambda: onward(j).wait_send())
        pl.when(place > 0)(lambda: backward(j).wait_send())
        across(j, core).wait_send()
        across(j, 1 - core).wait_recv()
        store(j).wait()


def reduce_dense(grads):
    count = lax.axis_size("wt")
    chips = lax.axis_size("ctx") // 2
    shapes = [(g.shape[0] // count, g.shape[1]) for g in grads]
    pieces = []
    for m, (rows, _) in enumerate(shapes):
        half, width = rows // 2, shapes[m][1]
        cuts = max(n for n in range(1, 5) if half % (16 * n) == 0 and (n == 1 or half * width > 120000 * (n - 1)))
        for i in range(cuts):
            pieces.append((m, i * (rows // 2 // cuts), rows // 2 // cuts))
    halves = [(rows // 2, width) for rows, width in shapes]
    dma = pltpu.SemaphoreType.DMA
    one, many = dma((len(pieces),)), dma((len(pieces), count - 1))
    return pl.pallas_call(
        functools.partial(dense_kernel, chips, count, len(grads), tuple(pieces)),
        out_shape=[jax.ShapeDtypeStruct(s, jnp.bfloat16) for s in shapes],
        in_specs=[pl.BlockSpec(memory_space=pl.ANY)] * len(grads),
        out_specs=[pl.BlockSpec(memory_space=pl.ANY)] * len(grads),
        scratch_shapes=[pltpu.VMEM((count,) + h, jnp.bfloat16) for h in halves]
        + [pltpu.VMEM((count,) + h, jnp.bfloat16) for h in halves]
        + [pltpu.VMEM((count - 1,) + h, jnp.bfloat16) for h in halves]
        + [pltpu.VMEM(h, jnp.bfloat16) for h in halves]
        + [pltpu.VMEM(h, jnp.bfloat16) for h in halves]
        + [one, one, one, many, many, one, one, one, one, one, one, one],
        compiler_params=pltpu.CompilerParams(
            collective_id=7, has_side_effects=True, vmem_limit_bytes=WIDE
        ),
        cost_estimate=LONG,
        name="reduce_dense",
    )(*[g.reshape((count,) + s) for g, s in zip(grads, shapes)])


def dot_of(a, b, left, right):
    return lax.dot_general(
        a, b, (((left,), (right,)), ((), ())), preferred_element_type=jnp.float32
    )


def stacked_heads(ref):
    return jnp.concatenate(
        [ref[:, h * HEAD_DIM : (h + 1) * HEAD_DIM] for h in range(ref.shape[1] // HEAD_DIM)], axis=0
    )


exponent_scale = HEAD_DIM ** (-0.5) * math.log2(math.e)


def attend_kernel(place_ref, query_ref, both_ref, row_ref, column_ref, out_ref, log_ref, best, total, accum):
    tokens = query_ref.shape[0]
    group = query_ref.shape[1] // HEAD_DIM
    width = 2 * tokens
    place = place_ref[0]
    queries = stacked_heads(query_ref)
    best[...] = jnp.full_like(best, masked_value)
    total[...] = jnp.zeros_like(total)
    accum[...] = jnp.zeros_like(accum)
    query_pos = place * tokens + lax.broadcasted_iota(jnp.int32, (tokens, width), 0)
    key_pos = lax.broadcasted_iota(jnp.int32, (tokens, width), 1)

    def step(j, carry):
        span = pl.ds(pl.multiple_of(j * width, width), width)
        allowed = (key_pos + j * width <= query_pos) & (row_ref[0:1, span] == column_ref[:, 0:1])
        bias = jnp.where(allowed, 0.0, masked_value)
        scores = dot_of(queries, both_ref[span, :HEAD_DIM], 1, 1)
        scores = (scores.reshape(group, tokens, width) + bias[None]).reshape(group * tokens, width)
        newest = jnp.maximum(best[...], jnp.max(scores, axis=1, keepdims=True))
        factor = jnp.exp2((best[...] - newest) * exponent_scale)
        weights = jnp.exp2((scores - newest[:, :1]) * exponent_scale)
        total[...] = total[...] * factor + jnp.sum(weights, axis=1, keepdims=True)
        accum[...] = accum[...] * factor + dot_of(
            weights.astype(jnp.bfloat16), both_ref[span, HEAD_DIM:], 1, 0
        )
        best[...] = newest
        return carry

    lax.fori_loop(0, place // 2 + 1, step, 0)
    heads = accum[...] / total[...]
    for h in range(group):
        out_ref[:, h * HEAD_DIM : (h + 1) * HEAD_DIM] = heads[h * tokens : (h + 1) * tokens]
    logs = best[...] * exponent_scale + jnp.log2(total[...])
    log_ref[0] = jnp.transpose(logs)[:8]


def attend(place, projected, both, seg_row, seg_column):
    tokens = projected.shape[0]
    group = HEADS // KV_HEADS
    rows, span = group * tokens, both.shape[0]
    stat = pltpu.VMEM((rows, HEAD_DIM), jnp.float32)
    return pl.pallas_call(
        attend_kernel,
        grid=(KV_HEADS,),
        out_shape=(
            jax.ShapeDtypeStruct((tokens, HEADS * HEAD_DIM), jnp.float32),
            jax.ShapeDtypeStruct((KV_HEADS, 8, rows), jnp.float32),
        ),
        in_specs=[
            pl.BlockSpec(memory_space=pltpu.SMEM),
            pl.BlockSpec((tokens, group * HEAD_DIM), lambda g: (0, g)),
            pl.BlockSpec((span, 2 * HEAD_DIM), lambda g: (0, g)),
            pl.BlockSpec((1, span), lambda g: (0, 0)),
            pl.BlockSpec((tokens, 1), lambda g: (0, 0)),
        ],
        out_specs=(
            pl.BlockSpec((tokens, group * HEAD_DIM), lambda g: (0, g)),
            pl.BlockSpec((1, 8, rows), lambda g: (g, 0, 0)),
        ),
        scratch_shapes=[stat, stat, stat],
        compiler_params=pltpu.CompilerParams(vmem_limit_bytes=WIDE),
        cost_estimate=CHEAP,
        name="attend",
    )(place, projected, both, seg_row, seg_column)


def attend_back_kernel(place_ref, query_ref, both_ref, row_ref, column_ref, heads_ref, grad_ref, log_ref, grad_query_ref, grad_both_ref, accum):
    tokens = query_ref.shape[0]
    group = query_ref.shape[1] // HEAD_DIM
    width = 2 * tokens
    rows = group * tokens
    scale = HEAD_DIM ** (-0.5)
    place = place_ref[0]
    queries, grads = stacked_heads(query_ref), stacked_heads(grad_ref)
    product = grads.astype(jnp.float32) * stacked_heads(heads_ref)
    delta = jnp.sum(product, axis=1, keepdims=True)
    delta = jnp.transpose(jnp.broadcast_to(delta, (rows, HEAD_DIM)))[0:1]
    logs = log_ref[0, 0:1, :]
    accum[...] = jnp.zeros_like(accum)
    grad_both_ref[...] = jnp.zeros_like(grad_both_ref)
    query_pos = place * tokens + lax.broadcasted_iota(jnp.int32, (width, tokens), 1)
    key_pos = lax.broadcasted_iota(jnp.int32, (width, tokens), 0)

    def step(j, carry):
        span = pl.ds(pl.multiple_of(j * width, width), width)
        allowed = (key_pos + j * width <= query_pos) & (column_ref[span, 0:1] == row_ref[0:1, :])
        bias = jnp.where(allowed, 0.0, masked_value)
        bias = jnp.concatenate([bias] * group, axis=1)
        keys, values = both_ref[span, :HEAD_DIM], both_ref[span, HEAD_DIM:]
        scores = dot_of(keys, queries, 1, 1)
        probs = jnp.exp2(scores * exponent_scale + bias - logs)
        grad_probs = dot_of(values, grads, 1, 1)
        grad_scores = (probs * (grad_probs - delta)).astype(jnp.bfloat16)
        accum[...] += dot_of(grad_scores, keys, 0, 0)
        grad_both_ref[span, :HEAD_DIM] = (dot_of(grad_scores, queries, 1, 0) * scale).astype(jnp.bfloat16)
        grad_both_ref[span, HEAD_DIM:] = dot_of(probs.astype(jnp.bfloat16), grads, 1, 0).astype(jnp.bfloat16)
        return carry

    lax.fori_loop(0, place // 2 + 1, step, 0)
    grad_queries = (accum[...] * scale).astype(jnp.bfloat16)
    for h in range(group):
        grad_query_ref[:, h * HEAD_DIM : (h + 1) * HEAD_DIM] = grad_queries[h * tokens : (h + 1) * tokens]


def attend_back(place, projected, both, query_seg_row, seg_column, heads_out, grad_attended, logs):
    tokens = projected.shape[0]
    group = HEADS // KV_HEADS
    rows, span = group * tokens, both.shape[0]
    per_group = pl.BlockSpec((tokens, group * HEAD_DIM), lambda g: (0, g))
    return pl.pallas_call(
        attend_back_kernel,
        grid=(KV_HEADS,),
        out_shape=(
            jax.ShapeDtypeStruct((tokens, HEADS * HEAD_DIM), jnp.bfloat16),
            jax.ShapeDtypeStruct(both.shape, jnp.bfloat16),
        ),
        in_specs=[
            pl.BlockSpec(memory_space=pltpu.SMEM),
            per_group,
            pl.BlockSpec((span, 2 * HEAD_DIM), lambda g: (0, g)),
            pl.BlockSpec((1, tokens), lambda g: (0, 0)),
            pl.BlockSpec((span, 1), lambda g: (0, 0)),
            per_group,
            per_group,
            pl.BlockSpec((1, 8, rows), lambda g: (g, 0, 0)),
        ],
        out_specs=(per_group, pl.BlockSpec((span, 2 * HEAD_DIM), lambda g: (0, g))),
        scratch_shapes=[pltpu.VMEM((rows, HEAD_DIM), jnp.float32)],
        compiler_params=pltpu.CompilerParams(vmem_limit_bytes=WIDE),
        cost_estimate=CHEAP,
        name="attend_back",
    )(place, projected, both, query_seg_row, seg_column, heads_out, grad_attended, logs)


def pick_rows_of(slot_rows, rows_of, local, depth, tokens):
    place = lax.broadcasted_iota(jnp.int32, (depth, tokens), 0)
    total, masks = None, []
    for core in range(2):
        chosen = [slot_rows[core][e : e + 1] == place for e in range(local)]
        ones = jnp.concatenate([c.astype(jnp.float32) for c in chosen], axis=0).astype(jnp.bfloat16)
        term = jnp.dot(ones, rows_of(core), preferred_element_type=jnp.float32)
        total = term if total is None else total + term
        masks.append(chosen)
    return total, masks


def pick_grads_kernel(local, first_ref, earlier_ref, rows_ref, out_ref, scale_ref, slot_ref):
    depth = out_ref.shape[3]
    tokens = slot_ref.shape[3] // 2
    slot_rows, gate_rows, count = [], [], None
    for core in range(2):
        table = rows_ref[0, core, 0, tokens : tokens + 16, :].astype(jnp.float32)
        member, gate = [], []
        for e in range(local):
            expert = (first_ref[0] + e).astype(jnp.float32)
            found, weight = None, None
            for k in range(TOPK):
                span = slice(k * tokens, (k + 1) * tokens)
                named = table[0:1, span] == expert
                value = jnp.where(named, table[1:2, span] + table[2:3, span] + table[3:4, span], 0.0)
                mark = jnp.where(named, 1.0, 0.0)
                found = mark if k == 0 else found + mark
                weight = value if k == 0 else weight + value
            member.append(found)
            gate.append(weight)
        member = jnp.concatenate(member + [jnp.zeros((8 - local, tokens), jnp.float32)], axis=0)
        rank = jnp.dot(member.astype(jnp.bfloat16), earlier_ref[...], preferred_element_type=jnp.float32)
        if core:
            rank = rank + count
        count = jnp.sum(member, axis=1, keepdims=True)
        slots = jnp.where(member > 0.5, rank.astype(jnp.int32), -1)[:local]
        slot_ref[0, 0, :, core * tokens : (core + 1) * tokens] = slots
        slot_rows.append(slots)
        gate_rows.append(gate)
    total, masks = pick_rows_of(
        slot_rows, lambda core: rows_ref[0, core, 0, :tokens, :], local, depth, tokens
    )
    weight = None
    for core in range(2):
        gates = jnp.concatenate(
            [
                jnp.sum(jnp.where(masks[core][e], gate_rows[core][e], 0.0), axis=1, keepdims=True)
                for e in range(local)
            ],
            axis=0,
        )
        weight = gates if core == 0 else weight + gates
    scale_ref[0, 0] = jnp.broadcast_to(weight, (local * depth, 128)).reshape(local, depth, 128)
    out_ref[0, 0] = (total * weight).astype(jnp.bfloat16).reshape(local, depth, total.shape[1])


def pick_grads(rows, first, local, tokens):
    chips, _, sides, long, width = rows.shape
    depth = 2 * CAP
    earlier = jnp.arange(tokens)[:, None] < jnp.arange(tokens)[None, :]
    return pl.pallas_call(
        functools.partial(pick_grads_kernel, local),
        grid=(chips, sides),
        out_shape=(
            jax.ShapeDtypeStruct((chips, sides, local, depth, width), jnp.bfloat16),
            jax.ShapeDtypeStruct((chips, sides, local, depth, 128), jnp.float32),
            jax.ShapeDtypeStruct((chips, sides, local, 2 * tokens), jnp.int32),
        ),
        in_specs=[
            pl.BlockSpec(memory_space=pltpu.SMEM),
            pl.BlockSpec((tokens, tokens), lambda z, s: (0, 0)),
            pl.BlockSpec((1, 2, 1, long, width), lambda z, s: (z, 0, s, 0, 0)),
        ],
        out_specs=(
            pl.BlockSpec((1, 1, local, depth, width), lambda z, s: (z, s, 0, 0, 0)),
            pl.BlockSpec((1, 1, local, depth, 128), lambda z, s: (z, s, 0, 0, 0)),
            pl.BlockSpec((1, 1, local, 2 * tokens), lambda z, s: (z, s, 0, 0)),
        ),
        compiler_params=pltpu.CompilerParams(vmem_limit_bytes=WIDE),
        cost_estimate=CHEAP,
        name="pick_grads",
    )(first, earlier.astype(jnp.bfloat16), rows)


def pick_tokens_kernel(slot_ref, rows_ref, out_ref):
    local, depth = out_ref.shape[2], out_ref.shape[3]
    tokens = rows_ref.shape[3]
    slot_rows = [slot_ref[0, 0, :, core * tokens : (core + 1) * tokens] for core in range(2)]
    total, _ = pick_rows_of(slot_rows, lambda core: rows_ref[0, 0, core], local, depth, tokens)
    out_ref[0, 0] = total.astype(jnp.bfloat16).reshape(local, depth, total.shape[1])


def pick_tokens(rows, slots):
    chips, sides, local, both = slots.shape
    tokens, width = rows.shape[3:]
    depth = 2 * CAP
    return pl.pallas_call(
        pick_tokens_kernel,
        grid=(chips, sides),
        out_shape=jax.ShapeDtypeStruct((chips, sides, local, depth, width), jnp.bfloat16),
        in_specs=[
            pl.BlockSpec((1, 1, local, both), lambda z, s: (z, s, 0, 0)),
            pl.BlockSpec((1, 1, 2, tokens, width), lambda z, s: (z, s, 0, 0, 0)),
        ],
        out_specs=pl.BlockSpec((1, 1, local, depth, width), lambda z, s: (z, s, 0, 0, 0)),
        compiler_params=pltpu.CompilerParams(vmem_limit_bytes=WIDE),
        cost_estimate=CHEAP,
        name="pick_tokens",
    )(slots, rows)


def spread_kernel(apart, slot_ref, rows_ref, out_ref):
    local, depth, width = rows_ref.shape[2:]
    tokens = out_ref.shape[3]
    place = lax.broadcasted_iota(jnp.int32, (depth, tokens), 0)
    rows = rows_ref[0, 0].reshape(local * depth, width)
    for core in range(2):
        span = slice(core * tokens, (core + 1) * tokens)
        ones = jnp.concatenate(
            [(slot_ref[0, 0, e : e + 1, span] == place).astype(jnp.float32) for e in range(local)], axis=0
        ).astype(jnp.bfloat16)
        spot = out_ref.at[0, core, 0] if apart else out_ref.at[0, 0, core]
        spot[...] = lax.dot_general(
            ones, rows, (((0,), (0,)), ((), ())), preferred_element_type=jnp.float32
        ).astype(jnp.bfloat16)


def spread_rows(rows, slots, name, apart):
    chips, sides, local, both = slots.shape
    depth, width = rows.shape[3:]
    tokens = both // 2
    return pl.pallas_call(
        functools.partial(spread_kernel, apart),
        grid=(chips, sides),
        out_shape=jax.ShapeDtypeStruct(
            (chips, 2, sides, tokens, width) if apart else (chips, sides, 2, tokens, width), jnp.bfloat16
        ),
        in_specs=[
            pl.BlockSpec((1, 1, local, both), lambda z, s: (z, s, 0, 0)),
            pl.BlockSpec((1, 1, local, depth, width), lambda z, s: (z, s, 0, 0, 0)),
        ],
        out_specs=pl.BlockSpec((1, 2, 1, tokens, width), lambda z, s: (z, 0, s, 0, 0))
        if apart
        else pl.BlockSpec((1, 1, 2, tokens, width), lambda z, s: (z, s, 0, 0, 0)),
        compiler_params=pltpu.CompilerParams(vmem_limit_bytes=WIDE),
        cost_estimate=CHEAP,
        name=name,
    )(slots, rows)


def expert_kernel(blocks, x_ref, g_ref, scale_ref, *refs):
    tall_refs, down_refs = refs[:blocks], refs[blocks : 2 * blocks]
    result_ref, back_ref, *grad_refs = refs[2 * blocks :]
    hops = len(grad_refs) // 3
    grad_gate_refs, grad_up_refs = grad_refs[:hops], grad_refs[hops : 2 * hops]
    grad_down_refs = grad_refs[2 * hops :]
    w = lax.axis_index("wt")
    chips, sides, _, depth, width = x_ref.shape
    rows = chips * sides * depth
    part = tall_refs[0].shape[2]
    nn, nt, tn = (((1,), (0,)), ((), ())), (((1,), (1,)), ((), ())), (((0,), (0,)), ((), ()))

    def dot(a, b, dims):
        return lax.dot_general(a, b, dims, preferred_element_type=jnp.float32)

    def columns(ref, q):
        if blocks == 1:
            return ref.at[:, :, 0]
        span = pl.ds(pl.multiple_of(flip(w, q) * part, 128), part)
        return ref.at[:, :, 0, :, span]

    def piece(ref, q):
        return columns(ref, q)[...].reshape(rows, part)

    gate, up, grad_inner = None, None, None
    for q in range(blocks):
        x = piece(x_ref, q)
        more_gate, more_up = dot(x, tall_refs[q][0, 0], nn), dot(x, tall_refs[q][0, 1], nn)
        gate, up = (more_gate, more_up) if q == 0 else (gate + more_gate, up + more_up)
    for q in range(blocks):
        more = dot(piece(g_ref, q), down_refs[q][0], nt)
        grad_inner = more if q == 0 else grad_inner + more
    sigmoid = jax.nn.sigmoid(gate)
    activated = gate * sigmoid
    inner = (activated * up).astype(jnp.bfloat16)
    grad_gate = (grad_inner * up * (sigmoid * (1.0 + gate * (1.0 - sigmoid)))).astype(jnp.bfloat16)
    grad_up = (grad_inner * activated).astype(jnp.bfloat16)
    scale = scale_ref[...].reshape(rows, 128)[:, :1]
    for q in range(blocks):
        result = dot(inner, down_refs[q][0], nn) * scale
        columns(result_ref, q)[...] = result.astype(jnp.bfloat16).reshape(chips, sides, depth, part)
        back = dot(grad_gate, tall_refs[q][0, 0], nt) + dot(grad_up, tall_refs[q][0, 1], nt)
        columns(back_ref, q)[...] = back.astype(jnp.bfloat16).reshape(chips, sides, depth, part)
        grad_down_refs[q // 2][q % 2, 0] = dot(inner, piece(g_ref, q), tn).astype(jnp.bfloat16)
        x = piece(x_ref, q)
        grad_gate_refs[q // 2][q % 2, 0] = dot(x, grad_gate, tn).astype(jnp.bfloat16)
        grad_up_refs[q // 2][q % 2, 0] = dot(x, grad_up, tn).astype(jnp.bfloat16)


def run_experts(x, g, scale, talls, downs):
    chips, sides, local, depth, width = x.shape
    blocks = len(talls)
    part, inner = talls[0].shape[2:]
    large = chips * sides * depth > 1024
    rows = pl.BlockSpec((chips, sides, 1, depth, width), lambda e: (0, 0, e, 0, 0))
    sources = pl.BlockSpec(
        (chips, sides, 1, depth, width),
        lambda e: (0, 0, e, 0, 0),
        pipeline_mode=pl.Buffered(1 if large else 2),
    )
    scales = pl.BlockSpec((chips, sides, 1, depth, 128), lambda e: (0, 0, e, 0, 0))
    tall = pl.BlockSpec((1, 2, part, inner), lambda e: (e, 0, 0, 0))
    flat = pl.BlockSpec((1, inner, part), lambda e: (e, 0, 0))
    hops, each = max(blocks // 2, 1), min(blocks, 2)
    tall_out = pl.BlockSpec((each, 1, part, inner), lambda e: (0, e, 0, 0))
    flat_out = pl.BlockSpec((each, 1, inner, part), lambda e: (0, e, 0, 0))
    return pl.pallas_call(
        functools.partial(expert_kernel, blocks),
        grid=(local,),
        out_shape=(
            jax.ShapeDtypeStruct(x.shape, jnp.bfloat16),
            jax.ShapeDtypeStruct(x.shape, jnp.bfloat16),
            *[jax.ShapeDtypeStruct((each, local, part, inner), jnp.bfloat16)] * (2 * hops),
            *[jax.ShapeDtypeStruct((each, local, inner, part), jnp.bfloat16)] * hops,
        ),
        in_specs=[sources, sources, scales] + [tall] * blocks + [flat] * blocks,
        out_specs=(rows, rows) + (tall_out,) * (2 * hops) + (flat_out,) * hops,
        compiler_params=pltpu.CompilerParams(vmem_limit_bytes=60 * 2**20),
        cost_estimate=CHEAP,
        name="experts",
    )(x, g, scale, *talls, *downs)


def place_kernel(arrivals, side_ref, *refs):
    own, other, more, outs = refs[:3], refs[3:6], refs[6 : 6 + 3 * arrivals], refs[6 + 3 * arrivals :]
    mine = pl.program_id(0) == side_ref[0]

    @pl.when(mine)
    def _():
        for i in range(3):
            value = own[i][0, 0].astype(jnp.float32)
            for m in more[i * arrivals : (i + 1) * arrivals]:
                value = value + m[0, 0].astype(jnp.float32)
            outs[i][0] = value

    @pl.when(jnp.logical_not(mine))
    def _():
        for i in range(3):
            outs[i][0] = other[i][0].astype(jnp.float32)


def place_experts(side, own, more, other):
    local = other[0].shape[0]
    arrivals = len(more[0])
    shapes = [o.shape[1:] for o in other]
    paired = [pl.BlockSpec((1, 1) + s, lambda h, e: (0, e, 0, 0)) for s in shapes]
    single = [pl.BlockSpec((1,) + s, lambda h, e: (e, 0, 0)) for s in shapes]
    return pl.pallas_call(
        functools.partial(place_kernel, arrivals),
        grid=(2, local),
        out_shape=[jax.ShapeDtypeStruct((2 * local,) + s, jnp.float32) for s in shapes],
        in_specs=[pl.BlockSpec(memory_space=pltpu.SMEM)]
        + paired
        + single
        + [p for p in paired for _ in range(arrivals)],
        out_specs=[pl.BlockSpec((1,) + s, lambda h, e: (h * local + e, 0, 0)) for s in shapes],
        compiler_params=pltpu.CompilerParams(vmem_limit_bytes=WIDE),
        cost_estimate=CHEAP,
        name="place_experts",
    )(side, *own, *other, *[m for group in more for m in group])


def swap_pairs(value, axis, distance):
    count = lax.axis_size(axis)
    return lax.ppermute(value, axis, [(i, i ^ distance) for i in range(count)])


def own_and_other(stacked, mine):
    return (
        lax.dynamic_index_in_dim(stacked, mine, 0, keepdims=False),
        lax.dynamic_index_in_dim(stacked, 1 - mine, 0, keepdims=False),
    )


def collect_expert(shard, side, pairs):
    local = shard.shape[0]
    kept, given = own_and_other(shard.reshape((2, local // 2) + shard.shape[1:]), side)
    return kept, swap_pairs(given, "wt", 1), [swap_pairs(kept, "wt", 2 * d) for d in range(1, pairs)]


def settle_blocks(blocks, index, axis):
    stacked = jnp.stack(blocks)
    return jnp.concatenate(
        [
            lax.dynamic_index_in_dim(stacked, jnp.bitwise_xor(j, index), 0, False)
            for j in range(len(blocks))
        ],
        axis=axis,
    )


def split_blocks(whole, index, count, axis):
    parts = jnp.stack(jnp.split(whole, count, axis=axis))
    return jnp.stack(
        [
            lax.dynamic_index_in_dim(parts, jnp.bitwise_xor(q, index), 0, False)
            for q in range(count)
        ]
    )


def body(
    hidden,
    segment_ids,
    routes,
    gates,
    cotangent,
    norm_one_gain,
    w_query,
    w_key,
    w_value,
    w_out,
    norm_two_gain,
    shared_gate,
    shared_up,
    shared_down,
    expert_gate,
    expert_up,
    expert_down,
):
    wt_index = lax.axis_index("wt")
    wt_count = lax.axis_size("wt")
    ctx_count = lax.axis_size("ctx")
    chips = ctx_count // 2
    pairs = wt_count // 2
    tokens, width_model = hidden.shape[1:]
    wide, kv_width = w_query.shape[1], w_key.shape[1]
    shared_width = shared_gate.shape[1]
    gates_here = gates[0]
    gate_high = gates_here.astype(jnp.bfloat16)
    gate_rest = gates_here - gate_high.astype(jnp.float32)
    gate_middle = gate_rest.astype(jnp.bfloat16)
    gate_low = (gate_rest - gate_middle.astype(jnp.float32)).astype(jnp.bfloat16)
    table = jnp.concatenate(
        [routes[0].astype(jnp.bfloat16), gate_high, gate_middle, gate_low], axis=1
    )
    grad_rows = cotangent[0]
    depth = norm_one_gain.shape[0]
    extra_rows = 16
    packed = jnp.pad(
        jnp.swapaxes(table, 0, 1).reshape(4, width_model), ((0, extra_rows - 4), (0, 0))
    )
    extended = jnp.concatenate([grad_rows, packed], axis=0)
    gain_pair = jnp.concatenate(
        [norm_one_gain[None], norm_two_gain[None], jnp.zeros((62, depth), jnp.bfloat16)]
    )
    query_weight, key_weight, value_weight, gains, grad_pair, zero = gather_weights(
        (w_query, w_key, w_value, gain_pair), (extended,)
    )
    query_weight = query_weight.reshape(-1, wide)
    key_weight = key_weight.reshape(-1, kv_width)
    value_weight = value_weight.reshape(-1, kv_width)
    zero = zero[0, 0]
    side = lax.rem(wt_index, 2)
    later = side + zero
    collected = [
        collect_expert(jnp.stack([expert_gate, expert_up], axis=1), later, pairs),
        collect_expert(expert_down, later, pairs),
    ]
    gain_one, gain_two = gains[:, 0].reshape(-1), gains[:, 1].reshape(-1)
    local = expert_gate.shape[0] // 2
    first_expert = (lax.axis_index("ctx") * 2 + side) * local

    inputs = hidden[0].astype(jnp.float32)
    offset = lax.axis_index("ctx") * tokens
    seg_all = segment_ids[0]
    query_seg = lax.dynamic_slice_in_dim(seg_all, offset, tokens)
    scale_one = inverse_rms(inputs)
    gain_one_full = gain_one.astype(jnp.float32)
    normed = (inputs * scale_one * gain_one_full).astype(jnp.bfloat16)

    def project(weight):
        return jnp.dot(normed, weight, preferred_element_type=jnp.float32).astype(jnp.bfloat16)

    queries = project(query_weight)
    fresh = jnp.stack(
        [
            project(key_weight).reshape(tokens, KV_HEADS, HEAD_DIM),
            project(value_weight).reshape(tokens, KV_HEADS, HEAD_DIM),
        ],
        axis=2,
    ).reshape(tokens, 2 * kv_width)
    both, out_weight, both_weight, down_weight, zero = gather_rows(
        fresh,
        2,
        False,
        False,
        "gather_keys",
        (w_out, jnp.concatenate([shared_gate, shared_up], axis=1), shared_down),
    )
    out_weight = out_weight.reshape(-1, out_weight.shape[2])
    both_weight = both_weight.reshape(-1, both_weight.shape[2])
    down_weight = down_weight.reshape(-1, down_weight.shape[2])
    both = both.reshape(-1, 2 * kv_width)

    grad_pair, both = lax.optimization_barrier((grad_pair, both))
    all_grads = lax.all_gather(grad_pair, "ctx", axis=0).reshape(
        chips, 2, 2, tokens + extra_rows, width_model
    )

    place = lax.axis_index("ctx").astype(jnp.int32).reshape(1)
    seg_row, seg_column = seg_all[None, :], seg_all[:, None]
    attended_full, logs = attend(place, queries, both, seg_row, query_seg[:, None])
    attended = attended_full.astype(jnp.bfloat16)
    middle = inputs + jnp.dot(attended, out_weight, preferred_element_type=jnp.float32)
    scale_two = inverse_rms(middle)
    gain_two_full = gain_two.astype(jnp.float32)
    normed_two = (middle * scale_two * gain_two_full).astype(jnp.bfloat16)

    shared_parts = jnp.dot(normed_two, both_weight, preferred_element_type=jnp.float32)
    shared_gate_part, shared_up_part = shared_parts[:, :shared_width], shared_parts[:, shared_width:]
    shared_inner = (jax.nn.silu(shared_gate_part) * shared_up_part).astype(jnp.bfloat16)
    shared_result = jnp.dot(shared_inner, down_weight, preferred_element_type=jnp.float32)
    grad_out = grad_rows.astype(jnp.float32)
    grad_shared_down = jnp.einsum(
        "tf,td->fd", shared_inner, grad_rows, preferred_element_type=jnp.float32
    )
    grad_shared_inner = jnp.einsum(
        "td,fd->tf", grad_rows, down_weight, preferred_element_type=jnp.float32
    )
    grad_shared_gate_part = (
        grad_shared_inner * shared_up_part * silu_slope(shared_gate_part)
    ).astype(jnp.bfloat16)
    grad_shared_up_part = (grad_shared_inner * jax.nn.silu(shared_gate_part)).astype(jnp.bfloat16)
    grad_shared_parts = jnp.concatenate([grad_shared_gate_part, grad_shared_up_part], axis=1)
    grad_shared_both = jnp.einsum(
        "td,tf->df", normed_two, grad_shared_parts, preferred_element_type=jnp.float32
    )
    grad_shared_rows = jnp.einsum(
        "tf,df->td", grad_shared_parts, both_weight, preferred_element_type=jnp.float32
    )
    grad_shared_both = grad_shared_both.astype(jnp.bfloat16)
    grad_shared_down = grad_shared_down.astype(jnp.bfloat16)
    normed_two, collected, shared_result, grad_shared_both, grad_shared_down, grad_shared_rows = (
        lax.optimization_barrier(
            (normed_two, collected, shared_result, grad_shared_both, grad_shared_down, grad_shared_rows)
        )
    )
    all_rows, *landed, zero = gather_rows(
        normed_two, 3, True, True, "gather_tokens", (), [c[1] for c in collected]
    )

    def blocks_of(i):
        kept, paired, straight = collected[i]
        blocks = [kept, paired]
        for d in range(pairs - 1):
            blocks += [straight[d], landed[i * (pairs - 1) + d]]
        return blocks

    tall_blocks, down_blocks = blocks_of(0), blocks_of(1)
    grad_received, row_gates, slots = pick_grads(
        all_grads, first_expert.astype(jnp.int32).reshape(1), local, tokens
    )
    received_rows = pick_tokens(all_rows, slots)
    if down_blocks[0].shape[2] % 128:
        results, backs, grads_gate, grads_up, grads_down = run_experts(
            received_rows,
            grad_received,
            row_gates,
            [settle_blocks(tall_blocks, wt_index, 2)],
            [settle_blocks(down_blocks, wt_index, 2)],
        )
        wholes = [
            split_blocks(grads_gate[0], wt_index, wt_count, 1),
            split_blocks(grads_up[0], wt_index, wt_count, 1),
            split_blocks(grads_down[0], wt_index, wt_count, 2),
        ]
        hop_grads = [[g[2 * d : 2 * d + 2] for d in range(pairs)] for g in wholes]
    else:
        results, backs, *rest = run_experts(
            received_rows, grad_received, row_gates, tall_blocks, down_blocks
        )
        hop_grads = [rest[i * pairs : (i + 1) * pairs] for i in range(3)]
    arrived = [[swap_pairs(g[d], "wt", 2 * d) for d in range(1, pairs)] for g in hop_grads]
    first_arrived, later_arrived = arrived[:1], arrived[1:]
    routed_grad = scatter_rows(
        spread_rows(backs, slots, "spread_grads", False), 5, True, True, "scatter_grads"
    )
    routed_grad, first_arrived = lax.optimization_barrier((routed_grad, first_arrived))

    def crossed(own, more):
        total = own[1].astype(jnp.float32)
        for m in more:
            total = total + m[1].astype(jnp.float32)
        return swap_pairs(total.astype(jnp.bfloat16), "wt", 1)

    gate_other = crossed(hop_grads[0][0], first_arrived[0])
    grad_normed_two = grad_shared_rows + routed_grad
    grad_gain_two = jnp.sum(grad_normed_two * middle * scale_two, axis=0)
    scaled_two = grad_normed_two * gain_two_full
    grad_middle = (
        grad_out
        + scale_two * scaled_two
        - middle * scale_two**3 * jnp.mean(scaled_two * middle, axis=-1, keepdims=True)
    )
    grad_branch = grad_middle.astype(jnp.bfloat16)
    grad_out_weight = jnp.einsum(
        "tq,td->qd", attended, grad_branch, preferred_element_type=jnp.float32
    )
    grad_attended = jnp.einsum(
        "td,qd->tq", grad_branch, out_weight, preferred_element_type=jnp.float32
    ).astype(jnp.bfloat16)
    grad_queries, grad_parts = attend_back(
        place, queries, both, query_seg[None, :], seg_column, attended_full, grad_attended, logs
    )
    grad_parts, up_arrived = lax.optimization_barrier((grad_parts, later_arrived[0]))
    up_other = crossed(hop_grads[1][0], up_arrived)
    grad_both = scatter_rows(
        grad_parts.reshape(chips, 1, 2, tokens, 2 * kv_width),
        6,
        False,
        False,
        "scatter_keys",
    ).astype(jnp.bfloat16)
    grad_both, down_arrived, gate_other, up_other, results = lax.optimization_barrier(
        (grad_both, later_arrived[1], gate_other, up_other, results)
    )
    arrived = [first_arrived[0], up_arrived, down_arrived]
    down_other = crossed(hop_grads[2][0], down_arrived)
    partial = lax.psum_scatter(
        spread_rows(results, slots, "spread_results", True).reshape(ctx_count, 2, tokens, width_model),
        "ctx",
        scatter_dimension=0,
        tiled=True,
    )[0]
    grad_both = grad_both.reshape(tokens, KV_HEADS, 2, HEAD_DIM)
    grad_keys = grad_both[:, :, 0].reshape(tokens, kv_width)
    grad_values = grad_both[:, :, 1].reshape(tokens, kv_width)

    def weight_grad(grad):
        return jnp.einsum("tc,tq->cq", normed, grad, preferred_element_type=jnp.float32).astype(
            jnp.bfloat16
        )

    def input_grad(grad, weight):
        return jnp.einsum("tq,cq->tc", grad, weight, preferred_element_type=jnp.float32)

    grad_normed = (
        input_grad(grad_queries, query_weight)
        + input_grad(grad_keys, key_weight)
        + input_grad(grad_values, value_weight)
    )
    grad_gain_one = jnp.sum(grad_normed * inputs * scale_one, axis=0)
    scaled_one = grad_normed * gain_one_full
    grad_inputs = (
        grad_middle
        + scale_one * scaled_one
        - inputs * scale_one**3 * jnp.mean(scaled_one * inputs, axis=-1, keepdims=True)
    )

    gain_grads = jnp.stack([grad_gain_one, grad_gain_two]).reshape(2, wt_count, 1, depth)
    gain_grads = jnp.pad(gain_grads.astype(jnp.bfloat16), ((0, 0), (0, 0), (0, 15), (0, 0)))
    gain_grads = jnp.swapaxes(gain_grads, 0, 1).reshape(wt_count * 32, depth)
    dense_grads = [
        weight_grad(grad_queries),
        grad_shared_both,
        grad_out_weight.astype(jnp.bfloat16),
        grad_shared_down,
        weight_grad(grad_keys),
        weight_grad(grad_values),
        gain_grads,
    ]
    totals = reduce_dense(dense_grads)
    totals, down_other, partial = lax.optimization_barrier((totals, down_other, partial))
    others = [gate_other, up_other, down_other]
    kept, given = own_and_other(partial, side)
    crossing = swap_pairs(given, "wt", 1)
    routed = kept.astype(jnp.float32) + crossing.astype(jnp.float32)
    output = (middle + shared_result + routed).astype(jnp.bfloat16)
    sum_experts_gate, sum_experts_up, sum_experts_down = place_experts(
        side.astype(jnp.int32).reshape(1), [g[0] for g in hop_grads], arrived, others
    )
    final_query, final_shared, final_out, final_down, final_key, final_value, final_gains = [
        total.astype(jnp.float32) for total in totals
    ]
    final_gate, final_up = final_shared[:, :shared_width], final_shared[:, shared_width:]
    final_gain_one, final_gain_two = final_gains[0], final_gains[16]
    return (
        output[None],
        grad_inputs[None],
        final_gain_one,
        final_query,
        final_key,
        final_value,
        final_out,
        final_gain_two,
        final_gate,
        final_up,
        final_down,
        sum_experts_gate,
        sum_experts_up,
        sum_experts_down,
    )


def solution(mesh):
    placed = (
        P("wt", "ctx", None),
        P("wt", None),
        P("wt", "ctx", None),
        P("wt", "ctx", None),
        P("wt", "ctx", None),
        P("wt"),
        P("wt", None),
        P("wt", None),
        P("wt", None),
        P("wt", None),
        P("wt"),
        P("wt", None),
        P("wt", None),
        P("wt", None),
        P("ctx", "wt", None),
        P("ctx", "wt", None),
        P("ctx", None, "wt"),
    )
    return jax.shard_map(
        body,
        mesh=mesh,
        in_specs=placed,
        out_specs=(
            P("wt", "ctx", None),
            P("wt", "ctx", None),
            P("wt"),
            P("wt", None),
            P("wt", None),
            P("wt", None),
            P("wt", None),
            P("wt"),
            P("wt", None),
            P("wt", None),
            P("wt", None),
            P("ctx", "wt", None),
            P("ctx", "wt", None),
            P("ctx", None, "wt"),
        ),
        check_vma=False,
    )
```

```python
import functools
import math

import jax
import jax.numpy as jnp
from jax import lax
from jax.experimental import pallas as pl
from jax.experimental.pallas import tpu as pltpu
from jax.sharding import PartitionSpec as P

HEADS = 12
KV_HEADS = 4
HEAD_DIM = 128
EXPERTS = 64
TOPK = 6
CAP = 40


epsilon = 1e-05
masked_value = -1e30


def inverse_rms(rows):
    return lax.rsqrt(jnp.mean(rows * rows, axis=-1, keepdims=True) + epsilon)


def silu_slope(gate_part):
    sigmoid = jax.nn.sigmoid(gate_part)
    return sigmoid * (1.0 + gate_part * (1.0 - sigmoid))


MESH = pl.DeviceIdType.MESH
WIDE = 56 * 2**20
LONG = pl.CostEstimate(flops=0, bytes_accessed=2_000_000_000, transcendentals=0)
CHEAP = pl.CostEstimate(flops=0, bytes_accessed=4096, transcendentals=0)


def flip(index, distance):
    result = index
    bit = 1
    while bit <= distance:
        if distance // bit % 2:
            result = result + bit - 2 * bit * (index // bit % 2)
        bit *= 2
    return result


def remote(src, dst, send_sem, recv_sem, device):
    return pltpu.make_async_remote_copy(
        src_ref=src,
        dst_ref=dst,
        send_sem=send_sem,
        recv_sem=recv_sem,
        device_id=device,
        device_id_type=MESH,
    )


def greet(devices):
    barrier = pltpu.get_barrier_semaphore()
    for device in devices:
        pl.semaphore_signal(barrier, inc=1, device_id=device, device_id_type=MESH)
    pl.semaphore_wait(barrier, len(devices))


class Slabs:
    def __init__(self, count, sources, targets, here, there, send, recv, near_send, near_recv, *stages):
        self.c, self.w = lax.axis_index("ctx"), lax.axis_index("wt")
        self.core = lax.rem(self.c, 2)
        self.near = (flip(self.c, 1), self.w)
        self.count = count
        self.pairs = list(zip(sources, targets))
        self.here, self.there, self.send, self.recv = here, there, send, recv
        self.near_send, self.near_recv = near_send, near_recv
        self.stages = stages
        dims = [1 << i for i in range(count.bit_length() - 1)]
        self.orders = [dims, dims[::-1]]

    def devices(self):
        return [(self.c, flip(self.w, d)) for d in self.orders[0]]

    def rows(self, s, p, core):
        rows = self.pairs[s][0].shape[0] // 4
        return pl.ds(pl.multiple_of((core * 2 + p) * rows, 16), rows)

    def block(self, s, p, f, core):
        return self.pairs[s][1].at[flip(self.w, f), self.rows(s, p, core)]

    def push(self, s, p, stage, held):
        step = self.orders[p][stage]
        part = self.rows(s, p, self.core)
        source = self.pairs[s][0].at[part] if held == 0 else self.block(s, p, held, self.core)
        index = (s, p, (step ^ held) - 1)
        return remote(
            source,
            self.block(s, p, held, self.core),
            self.send.at[index],
            self.recv.at[index],
            (self.c, flip(self.w, step)),
        )

    def arrival(self, s, p, f):
        spot = self.block(s, p, f, self.core)
        return remote(spot, spot, self.send.at[s, p, f - 1], self.recv.at[s, p, f - 1], self.near)

    def hand(self, s, p, f, core):
        spot = self.block(s, p, f, core)
        return remote(spot, spot, self.near_send.at[s, p, f - 1], self.near_recv.at[s, p, f - 1], self.near)

    def load(self, s):
        return pltpu.make_async_copy(self.pairs[s][0], self.stages[s], self.here.at[s])

    def keep(self, s):
        return pltpu.make_async_copy(self.stages[s], self.pairs[s][1].at[self.w], self.there.at[s])

    def last_stage(self, p, f):
        return max(i for i, d in enumerate(self.orders[p]) if f & d)

    def every(self):
        return [(s, p) for s in range(len(self.pairs)) for p in range(2)]

    def start(self):
        for stage in range(len(self.orders[0])):
            for s, p in self.every():
                self.push(s, p, stage, 0).start()
        for s in range(len(self.pairs)):
            self.load(s).start()

    def relay(self):
        for s in range(len(self.pairs)):
            self.load(s).wait()
            self.keep(s).start()
        last = len(self.orders[0])
        for stage in range(last):
            for s, p in self.every():
                for f in range(1, self.count):
                    if self.last_stage(p, f) == stage:
                        self.arrival(s, p, f).wait_recv()
                        for onward in range(stage + 1, last):
                            self.push(s, p, onward, f).start()
                        self.hand(s, p, f, self.core).start()

    def finish(self):
        for s, p in self.every():
            for f in range(1, self.count):
                stage = self.last_stage(p, f)
                self.hand(s, p, f, 1 - self.core).wait_recv()
                self.hand(s, p, f, self.core).wait_send()
                self.push(s, p, stage, f ^ self.orders[p][stage]).wait_send()
        for s in range(len(self.pairs)):
            self.keep(s).wait()

    @staticmethod
    def scratch(slabs, count):
        dma = pltpu.SemaphoreType.DMA
        number = len(slabs)
        return (
            [dma((number,))] * 2
            + [dma((number, 2, count - 1))] * 4
            + [pltpu.VMEM(s.shape, s.dtype) for s in slabs]
        )

    @staticmethod
    def shapes(slabs, count):
        return tuple(jax.ShapeDtypeStruct((count,) + s.shape, s.dtype) for s in slabs)


def weights_kernel(count, slabs, swaps, *refs):
    refs = list(refs)

    def take(number):
        taken = refs[:number]
        del refs[:number]
        return taken

    sources, given = take(slabs), take(swaps)
    targets, paired, (zero_ref,) = take(slabs), take(swaps), take(1)
    stages = take(swaps)
    load_sem, keep_sem, swap_send, swap_recv = take(4)
    plan = Slabs(count, sources, targets, *refs)
    c, w = lax.axis_index("ctx"), lax.axis_index("wt")
    side = lax.rem(w, 2)
    partner = (c, flip(w, 1))
    greet(plan.devices() + [plan.near])

    def swap(i):
        return remote(given[i], paired[i].at[side], swap_send.at[i], swap_recv.at[i], partner)

    def load(i):
        return pltpu.make_async_copy(given[i], stages[i], load_sem.at[i])

    def keep(i):
        return pltpu.make_async_copy(stages[i], paired[i].at[side], keep_sem.at[i])

    plan.start()
    for i in range(swaps):
        swap(i).start()
        load(i).start()
    zero_ref[...] = jnp.zeros_like(zero_ref)
    for i in range(swaps):
        load(i).wait()
        keep(i).start()
    plan.relay()
    plan.finish()
    for i in range(swaps):
        keep(i).wait()
        swap(i).wait()


def gather_weights(slabs, swaps):
    count = lax.axis_size("wt")
    dma = pltpu.SemaphoreType.DMA((len(swaps),))
    pairs = tuple(jax.ShapeDtypeStruct((2,) + s.shape, s.dtype) for s in swaps)
    shapes = Slabs.shapes(slabs, count) + pairs
    return pl.pallas_call(
        functools.partial(weights_kernel, count, len(slabs), len(swaps)),
        out_shape=shapes + (jax.ShapeDtypeStruct((8, 128), jnp.int32),),
        in_specs=[pl.BlockSpec(memory_space=pl.ANY)] * (len(slabs) + len(swaps)),
        out_specs=(pl.BlockSpec(memory_space=pl.ANY),) * len(shapes)
        + (pl.BlockSpec(memory_space=pltpu.VMEM),),
        scratch_shapes=[pltpu.VMEM(s.shape, s.dtype) for s in swaps]
        + [dma] * 4
        + Slabs.scratch(slabs, count),
        compiler_params=pltpu.CompilerParams(
            collective_id=1, has_side_effects=True, vmem_limit_bytes=WIDE
        ),
        cost_estimate=LONG,
        name="gather_weights",
    )(*slabs, *swaps)


def gather_kernel(chips, downward, paired, count, slabs, passed, rows_ref, *refs):
    refs = list(refs)

    def take(number):
        taken = refs[:number]
        del refs[:number]
        return taken

    hops = count // 2 - 1
    sources, moved = take(slabs), take(passed)
    (out_ref,), targets, landed, (zero_ref,) = take(1), take(slabs), take(passed * hops), take(1)
    (stage,) = take(1)
    here, up_send, up_recv, down_send, down_recv, pair_send, pair_recv, near_send, near_recv = take(9)
    plan = Slabs(count, sources, targets, *take(6 + slabs)) if slabs else None
    pass_send, pass_recv = take(2) if passed else (None, None)
    zero_ref[...] = jnp.zeros_like(zero_ref)
    c, w = lax.axis_index("ctx"), lax.axis_index("wt")
    z = c // 2
    core = lax.rem(c, 2)
    side = lax.rem(w, 2) if paired else 0
    near, partner = (flip(c, 1), w), (c, flip(w, 1))
    above = (lax.rem(c + 2, 2 * chips), w)
    below = (lax.rem(c + 2 * chips - 2, 2 * chips), w)
    far = [(c, flip(w, 2 * d + 2)) for d in range(hops)]
    greet([near, above, below] + ([partner] if paired else []) + (plan.devices() if plan else []) + (far if passed else []))

    def onward(i, d):
        return remote(
            moved[i], landed[i * hops + d], pass_send.at[i, d], pass_recv.at[i, d], far[d]
        )

    def spot(chip, which, parity):
        return out_ref.at[chip, which, parity]

    def lift(chip, source):
        return remote(source, spot(chip, side, core), up_send.at[chip], up_recv.at[chip], above)

    def drop(chip, source):
        return remote(source, spot(chip, side, core), down_send.at[chip], down_recv.at[chip], below)

    def give(chip, source):
        return remote(source, spot(chip, side, core), pair_send.at[chip], pair_recv.at[chip], partner)

    def taken(chip):
        return remote(
            spot(chip, 1 - side, core), spot(chip, 1 - side, core), pair_send.at[chip], pair_recv.at[chip], partner
        )

    def hand(chip, which, source):
        return remote(source, spot(chip, which, core), near_send.at[chip, which], near_recv.at[chip, which], near)

    def handed(chip, which):
        there = spot(chip, which, 1 - core)
        return remote(there, there, near_send.at[chip, which], near_recv.at[chip, which], near)

    def settle_pair(chip):
        taken(chip).wait_recv()
        hand(chip, 1 - side, spot(chip, 1 - side, core)).start()

    load = pltpu.make_async_copy(rows_ref, stage, here.at[0])
    keep = pltpu.make_async_copy(stage, spot(z, side, core), here.at[1])
    load.start()
    pl.when(z < chips - 1)(lambda: lift(z, rows_ref).start())
    if downward:
        pl.when(z > 0)(lambda: drop(z, rows_ref).start())
    if paired:
        give(z, rows_ref).start()
    hand(z, side, rows_ref).start()
    if plan:
        plan.start()
    for d in range(hops):
        for i in range(passed):
            onward(i, d).start()
    load.wait()
    keep.start()
    for step in range(1, chips):
        low, high = z - step, z + step

        @pl.when(low >= 0)
        def _():
            lift(low, spot(low, side, core)).wait_recv()
            pl.when(z < chips - 1)(lambda: lift(low, spot(low, side, core)).start())
            if paired:
                give(low, spot(low, side, core)).start()
            hand(low, side, spot(low, side, core)).start()

        if downward:

            @pl.when(high < chips)
            def _():
                drop(high, spot(high, side, core)).wait_recv()
                pl.when(z > 0)(lambda: drop(high, spot(high, side, core)).start())
                if paired:
                    give(high, spot(high, side, core)).start()
                hand(high, side, spot(high, side, core)).start()

        if paired:
            if step == 1:
                settle_pair(z)
            else:
                pl.when(z - step + 1 >= 0)(lambda: settle_pair(z - step + 1))
                pl.when(z + step - 1 < chips)(lambda: settle_pair(z + step - 1))
    if paired:
        pl.when(z - chips + 1 >= 0)(lambda: settle_pair(z - chips + 1))
        pl.when(z + chips - 1 < chips)(lambda: settle_pair(z + chips - 1))
    keep.wait()
    if plan:
        plan.relay()
        plan.finish()

    def finish(chip):
        here_now = spot(chip, side, core)
        pl.when((z < chips - 1) & (chip <= z))(lambda: lift(chip, here_now).wait_send())
        if downward:
            pl.when((z > 0) & (chip >= z))(lambda: drop(chip, here_now).wait_send())
        if paired:
            give(chip, here_now).wait_send()
            for which in range(2):
                hand(chip, which, spot(chip, which, core)).wait_send()
                handed(chip, which).wait_recv()
        else:
            hand(chip, side, here_now).wait_send()
            handed(chip, side).wait_recv()

    for chip in range(chips):
        if downward:
            finish(chip)
        else:
            pl.when(chip <= z)(lambda: finish(chip))
    for d in range(hops):
        for i in range(passed):
            onward(i, d).wait()


def gather_rows(rows, collective_id, downward, paired, name, slabs=(), moved=()):
    chips = lax.axis_size("ctx") // 2
    count = lax.axis_size("wt")
    hops = count // 2 - 1
    line = pltpu.SemaphoreType.DMA((chips,))
    both = pltpu.SemaphoreType.DMA((chips, 2))
    shape = jax.ShapeDtypeStruct((chips, 2 if paired else 1, 2) + rows.shape, rows.dtype)
    landed = tuple(jax.ShapeDtypeStruct(m.shape, m.dtype) for m in moved for _ in range(hops))
    shapes = (shape,) + Slabs.shapes(slabs, count) + landed
    *results, zero = pl.pallas_call(
        functools.partial(gather_kernel, chips, downward, paired, count, len(slabs), len(moved)),
        out_shape=shapes + (jax.ShapeDtypeStruct((8, 128), jnp.int32),),
        in_specs=[pl.BlockSpec(memory_space=pl.ANY)] * (1 + len(slabs) + len(moved)),
        out_specs=(pl.BlockSpec(memory_space=pl.ANY),) * len(shapes)
        + (pl.BlockSpec(memory_space=pltpu.VMEM),),
        scratch_shapes=[pltpu.VMEM(rows.shape, rows.dtype), pltpu.SemaphoreType.DMA((2,))]
        + [line] * 6
        + [both] * 2
        + (Slabs.scratch(slabs, count) if slabs else [])
        + ([pltpu.SemaphoreType.DMA((len(moved), hops))] * 2 if moved else []),
        compiler_params=pltpu.CompilerParams(
            collective_id=collective_id, has_side_effects=True, vmem_limit_bytes=WIDE
        ),
        cost_estimate=LONG,
        name=name,
    )(rows, *slabs, *moved)
    return results + [zero[0, 0]]


def scatter_kernel(chips, upward, paired, pieces, fused, *refs):
    if fused:
        rows_ref, slot_ref, out_ref, built, *refs = refs
        partial_ref = None
    else:
        partial_ref, out_ref, *refs = refs
    own, sib, mate, low_in, high_in, load, near_send, near_recv, *refs = refs
    pair_send, pair_recv, up_send, up_recv, down_send, down_recv = refs
    c, w = lax.axis_index("ctx"), lax.axis_index("wt")
    z = c // 2
    core = lax.rem(c, 2)
    side = lax.rem(w, 2) if paired else 0
    sides = 2 if paired else 1
    near, partner = (flip(c, 1), w), (c, flip(w, 1))
    above = (lax.rem(c + 2, 2 * chips), w)
    below = (lax.rem(c + 2 * chips - 2, 2 * chips), w)
    rows = own.shape[2] // pieces
    greet([near, above, below] + ([partner] if paired else []))
    order = []
    for i in range(chips // 2):
        order += [chips - 1 - i, i]
    if chips % 2:
        order.append(chips // 2)
    if not upward:
        order = list(range(chips))

    def wanted(chip, action):
        if upward:
            action()
        else:
            pl.when(chip <= z)(action)

    def fetch(chip, which):
        return pltpu.make_async_copy(
            partial_ref.at[chip, which, core], own.at[chip, which], load.at[chip, which]
        )

    def hand(chip, which):
        return remote(
            built.at[chip, which] if fused else partial_ref.at[chip, which, 1 - core],
            sib.at[chip, which],
            near_send.at[chip, which],
            near_recv.at[chip, which],
            near,
        )

    def cut(piece):
        return pl.ds(piece * rows, rows)

    def give(chip, piece):
        return remote(
            own.at[chip, 1 - side, cut(piece)],
            mate.at[chip, cut(piece)],
            pair_send.at[chip, piece],
            pair_recv.at[chip, piece],
            partner,
        )

    def lift(chip, piece):
        return remote(
            own.at[chip, side, cut(piece)],
            low_in.at[chip, cut(piece)],
            up_send.at[chip, piece],
            up_recv.at[chip, piece],
            above,
        )

    def drop(chip, piece):
        return remote(
            own.at[chip, side, cut(piece)],
            high_in.at[chip, cut(piece)],
            down_send.at[chip, piece],
            down_recv.at[chip, piece],
            below,
        )

    def add_into(chip, which, piece, other):
        spot = own.at[chip, which, cut(piece)]
        spot[...] = spot[...] + other[...]

    def spread(chip, which, parity, spot):
        local, depth, width = rows_ref.shape[2:]
        tokens = spot.shape[0]
        span = pl.ds(pl.multiple_of(parity * tokens, tokens), tokens)
        place = lax.broadcasted_iota(jnp.int32, (depth, tokens), 0)
        ones = jnp.concatenate(
            [
                (slot_ref[chip, which, e : e + 1, span] == place).astype(jnp.float32)
                for e in range(local)
            ],
            axis=0,
        ).astype(jnp.bfloat16)
        spot[...] = lax.dot_general(
            ones,
            rows_ref[chip, which].reshape(local * depth, width),
            (((0,), (0,)), ((), ())),
            preferred_element_type=jnp.float32,
        ).astype(jnp.bfloat16)

    def begin(chip):
        for which in range(sides):
            if fused:
                spread(chip, which, 1 - core, built.at[chip, which])
            hand(chip, which).start()
            if fused:
                spread(chip, which, core, own.at[chip, which])
            else:
                fetch(chip, which).start()

    if not fused:
        for chip in order:
            wanted(chip, lambda: begin(chip))
    else:
        begin(order[0])

    def meet(chip):
        for which in range(sides):
            if not fused:
                fetch(chip, which).wait()
            hand(chip, which).wait_recv()
        for piece in range(pieces):
            if paired:
                add_into(chip, 1 - side, piece, sib.at[chip, 1 - side, cut(piece)])
                give(chip, piece).start()
            add_into(chip, side, piece, sib.at[chip, side, cut(piece)])

    def travel(chip):
        for piece in range(pieces):
            if paired:
                give(chip, piece).wait_recv()
                add_into(chip, side, piece, mate.at[chip, cut(piece)])
            if upward:

                @pl.when(z < chip)
                def _():
                    @pl.when(z > 0)
                    def _():
                        lift(chip, piece).wait_recv()
                        add_into(chip, side, piece, low_in.at[chip, cut(piece)])

                    lift(chip, piece).start()

            @pl.when(z > chip)
            def _():
                @pl.when(z < chips - 1)
                def _():
                    drop(chip, piece).wait_recv()
                    add_into(chip, side, piece, high_in.at[chip, cut(piece)])

                drop(chip, piece).start()

    for i, chip in enumerate(order):
        if fused and i + 1 < len(order):
            begin(order[i + 1])
        wanted(chip, lambda: meet(chip))
        if i >= 1:
            wanted(order[i - 1], lambda: travel(order[i - 1]))
    wanted(order[-1], lambda: travel(order[-1]))
    for piece in range(pieces):
        out_ref[cut(piece), :] = own.at[z, side, cut(piece)][...].astype(jnp.float32)
    for piece in range(pieces):
        if upward:

            @pl.when(z > 0)
            def _():
                lift(z, piece).wait_recv()
                out_ref[cut(piece), :] += low_in.at[z, cut(piece)][...].astype(jnp.float32)

        @pl.when(z < chips - 1)
        def _():
            drop(z, piece).wait_recv()
            out_ref[cut(piece), :] += high_in.at[z, cut(piece)][...].astype(jnp.float32)

    def finish(chip):
        for which in range(sides):
            hand(chip, which).wait_send()
        for piece in range(pieces):
            if paired:
                give(chip, piece).wait_send()
            if upward:
                pl.when(z < chip)(lambda: lift(chip, piece).wait_send())
            pl.when(z > chip)(lambda: drop(chip, piece).wait_send())

    for chip in order:
        wanted(chip, lambda: finish(chip))


def scatter_rows(partial, collective_id, upward, paired, name, slots=None):
    fused = slots is not None
    dma = pltpu.SemaphoreType.DMA
    pieces = 2
    if fused:
        chips, sides, _, _, width = partial.shape
        tokens = slots.shape[3] // 2
    else:
        chips, sides, _, tokens, width = partial.shape
    block = (tokens, width)
    several = pltpu.VMEM((chips, sides) + block, jnp.bfloat16)
    return pl.pallas_call(
        functools.partial(scatter_kernel, chips, upward, paired, pieces, fused),
        out_shape=jax.ShapeDtypeStruct(block, jnp.float32),
        in_specs=[pl.BlockSpec(memory_space=pltpu.VMEM)] * 2
        if fused
        else [pl.BlockSpec(memory_space=pl.ANY)],
        out_specs=pl.BlockSpec(memory_space=pltpu.VMEM),
        scratch_shapes=([several] if fused else [])
        + [
            several,
            several,
            pltpu.VMEM((chips if paired else 1,) + block, jnp.bfloat16),
            pltpu.VMEM((chips if upward else 1,) + block, jnp.bfloat16),
            pltpu.VMEM((chips,) + block, jnp.bfloat16),
            dma((chips, 2)),
            dma((chips, 2)),
            dma((chips, 2)),
        ]
        + [dma((chips, pieces))] * 6,
        compiler_params=pltpu.CompilerParams(
            collective_id=collective_id, has_side_effects=True, vmem_limit_bytes=WIDE
        ),
        cost_estimate=LONG if paired else CHEAP,
        name=name,
    )(*((partial, slots) if fused else (partial,)))


def dense_kernel(chips, count, matrices, pieces, *refs):
    refs = list(refs)

    def take(number):
        taken = refs[:number]
        del refs[:number]
        return taken

    grads, outs = take(matrices), take(matrices)
    own, sib, mates, low, final = (take(matrices) for _ in range(5))
    (load, near_send, near_recv, send, recv, low_send, low_recv, back_send, back_recv, last_send, last_recv, keep) = refs
    c, w = lax.axis_index("ctx"), lax.axis_index("wt")
    z = c // 2
    core = lax.rem(c, 2)
    near = (flip(c, 1), w)
    above = (lax.rem(c + 2, 2 * chips), w)
    below = (lax.rem(c + 2 * chips - 2, 2 * chips), w)
    dims = [1 << i for i in range(count.bit_length() - 1)]
    greet([near, above, below] + [(c, flip(w, d)) for d in dims])

    def order(j):
        return dims if pieces[j][3] else dims[::-1]

    def sends(j, stage):
        step, rest = order(j)[stage], order(j)[stage + 1 :]
        offsets = [step]
        for r in rest:
            offsets += [o ^ r for o in offsets]
        return offsets

    def span(j, parity=None):
        m, first, rows, _ = pieces[j]
        if parity is None:
            return pl.ds(first, rows)
        half = grads[m].shape[1] // 2
        return pl.ds(pl.multiple_of(parity * half + first, 16), rows)

    def fetch(j):
        m = pieces[j][0]
        return pltpu.make_async_copy(grads[m].at[:, span(j, core)], own[m].at[:, span(j)], load.at[j])

    def hand(j):
        m = pieces[j][0]
        return remote(
            grads[m].at[:, span(j, 1 - core)], sib[m].at[:, span(j)], near_send.at[j], near_recv.at[j], near
        )

    def give(j, stage, o):
        m = pieces[j][0]
        step = order(j)[stage]
        return remote(
            own[m].at[flip(w, o), span(j)],
            mates[m].at[o - 1, span(j)],
            send.at[j, o - 1],
            recv.at[j, o - 1],
            (c, flip(w, step)),
        )

    def total(j):
        return own[pieces[j][0]].at[w, span(j)]

    def add(spot, other):
        spot[...] = spot[...] + other[...]

    def start(j):
        hand(j).start()
        fetch(j).start()

    def share(j):
        m = pieces[j][0]
        fetch(j).wait()
        hand(j).wait_recv()
        for o in sends(j, 0):
            add(own[m].at[flip(w, o), span(j)], sib[m].at[flip(w, o), span(j)])
            give(j, 0, o).start()
        for o in range(count):
            if o not in sends(j, 0):
                add(own[m].at[flip(w, o), span(j)], sib[m].at[flip(w, o), span(j)])

    def collect(j, stage):
        m = pieces[j][0]
        step = order(j)[stage]
        for o in sends(j, stage):
            give(j, stage, o).wait_recv()
        last = stage + 1 == len(dims)
        onward_blocks = [] if last else sends(j, stage + 1)
        for o in sends(j, stage):
            kept = o ^ step
            if kept in onward_blocks:
                add(own[m].at[flip(w, kept), span(j)], mates[m].at[o - 1, span(j)])
                give(j, stage + 1, kept).start()
        for o in sends(j, stage):
            kept = o ^ step
            if kept not in onward_blocks:
                add(own[m].at[flip(w, kept), span(j)], mates[m].at[o - 1, span(j)])

    def line(j):
        return (z, above, below) if j % 2 == 0 else (chips - 1 - z, below, above)

    def onward(j):
        m = pieces[j][0]
        return remote(total(j), low[m].at[span(j)], low_send.at[j], low_recv.at[j], line(j)[1])

    def backward(j):
        spot = final[pieces[j][0]].at[span(j)]
        return remote(spot, spot, back_send.at[j], back_recv.at[j], line(j)[2])

    def across(j, parity):
        m = pieces[j][0]
        return remote(
            final[m].at[span(j)], outs[m].at[span(j, parity)], last_send.at[j], last_recv.at[j], near
        )

    def store(j):
        m = pieces[j][0]
        return pltpu.make_async_copy(final[m].at[span(j)], outs[m].at[span(j, core)], keep.at[j])

    def accumulate(j):
        place = line(j)[0]
        m = pieces[j][0]

        @pl.when(place > 0)
        def _():
            onward(j).wait_recv()
            add(total(j), low[m].at[span(j)])

        @pl.when(place < chips - 1)
        def _():
            onward(j).start()

        @pl.when(place == chips - 1)
        def _():
            final[m][span(j), :] = total(j)[...]
            backward(j).start()
            across(j, core).start()
            store(j).start()

    def spread(j):
        place = line(j)[0]

        @pl.when(place < chips - 1)
        def _():
            backward(j).wait_recv()
            pl.when(place > 0)(lambda: backward(j).start())
            across(j, core).start()
            store(j).start()

    number = len(pieces)
    for j in range(number):
        start(j)
    last = chips - 1
    lead, gap = 2, 1
    behind = lead + gap * (len(dims) - 1)
    for t in range(number + 2 * last + behind):
        if t < number:
            share(t)
        for stage in range(len(dims)):
            if 0 <= t - lead - gap * stage < number:
                collect(t - lead - gap * stage, stage)
        for hop in range(2 * last, -1, -1):
            j = t - hop - behind
            if not 0 <= j < number:
                continue
            if hop <= last:
                pl.when(line(j)[0] == hop)(lambda: accumulate(j))
            if hop > last:
                pl.when(line(j)[0] == 2 * last - hop)(lambda: spread(j))
    for j in range(number):
        place = line(j)[0]
        hand(j).wait_send()
        for stage in range(len(dims)):
            for o in sends(j, stage):
                give(j, stage, o).wait_send()
        pl.when(place < chips - 1)(lambda: onward(j).wait_send())
        pl.when(place > 0)(lambda: backward(j).wait_send())
        across(j, core).wait_send()
        across(j, 1 - core).wait_recv()
        store(j).wait()


def reduce_dense(grads):
    count = lax.axis_size("wt")
    chips = lax.axis_size("ctx") // 2
    shapes = [(g.shape[0] // count, g.shape[1]) for g in grads]
    pieces = []
    for m, (rows, _) in enumerate(shapes):
        half, width = rows // 2, shapes[m][1]
        cuts = max(n for n in range(1, 9) if half % (16 * n) == 0 and (n == 1 or half * width > 60000 * (n - 1)))
        for i in range(cuts):
            pieces.append((m, i * (rows // 2 // cuts), rows // 2 // cuts, len(pieces) % 2))
    halves = [(rows // 2, width) for rows, width in shapes]
    dma = pltpu.SemaphoreType.DMA
    one, many = dma((len(pieces),)), dma((len(pieces), count - 1))
    return pl.pallas_call(
        functools.partial(dense_kernel, chips, count, len(grads), tuple(pieces)),
        out_shape=[jax.ShapeDtypeStruct(s, jnp.bfloat16) for s in shapes],
        in_specs=[pl.BlockSpec(memory_space=pl.ANY)] * len(grads),
        out_specs=[pl.BlockSpec(memory_space=pl.ANY)] * len(grads),
        scratch_shapes=[pltpu.VMEM((count,) + h, jnp.bfloat16) for h in halves]
        + [pltpu.VMEM((count,) + h, jnp.bfloat16) for h in halves]
        + [pltpu.VMEM((count - 1,) + h, jnp.bfloat16) for h in halves]
        + [pltpu.VMEM(h, jnp.bfloat16) for h in halves]
        + [pltpu.VMEM(h, jnp.bfloat16) for h in halves]
        + [one, one, one, many, many, one, one, one, one, one, one, one],
        compiler_params=pltpu.CompilerParams(
            collective_id=7, has_side_effects=True, vmem_limit_bytes=WIDE
        ),
        cost_estimate=LONG,
        name="reduce_dense",
    )(*[g.reshape((count,) + s) for g, s in zip(grads, shapes)])


def dot_of(a, b, left, right):
    return lax.dot_general(
        a, b, (((left,), (right,)), ((), ())), preferred_element_type=jnp.float32
    )


def stacked_heads(ref):
    return jnp.concatenate(
        [ref[:, h * HEAD_DIM : (h + 1) * HEAD_DIM] for h in range(ref.shape[1] // HEAD_DIM)], axis=0
    )


exponent_scale = HEAD_DIM ** (-0.5) * math.log2(math.e)


def attend_kernel(place_ref, query_ref, both_ref, row_ref, column_ref, out_ref, log_ref, best, total, accum):
    tokens = query_ref.shape[0]
    group = query_ref.shape[1] // HEAD_DIM
    width = 2 * tokens
    place = place_ref[0]
    queries = stacked_heads(query_ref)
    best[...] = jnp.full_like(best, masked_value)
    total[...] = jnp.zeros_like(total)
    accum[...] = jnp.zeros_like(accum)
    query_pos = place * tokens + lax.broadcasted_iota(jnp.int32, (tokens, width), 0)
    key_pos = lax.broadcasted_iota(jnp.int32, (tokens, width), 1)

    def step(j, carry):
        span = pl.ds(pl.multiple_of(j * width, width), width)
        allowed = (key_pos + j * width <= query_pos) & (row_ref[0:1, span] == column_ref[:, 0:1])
        bias = jnp.where(allowed, 0.0, masked_value)
        scores = dot_of(queries, both_ref[span, :HEAD_DIM], 1, 1)
        scores = (scores.reshape(group, tokens, width) + bias[None]).reshape(group * tokens, width)
        newest = jnp.maximum(best[...], jnp.max(scores, axis=1, keepdims=True))
        factor = jnp.exp2((best[...] - newest) * exponent_scale)
        weights = jnp.exp2((scores - newest[:, :1]) * exponent_scale)
        total[...] = total[...] * factor + jnp.sum(weights, axis=1, keepdims=True)
        accum[...] = accum[...] * factor + dot_of(
            weights.astype(jnp.bfloat16), both_ref[span, HEAD_DIM:], 1, 0
        )
        best[...] = newest
        return carry

    lax.fori_loop(0, place // 2 + 1, step, 0)
    heads = accum[...] / total[...]
    for h in range(group):
        out_ref[:, h * HEAD_DIM : (h + 1) * HEAD_DIM] = heads[h * tokens : (h + 1) * tokens]
    logs = best[...] * exponent_scale + jnp.log2(total[...])
    log_ref[0] = jnp.transpose(logs)[:8]


def attend(place, projected, both, seg_row, seg_column):
    tokens = projected.shape[0]
    group = HEADS // KV_HEADS
    rows, span = group * tokens, both.shape[0]
    stat = pltpu.VMEM((rows, HEAD_DIM), jnp.float32)
    return pl.pallas_call(
        attend_kernel,
        grid=(KV_HEADS,),
        out_shape=(
            jax.ShapeDtypeStruct((tokens, HEADS * HEAD_DIM), jnp.float32),
            jax.ShapeDtypeStruct((KV_HEADS, 8, rows), jnp.float32),
        ),
        in_specs=[
            pl.BlockSpec(memory_space=pltpu.SMEM),
            pl.BlockSpec((tokens, group * HEAD_DIM), lambda g: (0, g)),
            pl.BlockSpec((span, 2 * HEAD_DIM), lambda g: (0, g)),
            pl.BlockSpec((1, span), lambda g: (0, 0)),
            pl.BlockSpec((tokens, 1), lambda g: (0, 0)),
        ],
        out_specs=(
            pl.BlockSpec((tokens, group * HEAD_DIM), lambda g: (0, g)),
            pl.BlockSpec((1, 8, rows), lambda g: (g, 0, 0)),
        ),
        scratch_shapes=[stat, stat, stat],
        compiler_params=pltpu.CompilerParams(vmem_limit_bytes=WIDE),
        cost_estimate=CHEAP,
        name="attend",
    )(place, projected, both, seg_row, seg_column)


def attend_back_kernel(place_ref, query_ref, both_ref, row_ref, column_ref, heads_ref, grad_ref, log_ref, grad_query_ref, grad_both_ref, accum):
    tokens = query_ref.shape[0]
    group = query_ref.shape[1] // HEAD_DIM
    width = 2 * tokens
    rows = group * tokens
    scale = HEAD_DIM ** (-0.5)
    place = place_ref[0]
    queries, grads = stacked_heads(query_ref), stacked_heads(grad_ref)
    product = grads.astype(jnp.float32) * stacked_heads(heads_ref)
    delta = jnp.sum(product, axis=1, keepdims=True)
    delta = jnp.transpose(jnp.broadcast_to(delta, (rows, HEAD_DIM)))[0:1]
    logs = log_ref[0, 0:1, :]
    accum[...] = jnp.zeros_like(accum)
    grad_both_ref[...] = jnp.zeros_like(grad_both_ref)
    query_pos = place * tokens + lax.broadcasted_iota(jnp.int32, (width, tokens), 1)
    key_pos = lax.broadcasted_iota(jnp.int32, (width, tokens), 0)

    def step(j, carry):
        span = pl.ds(pl.multiple_of(j * width, width), width)
        allowed = (key_pos + j * width <= query_pos) & (column_ref[span, 0:1] == row_ref[0:1, :])
        bias = jnp.where(allowed, 0.0, masked_value)
        bias = jnp.concatenate([bias] * group, axis=1)
        keys, values = both_ref[span, :HEAD_DIM], both_ref[span, HEAD_DIM:]
        scores = dot_of(keys, queries, 1, 1)
        probs = jnp.exp2(scores * exponent_scale + bias - logs)
        grad_probs = dot_of(values, grads, 1, 1)
        grad_scores = (probs * (grad_probs - delta)).astype(jnp.bfloat16)
        accum[...] += dot_of(grad_scores, keys, 0, 0)
        grad_both_ref[span, :HEAD_DIM] = (dot_of(grad_scores, queries, 1, 0) * scale).astype(jnp.bfloat16)
        grad_both_ref[span, HEAD_DIM:] = dot_of(probs.astype(jnp.bfloat16), grads, 1, 0).astype(jnp.bfloat16)
        return carry

    lax.fori_loop(0, place // 2 + 1, step, 0)
    grad_queries = (accum[...] * scale).astype(jnp.bfloat16)
    for h in range(group):
        grad_query_ref[:, h * HEAD_DIM : (h + 1) * HEAD_DIM] = grad_queries[h * tokens : (h + 1) * tokens]


def attend_back(place, projected, both, query_seg_row, seg_column, heads_out, grad_attended, logs):
    tokens = projected.shape[0]
    group = HEADS // KV_HEADS
    rows, span = group * tokens, both.shape[0]
    per_group = pl.BlockSpec((tokens, group * HEAD_DIM), lambda g: (0, g))
    return pl.pallas_call(
        attend_back_kernel,
        grid=(KV_HEADS,),
        out_shape=(
            jax.ShapeDtypeStruct((tokens, HEADS * HEAD_DIM), jnp.bfloat16),
            jax.ShapeDtypeStruct(both.shape, jnp.bfloat16),
        ),
        in_specs=[
            pl.BlockSpec(memory_space=pltpu.SMEM),
            per_group,
            pl.BlockSpec((span, 2 * HEAD_DIM), lambda g: (0, g)),
            pl.BlockSpec((1, tokens), lambda g: (0, 0)),
            pl.BlockSpec((span, 1), lambda g: (0, 0)),
            per_group,
            per_group,
            pl.BlockSpec((1, 8, rows), lambda g: (g, 0, 0)),
        ],
        out_specs=(per_group, pl.BlockSpec((span, 2 * HEAD_DIM), lambda g: (0, g))),
        scratch_shapes=[pltpu.VMEM((rows, HEAD_DIM), jnp.float32)],
        compiler_params=pltpu.CompilerParams(vmem_limit_bytes=WIDE),
        cost_estimate=CHEAP,
        name="attend_back",
    )(place, projected, both, query_seg_row, seg_column, heads_out, grad_attended, logs)


def pick_rows_of(slot_rows, rows_of, local, depth, tokens):
    place = lax.broadcasted_iota(jnp.int32, (depth, tokens), 0)
    total, masks = None, []
    for core in range(2):
        chosen = [slot_rows[core][e : e + 1] == place for e in range(local)]
        ones = jnp.concatenate([c.astype(jnp.float32) for c in chosen], axis=0).astype(jnp.bfloat16)
        term = jnp.dot(ones, rows_of(core), preferred_element_type=jnp.float32)
        total = term if total is None else total + term
        masks.append(chosen)
    return total, masks


def pick_grads_kernel(local, first_ref, earlier_ref, rows_ref, out_ref, scale_ref, slot_ref):
    depth = out_ref.shape[3]
    tokens = slot_ref.shape[3] // 2
    slot_rows, gate_rows, count = [], [], None
    for core in range(2):
        table = rows_ref[0, core, 0, tokens : tokens + 16, :].astype(jnp.float32)
        member, gate = [], []
        for e in range(local):
            expert = (first_ref[0] + e).astype(jnp.float32)
            found, weight = None, None
            for k in range(TOPK):
                span = slice(k * tokens, (k + 1) * tokens)
                named = table[0:1, span] == expert
                value = jnp.where(named, table[1:2, span] + table[2:3, span] + table[3:4, span], 0.0)
                mark = jnp.where(named, 1.0, 0.0)
                found = mark if k == 0 else found + mark
                weight = value if k == 0 else weight + value
            member.append(found)
            gate.append(weight)
        member = jnp.concatenate(member + [jnp.zeros((8 - local, tokens), jnp.float32)], axis=0)
        rank = jnp.dot(member.astype(jnp.bfloat16), earlier_ref[...], preferred_element_type=jnp.float32)
        if core:
            rank = rank + count
        count = jnp.sum(member, axis=1, keepdims=True)
        slots = jnp.where(member > 0.5, rank.astype(jnp.int32), -1)[:local]
        slot_ref[0, 0, :, core * tokens : (core + 1) * tokens] = slots
        slot_rows.append(slots)
        gate_rows.append(gate)
    total, masks = pick_rows_of(
        slot_rows, lambda core: rows_ref[0, core, 0, :tokens, :], local, depth, tokens
    )
    weight = None
    for core in range(2):
        gates = jnp.concatenate(
            [
                jnp.sum(jnp.where(masks[core][e], gate_rows[core][e], 0.0), axis=1, keepdims=True)
                for e in range(local)
            ],
            axis=0,
        )
        weight = gates if core == 0 else weight + gates
    scale_ref[0, 0] = jnp.broadcast_to(weight, (local * depth, 128)).reshape(local, depth, 128)
    out_ref[0, 0] = (total * weight).astype(jnp.bfloat16).reshape(local, depth, total.shape[1])


def pick_grads(rows, first, local, tokens):
    chips, _, sides, long, width = rows.shape
    depth = 2 * CAP
    earlier = jnp.arange(tokens)[:, None] < jnp.arange(tokens)[None, :]
    return pl.pallas_call(
        functools.partial(pick_grads_kernel, local),
        grid=(chips, sides),
        out_shape=(
            jax.ShapeDtypeStruct((chips, sides, local, depth, width), jnp.bfloat16),
            jax.ShapeDtypeStruct((chips, sides, local, depth, 128), jnp.float32),
            jax.ShapeDtypeStruct((chips, sides, local, 2 * tokens), jnp.int32),
        ),
        in_specs=[
            pl.BlockSpec(memory_space=pltpu.SMEM),
            pl.BlockSpec((tokens, tokens), lambda z, s: (0, 0)),
            pl.BlockSpec((1, 2, 1, long, width), lambda z, s: (z, 0, s, 0, 0)),
        ],
        out_specs=(
            pl.BlockSpec((1, 1, local, depth, width), lambda z, s: (z, s, 0, 0, 0)),
            pl.BlockSpec((1, 1, local, depth, 128), lambda z, s: (z, s, 0, 0, 0)),
            pl.BlockSpec((1, 1, local, 2 * tokens), lambda z, s: (z, s, 0, 0)),
        ),
        compiler_params=pltpu.CompilerParams(vmem_limit_bytes=WIDE),
        cost_estimate=CHEAP,
        name="pick_grads",
    )(first, earlier.astype(jnp.bfloat16), rows)


def pick_tokens_kernel(slot_ref, rows_ref, out_ref):
    local, depth = out_ref.shape[2], out_ref.shape[3]
    tokens = rows_ref.shape[3]
    slot_rows = [slot_ref[0, 0, :, core * tokens : (core + 1) * tokens] for core in range(2)]
    total, _ = pick_rows_of(slot_rows, lambda core: rows_ref[0, 0, core], local, depth, tokens)
    out_ref[0, 0] = total.astype(jnp.bfloat16).reshape(local, depth, total.shape[1])


def pick_tokens(rows, slots):
    chips, sides, local, both = slots.shape
    tokens, width = rows.shape[3:]
    depth = 2 * CAP
    return pl.pallas_call(
        pick_tokens_kernel,
        grid=(chips, sides),
        out_shape=jax.ShapeDtypeStruct((chips, sides, local, depth, width), jnp.bfloat16),
        in_specs=[
            pl.BlockSpec((1, 1, local, both), lambda z, s: (z, s, 0, 0)),
            pl.BlockSpec((1, 1, 2, tokens, width), lambda z, s: (z, s, 0, 0, 0)),
        ],
        out_specs=pl.BlockSpec((1, 1, local, depth, width), lambda z, s: (z, s, 0, 0, 0)),
        compiler_params=pltpu.CompilerParams(vmem_limit_bytes=WIDE),
        cost_estimate=CHEAP,
        name="pick_tokens",
    )(slots, rows)


def spread_kernel(apart, slot_ref, rows_ref, out_ref):
    local, depth, width = rows_ref.shape[2:]
    tokens = out_ref.shape[3]
    place = lax.broadcasted_iota(jnp.int32, (depth, tokens), 0)
    rows = rows_ref[0, 0].reshape(local * depth, width)
    for core in range(2):
        span = slice(core * tokens, (core + 1) * tokens)
        ones = jnp.concatenate(
            [(slot_ref[0, 0, e : e + 1, span] == place).astype(jnp.float32) for e in range(local)], axis=0
        ).astype(jnp.bfloat16)
        spot = out_ref.at[0, core, 0] if apart else out_ref.at[0, 0, core]
        spot[...] = lax.dot_general(
            ones, rows, (((0,), (0,)), ((), ())), preferred_element_type=jnp.float32
        ).astype(jnp.bfloat16)


def spread_rows(rows, slots, name, apart):
    chips, sides, local, both = slots.shape
    depth, width = rows.shape[3:]
    tokens = both // 2
    return pl.pallas_call(
        functools.partial(spread_kernel, apart),
        grid=(chips, sides),
        out_shape=jax.ShapeDtypeStruct(
            (chips, 2, sides, tokens, width) if apart else (chips, sides, 2, tokens, width), jnp.bfloat16
        ),
        in_specs=[
            pl.BlockSpec((1, 1, local, both), lambda z, s: (z, s, 0, 0)),
            pl.BlockSpec((1, 1, local, depth, width), lambda z, s: (z, s, 0, 0, 0)),
        ],
        out_specs=pl.BlockSpec((1, 2, 1, tokens, width), lambda z, s: (z, 0, s, 0, 0))
        if apart
        else pl.BlockSpec((1, 1, 2, tokens, width), lambda z, s: (z, s, 0, 0, 0)),
        compiler_params=pltpu.CompilerParams(vmem_limit_bytes=WIDE),
        cost_estimate=CHEAP,
        name=name,
    )(slots, rows)


def expert_kernel(blocks, x_ref, g_ref, scale_ref, *refs):
    tall_refs, down_refs = refs[:blocks], refs[blocks : 2 * blocks]
    result_ref, back_ref, *grad_refs = refs[2 * blocks :]
    hops = len(grad_refs) // 3
    grad_gate_refs, grad_up_refs = grad_refs[:hops], grad_refs[hops : 2 * hops]
    grad_down_refs = grad_refs[2 * hops :]
    w = lax.axis_index("wt")
    chips, sides, _, depth, width = x_ref.shape
    rows = chips * sides * depth
    part = tall_refs[0].shape[2]
    nn, nt, tn = (((1,), (0,)), ((), ())), (((1,), (1,)), ((), ())), (((0,), (0,)), ((), ()))

    def dot(a, b, dims):
        return lax.dot_general(a, b, dims, preferred_element_type=jnp.float32)

    def columns(ref, q):
        if blocks == 1:
            return ref.at[:, :, 0]
        span = pl.ds(pl.multiple_of(flip(w, q) * part, 128), part)
        return ref.at[:, :, 0, :, span]

    def piece(ref, q):
        return columns(ref, q)[...].reshape(rows, part)

    gate, up, grad_inner = None, None, None
    for q in range(blocks):
        x = piece(x_ref, q)
        more_gate, more_up = dot(x, tall_refs[q][0, 0], nn), dot(x, tall_refs[q][0, 1], nn)
        gate, up = (more_gate, more_up) if q == 0 else (gate + more_gate, up + more_up)
    for q in range(blocks):
        more = dot(piece(g_ref, q), down_refs[q][0], nt)
        grad_inner = more if q == 0 else grad_inner + more
    sigmoid = jax.nn.sigmoid(gate)
    activated = gate * sigmoid
    inner = (activated * up).astype(jnp.bfloat16)
    grad_gate = (grad_inner * up * (sigmoid * (1.0 + gate * (1.0 - sigmoid)))).astype(jnp.bfloat16)
    grad_up = (grad_inner * activated).astype(jnp.bfloat16)
    scale = scale_ref[...].reshape(rows, 128)[:, :1]
    for q in range(blocks):
        result = dot(inner, down_refs[q][0], nn) * scale
        columns(result_ref, q)[...] = result.astype(jnp.bfloat16).reshape(chips, sides, depth, part)
        back = dot(grad_gate, tall_refs[q][0, 0], nt) + dot(grad_up, tall_refs[q][0, 1], nt)
        columns(back_ref, q)[...] = back.astype(jnp.bfloat16).reshape(chips, sides, depth, part)
        grad_down_refs[q // 2][q % 2, 0] = dot(inner, piece(g_ref, q), tn).astype(jnp.bfloat16)
        x = piece(x_ref, q)
        grad_gate_refs[q // 2][q % 2, 0] = dot(x, grad_gate, tn).astype(jnp.bfloat16)
        grad_up_refs[q // 2][q % 2, 0] = dot(x, grad_up, tn).astype(jnp.bfloat16)


def run_experts(x, g, scale, talls, downs):
    chips, sides, local, depth, width = x.shape
    blocks = len(talls)
    part, inner = talls[0].shape[2:]
    large = chips * sides * depth > 1024
    rows = pl.BlockSpec((chips, sides, 1, depth, width), lambda e: (0, 0, e, 0, 0))
    sources = pl.BlockSpec(
        (chips, sides, 1, depth, width),
        lambda e: (0, 0, e, 0, 0),
        pipeline_mode=pl.Buffered(1 if large else 2),
    )
    scales = pl.BlockSpec((chips, sides, 1, depth, 128), lambda e: (0, 0, e, 0, 0))
    tall = pl.BlockSpec((1, 2, part, inner), lambda e: (e, 0, 0, 0))
    flat = pl.BlockSpec((1, inner, part), lambda e: (e, 0, 0))
    hops, each = max(blocks // 2, 1), min(blocks, 2)
    tall_out = pl.BlockSpec((each, 1, part, inner), lambda e: (0, e, 0, 0))
    flat_out = pl.BlockSpec((each, 1, inner, part), lambda e: (0, e, 0, 0))
    return pl.pallas_call(
        functools.partial(expert_kernel, blocks),
        grid=(local,),
        out_shape=(
            jax.ShapeDtypeStruct(x.shape, jnp.bfloat16),
            jax.ShapeDtypeStruct(x.shape, jnp.bfloat16),
            *[jax.ShapeDtypeStruct((each, local, part, inner), jnp.bfloat16)] * (2 * hops),
            *[jax.ShapeDtypeStruct((each, local, inner, part), jnp.bfloat16)] * hops,
        ),
        in_specs=[sources, sources, scales] + [tall] * blocks + [flat] * blocks,
        out_specs=(rows, rows) + (tall_out,) * (2 * hops) + (flat_out,) * hops,
        compiler_params=pltpu.CompilerParams(vmem_limit_bytes=60 * 2**20),
        cost_estimate=CHEAP,
        name="experts",
    )(x, g, scale, *talls, *downs)


def place_kernel(arrivals, side_ref, *refs):
    own, other, more, outs = refs[:3], refs[3:6], refs[6 : 6 + 3 * arrivals], refs[6 + 3 * arrivals :]
    mine = pl.program_id(0) == side_ref[0]

    @pl.when(mine)
    def _():
        for i in range(3):
            value = own[i][0, 0].astype(jnp.float32)
            for m in more[i * arrivals : (i + 1) * arrivals]:
                value = value + m[0, 0].astype(jnp.float32)
            outs[i][0] = value

    @pl.when(jnp.logical_not(mine))
    def _():
        for i in range(3):
            outs[i][0] = other[i][0].astype(jnp.float32)


def place_experts(side, own, more, other):
    local = other[0].shape[0]
    arrivals = len(more[0])
    shapes = [o.shape[1:] for o in other]
    paired = [pl.BlockSpec((1, 1) + s, lambda h, e: (0, e, 0, 0)) for s in shapes]
    single = [pl.BlockSpec((1,) + s, lambda h, e: (e, 0, 0)) for s in shapes]
    return pl.pallas_call(
        functools.partial(place_kernel, arrivals),
        grid=(2, local),
        out_shape=[jax.ShapeDtypeStruct((2 * local,) + s, jnp.float32) for s in shapes],
        in_specs=[pl.BlockSpec(memory_space=pltpu.SMEM)]
        + paired
        + single
        + [p for p in paired for _ in range(arrivals)],
        out_specs=[pl.BlockSpec((1,) + s, lambda h, e: (h * local + e, 0, 0)) for s in shapes],
        compiler_params=pltpu.CompilerParams(vmem_limit_bytes=WIDE),
        cost_estimate=CHEAP,
        name="place_experts",
    )(side, *own, *other, *[m for group in more for m in group])


def swap_pairs(value, axis, distance):
    count = lax.axis_size(axis)
    return lax.ppermute(value, axis, [(i, i ^ distance) for i in range(count)])


def own_and_other(stacked, mine):
    return (
        lax.dynamic_index_in_dim(stacked, mine, 0, keepdims=False),
        lax.dynamic_index_in_dim(stacked, 1 - mine, 0, keepdims=False),
    )


def collect_expert(shard, side, pairs):
    local = shard.shape[0]
    kept, given = own_and_other(shard.reshape((2, local // 2) + shard.shape[1:]), side)
    return kept, swap_pairs(given, "wt", 1), [swap_pairs(kept, "wt", 2 * d) for d in range(1, pairs)]


def settle_blocks(blocks, index, axis):
    stacked = jnp.stack(blocks)
    return jnp.concatenate(
        [
            lax.dynamic_index_in_dim(stacked, jnp.bitwise_xor(j, index), 0, False)
            for j in range(len(blocks))
        ],
        axis=axis,
    )


def split_blocks(whole, index, count, axis):
    parts = jnp.stack(jnp.split(whole, count, axis=axis))
    return jnp.stack(
        [
            lax.dynamic_index_in_dim(parts, jnp.bitwise_xor(q, index), 0, False)
            for q in range(count)
        ]
    )


def body(
    hidden,
    segment_ids,
    routes,
    gates,
    cotangent,
    norm_one_gain,
    w_query,
    w_key,
    w_value,
    w_out,
    norm_two_gain,
    shared_gate,
    shared_up,
    shared_down,
    expert_gate,
    expert_up,
    expert_down,
):
    wt_index = lax.axis_index("wt")
    wt_count = lax.axis_size("wt")
    ctx_count = lax.axis_size("ctx")
    chips = ctx_count // 2
    pairs = wt_count // 2
    tokens, width_model = hidden.shape[1:]
    wide, kv_width = w_query.shape[1], w_key.shape[1]
    shared_width = shared_gate.shape[1]
    gates_here = gates[0]
    gate_high = gates_here.astype(jnp.bfloat16)
    gate_rest = gates_here - gate_high.astype(jnp.float32)
    gate_middle = gate_rest.astype(jnp.bfloat16)
    gate_low = (gate_rest - gate_middle.astype(jnp.float32)).astype(jnp.bfloat16)
    table = jnp.concatenate(
        [routes[0].astype(jnp.bfloat16), gate_high, gate_middle, gate_low], axis=1
    )
    grad_rows = cotangent[0]
    depth = norm_one_gain.shape[0]
    extra_rows = 16
    packed = jnp.pad(
        jnp.swapaxes(table, 0, 1).reshape(4, width_model), ((0, extra_rows - 4), (0, 0))
    )
    extended = jnp.concatenate([grad_rows, packed], axis=0)
    gain_pair = jnp.concatenate(
        [norm_one_gain[None], norm_two_gain[None], jnp.zeros((62, depth), jnp.bfloat16)]
    )
    query_weight, key_weight, value_weight, gains, grad_pair, zero = gather_weights(
        (w_query, w_key, w_value, gain_pair), (extended,)
    )
    query_weight = query_weight.reshape(-1, wide)
    key_weight = key_weight.reshape(-1, kv_width)
    value_weight = value_weight.reshape(-1, kv_width)
    zero = zero[0, 0]
    side = lax.rem(wt_index, 2)
    later = side + zero
    collected = [
        collect_expert(jnp.stack([expert_gate, expert_up], axis=1), later, pairs),
        collect_expert(expert_down, later, pairs),
    ]
    gain_one, gain_two = gains[:, 0].reshape(-1), gains[:, 1].reshape(-1)
    local = expert_gate.shape[0] // 2
    first_expert = (lax.axis_index("ctx") * 2 + side) * local

    inputs = hidden[0].astype(jnp.float32)
    offset = lax.axis_index("ctx") * tokens
    seg_all = segment_ids[0]
    query_seg = lax.dynamic_slice_in_dim(seg_all, offset, tokens)
    scale_one = inverse_rms(inputs)
    gain_one_full = gain_one.astype(jnp.float32)
    normed = (inputs * scale_one * gain_one_full).astype(jnp.bfloat16)

    def project(weight):
        return jnp.dot(normed, weight, preferred_element_type=jnp.float32).astype(jnp.bfloat16)

    queries = project(query_weight)
    fresh = jnp.stack(
        [
            project(key_weight).reshape(tokens, KV_HEADS, HEAD_DIM),
            project(value_weight).reshape(tokens, KV_HEADS, HEAD_DIM),
        ],
        axis=2,
    ).reshape(tokens, 2 * kv_width)
    both, out_weight, both_weight, down_weight, zero = gather_rows(
        fresh,
        2,
        False,
        False,
        "gather_keys",
        (w_out, jnp.concatenate([shared_gate, shared_up], axis=1), shared_down),
    )
    out_weight = out_weight.reshape(-1, out_weight.shape[2])
    both_weight = both_weight.reshape(-1, both_weight.shape[2])
    down_weight = down_weight.reshape(-1, down_weight.shape[2])
    both = both.reshape(-1, 2 * kv_width)

    grad_pair, both = lax.optimization_barrier((grad_pair, both))
    all_grads = lax.all_gather(grad_pair, "ctx", axis=0).reshape(
        chips, 2, 2, tokens + extra_rows, width_model
    )

    place = lax.axis_index("ctx").astype(jnp.int32).reshape(1)
    seg_row, seg_column = seg_all[None, :], seg_all[:, None]
    attended_full, logs = attend(place, queries, both, seg_row, query_seg[:, None])
    attended = attended_full.astype(jnp.bfloat16)
    middle = inputs + jnp.dot(attended, out_weight, preferred_element_type=jnp.float32)
    scale_two = inverse_rms(middle)
    gain_two_full = gain_two.astype(jnp.float32)
    normed_two = (middle * scale_two * gain_two_full).astype(jnp.bfloat16)

    shared_parts = jnp.dot(normed_two, both_weight, preferred_element_type=jnp.float32)
    shared_gate_part, shared_up_part = shared_parts[:, :shared_width], shared_parts[:, shared_width:]
    shared_inner = (jax.nn.silu(shared_gate_part) * shared_up_part).astype(jnp.bfloat16)
    shared_result = jnp.dot(shared_inner, down_weight, preferred_element_type=jnp.float32)
    grad_out = grad_rows.astype(jnp.float32)
    grad_shared_down = jnp.einsum(
        "tf,td->fd", shared_inner, grad_rows, preferred_element_type=jnp.float32
    )
    grad_shared_inner = jnp.einsum(
        "td,fd->tf", grad_rows, down_weight, preferred_element_type=jnp.float32
    )
    grad_shared_gate_part = (
        grad_shared_inner * shared_up_part * silu_slope(shared_gate_part)
    ).astype(jnp.bfloat16)
    grad_shared_up_part = (grad_shared_inner * jax.nn.silu(shared_gate_part)).astype(jnp.bfloat16)
    grad_shared_parts = jnp.concatenate([grad_shared_gate_part, grad_shared_up_part], axis=1)
    grad_shared_both = jnp.einsum(
        "td,tf->df", normed_two, grad_shared_parts, preferred_element_type=jnp.float32
    )
    grad_shared_rows = jnp.einsum(
        "tf,df->td", grad_shared_parts, both_weight, preferred_element_type=jnp.float32
    )
    grad_shared_both = grad_shared_both.astype(jnp.bfloat16)
    grad_shared_down = grad_shared_down.astype(jnp.bfloat16)
    normed_two, collected, shared_result, grad_shared_both, grad_shared_down, grad_shared_rows = (
        lax.optimization_barrier(
            (normed_two, collected, shared_result, grad_shared_both, grad_shared_down, grad_shared_rows)
        )
    )
    all_rows, *landed, zero = gather_rows(
        normed_two, 3, True, True, "gather_tokens", (), [c[1] for c in collected]
    )

    def blocks_of(i):
        kept, paired, straight = collected[i]
        blocks = [kept, paired]
        for d in range(pairs - 1):
            blocks += [straight[d], landed[i * (pairs - 1) + d]]
        return blocks

    tall_blocks, down_blocks = blocks_of(0), blocks_of(1)
    grad_received, row_gates, slots = pick_grads(
        all_grads, first_expert.astype(jnp.int32).reshape(1), local, tokens
    )
    received_rows = pick_tokens(all_rows, slots)
    if down_blocks[0].shape[2] % 128:
        results, backs, grads_gate, grads_up, grads_down = run_experts(
            received_rows,
            grad_received,
            row_gates,
            [settle_blocks(tall_blocks, wt_index, 2)],
            [settle_blocks(down_blocks, wt_index, 2)],
        )
        wholes = [
            split_blocks(grads_gate[0], wt_index, wt_count, 1),
            split_blocks(grads_up[0], wt_index, wt_count, 1),
            split_blocks(grads_down[0], wt_index, wt_count, 2),
        ]
        hop_grads = [[g[2 * d : 2 * d + 2] for d in range(pairs)] for g in wholes]
    else:
        results, backs, *rest = run_experts(
            received_rows, grad_received, row_gates, tall_blocks, down_blocks
        )
        hop_grads = [rest[i * pairs : (i + 1) * pairs] for i in range(3)]
    arrived = [[swap_pairs(g[d], "wt", 2 * d) for d in range(1, pairs)] for g in hop_grads]
    first_arrived, later_arrived = arrived[:1], arrived[1:]
    if chips > 4:
        routed_grad = scatter_rows(
            spread_rows(backs, slots, "spread_grads", False), 5, True, True, "scatter_grads"
        )
    else:
        routed_grad = scatter_rows(backs, 5, True, True, "scatter_grads", slots)
    routed_grad, first_arrived = lax.optimization_barrier((routed_grad, first_arrived))

    def crossed(own, more):
        total = own[1].astype(jnp.float32)
        for m in more:
            total = total + m[1].astype(jnp.float32)
        return swap_pairs(total.astype(jnp.bfloat16), "wt", 1)

    gate_other = crossed(hop_grads[0][0], first_arrived[0])
    grad_normed_two = grad_shared_rows + routed_grad
    grad_gain_two = jnp.sum(grad_normed_two * middle * scale_two, axis=0)
    scaled_two = grad_normed_two * gain_two_full
    grad_middle = (
        grad_out
        + scale_two * scaled_two
        - middle * scale_two**3 * jnp.mean(scaled_two * middle, axis=-1, keepdims=True)
    )
    grad_branch = grad_middle.astype(jnp.bfloat16)
    grad_out_weight = jnp.einsum(
        "tq,td->qd", attended, grad_branch, preferred_element_type=jnp.float32
    )
    grad_attended = jnp.einsum(
        "td,qd->tq", grad_branch, out_weight, preferred_element_type=jnp.float32
    ).astype(jnp.bfloat16)
    grad_queries, grad_parts = attend_back(
        place, queries, both, query_seg[None, :], seg_column, attended_full, grad_attended, logs
    )
    grad_parts, up_arrived = lax.optimization_barrier((grad_parts, later_arrived[0]))
    up_other = crossed(hop_grads[1][0], up_arrived)
    grad_both = scatter_rows(
        grad_parts.reshape(chips, 1, 2, tokens, 2 * kv_width),
        6,
        False,
        False,
        "scatter_keys",
    ).astype(jnp.bfloat16)
    grad_both, down_arrived, gate_other, up_other, results = lax.optimization_barrier(
        (grad_both, later_arrived[1], gate_other, up_other, results)
    )
    arrived = [first_arrived[0], up_arrived, down_arrived]
    down_other = crossed(hop_grads[2][0], down_arrived)
    partial = lax.psum_scatter(
        spread_rows(results, slots, "spread_results", True).reshape(ctx_count, 2, tokens, width_model),
        "ctx",
        scatter_dimension=0,
        tiled=True,
    )[0]
    grad_both = grad_both.reshape(tokens, KV_HEADS, 2, HEAD_DIM)
    grad_keys = grad_both[:, :, 0].reshape(tokens, kv_width)
    grad_values = grad_both[:, :, 1].reshape(tokens, kv_width)

    def weight_grad(grad):
        return jnp.einsum("tc,tq->cq", normed, grad, preferred_element_type=jnp.float32).astype(
            jnp.bfloat16
        )

    def input_grad(grad, weight):
        return jnp.einsum("tq,cq->tc", grad, weight, preferred_element_type=jnp.float32)

    grad_normed = (
        input_grad(grad_queries, query_weight)
        + input_grad(grad_keys, key_weight)
        + input_grad(grad_values, value_weight)
    )
    grad_gain_one = jnp.sum(grad_normed * inputs * scale_one, axis=0)
    scaled_one = grad_normed * gain_one_full
    grad_inputs = (
        grad_middle
        + scale_one * scaled_one
        - inputs * scale_one**3 * jnp.mean(scaled_one * inputs, axis=-1, keepdims=True)
    )

    gain_grads = jnp.stack([grad_gain_one, grad_gain_two]).reshape(2, wt_count, 1, depth)
    gain_grads = jnp.pad(gain_grads.astype(jnp.bfloat16), ((0, 0), (0, 0), (0, 15), (0, 0)))
    gain_grads = jnp.swapaxes(gain_grads, 0, 1).reshape(wt_count * 32, depth)
    dense_grads = [
        weight_grad(grad_queries),
        grad_shared_both,
        grad_out_weight.astype(jnp.bfloat16),
        grad_shared_down,
        weight_grad(grad_keys),
        weight_grad(grad_values),
        gain_grads,
    ]
    totals = reduce_dense(dense_grads)
    totals, down_other, partial = lax.optimization_barrier((totals, down_other, partial))
    others = [gate_other, up_other, down_other]
    kept, given = own_and_other(partial, side)
    crossing = swap_pairs(given, "wt", 1)
    routed = kept.astype(jnp.float32) + crossing.astype(jnp.float32)
    output = (middle + shared_result + routed).astype(jnp.bfloat16)
    sum_experts_gate, sum_experts_up, sum_experts_down = place_experts(
        side.astype(jnp.int32).reshape(1), [g[0] for g in hop_grads], arrived, others
    )
    final_query, final_shared, final_out, final_down, final_key, final_value, final_gains = [
        total.astype(jnp.float32) for total in totals
    ]
    final_gate, final_up = final_shared[:, :shared_width], final_shared[:, shared_width:]
    final_gain_one, final_gain_two = final_gains[0], final_gains[16]
    return (
        output[None],
        grad_inputs[None],
        final_gain_one,
        final_query,
        final_key,
        final_value,
        final_out,
        final_gain_two,
        final_gate,
        final_up,
        final_down,
        sum_experts_gate,
        sum_experts_up,
        sum_experts_down,
    )


def solution(mesh):
    placed = (
        P("wt", "ctx", None),
        P("wt", None),
        P("wt", "ctx", None),
        P("wt", "ctx", None),
        P("wt", "ctx", None),
        P("wt"),
        P("wt", None),
        P("wt", None),
        P("wt", None),
        P("wt", None),
        P("wt"),
        P("wt", None),
        P("wt", None),
        P("wt", None),
        P("ctx", "wt", None),
        P("ctx", "wt", None),
        P("ctx", None, "wt"),
    )
    return jax.shard_map(
        body,
        mesh=mesh,
        in_specs=placed,
        out_specs=(
            P("wt", "ctx", None),
            P("wt", "ctx", None),
            P("wt"),
            P("wt", None),
            P("wt", None),
            P("wt", None),
            P("wt", None),
            P("wt"),
            P("wt", None),
            P("wt", None),
            P("wt", None),
            P("ctx", "wt", None),
            P("ctx", "wt", None),
            P("ctx", None, "wt"),
        ),
        check_vma=False,
    )
```

```python
import functools
import math

import jax
import jax.numpy as jnp
from jax import lax
from jax.experimental import pallas as pl
from jax.experimental.pallas import tpu as pltpu
from jax.sharding import PartitionSpec as P

HEADS = 12
KV_HEADS = 4
HEAD_DIM = 128
EXPERTS = 64
TOPK = 6
CAP = 40


epsilon = 1e-05
masked_value = -1e30


def inverse_rms(rows):
    return lax.rsqrt(jnp.mean(rows * rows, axis=-1, keepdims=True) + epsilon)


def silu_slope(gate_part):
    sigmoid = jax.nn.sigmoid(gate_part)
    return sigmoid * (1.0 + gate_part * (1.0 - sigmoid))


MESH = pl.DeviceIdType.MESH
WIDE = 56 * 2**20
LONG = pl.CostEstimate(flops=0, bytes_accessed=2_000_000_000, transcendentals=0)
CHEAP = pl.CostEstimate(flops=0, bytes_accessed=4096, transcendentals=0)


def flip(index, distance):
    result = index
    bit = 1
    while bit <= distance:
        if distance // bit % 2:
            result = result + bit - 2 * bit * (index // bit % 2)
        bit *= 2
    return result


def remote(src, dst, send_sem, recv_sem, device):
    return pltpu.make_async_remote_copy(
        src_ref=src,
        dst_ref=dst,
        send_sem=send_sem,
        recv_sem=recv_sem,
        device_id=device,
        device_id_type=MESH,
    )


def greet(devices):
    barrier = pltpu.get_barrier_semaphore()
    for device in devices:
        pl.semaphore_signal(barrier, inc=1, device_id=device, device_id_type=MESH)
    pl.semaphore_wait(barrier, len(devices))


class Slabs:
    def __init__(self, count, sources, targets, here, there, send, recv, near_send, near_recv, *stages):
        self.c, self.w = lax.axis_index("ctx"), lax.axis_index("wt")
        self.core = lax.rem(self.c, 2)
        self.near = (flip(self.c, 1), self.w)
        self.count = count
        self.pairs = list(zip(sources, targets))
        self.here, self.there, self.send, self.recv = here, there, send, recv
        self.near_send, self.near_recv = near_send, near_recv
        self.stages = stages
        dims = [1 << i for i in range(count.bit_length() - 1)]
        self.orders = [dims, dims[::-1]]

    def devices(self):
        return [(self.c, flip(self.w, d)) for d in self.orders[0]]

    def rows(self, s, p, core):
        rows = self.pairs[s][0].shape[0] // 4
        return pl.ds(pl.multiple_of((core * 2 + p) * rows, 16), rows)

    def block(self, s, p, f, core):
        return self.pairs[s][1].at[flip(self.w, f), self.rows(s, p, core)]

    def push(self, s, p, stage, held):
        step = self.orders[p][stage]
        part = self.rows(s, p, self.core)
        source = self.pairs[s][0].at[part] if held == 0 else self.block(s, p, held, self.core)
        index = (s, p, (step ^ held) - 1)
        return remote(
            source,
            self.block(s, p, held, self.core),
            self.send.at[index],
            self.recv.at[index],
            (self.c, flip(self.w, step)),
        )

    def arrival(self, s, p, f):
        spot = self.block(s, p, f, self.core)
        return remote(spot, spot, self.send.at[s, p, f - 1], self.recv.at[s, p, f - 1], self.near)

    def hand(self, s, p, f, core):
        spot = self.block(s, p, f, core)
        return remote(spot, spot, self.near_send.at[s, p, f - 1], self.near_recv.at[s, p, f - 1], self.near)

    def load(self, s):
        return pltpu.make_async_copy(self.pairs[s][0], self.stages[s], self.here.at[s])

    def keep(self, s):
        return pltpu.make_async_copy(self.stages[s], self.pairs[s][1].at[self.w], self.there.at[s])

    def last_stage(self, p, f):
        return max(i for i, d in enumerate(self.orders[p]) if f & d)

    def every(self):
        return [(s, p) for s in range(len(self.pairs)) for p in range(2)]

    def start(self):
        for stage in range(len(self.orders[0])):
            for s, p in self.every():
                self.push(s, p, stage, 0).start()
        for s in range(len(self.pairs)):
            self.load(s).start()

    def relay(self):
        for s in range(len(self.pairs)):
            self.load(s).wait()
            self.keep(s).start()
        last = len(self.orders[0])
        for stage in range(last):
            for s, p in self.every():
                for f in range(1, self.count):
                    if self.last_stage(p, f) == stage:
                        self.arrival(s, p, f).wait_recv()
                        for onward in range(stage + 1, last):
                            self.push(s, p, onward, f).start()
                        self.hand(s, p, f, self.core).start()

    def finish(self):
        for s, p in self.every():
            for f in range(1, self.count):
                stage = self.last_stage(p, f)
                self.hand(s, p, f, 1 - self.core).wait_recv()
                self.hand(s, p, f, self.core).wait_send()
                self.push(s, p, stage, f ^ self.orders[p][stage]).wait_send()
        for s in range(len(self.pairs)):
            self.keep(s).wait()

    @staticmethod
    def scratch(slabs, count):
        dma = pltpu.SemaphoreType.DMA
        number = len(slabs)
        return (
            [dma((number,))] * 2
            + [dma((number, 2, count - 1))] * 4
            + [pltpu.VMEM(s.shape, s.dtype) for s in slabs]
        )

    @staticmethod
    def shapes(slabs, count):
        return tuple(jax.ShapeDtypeStruct((count,) + s.shape, s.dtype) for s in slabs)


def weights_kernel(count, slabs, swaps, *refs):
    refs = list(refs)

    def take(number):
        taken = refs[:number]
        del refs[:number]
        return taken

    sources, given = take(slabs), take(swaps)
    targets, paired, (zero_ref,) = take(slabs), take(swaps), take(1)
    stages = take(swaps)
    load_sem, keep_sem, swap_send, swap_recv = take(4)
    plan = Slabs(count, sources, targets, *refs)
    c, w = lax.axis_index("ctx"), lax.axis_index("wt")
    side = lax.rem(w, 2)
    partner = (c, flip(w, 1))
    greet(plan.devices() + [plan.near])

    def swap(i):
        return remote(given[i], paired[i].at[side], swap_send.at[i], swap_recv.at[i], partner)

    def load(i):
        return pltpu.make_async_copy(given[i], stages[i], load_sem.at[i])

    def keep(i):
        return pltpu.make_async_copy(stages[i], paired[i].at[side], keep_sem.at[i])

    plan.start()
    for i in range(swaps):
        swap(i).start()
        load(i).start()
    zero_ref[...] = jnp.zeros_like(zero_ref)
    for i in range(swaps):
        load(i).wait()
        keep(i).start()
    plan.relay()
    plan.finish()
    for i in range(swaps):
        keep(i).wait()
        swap(i).wait()


def gather_weights(slabs, swaps):
    count = lax.axis_size("wt")
    dma = pltpu.SemaphoreType.DMA((len(swaps),))
    pairs = tuple(jax.ShapeDtypeStruct((2,) + s.shape, s.dtype) for s in swaps)
    shapes = Slabs.shapes(slabs, count) + pairs
    return pl.pallas_call(
        functools.partial(weights_kernel, count, len(slabs), len(swaps)),
        out_shape=shapes + (jax.ShapeDtypeStruct((8, 128), jnp.int32),),
        in_specs=[pl.BlockSpec(memory_space=pl.ANY)] * (len(slabs) + len(swaps)),
        out_specs=(pl.BlockSpec(memory_space=pl.ANY),) * len(shapes)
        + (pl.BlockSpec(memory_space=pltpu.VMEM),),
        scratch_shapes=[pltpu.VMEM(s.shape, s.dtype) for s in swaps]
        + [dma] * 4
        + Slabs.scratch(slabs, count),
        compiler_params=pltpu.CompilerParams(
            collective_id=1, has_side_effects=True, vmem_limit_bytes=WIDE
        ),
        cost_estimate=LONG,
        name="gather_weights",
    )(*slabs, *swaps)


def gather_kernel(chips, downward, paired, count, slabs, passed, rows_ref, *refs):
    refs = list(refs)

    def take(number):
        taken = refs[:number]
        del refs[:number]
        return taken

    hops = count // 2 - 1
    sources, moved = take(slabs), take(passed)
    (out_ref,), targets, landed, (zero_ref,) = take(1), take(slabs), take(passed * hops), take(1)
    (stage,) = take(1)
    here, up_send, up_recv, down_send, down_recv, pair_send, pair_recv, near_send, near_recv = take(9)
    plan = Slabs(count, sources, targets, *take(6 + slabs)) if slabs else None
    pass_send, pass_recv = take(2) if passed else (None, None)
    zero_ref[...] = jnp.zeros_like(zero_ref)
    c, w = lax.axis_index("ctx"), lax.axis_index("wt")
    z = c // 2
    core = lax.rem(c, 2)
    side = lax.rem(w, 2) if paired else 0
    near, partner = (flip(c, 1), w), (c, flip(w, 1))
    above = (lax.rem(c + 2, 2 * chips), w)
    below = (lax.rem(c + 2 * chips - 2, 2 * chips), w)
    far = [(c, flip(w, 2 * d + 2)) for d in range(hops)]
    greet([near, above, below] + ([partner] if paired else []) + (plan.devices() if plan else []) + (far if passed else []))

    def onward(i, d):
        return remote(
            moved[i], landed[i * hops + d], pass_send.at[i, d], pass_recv.at[i, d], far[d]
        )

    def spot(chip, which, parity):
        return out_ref.at[chip, which, parity]

    def lift(chip, source):
        return remote(source, spot(chip, side, core), up_send.at[chip], up_recv.at[chip], above)

    def drop(chip, source):
        return remote(source, spot(chip, side, core), down_send.at[chip], down_recv.at[chip], below)

    def give(chip, source):
        return remote(source, spot(chip, side, core), pair_send.at[chip], pair_recv.at[chip], partner)

    def taken(chip):
        return remote(
            spot(chip, 1 - side, core), spot(chip, 1 - side, core), pair_send.at[chip], pair_recv.at[chip], partner
        )

    def hand(chip, which, source):
        return remote(source, spot(chip, which, core), near_send.at[chip, which], near_recv.at[chip, which], near)

    def handed(chip, which):
        there = spot(chip, which, 1 - core)
        return remote(there, there, near_send.at[chip, which], near_recv.at[chip, which], near)

    def settle_pair(chip):
        taken(chip).wait_recv()
        hand(chip, 1 - side, spot(chip, 1 - side, core)).start()

    load = pltpu.make_async_copy(rows_ref, stage, here.at[0])
    keep = pltpu.make_async_copy(stage, spot(z, side, core), here.at[1])
    load.start()
    pl.when(z < chips - 1)(lambda: lift(z, rows_ref).start())
    if downward:
        pl.when(z > 0)(lambda: drop(z, rows_ref).start())
    if paired:
        give(z, rows_ref).start()
    hand(z, side, rows_ref).start()
    if plan:
        plan.start()
    for d in range(hops):
        for i in range(passed):
            onward(i, d).start()
    load.wait()
    keep.start()
    for step in range(1, chips):
        low, high = z - step, z + step

        @pl.when(low >= 0)
        def _():
            lift(low, spot(low, side, core)).wait_recv()
            pl.when(z < chips - 1)(lambda: lift(low, spot(low, side, core)).start())
            if paired:
                give(low, spot(low, side, core)).start()
            hand(low, side, spot(low, side, core)).start()

        if downward:

            @pl.when(high < chips)
            def _():
                drop(high, spot(high, side, core)).wait_recv()
                pl.when(z > 0)(lambda: drop(high, spot(high, side, core)).start())
                if paired:
                    give(high, spot(high, side, core)).start()
                hand(high, side, spot(high, side, core)).start()

        if paired:
            if step == 1:
                settle_pair(z)
            else:
                pl.when(z - step + 1 >= 0)(lambda: settle_pair(z - step + 1))
                pl.when(z + step - 1 < chips)(lambda: settle_pair(z + step - 1))
    if paired:
        pl.when(z - chips + 1 >= 0)(lambda: settle_pair(z - chips + 1))
        pl.when(z + chips - 1 < chips)(lambda: settle_pair(z + chips - 1))
    keep.wait()
    if plan:
        plan.relay()
        plan.finish()

    def finish(chip):
        here_now = spot(chip, side, core)
        pl.when((z < chips - 1) & (chip <= z))(lambda: lift(chip, here_now).wait_send())
        if downward:
            pl.when((z > 0) & (chip >= z))(lambda: drop(chip, here_now).wait_send())
        if paired:
            give(chip, here_now).wait_send()
            for which in range(2):
                hand(chip, which, spot(chip, which, core)).wait_send()
                handed(chip, which).wait_recv()
        else:
            hand(chip, side, here_now).wait_send()
            handed(chip, side).wait_recv()

    for chip in range(chips):
        if downward:
            finish(chip)
        else:
            pl.when(chip <= z)(lambda: finish(chip))
    for d in range(hops):
        for i in range(passed):
            onward(i, d).wait()


def gather_rows(rows, collective_id, downward, paired, name, slabs=(), moved=()):
    chips = lax.axis_size("ctx") // 2
    count = lax.axis_size("wt")
    hops = count // 2 - 1
    line = pltpu.SemaphoreType.DMA((chips,))
    both = pltpu.SemaphoreType.DMA((chips, 2))
    shape = jax.ShapeDtypeStruct((chips, 2 if paired else 1, 2) + rows.shape, rows.dtype)
    landed = tuple(jax.ShapeDtypeStruct(m.shape, m.dtype) for m in moved for _ in range(hops))
    shapes = (shape,) + Slabs.shapes(slabs, count) + landed
    *results, zero = pl.pallas_call(
        functools.partial(gather_kernel, chips, downward, paired, count, len(slabs), len(moved)),
        out_shape=shapes + (jax.ShapeDtypeStruct((8, 128), jnp.int32),),
        in_specs=[pl.BlockSpec(memory_space=pl.ANY)] * (1 + len(slabs) + len(moved)),
        out_specs=(pl.BlockSpec(memory_space=pl.ANY),) * len(shapes)
        + (pl.BlockSpec(memory_space=pltpu.VMEM),),
        scratch_shapes=[pltpu.VMEM(rows.shape, rows.dtype), pltpu.SemaphoreType.DMA((2,))]
        + [line] * 6
        + [both] * 2
        + (Slabs.scratch(slabs, count) if slabs else [])
        + ([pltpu.SemaphoreType.DMA((len(moved), hops))] * 2 if moved else []),
        compiler_params=pltpu.CompilerParams(
            collective_id=collective_id, has_side_effects=True, vmem_limit_bytes=WIDE
        ),
        cost_estimate=LONG,
        name=name,
    )(rows, *slabs, *moved)
    return results + [zero[0, 0]]


def scatter_kernel(chips, upward, paired, pieces, fused, *refs):
    if fused:
        rows_ref, slot_ref, out_ref, built, *refs = refs
        partial_ref = None
    else:
        partial_ref, out_ref, *refs = refs
    own, sib, mate, low_in, high_in, load, near_send, near_recv, *refs = refs
    pair_send, pair_recv, up_send, up_recv, down_send, down_recv = refs
    c, w = lax.axis_index("ctx"), lax.axis_index("wt")
    z = c // 2
    core = lax.rem(c, 2)
    side = lax.rem(w, 2) if paired else 0
    sides = 2 if paired else 1
    near, partner = (flip(c, 1), w), (c, flip(w, 1))
    above = (lax.rem(c + 2, 2 * chips), w)
    below = (lax.rem(c + 2 * chips - 2, 2 * chips), w)
    rows = own.shape[2] // pieces
    greet([near, above, below] + ([partner] if paired else []))
    order = []
    for i in range(chips // 2):
        order += [chips - 1 - i, i]
    if chips % 2:
        order.append(chips // 2)
    if not upward:
        order = list(range(chips))

    def wanted(chip, action):
        if upward:
            action()
        else:
            pl.when(chip <= z)(action)

    def fetch(chip, which):
        return pltpu.make_async_copy(
            partial_ref.at[chip, which, core], own.at[chip, which], load.at[chip, which]
        )

    def hand(chip, which):
        return remote(
            built.at[chip, which] if fused else partial_ref.at[chip, which, 1 - core],
            sib.at[chip, which],
            near_send.at[chip, which],
            near_recv.at[chip, which],
            near,
        )

    def cut(piece):
        return pl.ds(piece * rows, rows)

    def give(chip, piece):
        return remote(
            own.at[chip, 1 - side, cut(piece)],
            mate.at[chip, cut(piece)],
            pair_send.at[chip, piece],
            pair_recv.at[chip, piece],
            partner,
        )

    def lift(chip, piece):
        return remote(
            own.at[chip, side, cut(piece)],
            low_in.at[chip, cut(piece)],
            up_send.at[chip, piece],
            up_recv.at[chip, piece],
            above,
        )

    def drop(chip, piece):
        return remote(
            own.at[chip, side, cut(piece)],
            high_in.at[chip, cut(piece)],
            down_send.at[chip, piece],
            down_recv.at[chip, piece],
            below,
        )

    def add_into(chip, which, piece, other):
        spot = own.at[chip, which, cut(piece)]
        spot[...] = spot[...] + other[...]

    def spread(chip, which, parity, spot):
        local, depth, width = rows_ref.shape[2:]
        tokens = spot.shape[0]
        span = pl.ds(pl.multiple_of(parity * tokens, tokens), tokens)
        place = lax.broadcasted_iota(jnp.int32, (depth, tokens), 0)
        ones = jnp.concatenate(
            [
                (slot_ref[chip, which, e : e + 1, span] == place).astype(jnp.float32)
                for e in range(local)
            ],
            axis=0,
        ).astype(jnp.bfloat16)
        spot[...] = lax.dot_general(
            ones,
            rows_ref[chip, which].reshape(local * depth, width),
            (((0,), (0,)), ((), ())),
            preferred_element_type=jnp.float32,
        ).astype(jnp.bfloat16)

    def begin(chip):
        for which in range(sides):
            if fused:
                spread(chip, which, 1 - core, built.at[chip, which])
            hand(chip, which).start()
            if fused:
                spread(chip, which, core, own.at[chip, which])
            else:
                fetch(chip, which).start()

    if not fused:
        for chip in order:
            wanted(chip, lambda: begin(chip))
    else:
        begin(order[0])

    def meet(chip):
        for which in range(sides):
            if not fused:
                fetch(chip, which).wait()
            hand(chip, which).wait_recv()
        for piece in range(pieces):
            if paired:
                add_into(chip, 1 - side, piece, sib.at[chip, 1 - side, cut(piece)])
                give(chip, piece).start()
            add_into(chip, side, piece, sib.at[chip, side, cut(piece)])

    def travel(chip):
        for piece in range(pieces):
            if paired:
                give(chip, piece).wait_recv()
                add_into(chip, side, piece, mate.at[chip, cut(piece)])
            if upward:

                @pl.when(z < chip)
                def _():
                    @pl.when(z > 0)
                    def _():
                        lift(chip, piece).wait_recv()
                        add_into(chip, side, piece, low_in.at[chip, cut(piece)])

                    lift(chip, piece).start()

            @pl.when(z > chip)
            def _():
                @pl.when(z < chips - 1)
                def _():
                    drop(chip, piece).wait_recv()
                    add_into(chip, side, piece, high_in.at[chip, cut(piece)])

                drop(chip, piece).start()

    for i, chip in enumerate(order):
        if fused and i + 1 < len(order):
            begin(order[i + 1])
        wanted(chip, lambda: meet(chip))
        if i >= 1:
            wanted(order[i - 1], lambda: travel(order[i - 1]))
    wanted(order[-1], lambda: travel(order[-1]))
    for piece in range(pieces):
        out_ref[cut(piece), :] = own.at[z, side, cut(piece)][...].astype(jnp.float32)
    for piece in range(pieces):
        if upward:

            @pl.when(z > 0)
            def _():
                lift(z, piece).wait_recv()
                out_ref[cut(piece), :] += low_in.at[z, cut(piece)][...].astype(jnp.float32)

        @pl.when(z < chips - 1)
        def _():
            drop(z, piece).wait_recv()
            out_ref[cut(piece), :] += high_in.at[z, cut(piece)][...].astype(jnp.float32)

    def finish(chip):
        for which in range(sides):
            hand(chip, which).wait_send()
        for piece in range(pieces):
            if paired:
                give(chip, piece).wait_send()
            if upward:
                pl.when(z < chip)(lambda: lift(chip, piece).wait_send())
            pl.when(z > chip)(lambda: drop(chip, piece).wait_send())

    for chip in order:
        wanted(chip, lambda: finish(chip))


def scatter_rows(partial, collective_id, upward, paired, name, slots=None):
    fused = slots is not None
    dma = pltpu.SemaphoreType.DMA
    pieces = 2
    if fused:
        chips, sides, _, _, width = partial.shape
        tokens = slots.shape[3] // 2
    else:
        chips, sides, _, tokens, width = partial.shape
    block = (tokens, width)
    several = pltpu.VMEM((chips, sides) + block, jnp.bfloat16)
    return pl.pallas_call(
        functools.partial(scatter_kernel, chips, upward, paired, pieces, fused),
        out_shape=jax.ShapeDtypeStruct(block, jnp.float32),
        in_specs=[pl.BlockSpec(memory_space=pltpu.VMEM)] * 2
        if fused
        else [pl.BlockSpec(memory_space=pl.ANY)],
        out_specs=pl.BlockSpec(memory_space=pltpu.VMEM),
        scratch_shapes=([several] if fused else [])
        + [
            several,
            several,
            pltpu.VMEM((chips if paired else 1,) + block, jnp.bfloat16),
            pltpu.VMEM((chips if upward else 1,) + block, jnp.bfloat16),
            pltpu.VMEM((chips,) + block, jnp.bfloat16),
            dma((chips, 2)),
            dma((chips, 2)),
            dma((chips, 2)),
        ]
        + [dma((chips, pieces))] * 6,
        compiler_params=pltpu.CompilerParams(
            collective_id=collective_id, has_side_effects=True, vmem_limit_bytes=WIDE
        ),
        cost_estimate=LONG if paired else CHEAP,
        name=name,
    )(*((partial, slots) if fused else (partial,)))


def dense_kernel(chips, count, matrices, pieces, *refs):
    refs = list(refs)

    def take(number):
        taken = refs[:number]
        del refs[:number]
        return taken

    grads, outs = take(matrices), take(matrices)
    own, sib, mates, low, final = (take(matrices) for _ in range(5))
    (load, near_send, near_recv, send, recv, low_send, low_recv, back_send, back_recv, last_send, last_recv, keep) = refs
    c, w = lax.axis_index("ctx"), lax.axis_index("wt")
    z = c // 2
    core = lax.rem(c, 2)
    near = (flip(c, 1), w)
    above = (lax.rem(c + 2, 2 * chips), w)
    below = (lax.rem(c + 2 * chips - 2, 2 * chips), w)
    dims = [1 << i for i in range(count.bit_length() - 1)]
    greet([near, above, below] + [(c, flip(w, d)) for d in dims])

    def order(j):
        return dims if pieces[j][3] else dims[::-1]

    def sends(j, stage):
        step, rest = order(j)[stage], order(j)[stage + 1 :]
        offsets = [step]
        for r in rest:
            offsets += [o ^ r for o in offsets]
        return offsets

    def span(j, parity=None):
        m, first, rows, _ = pieces[j]
        if parity is None:
            return pl.ds(first, rows)
        half = grads[m].shape[1] // 2
        return pl.ds(pl.multiple_of(parity * half + first, 16), rows)

    def fetch(j):
        m = pieces[j][0]
        return pltpu.make_async_copy(grads[m].at[:, span(j, core)], own[m].at[:, span(j)], load.at[j])

    def hand(j):
        m = pieces[j][0]
        return remote(
            grads[m].at[:, span(j, 1 - core)], sib[m].at[:, span(j)], near_send.at[j], near_recv.at[j], near
        )

    def give(j, stage, o):
        m = pieces[j][0]
        step = order(j)[stage]
        return remote(
            own[m].at[flip(w, o), span(j)],
            mates[m].at[o - 1, span(j)],
            send.at[j, o - 1],
            recv.at[j, o - 1],
            (c, flip(w, step)),
        )

    def total(j):
        return own[pieces[j][0]].at[w, span(j)]

    def add(spot, other):
        spot[...] = spot[...] + other[...]

    def start(j):
        hand(j).start()
        fetch(j).start()

    def share(j):
        m = pieces[j][0]
        fetch(j).wait()
        hand(j).wait_recv()
        for o in sends(j, 0):
            add(own[m].at[flip(w, o), span(j)], sib[m].at[flip(w, o), span(j)])
            give(j, 0, o).start()
        for o in range(count):
            if o not in sends(j, 0):
                add(own[m].at[flip(w, o), span(j)], sib[m].at[flip(w, o), span(j)])

    def collect(j, stage):
        m = pieces[j][0]
        step = order(j)[stage]
        for o in sends(j, stage):
            give(j, stage, o).wait_recv()
        last = stage + 1 == len(dims)
        onward_blocks = [] if last else sends(j, stage + 1)
        for o in sends(j, stage):
            kept = o ^ step
            if kept in onward_blocks:
                add(own[m].at[flip(w, kept), span(j)], mates[m].at[o - 1, span(j)])
                give(j, stage + 1, kept).start()
        for o in sends(j, stage):
            kept = o ^ step
            if kept not in onward_blocks:
                add(own[m].at[flip(w, kept), span(j)], mates[m].at[o - 1, span(j)])

    def line(j):
        return (z, above, below) if j % 2 == 0 else (chips - 1 - z, below, above)

    def onward(j):
        m = pieces[j][0]
        return remote(total(j), low[m].at[span(j)], low_send.at[j], low_recv.at[j], line(j)[1])

    def backward(j):
        spot = final[pieces[j][0]].at[span(j)]
        return remote(spot, spot, back_send.at[j], back_recv.at[j], line(j)[2])

    def across(j, parity):
        m = pieces[j][0]
        return remote(
            final[m].at[span(j)], outs[m].at[span(j, parity)], last_send.at[j], last_recv.at[j], near
        )

    def store(j):
        m = pieces[j][0]
        return pltpu.make_async_copy(final[m].at[span(j)], outs[m].at[span(j, core)], keep.at[j])

    def accumulate(j):
        place = line(j)[0]
        m = pieces[j][0]

        @pl.when(place > 0)
        def _():
            onward(j).wait_recv()
            add(total(j), low[m].at[span(j)])

        @pl.when(place < chips - 1)
        def _():
            onward(j).start()

        @pl.when(place == chips - 1)
        def _():
            final[m][span(j), :] = total(j)[...]
            backward(j).start()
            across(j, core).start()
            store(j).start()

    def spread(j):
        place = line(j)[0]

        @pl.when(place < chips - 1)
        def _():
            backward(j).wait_recv()
            pl.when(place > 0)(lambda: backward(j).start())
            across(j, core).start()
            store(j).start()

    number = len(pieces)
    for j in range(number):
        start(j)
    last = chips - 1
    lead, gap = 2, 1
    behind = lead + gap * (len(dims) - 1)
    for t in range(number + 2 * last + behind):
        if t < number:
            share(t)
        for stage in range(len(dims)):
            if 0 <= t - lead - gap * stage < number:
                collect(t - lead - gap * stage, stage)
        for hop in range(2 * last, -1, -1):
            j = t - hop - behind
            if not 0 <= j < number:
                continue
            if hop <= last:
                pl.when(line(j)[0] == hop)(lambda: accumulate(j))
            if hop > last:
                pl.when(line(j)[0] == 2 * last - hop)(lambda: spread(j))
    for j in range(number):
        place = line(j)[0]
        hand(j).wait_send()
        for stage in range(len(dims)):
            for o in sends(j, stage):
                give(j, stage, o).wait_send()
        pl.when(place < chips - 1)(lambda: onward(j).wait_send())
        pl.when(place > 0)(lambda: backward(j).wait_send())
        across(j, core).wait_send()
        across(j, 1 - core).wait_recv()
        store(j).wait()


def reduce_dense(grads):
    count = lax.axis_size("wt")
    chips = lax.axis_size("ctx") // 2
    shapes = [(g.shape[0] // count, g.shape[1]) for g in grads]
    pieces = []
    for m, (rows, _) in enumerate(shapes):
        half, width = rows // 2, shapes[m][1]
        cuts = max(n for n in range(1, 9) if half % (16 * n) == 0 and (n == 1 or half * width > 60000 * (n - 1)))
        for i in range(cuts):
            pieces.append((m, i * (rows // 2 // cuts), rows // 2 // cuts, len(pieces) % 2))
    halves = [(rows // 2, width) for rows, width in shapes]
    dma = pltpu.SemaphoreType.DMA
    one, many = dma((len(pieces),)), dma((len(pieces), count - 1))
    return pl.pallas_call(
        functools.partial(dense_kernel, chips, count, len(grads), tuple(pieces)),
        out_shape=[jax.ShapeDtypeStruct(s, jnp.bfloat16) for s in shapes],
        in_specs=[pl.BlockSpec(memory_space=pl.ANY)] * len(grads),
        out_specs=[pl.BlockSpec(memory_space=pl.ANY)] * len(grads),
        scratch_shapes=[pltpu.VMEM((count,) + h, jnp.bfloat16) for h in halves]
        + [pltpu.VMEM((count,) + h, jnp.bfloat16) for h in halves]
        + [pltpu.VMEM((count - 1,) + h, jnp.bfloat16) for h in halves]
        + [pltpu.VMEM(h, jnp.bfloat16) for h in halves]
        + [pltpu.VMEM(h, jnp.bfloat16) for h in halves]
        + [one, one, one, many, many, one, one, one, one, one, one, one],
        compiler_params=pltpu.CompilerParams(
            collective_id=7, has_side_effects=True, vmem_limit_bytes=WIDE
        ),
        cost_estimate=LONG,
        name="reduce_dense",
    )(*[g.reshape((count,) + s) for g, s in zip(grads, shapes)])


def dot_of(a, b, left, right):
    return lax.dot_general(
        a, b, (((left,), (right,)), ((), ())), preferred_element_type=jnp.float32
    )


def stacked_heads(ref):
    return jnp.concatenate(
        [ref[:, h * HEAD_DIM : (h + 1) * HEAD_DIM] for h in range(ref.shape[1] // HEAD_DIM)], axis=0
    )


exponent_scale = HEAD_DIM ** (-0.5) * math.log2(math.e)


def attend_kernel(place_ref, query_ref, both_ref, row_ref, column_ref, out_ref, log_ref, best, total, accum):
    tokens = query_ref.shape[0]
    group = query_ref.shape[1] // HEAD_DIM
    width = 2 * tokens
    place = place_ref[0]
    queries = stacked_heads(query_ref)
    best[...] = jnp.full_like(best, masked_value)
    total[...] = jnp.zeros_like(total)
    accum[...] = jnp.zeros_like(accum)
    query_pos = place * tokens + lax.broadcasted_iota(jnp.int32, (tokens, width), 0)
    key_pos = lax.broadcasted_iota(jnp.int32, (tokens, width), 1)

    def step(j, carry):
        span = pl.ds(pl.multiple_of(j * width, width), width)
        allowed = (key_pos + j * width <= query_pos) & (row_ref[0:1, span] == column_ref[:, 0:1])
        bias = jnp.where(allowed, 0.0, masked_value)
        scores = dot_of(queries, both_ref[span, :HEAD_DIM], 1, 1)
        scores = (scores.reshape(group, tokens, width) + bias[None]).reshape(group * tokens, width)
        newest = jnp.maximum(best[...], jnp.max(scores, axis=1, keepdims=True))
        factor = jnp.exp2((best[...] - newest) * exponent_scale)
        weights = jnp.exp2((scores - newest[:, :1]) * exponent_scale)
        total[...] = total[...] * factor + jnp.sum(weights, axis=1, keepdims=True)
        accum[...] = accum[...] * factor + dot_of(
            weights.astype(jnp.bfloat16), both_ref[span, HEAD_DIM:], 1, 0
        )
        best[...] = newest
        return carry

    lax.fori_loop(0, place // 2 + 1, step, 0)
    heads = accum[...] / total[...]
    for h in range(group):
        out_ref[:, h * HEAD_DIM : (h + 1) * HEAD_DIM] = heads[h * tokens : (h + 1) * tokens]
    logs = best[...] * exponent_scale + jnp.log2(total[...])
    log_ref[0] = jnp.transpose(logs)[:8]


def attend(place, projected, both, seg_row, seg_column):
    tokens = projected.shape[0]
    group = HEADS // KV_HEADS
    rows, span = group * tokens, both.shape[0]
    stat = pltpu.VMEM((rows, HEAD_DIM), jnp.float32)
    return pl.pallas_call(
        attend_kernel,
        grid=(KV_HEADS,),
        out_shape=(
            jax.ShapeDtypeStruct((tokens, HEADS * HEAD_DIM), jnp.float32),
            jax.ShapeDtypeStruct((KV_HEADS, 8, rows), jnp.float32),
        ),
        in_specs=[
            pl.BlockSpec(memory_space=pltpu.SMEM),
            pl.BlockSpec((tokens, group * HEAD_DIM), lambda g: (0, g)),
            pl.BlockSpec((span, 2 * HEAD_DIM), lambda g: (0, g)),
            pl.BlockSpec((1, span), lambda g: (0, 0)),
            pl.BlockSpec((tokens, 1), lambda g: (0, 0)),
        ],
        out_specs=(
            pl.BlockSpec((tokens, group * HEAD_DIM), lambda g: (0, g)),
            pl.BlockSpec((1, 8, rows), lambda g: (g, 0, 0)),
        ),
        scratch_shapes=[stat, stat, stat],
        compiler_params=pltpu.CompilerParams(vmem_limit_bytes=WIDE),
        cost_estimate=CHEAP,
        name="attend",
    )(place, projected, both, seg_row, seg_column)


def attend_back_kernel(place_ref, query_ref, both_ref, row_ref, column_ref, heads_ref, grad_ref, log_ref, grad_query_ref, grad_both_ref, accum):
    tokens = query_ref.shape[0]
    group = query_ref.shape[1] // HEAD_DIM
    width = 2 * tokens
    rows = group * tokens
    scale = HEAD_DIM ** (-0.5)
    place = place_ref[0]
    queries, grads = stacked_heads(query_ref), stacked_heads(grad_ref)
    product = grads.astype(jnp.float32) * stacked_heads(heads_ref)
    delta = jnp.sum(product, axis=1, keepdims=True)
    delta = jnp.transpose(jnp.broadcast_to(delta, (rows, HEAD_DIM)))[0:1]
    logs = log_ref[0, 0:1, :]
    accum[...] = jnp.zeros_like(accum)
    grad_both_ref[...] = jnp.zeros_like(grad_both_ref)
    query_pos = place * tokens + lax.broadcasted_iota(jnp.int32, (width, tokens), 1)
    key_pos = lax.broadcasted_iota(jnp.int32, (width, tokens), 0)

    def step(j, carry):
        span = pl.ds(pl.multiple_of(j * width, width), width)
        allowed = (key_pos + j * width <= query_pos) & (column_ref[span, 0:1] == row_ref[0:1, :])
        bias = jnp.where(allowed, 0.0, masked_value)
        bias = jnp.concatenate([bias] * group, axis=1)
        keys, values = both_ref[span, :HEAD_DIM], both_ref[span, HEAD_DIM:]
        scores = dot_of(keys, queries, 1, 1)
        probs = jnp.exp2(scores * exponent_scale + bias - logs)
        grad_probs = dot_of(values, grads, 1, 1)
        grad_scores = (probs * (grad_probs - delta)).astype(jnp.bfloat16)
        accum[...] += dot_of(grad_scores, keys, 0, 0)
        grad_both_ref[span, :HEAD_DIM] = (dot_of(grad_scores, queries, 1, 0) * scale).astype(jnp.bfloat16)
        grad_both_ref[span, HEAD_DIM:] = dot_of(probs.astype(jnp.bfloat16), grads, 1, 0).astype(jnp.bfloat16)
        return carry

    lax.fori_loop(0, place // 2 + 1, step, 0)
    grad_queries = (accum[...] * scale).astype(jnp.bfloat16)
    for h in range(group):
        grad_query_ref[:, h * HEAD_DIM : (h + 1) * HEAD_DIM] = grad_queries[h * tokens : (h + 1) * tokens]


def attend_back(place, projected, both, query_seg_row, seg_column, heads_out, grad_attended, logs):
    tokens = projected.shape[0]
    group = HEADS // KV_HEADS
    rows, span = group * tokens, both.shape[0]
    per_group = pl.BlockSpec((tokens, group * HEAD_DIM), lambda g: (0, g))
    return pl.pallas_call(
        attend_back_kernel,
        grid=(KV_HEADS,),
        out_shape=(
            jax.ShapeDtypeStruct((tokens, HEADS * HEAD_DIM), jnp.bfloat16),
            jax.ShapeDtypeStruct(both.shape, jnp.bfloat16),
        ),
        in_specs=[
            pl.BlockSpec(memory_space=pltpu.SMEM),
            per_group,
            pl.BlockSpec((span, 2 * HEAD_DIM), lambda g: (0, g)),
            pl.BlockSpec((1, tokens), lambda g: (0, 0)),
            pl.BlockSpec((span, 1), lambda g: (0, 0)),
            per_group,
            per_group,
            pl.BlockSpec((1, 8, rows), lambda g: (g, 0, 0)),
        ],
        out_specs=(per_group, pl.BlockSpec((span, 2 * HEAD_DIM), lambda g: (0, g))),
        scratch_shapes=[pltpu.VMEM((rows, HEAD_DIM), jnp.float32)],
        compiler_params=pltpu.CompilerParams(vmem_limit_bytes=WIDE),
        cost_estimate=CHEAP,
        name="attend_back",
    )(place, projected, both, query_seg_row, seg_column, heads_out, grad_attended, logs)


def pick_rows_of(slot_rows, rows_of, local, depth, tokens):
    place = lax.broadcasted_iota(jnp.int32, (depth, tokens), 0)
    total, masks = None, []
    for core in range(2):
        chosen = [slot_rows[core][e : e + 1] == place for e in range(local)]
        ones = jnp.concatenate([c.astype(jnp.float32) for c in chosen], axis=0).astype(jnp.bfloat16)
        term = jnp.dot(ones, rows_of(core), preferred_element_type=jnp.float32)
        total = term if total is None else total + term
        masks.append(chosen)
    return total, masks


def pick_grads_kernel(local, first_ref, earlier_ref, rows_ref, out_ref, scale_ref, slot_ref):
    depth = out_ref.shape[3]
    tokens = slot_ref.shape[3] // 2
    slot_rows, gate_rows, count = [], [], None
    for core in range(2):
        table = rows_ref[0, core, 0, tokens : tokens + 16, :].astype(jnp.float32)
        member, gate = [], []
        for e in range(local):
            expert = (first_ref[0] + e).astype(jnp.float32)
            found, weight = None, None
            for k in range(TOPK):
                span = slice(k * tokens, (k + 1) * tokens)
                named = table[0:1, span] == expert
                value = jnp.where(named, table[1:2, span] + table[2:3, span] + table[3:4, span], 0.0)
                mark = jnp.where(named, 1.0, 0.0)
                found = mark if k == 0 else found + mark
                weight = value if k == 0 else weight + value
            member.append(found)
            gate.append(weight)
        member = jnp.concatenate(member + [jnp.zeros((8 - local, tokens), jnp.float32)], axis=0)
        rank = jnp.dot(member.astype(jnp.bfloat16), earlier_ref[...], preferred_element_type=jnp.float32)
        if core:
            rank = rank + count
        count = jnp.sum(member, axis=1, keepdims=True)
        slots = jnp.where(member > 0.5, rank.astype(jnp.int32), -1)[:local]
        slot_ref[0, 0, :, core * tokens : (core + 1) * tokens] = slots
        slot_rows.append(slots)
        gate_rows.append(gate)
    total, masks = pick_rows_of(
        slot_rows, lambda core: rows_ref[0, core, 0, :tokens, :], local, depth, tokens
    )
    weight = None
    for core in range(2):
        gates = jnp.concatenate(
            [
                jnp.sum(jnp.where(masks[core][e], gate_rows[core][e], 0.0), axis=1, keepdims=True)
                for e in range(local)
            ],
            axis=0,
        )
        weight = gates if core == 0 else weight + gates
    scale_ref[0, 0] = jnp.broadcast_to(weight, (local * depth, 128)).reshape(local, depth, 128)
    out_ref[0, 0] = (total * weight).astype(jnp.bfloat16).reshape(local, depth, total.shape[1])


def pick_grads(rows, first, local, tokens):
    chips, _, sides, long, width = rows.shape
    depth = 2 * CAP
    earlier = jnp.arange(tokens)[:, None] < jnp.arange(tokens)[None, :]
    return pl.pallas_call(
        functools.partial(pick_grads_kernel, local),
        grid=(chips, sides),
        out_shape=(
            jax.ShapeDtypeStruct((chips, sides, local, depth, width), jnp.bfloat16),
            jax.ShapeDtypeStruct((chips, sides, local, depth, 128), jnp.float32),
            jax.ShapeDtypeStruct((chips, sides, local, 2 * tokens), jnp.int32),
        ),
        in_specs=[
            pl.BlockSpec(memory_space=pltpu.SMEM),
            pl.BlockSpec((tokens, tokens), lambda z, s: (0, 0)),
            pl.BlockSpec((1, 2, 1, long, width), lambda z, s: (z, 0, s, 0, 0)),
        ],
        out_specs=(
            pl.BlockSpec((1, 1, local, depth, width), lambda z, s: (z, s, 0, 0, 0)),
            pl.BlockSpec((1, 1, local, depth, 128), lambda z, s: (z, s, 0, 0, 0)),
            pl.BlockSpec((1, 1, local, 2 * tokens), lambda z, s: (z, s, 0, 0)),
        ),
        compiler_params=pltpu.CompilerParams(vmem_limit_bytes=WIDE),
        cost_estimate=CHEAP,
        name="pick_grads",
    )(first, earlier.astype(jnp.bfloat16), rows)


def pick_tokens_kernel(slot_ref, rows_ref, out_ref):
    local, depth = out_ref.shape[2], out_ref.shape[3]
    tokens = rows_ref.shape[3]
    slot_rows = [slot_ref[0, 0, :, core * tokens : (core + 1) * tokens] for core in range(2)]
    total, _ = pick_rows_of(slot_rows, lambda core: rows_ref[0, 0, core], local, depth, tokens)
    out_ref[0, 0] = total.astype(jnp.bfloat16).reshape(local, depth, total.shape[1])


def pick_tokens(rows, slots):
    chips, sides, local, both = slots.shape
    tokens, width = rows.shape[3:]
    depth = 2 * CAP
    return pl.pallas_call(
        pick_tokens_kernel,
        grid=(chips, sides),
        out_shape=jax.ShapeDtypeStruct((chips, sides, local, depth, width), jnp.bfloat16),
        in_specs=[
            pl.BlockSpec((1, 1, local, both), lambda z, s: (z, s, 0, 0)),
            pl.BlockSpec((1, 1, 2, tokens, width), lambda z, s: (z, s, 0, 0, 0)),
        ],
        out_specs=pl.BlockSpec((1, 1, local, depth, width), lambda z, s: (z, s, 0, 0, 0)),
        compiler_params=pltpu.CompilerParams(vmem_limit_bytes=WIDE),
        cost_estimate=CHEAP,
        name="pick_tokens",
    )(slots, rows)


def spread_kernel(apart, slot_ref, rows_ref, out_ref):
    local, depth, width = rows_ref.shape[2:]
    tokens = out_ref.shape[3]
    place = lax.broadcasted_iota(jnp.int32, (depth, tokens), 0)
    rows = rows_ref[0, 0].reshape(local * depth, width)
    for core in range(2):
        span = slice(core * tokens, (core + 1) * tokens)
        ones = jnp.concatenate(
            [(slot_ref[0, 0, e : e + 1, span] == place).astype(jnp.float32) for e in range(local)], axis=0
        ).astype(jnp.bfloat16)
        spot = out_ref.at[0, core, 0] if apart else out_ref.at[0, 0, core]
        spot[...] = lax.dot_general(
            ones, rows, (((0,), (0,)), ((), ())), preferred_element_type=jnp.float32
        ).astype(jnp.bfloat16)


def spread_rows(rows, slots, name, apart):
    chips, sides, local, both = slots.shape
    depth, width = rows.shape[3:]
    tokens = both // 2
    return pl.pallas_call(
        functools.partial(spread_kernel, apart),
        grid=(chips, sides),
        out_shape=jax.ShapeDtypeStruct(
            (chips, 2, sides, tokens, width) if apart else (chips, sides, 2, tokens, width), jnp.bfloat16
        ),
        in_specs=[
            pl.BlockSpec((1, 1, local, both), lambda z, s: (z, s, 0, 0)),
            pl.BlockSpec((1, 1, local, depth, width), lambda z, s: (z, s, 0, 0, 0)),
        ],
        out_specs=pl.BlockSpec((1, 2, 1, tokens, width), lambda z, s: (z, 0, s, 0, 0))
        if apart
        else pl.BlockSpec((1, 1, 2, tokens, width), lambda z, s: (z, s, 0, 0, 0)),
        compiler_params=pltpu.CompilerParams(vmem_limit_bytes=WIDE),
        cost_estimate=CHEAP,
        name=name,
    )(slots, rows)


def expert_kernel(blocks, x_ref, g_ref, scale_ref, *refs):
    tall_refs, down_refs = refs[:blocks], refs[blocks : 2 * blocks]
    result_ref, back_ref, *grad_refs = refs[2 * blocks : -3]
    tall_all, flat_all, flat_grad = refs[-3:]
    hops = len(grad_refs) // 3
    grad_gate_refs, grad_up_refs = grad_refs[:hops], grad_refs[hops : 2 * hops]
    grad_down_refs = grad_refs[2 * hops :]
    w = lax.axis_index("wt")
    chips, sides, _, depth, width = x_ref.shape
    rows = chips * sides * depth
    part = tall_refs[0].shape[2]
    nn, nt, tn = (((1,), (0,)), ((), ())), (((1,), (1,)), ((), ())), (((0,), (0,)), ((), ()))

    def dot(a, b, dims):
        return lax.dot_general(a, b, dims, preferred_element_type=jnp.float32)

    def columns(ref, q):
        if blocks == 1:
            return ref.at[:, :, 0]
        span = pl.ds(pl.multiple_of(flip(w, q) * part, 128), part)
        return ref.at[:, :, 0, :, span]

    def piece(ref, q):
        return columns(ref, q)[...].reshape(rows, part)

    def offset(q):
        return 0 if blocks == 1 else pl.multiple_of(flip(w, q) * part, 128)

    inner_width = tall_refs[0].shape[3]
    for q in range(blocks):
        span = pl.ds(offset(q), part)
        tall_all[span, :inner_width] = tall_refs[q][0, 0]
        tall_all[span, inner_width:] = tall_refs[q][0, 1]
        flat_all[:, span] = down_refs[q][0]
    x = x_ref[...].reshape(rows, width)
    g = g_ref[...].reshape(rows, width)
    gate = dot(x, tall_all[:, :inner_width], nn)
    up = dot(x, tall_all[:, inner_width:], nn)
    grad_inner = dot(g, flat_all[...], nt)
    sigmoid = jax.nn.sigmoid(gate)
    activated = gate * sigmoid
    inner = (activated * up).astype(jnp.bfloat16)
    grad_gate = (grad_inner * up * (sigmoid * (1.0 + gate * (1.0 - sigmoid)))).astype(jnp.bfloat16)
    grad_up = (grad_inner * activated).astype(jnp.bfloat16)
    grad_both = jnp.concatenate([grad_gate, grad_up], axis=1)
    scale = scale_ref[...].reshape(rows, 128)[:, :1]
    chunk = 512
    for first in range(0, width, chunk):
        span = slice(first, first + chunk)
        result = dot(inner, flat_all[:, span], nn) * scale
        result_ref[:, :, 0, :, span] = result.astype(jnp.bfloat16).reshape(chips, sides, depth, chunk)
        back = dot(grad_both, tall_all[span, :], nt)
        back_ref[:, :, 0, :, span] = back.astype(jnp.bfloat16).reshape(chips, sides, depth, chunk)
        flat_grad[:, span] = dot(inner, g[:, span], tn).astype(jnp.bfloat16)
    for q in range(blocks):
        more = dot(piece(x_ref, q), grad_both, tn).astype(jnp.bfloat16)
        grad_gate_refs[q // 2][q % 2, 0] = more[:, :inner_width]
        grad_up_refs[q // 2][q % 2, 0] = more[:, inner_width:]
        grad_down_refs[q // 2][q % 2, 0] = flat_grad[:, pl.ds(offset(q), part)]


def run_experts(x, g, scale, talls, downs):
    chips, sides, local, depth, width = x.shape
    blocks = len(talls)
    part, inner = talls[0].shape[2:]
    large = chips * sides * depth > 1024
    rows = pl.BlockSpec((chips, sides, 1, depth, width), lambda e: (0, 0, e, 0, 0))
    sources = pl.BlockSpec(
        (chips, sides, 1, depth, width),
        lambda e: (0, 0, e, 0, 0),
        pipeline_mode=pl.Buffered(1 if large else 2),
    )
    scales = pl.BlockSpec((chips, sides, 1, depth, 128), lambda e: (0, 0, e, 0, 0))
    tall = pl.BlockSpec((1, 2, part, inner), lambda e: (e, 0, 0, 0))
    flat = pl.BlockSpec((1, inner, part), lambda e: (e, 0, 0))
    hops, each = max(blocks // 2, 1), min(blocks, 2)
    tall_out = pl.BlockSpec((each, 1, part, inner), lambda e: (0, e, 0, 0))
    flat_out = pl.BlockSpec((each, 1, inner, part), lambda e: (0, e, 0, 0))
    return pl.pallas_call(
        functools.partial(expert_kernel, blocks),
        grid=(local,),
        out_shape=(
            jax.ShapeDtypeStruct(x.shape, jnp.bfloat16),
            jax.ShapeDtypeStruct(x.shape, jnp.bfloat16),
            *[jax.ShapeDtypeStruct((each, local, part, inner), jnp.bfloat16)] * (2 * hops),
            *[jax.ShapeDtypeStruct((each, local, inner, part), jnp.bfloat16)] * hops,
        ),
        in_specs=[sources, sources, scales] + [tall] * blocks + [flat] * blocks,
        out_specs=(rows, rows) + (tall_out,) * (2 * hops) + (flat_out,) * hops,
        scratch_shapes=[
            pltpu.VMEM((width, 2 * inner), jnp.bfloat16),
            pltpu.VMEM((inner, width), jnp.bfloat16),
            pltpu.VMEM((inner, width), jnp.bfloat16),
        ],
        compiler_params=pltpu.CompilerParams(vmem_limit_bytes=60 * 2**20),
        cost_estimate=CHEAP,
        name="experts",
    )(x, g, scale, *talls, *downs)


def place_kernel(arrivals, side_ref, *refs):
    own, other, more, outs = refs[:3], refs[3:6], refs[6 : 6 + 3 * arrivals], refs[6 + 3 * arrivals :]
    mine = pl.program_id(0) == side_ref[0]

    @pl.when(mine)
    def _():
        for i in range(3):
            value = own[i][0, 0].astype(jnp.float32)
            for m in more[i * arrivals : (i + 1) * arrivals]:
                value = value + m[0, 0].astype(jnp.float32)
            outs[i][0] = value

    @pl.when(jnp.logical_not(mine))
    def _():
        for i in range(3):
            outs[i][0] = other[i][0].astype(jnp.float32)


def place_experts(side, own, more, other):
    local = other[0].shape[0]
    arrivals = len(more[0])
    shapes = [o.shape[1:] for o in other]
    paired = [pl.BlockSpec((1, 1) + s, lambda h, e: (0, e, 0, 0)) for s in shapes]
    single = [pl.BlockSpec((1,) + s, lambda h, e: (e, 0, 0)) for s in shapes]
    return pl.pallas_call(
        functools.partial(place_kernel, arrivals),
        grid=(2, local),
        out_shape=[jax.ShapeDtypeStruct((2 * local,) + s, jnp.float32) for s in shapes],
        in_specs=[pl.BlockSpec(memory_space=pltpu.SMEM)]
        + paired
        + single
        + [p for p in paired for _ in range(arrivals)],
        out_specs=[pl.BlockSpec((1,) + s, lambda h, e: (h * local + e, 0, 0)) for s in shapes],
        compiler_params=pltpu.CompilerParams(vmem_limit_bytes=WIDE),
        cost_estimate=CHEAP,
        name="place_experts",
    )(side, *own, *other, *[m for group in more for m in group])


def swap_pairs(value, axis, distance):
    count = lax.axis_size(axis)
    return lax.ppermute(value, axis, [(i, i ^ distance) for i in range(count)])


def own_and_other(stacked, mine):
    return (
        lax.dynamic_index_in_dim(stacked, mine, 0, keepdims=False),
        lax.dynamic_index_in_dim(stacked, 1 - mine, 0, keepdims=False),
    )


def collect_expert(shard, side, pairs):
    local = shard.shape[0]
    kept, given = own_and_other(shard.reshape((2, local // 2) + shard.shape[1:]), side)
    return kept, swap_pairs(given, "wt", 1), [swap_pairs(kept, "wt", 2 * d) for d in range(1, pairs)]


def settle_blocks(blocks, index, axis):
    stacked = jnp.stack(blocks)
    return jnp.concatenate(
        [
            lax.dynamic_index_in_dim(stacked, jnp.bitwise_xor(j, index), 0, False)
            for j in range(len(blocks))
        ],
        axis=axis,
    )


def split_blocks(whole, index, count, axis):
    parts = jnp.stack(jnp.split(whole, count, axis=axis))
    return jnp.stack(
        [
            lax.dynamic_index_in_dim(parts, jnp.bitwise_xor(q, index), 0, False)
            for q in range(count)
        ]
    )


def body(
    hidden,
    segment_ids,
    routes,
    gates,
    cotangent,
    norm_one_gain,
    w_query,
    w_key,
    w_value,
    w_out,
    norm_two_gain,
    shared_gate,
    shared_up,
    shared_down,
    expert_gate,
    expert_up,
    expert_down,
):
    wt_index = lax.axis_index("wt")
    wt_count = lax.axis_size("wt")
    ctx_count = lax.axis_size("ctx")
    chips = ctx_count // 2
    pairs = wt_count // 2
    tokens, width_model = hidden.shape[1:]
    wide, kv_width = w_query.shape[1], w_key.shape[1]
    shared_width = shared_gate.shape[1]
    gates_here = gates[0]
    gate_high = gates_here.astype(jnp.bfloat16)
    gate_rest = gates_here - gate_high.astype(jnp.float32)
    gate_middle = gate_rest.astype(jnp.bfloat16)
    gate_low = (gate_rest - gate_middle.astype(jnp.float32)).astype(jnp.bfloat16)
    table = jnp.concatenate(
        [routes[0].astype(jnp.bfloat16), gate_high, gate_middle, gate_low], axis=1
    )
    grad_rows = cotangent[0]
    depth = norm_one_gain.shape[0]
    extra_rows = 16
    packed = jnp.pad(
        jnp.swapaxes(table, 0, 1).reshape(4, width_model), ((0, extra_rows - 4), (0, 0))
    )
    extended = jnp.concatenate([grad_rows, packed], axis=0)
    gain_pair = jnp.concatenate(
        [norm_one_gain[None], norm_two_gain[None], jnp.zeros((62, depth), jnp.bfloat16)]
    )
    query_weight, key_weight, value_weight, gains, grad_pair, zero = gather_weights(
        (w_query, w_key, w_value, gain_pair), (extended,)
    )
    query_weight = query_weight.reshape(-1, wide)
    key_weight = key_weight.reshape(-1, kv_width)
    value_weight = value_weight.reshape(-1, kv_width)
    zero = zero[0, 0]
    side = lax.rem(wt_index, 2)
    later = side + zero
    collected = [
        collect_expert(jnp.stack([expert_gate, expert_up], axis=1), later, pairs),
        collect_expert(expert_down, later, pairs),
    ]
    gain_one, gain_two = gains[:, 0].reshape(-1), gains[:, 1].reshape(-1)
    local = expert_gate.shape[0] // 2
    first_expert = (lax.axis_index("ctx") * 2 + side) * local

    inputs = hidden[0].astype(jnp.float32)
    offset = lax.axis_index("ctx") * tokens
    seg_all = segment_ids[0]
    query_seg = lax.dynamic_slice_in_dim(seg_all, offset, tokens)
    scale_one = inverse_rms(inputs)
    gain_one_full = gain_one.astype(jnp.float32)
    normed = (inputs * scale_one * gain_one_full).astype(jnp.bfloat16)

    def project(weight):
        return jnp.dot(normed, weight, preferred_element_type=jnp.float32).astype(jnp.bfloat16)

    queries = project(query_weight)
    fresh = jnp.stack(
        [
            project(key_weight).reshape(tokens, KV_HEADS, HEAD_DIM),
            project(value_weight).reshape(tokens, KV_HEADS, HEAD_DIM),
        ],
        axis=2,
    ).reshape(tokens, 2 * kv_width)
    both, out_weight, both_weight, down_weight, zero = gather_rows(
        fresh,
        2,
        False,
        False,
        "gather_keys",
        (w_out, jnp.concatenate([shared_gate, shared_up], axis=1), shared_down),
    )
    out_weight = out_weight.reshape(-1, out_weight.shape[2])
    both_weight = both_weight.reshape(-1, both_weight.shape[2])
    down_weight = down_weight.reshape(-1, down_weight.shape[2])
    both = both.reshape(-1, 2 * kv_width)

    grad_pair, both = lax.optimization_barrier((grad_pair, both))
    all_grads = lax.all_gather(grad_pair, "ctx", axis=0).reshape(
        chips, 2, 2, tokens + extra_rows, width_model
    )

    place = lax.axis_index("ctx").astype(jnp.int32).reshape(1)
    seg_row, seg_column = seg_all[None, :], seg_all[:, None]
    attended_full, logs = attend(place, queries, both, seg_row, query_seg[:, None])
    attended = attended_full.astype(jnp.bfloat16)
    middle = inputs + jnp.dot(attended, out_weight, preferred_element_type=jnp.float32)
    scale_two = inverse_rms(middle)
    gain_two_full = gain_two.astype(jnp.float32)
    normed_two = (middle * scale_two * gain_two_full).astype(jnp.bfloat16)

    shared_parts = jnp.dot(normed_two, both_weight, preferred_element_type=jnp.float32)
    shared_gate_part, shared_up_part = shared_parts[:, :shared_width], shared_parts[:, shared_width:]
    shared_inner = (jax.nn.silu(shared_gate_part) * shared_up_part).astype(jnp.bfloat16)
    shared_result = jnp.dot(shared_inner, down_weight, preferred_element_type=jnp.float32)
    grad_out = grad_rows.astype(jnp.float32)
    grad_shared_down = jnp.einsum(
        "tf,td->fd", shared_inner, grad_rows, preferred_element_type=jnp.float32
    )
    grad_shared_inner = jnp.einsum(
        "td,fd->tf", grad_rows, down_weight, preferred_element_type=jnp.float32
    )
    grad_shared_gate_part = (
        grad_shared_inner * shared_up_part * silu_slope(shared_gate_part)
    ).astype(jnp.bfloat16)
    grad_shared_up_part = (grad_shared_inner * jax.nn.silu(shared_gate_part)).astype(jnp.bfloat16)
    grad_shared_parts = jnp.concatenate([grad_shared_gate_part, grad_shared_up_part], axis=1)
    grad_shared_both = jnp.einsum(
        "td,tf->df", normed_two, grad_shared_parts, preferred_element_type=jnp.float32
    )
    grad_shared_rows = jnp.einsum(
        "tf,df->td", grad_shared_parts, both_weight, preferred_element_type=jnp.float32
    )
    grad_shared_both = grad_shared_both.astype(jnp.bfloat16)
    grad_shared_down = grad_shared_down.astype(jnp.bfloat16)
    normed_two, collected, shared_result, grad_shared_both, grad_shared_down, grad_shared_rows = (
        lax.optimization_barrier(
            (normed_two, collected, shared_result, grad_shared_both, grad_shared_down, grad_shared_rows)
        )
    )
    all_rows, *landed, zero = gather_rows(
        normed_two, 3, True, True, "gather_tokens", (), [c[1] for c in collected]
    )

    def blocks_of(i):
        kept, paired, straight = collected[i]
        blocks = [kept, paired]
        for d in range(pairs - 1):
            blocks += [straight[d], landed[i * (pairs - 1) + d]]
        return blocks

    tall_blocks, down_blocks = blocks_of(0), blocks_of(1)
    grad_received, row_gates, slots = pick_grads(
        all_grads, first_expert.astype(jnp.int32).reshape(1), local, tokens
    )
    received_rows = pick_tokens(all_rows, slots)
    if down_blocks[0].shape[2] % 128:
        results, backs, grads_gate, grads_up, grads_down = run_experts(
            received_rows,
            grad_received,
            row_gates,
            [settle_blocks(tall_blocks, wt_index, 2)],
            [settle_blocks(down_blocks, wt_index, 2)],
        )
        wholes = [
            split_blocks(grads_gate[0], wt_index, wt_count, 1),
            split_blocks(grads_up[0], wt_index, wt_count, 1),
            split_blocks(grads_down[0], wt_index, wt_count, 2),
        ]
        hop_grads = [[g[2 * d : 2 * d + 2] for d in range(pairs)] for g in wholes]
    else:
        results, backs, *rest = run_experts(
            received_rows, grad_received, row_gates, tall_blocks, down_blocks
        )
        hop_grads = [rest[i * pairs : (i + 1) * pairs] for i in range(3)]
    arrived = [[swap_pairs(g[d], "wt", 2 * d) for d in range(1, pairs)] for g in hop_grads]
    first_arrived, later_arrived = arrived[:1], arrived[1:]
    if chips > 4:
        routed_grad = scatter_rows(
            spread_rows(backs, slots, "spread_grads", False), 5, True, True, "scatter_grads"
        )
    else:
        routed_grad = scatter_rows(backs, 5, True, True, "scatter_grads", slots)
    routed_grad, first_arrived, results = lax.optimization_barrier(
        (routed_grad, first_arrived, results)
    )
    partial = lax.psum_scatter(
        spread_rows(results, slots, "spread_results", True).reshape(ctx_count, 2, tokens, width_model),
        "ctx",
        scatter_dimension=0,
        tiled=True,
    )[0]

    def crossed(own, more):
        total = own[1].astype(jnp.float32)
        for m in more:
            total = total + m[1].astype(jnp.float32)
        return swap_pairs(total.astype(jnp.bfloat16), "wt", 1)

    gate_other = crossed(hop_grads[0][0], first_arrived[0])
    grad_normed_two = grad_shared_rows + routed_grad
    grad_gain_two = jnp.sum(grad_normed_two * middle * scale_two, axis=0)
    scaled_two = grad_normed_two * gain_two_full
    grad_middle = (
        grad_out
        + scale_two * scaled_two
        - middle * scale_two**3 * jnp.mean(scaled_two * middle, axis=-1, keepdims=True)
    )
    grad_branch = grad_middle.astype(jnp.bfloat16)
    grad_out_weight = jnp.einsum(
        "tq,td->qd", attended, grad_branch, preferred_element_type=jnp.float32
    )
    grad_attended = jnp.einsum(
        "td,qd->tq", grad_branch, out_weight, preferred_element_type=jnp.float32
    ).astype(jnp.bfloat16)
    grad_queries, grad_parts = attend_back(
        place, queries, both, query_seg[None, :], seg_column, attended_full, grad_attended, logs
    )
    grad_parts, up_arrived = lax.optimization_barrier((grad_parts, later_arrived[0]))
    up_other = crossed(hop_grads[1][0], up_arrived)
    grad_both = scatter_rows(
        grad_parts.reshape(chips, 1, 2, tokens, 2 * kv_width),
        6,
        False,
        False,
        "scatter_keys",
    ).astype(jnp.bfloat16)
    grad_both, down_arrived, gate_other, up_other = lax.optimization_barrier(
        (grad_both, later_arrived[1], gate_other, up_other)
    )
    arrived = [first_arrived[0], up_arrived, down_arrived]
    down_other = crossed(hop_grads[2][0], down_arrived)
    grad_both = grad_both.reshape(tokens, KV_HEADS, 2, HEAD_DIM)
    grad_keys = grad_both[:, :, 0].reshape(tokens, kv_width)
    grad_values = grad_both[:, :, 1].reshape(tokens, kv_width)

    def weight_grad(grad):
        return jnp.einsum("tc,tq->cq", normed, grad, preferred_element_type=jnp.float32).astype(
            jnp.bfloat16
        )

    def input_grad(grad, weight):
        return jnp.einsum("tq,cq->tc", grad, weight, preferred_element_type=jnp.float32)

    grad_normed = (
        input_grad(grad_queries, query_weight)
        + input_grad(grad_keys, key_weight)
        + input_grad(grad_values, value_weight)
    )
    grad_gain_one = jnp.sum(grad_normed * inputs * scale_one, axis=0)
    scaled_one = grad_normed * gain_one_full
    grad_inputs = (
        grad_middle
        + scale_one * scaled_one
        - inputs * scale_one**3 * jnp.mean(scaled_one * inputs, axis=-1, keepdims=True)
    )

    gain_grads = jnp.stack([grad_gain_one, grad_gain_two]).reshape(2, wt_count, 1, depth)
    gain_grads = jnp.pad(gain_grads.astype(jnp.bfloat16), ((0, 0), (0, 0), (0, 15), (0, 0)))
    gain_grads = jnp.swapaxes(gain_grads, 0, 1).reshape(wt_count * 32, depth)
    dense_grads = [
        weight_grad(grad_queries),
        grad_shared_both,
        grad_out_weight.astype(jnp.bfloat16),
        grad_shared_down,
        weight_grad(grad_keys),
        weight_grad(grad_values),
        gain_grads,
    ]
    totals = reduce_dense(dense_grads)
    totals, down_other, partial = lax.optimization_barrier((totals, down_other, partial))
    others = [gate_other, up_other, down_other]
    kept, given = own_and_other(partial, side)
    crossing = swap_pairs(given, "wt", 1)
    routed = kept.astype(jnp.float32) + crossing.astype(jnp.float32)
    output = (middle + shared_result + routed).astype(jnp.bfloat16)
    sum_experts_gate, sum_experts_up, sum_experts_down = place_experts(
        side.astype(jnp.int32).reshape(1), [g[0] for g in hop_grads], arrived, others
    )
    final_query, final_shared, final_out, final_down, final_key, final_value, final_gains = [
        total.astype(jnp.float32) for total in totals
    ]
    final_gate, final_up = final_shared[:, :shared_width], final_shared[:, shared_width:]
    final_gain_one, final_gain_two = final_gains[0], final_gains[16]
    return (
        output[None],
        grad_inputs[None],
        final_gain_one,
        final_query,
        final_key,
        final_value,
        final_out,
        final_gain_two,
        final_gate,
        final_up,
        final_down,
        sum_experts_gate,
        sum_experts_up,
        sum_experts_down,
    )


def solution(mesh):
    placed = (
        P("wt", "ctx", None),
        P("wt", None),
        P("wt", "ctx", None),
        P("wt", "ctx", None),
        P("wt", "ctx", None),
        P("wt"),
        P("wt", None),
        P("wt", None),
        P("wt", None),
        P("wt", None),
        P("wt"),
        P("wt", None),
        P("wt", None),
        P("wt", None),
        P("ctx", "wt", None),
        P("ctx", "wt", None),
        P("ctx", None, "wt"),
    )
    return jax.shard_map(
        body,
        mesh=mesh,
        in_specs=placed,
        out_specs=(
            P("wt", "ctx", None),
            P("wt", "ctx", None),
            P("wt"),
            P("wt", None),
            P("wt", None),
            P("wt", None),
            P("wt", None),
            P("wt"),
            P("wt", None),
            P("wt", None),
            P("wt", None),
            P("ctx", "wt", None),
            P("ctx", "wt", None),
            P("ctx", None, "wt"),
        ),
        check_vma=False,
    )
```

```python
import functools
import math

import jax
import jax.numpy as jnp
from jax import lax
from jax.experimental import pallas as pl
from jax.experimental.pallas import tpu as pltpu
from jax.sharding import PartitionSpec as P

HEADS = 12
KV_HEADS = 4
HEAD_DIM = 128
EXPERTS = 64
TOPK = 6
CAP = 40


epsilon = 1e-05
masked_value = -1e30


def inverse_rms(rows):
    return lax.rsqrt(jnp.mean(rows * rows, axis=-1, keepdims=True) + epsilon)


def silu_slope(gate_part):
    sigmoid = jax.nn.sigmoid(gate_part)
    return sigmoid * (1.0 + gate_part * (1.0 - sigmoid))


MESH = pl.DeviceIdType.MESH
WIDE = 56 * 2**20
LONG = pl.CostEstimate(flops=0, bytes_accessed=2_000_000_000, transcendentals=0)
CHEAP = pl.CostEstimate(flops=0, bytes_accessed=4096, transcendentals=0)


def flip(index, distance):
    result = index
    bit = 1
    while bit <= distance:
        if distance // bit % 2:
            result = result + bit - 2 * bit * (index // bit % 2)
        bit *= 2
    return result


def remote(src, dst, send_sem, recv_sem, device):
    return pltpu.make_async_remote_copy(
        src_ref=src,
        dst_ref=dst,
        send_sem=send_sem,
        recv_sem=recv_sem,
        device_id=device,
        device_id_type=MESH,
    )


def greet(devices):
    barrier = pltpu.get_barrier_semaphore()
    for device in devices:
        pl.semaphore_signal(barrier, inc=1, device_id=device, device_id_type=MESH)
    pl.semaphore_wait(barrier, len(devices))


class Slabs:
    def __init__(self, count, sources, targets, here, there, send, recv, near_send, near_recv, *stages):
        self.c, self.w = lax.axis_index("ctx"), lax.axis_index("wt")
        self.core = lax.rem(self.c, 2)
        self.near = (flip(self.c, 1), self.w)
        self.count = count
        self.pairs = list(zip(sources, targets))
        self.here, self.there, self.send, self.recv = here, there, send, recv
        self.near_send, self.near_recv = near_send, near_recv
        self.stages = stages
        dims = [1 << i for i in range(count.bit_length() - 1)]
        self.orders = [dims, dims[::-1]]

    def devices(self):
        return [(self.c, flip(self.w, d)) for d in self.orders[0]]

    def rows(self, s, p, core):
        rows = self.pairs[s][0].shape[0] // 4
        return pl.ds(pl.multiple_of((core * 2 + p) * rows, 16), rows)

    def block(self, s, p, f, core):
        return self.pairs[s][1].at[flip(self.w, f), self.rows(s, p, core)]

    def push(self, s, p, stage, held):
        step = self.orders[p][stage]
        part = self.rows(s, p, self.core)
        source = self.pairs[s][0].at[part] if held == 0 else self.block(s, p, held, self.core)
        index = (s, p, (step ^ held) - 1)
        return remote(
            source,
            self.block(s, p, held, self.core),
            self.send.at[index],
            self.recv.at[index],
            (self.c, flip(self.w, step)),
        )

    def arrival(self, s, p, f):
        spot = self.block(s, p, f, self.core)
        return remote(spot, spot, self.send.at[s, p, f - 1], self.recv.at[s, p, f - 1], self.near)

    def hand(self, s, p, f, core):
        spot = self.block(s, p, f, core)
        return remote(spot, spot, self.near_send.at[s, p, f - 1], self.near_recv.at[s, p, f - 1], self.near)

    def load(self, s):
        return pltpu.make_async_copy(self.pairs[s][0], self.stages[s], self.here.at[s])

    def keep(self, s):
        return pltpu.make_async_copy(self.stages[s], self.pairs[s][1].at[self.w], self.there.at[s])

    def last_stage(self, p, f):
        return max(i for i, d in enumerate(self.orders[p]) if f & d)

    def every(self):
        return [(s, p) for s in range(len(self.pairs)) for p in range(2)]

    def start(self):
        for stage in range(len(self.orders[0])):
            for s, p in self.every():
                self.push(s, p, stage, 0).start()
        for s in range(len(self.pairs)):
            self.load(s).start()

    def relay(self):
        for s in range(len(self.pairs)):
            self.load(s).wait()
            self.keep(s).start()
        last = len(self.orders[0])
        for stage in range(last):
            for s, p in self.every():
                for f in range(1, self.count):
                    if self.last_stage(p, f) == stage:
                        self.arrival(s, p, f).wait_recv()
                        for onward in range(stage + 1, last):
                            self.push(s, p, onward, f).start()
                        self.hand(s, p, f, self.core).start()

    def finish(self):
        for s, p in self.every():
            for f in range(1, self.count):
                stage = self.last_stage(p, f)
                self.hand(s, p, f, 1 - self.core).wait_recv()
                self.hand(s, p, f, self.core).wait_send()
                self.push(s, p, stage, f ^ self.orders[p][stage]).wait_send()
        for s in range(len(self.pairs)):
            self.keep(s).wait()

    @staticmethod
    def scratch(slabs, count):
        dma = pltpu.SemaphoreType.DMA
        number = len(slabs)
        return (
            [dma((number,))] * 2
            + [dma((number, 2, count - 1))] * 4
            + [pltpu.VMEM(s.shape, s.dtype) for s in slabs]
        )

    @staticmethod
    def shapes(slabs, count):
        return tuple(jax.ShapeDtypeStruct((count,) + s.shape, s.dtype) for s in slabs)


def weights_kernel(count, slabs, swaps, *refs):
    refs = list(refs)

    def take(number):
        taken = refs[:number]
        del refs[:number]
        return taken

    sources, given = take(slabs), take(swaps)
    targets, paired, (zero_ref,) = take(slabs), take(swaps), take(1)
    stages = take(swaps)
    load_sem, keep_sem, swap_send, swap_recv = take(4)
    plan = Slabs(count, sources, targets, *refs)
    c, w = lax.axis_index("ctx"), lax.axis_index("wt")
    side = lax.rem(w, 2)
    partner = (c, flip(w, 1))
    greet(plan.devices() + [plan.near])

    def swap(i):
        return remote(given[i], paired[i].at[side], swap_send.at[i], swap_recv.at[i], partner)

    def load(i):
        return pltpu.make_async_copy(given[i], stages[i], load_sem.at[i])

    def keep(i):
        return pltpu.make_async_copy(stages[i], paired[i].at[side], keep_sem.at[i])

    plan.start()
    for i in range(swaps):
        swap(i).start()
        load(i).start()
    zero_ref[...] = jnp.zeros_like(zero_ref)
    for i in range(swaps):
        load(i).wait()
        keep(i).start()
    plan.relay()
    plan.finish()
    for i in range(swaps):
        keep(i).wait()
        swap(i).wait()


def gather_weights(slabs, swaps):
    count = lax.axis_size("wt")
    dma = pltpu.SemaphoreType.DMA((len(swaps),))
    pairs = tuple(jax.ShapeDtypeStruct((2,) + s.shape, s.dtype) for s in swaps)
    shapes = Slabs.shapes(slabs, count) + pairs
    return pl.pallas_call(
        functools.partial(weights_kernel, count, len(slabs), len(swaps)),
        out_shape=shapes + (jax.ShapeDtypeStruct((8, 128), jnp.int32),),
        in_specs=[pl.BlockSpec(memory_space=pl.ANY)] * (len(slabs) + len(swaps)),
        out_specs=(pl.BlockSpec(memory_space=pl.ANY),) * len(shapes)
        + (pl.BlockSpec(memory_space=pltpu.VMEM),),
        scratch_shapes=[pltpu.VMEM(s.shape, s.dtype) for s in swaps]
        + [dma] * 4
        + Slabs.scratch(slabs, count),
        compiler_params=pltpu.CompilerParams(
            collective_id=1, has_side_effects=True, vmem_limit_bytes=WIDE
        ),
        cost_estimate=LONG,
        name="gather_weights",
    )(*slabs, *swaps)


def gather_kernel(chips, downward, paired, count, slabs, passed, rows_ref, *refs):
    refs = list(refs)

    def take(number):
        taken = refs[:number]
        del refs[:number]
        return taken

    hops = count // 2 - 1
    sources, moved = take(slabs), take(passed)
    (out_ref,), targets, landed, (zero_ref,) = take(1), take(slabs), take(passed * hops), take(1)
    (stage,) = take(1)
    here, up_send, up_recv, down_send, down_recv, pair_send, pair_recv, near_send, near_recv = take(9)
    plan = Slabs(count, sources, targets, *take(6 + slabs)) if slabs else None
    pass_send, pass_recv = take(2) if passed else (None, None)
    zero_ref[...] = jnp.zeros_like(zero_ref)
    c, w = lax.axis_index("ctx"), lax.axis_index("wt")
    z = c // 2
    core = lax.rem(c, 2)
    side = lax.rem(w, 2) if paired else 0
    near, partner = (flip(c, 1), w), (c, flip(w, 1))
    above = (lax.rem(c + 2, 2 * chips), w)
    below = (lax.rem(c + 2 * chips - 2, 2 * chips), w)
    far = [(c, flip(w, 2 * d + 2)) for d in range(hops)]
    greet([near, above, below] + ([partner] if paired else []) + (plan.devices() if plan else []) + (far if passed else []))

    def onward(i, d):
        return remote(
            moved[i], landed[i * hops + d], pass_send.at[i, d], pass_recv.at[i, d], far[d]
        )

    def spot(chip, which, parity):
        return out_ref.at[chip, which, parity]

    def lift(chip, source):
        return remote(source, spot(chip, side, core), up_send.at[chip], up_recv.at[chip], above)

    def drop(chip, source):
        return remote(source, spot(chip, side, core), down_send.at[chip], down_recv.at[chip], below)

    def give(chip, source):
        return remote(source, spot(chip, side, core), pair_send.at[chip], pair_recv.at[chip], partner)

    def taken(chip):
        return remote(
            spot(chip, 1 - side, core), spot(chip, 1 - side, core), pair_send.at[chip], pair_recv.at[chip], partner
        )

    def hand(chip, which, source):
        return remote(source, spot(chip, which, core), near_send.at[chip, which], near_recv.at[chip, which], near)

    def handed(chip, which):
        there = spot(chip, which, 1 - core)
        return remote(there, there, near_send.at[chip, which], near_recv.at[chip, which], near)

    def settle_pair(chip):
        taken(chip).wait_recv()
        hand(chip, 1 - side, spot(chip, 1 - side, core)).start()

    load = pltpu.make_async_copy(rows_ref, stage, here.at[0])
    keep = pltpu.make_async_copy(stage, spot(z, side, core), here.at[1])
    load.start()
    pl.when(z < chips - 1)(lambda: lift(z, rows_ref).start())
    if downward:
        pl.when(z > 0)(lambda: drop(z, rows_ref).start())
    if paired:
        give(z, rows_ref).start()
    hand(z, side, rows_ref).start()
    if plan:
        plan.start()
    for d in range(hops):
        for i in range(passed):
            onward(i, d).start()
    load.wait()
    keep.start()
    for step in range(1, chips):
        low, high = z - step, z + step

        @pl.when(low >= 0)
        def _():
            lift(low, spot(low, side, core)).wait_recv()
            pl.when(z < chips - 1)(lambda: lift(low, spot(low, side, core)).start())
            if paired:
                give(low, spot(low, side, core)).start()
            hand(low, side, spot(low, side, core)).start()

        if downward:

            @pl.when(high < chips)
            def _():
                drop(high, spot(high, side, core)).wait_recv()
                pl.when(z > 0)(lambda: drop(high, spot(high, side, core)).start())
                if paired:
                    give(high, spot(high, side, core)).start()
                hand(high, side, spot(high, side, core)).start()

        if paired:
            if step == 1:
                settle_pair(z)
            else:
                pl.when(z - step + 1 >= 0)(lambda: settle_pair(z - step + 1))
                pl.when(z + step - 1 < chips)(lambda: settle_pair(z + step - 1))
    if paired:
        pl.when(z - chips + 1 >= 0)(lambda: settle_pair(z - chips + 1))
        pl.when(z + chips - 1 < chips)(lambda: settle_pair(z + chips - 1))
    keep.wait()
    if plan:
        plan.relay()
        plan.finish()

    def finish(chip):
        here_now = spot(chip, side, core)
        pl.when((z < chips - 1) & (chip <= z))(lambda: lift(chip, here_now).wait_send())
        if downward:
            pl.when((z > 0) & (chip >= z))(lambda: drop(chip, here_now).wait_send())
        if paired:
            give(chip, here_now).wait_send()
            for which in range(2):
                hand(chip, which, spot(chip, which, core)).wait_send()
                handed(chip, which).wait_recv()
        else:
            hand(chip, side, here_now).wait_send()
            handed(chip, side).wait_recv()

    for chip in range(chips):
        if downward:
            finish(chip)
        else:
            pl.when(chip <= z)(lambda: finish(chip))
    for d in range(hops):
        for i in range(passed):
            onward(i, d).wait()


def gather_rows(rows, collective_id, downward, paired, name, slabs=(), moved=()):
    chips = lax.axis_size("ctx") // 2
    count = lax.axis_size("wt")
    hops = count // 2 - 1
    line = pltpu.SemaphoreType.DMA((chips,))
    both = pltpu.SemaphoreType.DMA((chips, 2))
    shape = jax.ShapeDtypeStruct((chips, 2 if paired else 1, 2) + rows.shape, rows.dtype)
    landed = tuple(jax.ShapeDtypeStruct(m.shape, m.dtype) for m in moved for _ in range(hops))
    shapes = (shape,) + Slabs.shapes(slabs, count) + landed
    *results, zero = pl.pallas_call(
        functools.partial(gather_kernel, chips, downward, paired, count, len(slabs), len(moved)),
        out_shape=shapes + (jax.ShapeDtypeStruct((8, 128), jnp.int32),),
        in_specs=[pl.BlockSpec(memory_space=pl.ANY)] * (1 + len(slabs) + len(moved)),
        out_specs=(pl.BlockSpec(memory_space=pl.ANY),) * len(shapes)
        + (pl.BlockSpec(memory_space=pltpu.VMEM),),
        scratch_shapes=[pltpu.VMEM(rows.shape, rows.dtype), pltpu.SemaphoreType.DMA((2,))]
        + [line] * 6
        + [both] * 2
        + (Slabs.scratch(slabs, count) if slabs else [])
        + ([pltpu.SemaphoreType.DMA((len(moved), hops))] * 2 if moved else []),
        compiler_params=pltpu.CompilerParams(
            collective_id=collective_id, has_side_effects=True, vmem_limit_bytes=WIDE
        ),
        cost_estimate=LONG,
        name=name,
    )(rows, *slabs, *moved)
    return results + [zero[0, 0]]


def scatter_kernel(chips, upward, paired, pieces, fused, passed, *refs):
    refs = list(refs)

    def take(number):
        taken = refs[:number]
        del refs[:number]
        return taken

    if fused:
        rows_ref, slot_ref = take(2)
        partial_ref = None
    else:
        (partial_ref,) = take(1)
    moved = take(passed)
    (out_ref,) = take(1)
    landed = take(passed)
    (built,) = take(1) if fused else (None,)
    pass_send, pass_recv = take(2) if passed else (None, None)
    own, sib, mate, low_in, high_in, load, near_send, near_recv, *refs = refs
    pair_send, pair_recv, up_send, up_recv, down_send, down_recv = refs
    c, w = lax.axis_index("ctx"), lax.axis_index("wt")
    z = c // 2
    core = lax.rem(c, 2)
    side = lax.rem(w, 2) if paired else 0
    sides = 2 if paired else 1
    near, partner = (flip(c, 1), w), (c, flip(w, 1))
    above = (lax.rem(c + 2, 2 * chips), w)
    below = (lax.rem(c + 2 * chips - 2, 2 * chips), w)
    rows = own.shape[2] // pieces
    far = [(c, flip(w, 2 * d + 2)) for d in range(passed)]
    greet([near, above, below] + ([partner] if paired else []) + far)

    def onward(d):
        return remote(moved[d], landed[d], pass_send.at[d], pass_recv.at[d], far[d])

    order = []
    for i in range(chips // 2):
        order += [chips - 1 - i, i]
    if chips % 2:
        order.append(chips // 2)
    if not upward:
        order = list(range(chips))

    def wanted(chip, action):
        if upward:
            action()
        else:
            pl.when(chip <= z)(action)

    def fetch(chip, which):
        return pltpu.make_async_copy(
            partial_ref.at[chip, which, core], own.at[chip, which], load.at[chip, which]
        )

    def hand(chip, which):
        return remote(
            built.at[chip, which] if fused else partial_ref.at[chip, which, 1 - core],
            sib.at[chip, which],
            near_send.at[chip, which],
            near_recv.at[chip, which],
            near,
        )

    def cut(piece):
        return pl.ds(piece * rows, rows)

    def give(chip, piece):
        return remote(
            own.at[chip, 1 - side, cut(piece)],
            mate.at[chip, cut(piece)],
            pair_send.at[chip, piece],
            pair_recv.at[chip, piece],
            partner,
        )

    def lift(chip, piece):
        return remote(
            own.at[chip, side, cut(piece)],
            low_in.at[chip, cut(piece)],
            up_send.at[chip, piece],
            up_recv.at[chip, piece],
            above,
        )

    def drop(chip, piece):
        return remote(
            own.at[chip, side, cut(piece)],
            high_in.at[chip, cut(piece)],
            down_send.at[chip, piece],
            down_recv.at[chip, piece],
            below,
        )

    def add_into(chip, which, piece, other):
        spot = own.at[chip, which, cut(piece)]
        spot[...] = spot[...] + other[...]

    def spread(chip, which, parity, spot):
        local, depth, width = rows_ref.shape[2:]
        tokens = spot.shape[0]
        span = pl.ds(pl.multiple_of(parity * tokens, tokens), tokens)
        place = lax.broadcasted_iota(jnp.int32, (depth, tokens), 0)
        ones = jnp.concatenate(
            [
                (slot_ref[chip, which, e : e + 1, span] == place).astype(jnp.float32)
                for e in range(local)
            ],
            axis=0,
        ).astype(jnp.bfloat16)
        spot[...] = lax.dot_general(
            ones,
            rows_ref[chip, which].reshape(local * depth, width),
            (((0,), (0,)), ((), ())),
            preferred_element_type=jnp.float32,
        ).astype(jnp.bfloat16)

    def begin(chip):
        for which in range(sides):
            if fused:
                spread(chip, which, 1 - core, built.at[chip, which])
            hand(chip, which).start()
            if fused:
                spread(chip, which, core, own.at[chip, which])
            else:
                fetch(chip, which).start()

    if not fused:
        for chip in order:
            wanted(chip, lambda: begin(chip))
    else:
        begin(order[0])
    for d in range(passed):
        onward(d).start()

    def meet(chip):
        for which in range(sides):
            if not fused:
                fetch(chip, which).wait()
            hand(chip, which).wait_recv()
        for piece in range(pieces):
            if paired:
                add_into(chip, 1 - side, piece, sib.at[chip, 1 - side, cut(piece)])
                give(chip, piece).start()
            add_into(chip, side, piece, sib.at[chip, side, cut(piece)])

    def travel(chip):
        for piece in range(pieces):
            if paired:
                give(chip, piece).wait_recv()
                add_into(chip, side, piece, mate.at[chip, cut(piece)])
            if upward:

                @pl.when(z < chip)
                def _():
                    @pl.when(z > 0)
                    def _():
                        lift(chip, piece).wait_recv()
                        add_into(chip, side, piece, low_in.at[chip, cut(piece)])

                    lift(chip, piece).start()

            @pl.when(z > chip)
            def _():
                @pl.when(z < chips - 1)
                def _():
                    drop(chip, piece).wait_recv()
                    add_into(chip, side, piece, high_in.at[chip, cut(piece)])

                drop(chip, piece).start()

    for i, chip in enumerate(order):
        if fused and i + 1 < len(order):
            begin(order[i + 1])
        wanted(chip, lambda: meet(chip))
        if i >= 1:
            wanted(order[i - 1], lambda: travel(order[i - 1]))
    wanted(order[-1], lambda: travel(order[-1]))
    for piece in range(pieces):
        out_ref[cut(piece), :] = own.at[z, side, cut(piece)][...].astype(jnp.float32)
    for piece in range(pieces):
        if upward:

            @pl.when(z > 0)
            def _():
                lift(z, piece).wait_recv()
                out_ref[cut(piece), :] += low_in.at[z, cut(piece)][...].astype(jnp.float32)

        @pl.when(z < chips - 1)
        def _():
            drop(z, piece).wait_recv()
            out_ref[cut(piece), :] += high_in.at[z, cut(piece)][...].astype(jnp.float32)

    def finish(chip):
        for which in range(sides):
            hand(chip, which).wait_send()
        for piece in range(pieces):
            if paired:
                give(chip, piece).wait_send()
            if upward:
                pl.when(z < chip)(lambda: lift(chip, piece).wait_send())
            pl.when(z > chip)(lambda: drop(chip, piece).wait_send())

    for chip in order:
        wanted(chip, lambda: finish(chip))
    for d in range(passed):
        onward(d).wait()


def scatter_rows(partial, collective_id, upward, paired, name, slots=None, moved=()):
    fused = slots is not None
    dma = pltpu.SemaphoreType.DMA
    pieces = 2
    if fused:
        chips, sides, _, _, width = partial.shape
        tokens = slots.shape[3] // 2
    else:
        chips, sides, _, tokens, width = partial.shape
    block = (tokens, width)
    several = pltpu.VMEM((chips, sides) + block, jnp.bfloat16)
    return pl.pallas_call(
        functools.partial(scatter_kernel, chips, upward, paired, pieces, fused, len(moved)),
        out_shape=[jax.ShapeDtypeStruct(block, jnp.float32)]
        + [jax.ShapeDtypeStruct(m.shape, m.dtype) for m in moved],
        in_specs=(
            [pl.BlockSpec(memory_space=pltpu.VMEM)] * 2 if fused else [pl.BlockSpec(memory_space=pl.ANY)]
        )
        + [pl.BlockSpec(memory_space=pl.ANY)] * len(moved),
        out_specs=[pl.BlockSpec(memory_space=pltpu.VMEM)]
        + [pl.BlockSpec(memory_space=pl.ANY)] * len(moved),
        scratch_shapes=([several] if fused else [])
        + ([dma((len(moved),))] * 2 if moved else [])
        + [
            several,
            several,
            pltpu.VMEM((chips if paired else 1,) + block, jnp.bfloat16),
            pltpu.VMEM((chips if upward else 1,) + block, jnp.bfloat16),
            pltpu.VMEM((chips,) + block, jnp.bfloat16),
            dma((chips, 2)),
            dma((chips, 2)),
            dma((chips, 2)),
        ]
        + [dma((chips, pieces))] * 6,
        compiler_params=pltpu.CompilerParams(
            collective_id=collective_id, has_side_effects=True, vmem_limit_bytes=WIDE
        ),
        cost_estimate=LONG if paired else CHEAP,
        name=name,
    )(*((partial, slots) if fused else (partial,)), *moved)


def dense_kernel(chips, count, matrices, pieces, *refs):
    refs = list(refs)

    def take(number):
        taken = refs[:number]
        del refs[:number]
        return taken

    grads, outs = take(matrices), take(matrices)
    own, sib, mates, low, final = (take(matrices) for _ in range(5))
    (load, near_send, near_recv, send, recv, low_send, low_recv, back_send, back_recv, last_send, last_recv, keep) = refs
    c, w = lax.axis_index("ctx"), lax.axis_index("wt")
    z = c // 2
    core = lax.rem(c, 2)
    near = (flip(c, 1), w)
    above = (lax.rem(c + 2, 2 * chips), w)
    below = (lax.rem(c + 2 * chips - 2, 2 * chips), w)
    dims = [1 << i for i in range(count.bit_length() - 1)]
    greet([near, above, below] + [(c, flip(w, d)) for d in dims])

    def order(j):
        return dims if pieces[j][3] else dims[::-1]

    def sends(j, stage):
        step, rest = order(j)[stage], order(j)[stage + 1 :]
        offsets = [step]
        for r in rest:
            offsets += [o ^ r for o in offsets]
        return offsets

    def span(j, parity=None):
        m, first, rows, _ = pieces[j]
        if parity is None:
            return pl.ds(first, rows)
        half = grads[m].shape[1] // 2
        return pl.ds(pl.multiple_of(parity * half + first, 16), rows)

    def fetch(j):
        m = pieces[j][0]
        return pltpu.make_async_copy(grads[m].at[:, span(j, core)], own[m].at[:, span(j)], load.at[j])

    def hand(j):
        m = pieces[j][0]
        return remote(
            grads[m].at[:, span(j, 1 - core)], sib[m].at[:, span(j)], near_send.at[j], near_recv.at[j], near
        )

    def give(j, stage, o):
        m = pieces[j][0]
        step = order(j)[stage]
        return remote(
            own[m].at[flip(w, o), span(j)],
            mates[m].at[o - 1, span(j)],
            send.at[j, o - 1],
            recv.at[j, o - 1],
            (c, flip(w, step)),
        )

    def total(j):
        return own[pieces[j][0]].at[w, span(j)]

    def add(spot, other):
        spot[...] = spot[...] + other[...]

    def start(j):
        hand(j).start()
        fetch(j).start()

    def share(j):
        m = pieces[j][0]
        fetch(j).wait()
        hand(j).wait_recv()
        for o in sends(j, 0):
            add(own[m].at[flip(w, o), span(j)], sib[m].at[flip(w, o), span(j)])
            give(j, 0, o).start()
        for o in range(count):
            if o not in sends(j, 0):
                add(own[m].at[flip(w, o), span(j)], sib[m].at[flip(w, o), span(j)])

    def collect(j, stage):
        m = pieces[j][0]
        step = order(j)[stage]
        for o in sends(j, stage):
            give(j, stage, o).wait_recv()
        last = stage + 1 == len(dims)
        onward_blocks = [] if last else sends(j, stage + 1)
        for o in sends(j, stage):
            kept = o ^ step
            if kept in onward_blocks:
                add(own[m].at[flip(w, kept), span(j)], mates[m].at[o - 1, span(j)])
                give(j, stage + 1, kept).start()
        for o in sends(j, stage):
            kept = o ^ step
            if kept not in onward_blocks:
                add(own[m].at[flip(w, kept), span(j)], mates[m].at[o - 1, span(j)])

    def line(j):
        return (z, above, below) if j % 2 == 0 else (chips - 1 - z, below, above)

    def onward(j):
        m = pieces[j][0]
        return remote(total(j), low[m].at[span(j)], low_send.at[j], low_recv.at[j], line(j)[1])

    def backward(j):
        spot = final[pieces[j][0]].at[span(j)]
        return remote(spot, spot, back_send.at[j], back_recv.at[j], line(j)[2])

    def across(j, parity):
        m = pieces[j][0]
        return remote(
            final[m].at[span(j)], outs[m].at[span(j, parity)], last_send.at[j], last_recv.at[j], near
        )

    def store(j):
        m = pieces[j][0]
        return pltpu.make_async_copy(final[m].at[span(j)], outs[m].at[span(j, core)], keep.at[j])

    def accumulate(j):
        place = line(j)[0]
        m = pieces[j][0]

        @pl.when(place > 0)
        def _():
            onward(j).wait_recv()
            add(total(j), low[m].at[span(j)])

        @pl.when(place < chips - 1)
        def _():
            onward(j).start()

        @pl.when(place == chips - 1)
        def _():
            final[m][span(j), :] = total(j)[...]
            backward(j).start()
            across(j, core).start()
            store(j).start()

    def spread(j):
        place = line(j)[0]

        @pl.when(place < chips - 1)
        def _():
            backward(j).wait_recv()
            pl.when(place > 0)(lambda: backward(j).start())
            across(j, core).start()
            store(j).start()

    number = len(pieces)
    for j in range(number):
        start(j)
    last = chips - 1
    lead, gap = 2, 1
    behind = lead + gap * (len(dims) - 1)
    for t in range(number + 2 * last + behind):
        if t < number:
            share(t)
        for stage in range(len(dims)):
            if 0 <= t - lead - gap * stage < number:
                collect(t - lead - gap * stage, stage)
        for hop in range(2 * last, -1, -1):
            j = t - hop - behind
            if not 0 <= j < number:
                continue
            if hop <= last:
                pl.when(line(j)[0] == hop)(lambda: accumulate(j))
            if hop > last:
                pl.when(line(j)[0] == 2 * last - hop)(lambda: spread(j))
    for j in range(number):
        place = line(j)[0]
        hand(j).wait_send()
        for stage in range(len(dims)):
            for o in sends(j, stage):
                give(j, stage, o).wait_send()
        pl.when(place < chips - 1)(lambda: onward(j).wait_send())
        pl.when(place > 0)(lambda: backward(j).wait_send())
        across(j, core).wait_send()
        across(j, 1 - core).wait_recv()
        store(j).wait()


def reduce_dense(grads):
    count = lax.axis_size("wt")
    chips = lax.axis_size("ctx") // 2
    shapes = [(g.shape[0] // count, g.shape[1]) for g in grads]
    pieces = []
    for m, (rows, _) in enumerate(shapes):
        half, width = rows // 2, shapes[m][1]
        cuts = max(n for n in range(1, 9) if half % (16 * n) == 0 and (n == 1 or half * width > 60000 * (n - 1)))
        for i in range(cuts):
            pieces.append((m, i * (rows // 2 // cuts), rows // 2 // cuts, len(pieces) % 2))
    halves = [(rows // 2, width) for rows, width in shapes]
    dma = pltpu.SemaphoreType.DMA
    one, many = dma((len(pieces),)), dma((len(pieces), count - 1))
    return pl.pallas_call(
        functools.partial(dense_kernel, chips, count, len(grads), tuple(pieces)),
        out_shape=[jax.ShapeDtypeStruct(s, jnp.bfloat16) for s in shapes],
        in_specs=[pl.BlockSpec(memory_space=pl.ANY)] * len(grads),
        out_specs=[pl.BlockSpec(memory_space=pl.ANY)] * len(grads),
        scratch_shapes=[pltpu.VMEM((count,) + h, jnp.bfloat16) for h in halves]
        + [pltpu.VMEM((count,) + h, jnp.bfloat16) for h in halves]
        + [pltpu.VMEM((count - 1,) + h, jnp.bfloat16) for h in halves]
        + [pltpu.VMEM(h, jnp.bfloat16) for h in halves]
        + [pltpu.VMEM(h, jnp.bfloat16) for h in halves]
        + [one, one, one, many, many, one, one, one, one, one, one, one],
        compiler_params=pltpu.CompilerParams(
            collective_id=7, has_side_effects=True, vmem_limit_bytes=WIDE
        ),
        cost_estimate=LONG,
        name="reduce_dense",
    )(*[g.reshape((count,) + s) for g, s in zip(grads, shapes)])


def dot_of(a, b, left, right):
    return lax.dot_general(
        a, b, (((left,), (right,)), ((), ())), preferred_element_type=jnp.float32
    )


def stacked_heads(ref):
    return jnp.concatenate(
        [ref[:, h * HEAD_DIM : (h + 1) * HEAD_DIM] for h in range(ref.shape[1] // HEAD_DIM)], axis=0
    )


exponent_scale = HEAD_DIM ** (-0.5) * math.log2(math.e)


def attend_kernel(place_ref, query_ref, both_ref, row_ref, column_ref, out_ref, log_ref, best, total, accum):
    tokens = query_ref.shape[0]
    group = query_ref.shape[1] // HEAD_DIM
    width = 2 * tokens
    place = place_ref[0]
    queries = stacked_heads(query_ref)
    best[...] = jnp.full_like(best, masked_value)
    total[...] = jnp.zeros_like(total)
    accum[...] = jnp.zeros_like(accum)
    query_pos = place * tokens + lax.broadcasted_iota(jnp.int32, (tokens, width), 0)
    key_pos = lax.broadcasted_iota(jnp.int32, (tokens, width), 1)

    def step(j, carry):
        span = pl.ds(pl.multiple_of(j * width, width), width)
        allowed = (key_pos + j * width <= query_pos) & (row_ref[0:1, span] == column_ref[:, 0:1])
        bias = jnp.where(allowed, 0.0, masked_value)
        scores = dot_of(queries, both_ref[span, :HEAD_DIM], 1, 1)
        scores = (scores.reshape(group, tokens, width) + bias[None]).reshape(group * tokens, width)
        newest = jnp.maximum(best[...], jnp.max(scores, axis=1, keepdims=True))
        factor = jnp.exp2((best[...] - newest) * exponent_scale)
        weights = jnp.exp2((scores - newest[:, :1]) * exponent_scale)
        total[...] = total[...] * factor + jnp.sum(weights, axis=1, keepdims=True)
        accum[...] = accum[...] * factor + dot_of(
            weights.astype(jnp.bfloat16), both_ref[span, HEAD_DIM:], 1, 0
        )
        best[...] = newest
        return carry

    lax.fori_loop(0, place // 2 + 1, step, 0)
    heads = accum[...] / total[...]
    for h in range(group):
        out_ref[:, h * HEAD_DIM : (h + 1) * HEAD_DIM] = heads[h * tokens : (h + 1) * tokens]
    logs = best[...] * exponent_scale + jnp.log2(total[...])
    log_ref[0] = jnp.transpose(logs)[:8]


def attend(place, projected, both, seg_row, seg_column):
    tokens = projected.shape[0]
    group = HEADS // KV_HEADS
    rows, span = group * tokens, both.shape[0]
    stat = pltpu.VMEM((rows, HEAD_DIM), jnp.float32)
    return pl.pallas_call(
        attend_kernel,
        grid=(KV_HEADS,),
        out_shape=(
            jax.ShapeDtypeStruct((tokens, HEADS * HEAD_DIM), jnp.float32),
            jax.ShapeDtypeStruct((KV_HEADS, 8, rows), jnp.float32),
        ),
        in_specs=[
            pl.BlockSpec(memory_space=pltpu.SMEM),
            pl.BlockSpec((tokens, group * HEAD_DIM), lambda g: (0, g)),
            pl.BlockSpec((span, 2 * HEAD_DIM), lambda g: (0, g)),
            pl.BlockSpec((1, span), lambda g: (0, 0)),
            pl.BlockSpec((tokens, 1), lambda g: (0, 0)),
        ],
        out_specs=(
            pl.BlockSpec((tokens, group * HEAD_DIM), lambda g: (0, g)),
            pl.BlockSpec((1, 8, rows), lambda g: (g, 0, 0)),
        ),
        scratch_shapes=[stat, stat, stat],
        compiler_params=pltpu.CompilerParams(vmem_limit_bytes=WIDE),
        cost_estimate=CHEAP,
        name="attend",
    )(place, projected, both, seg_row, seg_column)


def attend_back_kernel(place_ref, query_ref, both_ref, row_ref, column_ref, heads_ref, grad_ref, log_ref, grad_query_ref, grad_both_ref, accum):
    tokens = query_ref.shape[0]
    group = query_ref.shape[1] // HEAD_DIM
    width = 2 * tokens
    rows = group * tokens
    scale = HEAD_DIM ** (-0.5)
    place = place_ref[0]
    queries, grads = stacked_heads(query_ref), stacked_heads(grad_ref)
    product = grads.astype(jnp.float32) * stacked_heads(heads_ref)
    delta = jnp.sum(product, axis=1, keepdims=True)
    delta = jnp.transpose(jnp.broadcast_to(delta, (rows, HEAD_DIM)))[0:1]
    logs = log_ref[0, 0:1, :]
    accum[...] = jnp.zeros_like(accum)
    grad_both_ref[...] = jnp.zeros_like(grad_both_ref)
    query_pos = place * tokens + lax.broadcasted_iota(jnp.int32, (width, tokens), 1)
    key_pos = lax.broadcasted_iota(jnp.int32, (width, tokens), 0)

    def step(j, carry):
        span = pl.ds(pl.multiple_of(j * width, width), width)
        allowed = (key_pos + j * width <= query_pos) & (column_ref[span, 0:1] == row_ref[0:1, :])
        bias = jnp.where(allowed, 0.0, masked_value)
        bias = jnp.concatenate([bias] * group, axis=1)
        keys, values = both_ref[span, :HEAD_DIM], both_ref[span, HEAD_DIM:]
        scores = dot_of(keys, queries, 1, 1)
        probs = jnp.exp2(scores * exponent_scale + bias - logs)
        grad_probs = dot_of(values, grads, 1, 1)
        grad_scores = (probs * (grad_probs - delta)).astype(jnp.bfloat16)
        accum[...] += dot_of(grad_scores, keys, 0, 0)
        grad_both_ref[span, :HEAD_DIM] = (dot_of(grad_scores, queries, 1, 0) * scale).astype(jnp.bfloat16)
        grad_both_ref[span, HEAD_DIM:] = dot_of(probs.astype(jnp.bfloat16), grads, 1, 0).astype(jnp.bfloat16)
        return carry

    lax.fori_loop(0, place // 2 + 1, step, 0)
    grad_queries = (accum[...] * scale).astype(jnp.bfloat16)
    for h in range(group):
        grad_query_ref[:, h * HEAD_DIM : (h + 1) * HEAD_DIM] = grad_queries[h * tokens : (h + 1) * tokens]


def attend_back(place, projected, both, query_seg_row, seg_column, heads_out, grad_attended, logs):
    tokens = projected.shape[0]
    group = HEADS // KV_HEADS
    rows, span = group * tokens, both.shape[0]
    per_group = pl.BlockSpec((tokens, group * HEAD_DIM), lambda g: (0, g))
    return pl.pallas_call(
        attend_back_kernel,
        grid=(KV_HEADS,),
        out_shape=(
            jax.ShapeDtypeStruct((tokens, HEADS * HEAD_DIM), jnp.bfloat16),
            jax.ShapeDtypeStruct(both.shape, jnp.bfloat16),
        ),
        in_specs=[
            pl.BlockSpec(memory_space=pltpu.SMEM),
            per_group,
            pl.BlockSpec((span, 2 * HEAD_DIM), lambda g: (0, g)),
            pl.BlockSpec((1, tokens), lambda g: (0, 0)),
            pl.BlockSpec((span, 1), lambda g: (0, 0)),
            per_group,
            per_group,
            pl.BlockSpec((1, 8, rows), lambda g: (g, 0, 0)),
        ],
        out_specs=(per_group, pl.BlockSpec((span, 2 * HEAD_DIM), lambda g: (0, g))),
        scratch_shapes=[pltpu.VMEM((rows, HEAD_DIM), jnp.float32)],
        compiler_params=pltpu.CompilerParams(vmem_limit_bytes=WIDE),
        cost_estimate=CHEAP,
        name="attend_back",
    )(place, projected, both, query_seg_row, seg_column, heads_out, grad_attended, logs)


def pick_rows_of(slot_rows, rows_of, local, depth, tokens):
    place = lax.broadcasted_iota(jnp.int32, (depth, tokens), 0)
    total, masks = None, []
    for core in range(2):
        chosen = [slot_rows[core][e : e + 1] == place for e in range(local)]
        ones = jnp.concatenate([c.astype(jnp.float32) for c in chosen], axis=0).astype(jnp.bfloat16)
        term = jnp.dot(ones, rows_of(core), preferred_element_type=jnp.float32)
        total = term if total is None else total + term
        masks.append(chosen)
    return total, masks


def pick_grads_kernel(local, first_ref, earlier_ref, rows_ref, out_ref, scale_ref, slot_ref):
    depth = out_ref.shape[3]
    tokens = slot_ref.shape[3] // 2
    slot_rows, gate_rows, count = [], [], None
    for core in range(2):
        table = rows_ref[0, core, 0, tokens : tokens + 16, :].astype(jnp.float32)
        member, gate = [], []
        for e in range(local):
            expert = (first_ref[0] + e).astype(jnp.float32)
            found, weight = None, None
            for k in range(TOPK):
                span = slice(k * tokens, (k + 1) * tokens)
                named = table[0:1, span] == expert
                value = jnp.where(named, table[1:2, span] + table[2:3, span] + table[3:4, span], 0.0)
                mark = jnp.where(named, 1.0, 0.0)
                found = mark if k == 0 else found + mark
                weight = value if k == 0 else weight + value
            member.append(found)
            gate.append(weight)
        member = jnp.concatenate(member + [jnp.zeros((8 - local, tokens), jnp.float32)], axis=0)
        rank = jnp.dot(member.astype(jnp.bfloat16), earlier_ref[...], preferred_element_type=jnp.float32)
        if core:
            rank = rank + count
        count = jnp.sum(member, axis=1, keepdims=True)
        slots = jnp.where(member > 0.5, rank.astype(jnp.int32), -1)[:local]
        slot_ref[0, 0, :, core * tokens : (core + 1) * tokens] = slots
        slot_rows.append(slots)
        gate_rows.append(gate)
    total, masks = pick_rows_of(
        slot_rows, lambda core: rows_ref[0, core, 0, :tokens, :], local, depth, tokens
    )
    weight = None
    for core in range(2):
        gates = jnp.concatenate(
            [
                jnp.sum(jnp.where(masks[core][e], gate_rows[core][e], 0.0), axis=1, keepdims=True)
                for e in range(local)
            ],
            axis=0,
        )
        weight = gates if core == 0 else weight + gates
    scale_ref[0, 0] = jnp.broadcast_to(weight, (local * depth, 128)).reshape(local, depth, 128)
    out_ref[0, 0] = (total * weight).astype(jnp.bfloat16).reshape(local, depth, total.shape[1])


def pick_grads(rows, first, local, tokens):
    chips, _, sides, long, width = rows.shape
    depth = 2 * CAP
    earlier = jnp.arange(tokens)[:, None] < jnp.arange(tokens)[None, :]
    return pl.pallas_call(
        functools.partial(pick_grads_kernel, local),
        grid=(chips, sides),
        out_shape=(
            jax.ShapeDtypeStruct((chips, sides, local, depth, width), jnp.bfloat16),
            jax.ShapeDtypeStruct((chips, sides, local, depth, 128), jnp.float32),
            jax.ShapeDtypeStruct((chips, sides, local, 2 * tokens), jnp.int32),
        ),
        in_specs=[
            pl.BlockSpec(memory_space=pltpu.SMEM),
            pl.BlockSpec((tokens, tokens), lambda z, s: (0, 0)),
            pl.BlockSpec((1, 2, 1, long, width), lambda z, s: (z, 0, s, 0, 0)),
        ],
        out_specs=(
            pl.BlockSpec((1, 1, local, depth, width), lambda z, s: (z, s, 0, 0, 0)),
            pl.BlockSpec((1, 1, local, depth, 128), lambda z, s: (z, s, 0, 0, 0)),
            pl.BlockSpec((1, 1, local, 2 * tokens), lambda z, s: (z, s, 0, 0)),
        ),
        compiler_params=pltpu.CompilerParams(vmem_limit_bytes=WIDE),
        cost_estimate=CHEAP,
        name="pick_grads",
    )(first, earlier.astype(jnp.bfloat16), rows)


def pick_tokens_kernel(slot_ref, rows_ref, out_ref):
    local, depth = out_ref.shape[2], out_ref.shape[3]
    tokens = rows_ref.shape[3]
    slot_rows = [slot_ref[0, 0, :, core * tokens : (core + 1) * tokens] for core in range(2)]
    total, _ = pick_rows_of(slot_rows, lambda core: rows_ref[0, 0, core], local, depth, tokens)
    out_ref[0, 0] = total.astype(jnp.bfloat16).reshape(local, depth, total.shape[1])


def pick_tokens(rows, slots):
    chips, sides, local, both = slots.shape
    tokens, width = rows.shape[3:]
    depth = 2 * CAP
    return pl.pallas_call(
        pick_tokens_kernel,
        grid=(chips, sides),
        out_shape=jax.ShapeDtypeStruct((chips, sides, local, depth, width), jnp.bfloat16),
        in_specs=[
            pl.BlockSpec((1, 1, local, both), lambda z, s: (z, s, 0, 0)),
            pl.BlockSpec((1, 1, 2, tokens, width), lambda z, s: (z, s, 0, 0, 0)),
        ],
        out_specs=pl.BlockSpec((1, 1, local, depth, width), lambda z, s: (z, s, 0, 0, 0)),
        compiler_params=pltpu.CompilerParams(vmem_limit_bytes=WIDE),
        cost_estimate=CHEAP,
        name="pick_tokens",
    )(slots, rows)


def spread_kernel(apart, slot_ref, rows_ref, out_ref):
    local, depth, width = rows_ref.shape[2:]
    tokens = out_ref.shape[3]
    place = lax.broadcasted_iota(jnp.int32, (depth, tokens), 0)
    rows = rows_ref[0, 0].reshape(local * depth, width)
    for core in range(2):
        span = slice(core * tokens, (core + 1) * tokens)
        ones = jnp.concatenate(
            [(slot_ref[0, 0, e : e + 1, span] == place).astype(jnp.float32) for e in range(local)], axis=0
        ).astype(jnp.bfloat16)
        spot = out_ref.at[0, core, 0] if apart else out_ref.at[0, 0, core]
        spot[...] = lax.dot_general(
            ones, rows, (((0,), (0,)), ((), ())), preferred_element_type=jnp.float32
        ).astype(jnp.bfloat16)


def spread_rows(rows, slots, name, apart):
    chips, sides, local, both = slots.shape
    depth, width = rows.shape[3:]
    tokens = both // 2
    return pl.pallas_call(
        functools.partial(spread_kernel, apart),
        grid=(chips, sides),
        out_shape=jax.ShapeDtypeStruct(
            (chips, 2, sides, tokens, width) if apart else (chips, sides, 2, tokens, width), jnp.bfloat16
        ),
        in_specs=[
            pl.BlockSpec((1, 1, local, both), lambda z, s: (z, s, 0, 0)),
            pl.BlockSpec((1, 1, local, depth, width), lambda z, s: (z, s, 0, 0, 0)),
        ],
        out_specs=pl.BlockSpec((1, 2, 1, tokens, width), lambda z, s: (z, 0, s, 0, 0))
        if apart
        else pl.BlockSpec((1, 1, 2, tokens, width), lambda z, s: (z, s, 0, 0, 0)),
        compiler_params=pltpu.CompilerParams(vmem_limit_bytes=WIDE),
        cost_estimate=CHEAP,
        name=name,
    )(slots, rows)


def expert_kernel(blocks, x_ref, g_ref, scale_ref, *refs):
    tall_refs, down_refs = refs[:blocks], refs[blocks : 2 * blocks]
    result_ref, back_ref, *grad_refs = refs[2 * blocks : -3]
    tall_all, flat_all, flat_grad = refs[-3:]
    hops = len(grad_refs) // 3
    grad_gate_refs, grad_up_refs = grad_refs[:hops], grad_refs[hops : 2 * hops]
    grad_down_refs = grad_refs[2 * hops :]
    w = lax.axis_index("wt")
    chips, sides, _, depth, width = x_ref.shape
    rows = chips * sides * depth
    part = tall_refs[0].shape[2]
    nn, nt, tn = (((1,), (0,)), ((), ())), (((1,), (1,)), ((), ())), (((0,), (0,)), ((), ()))

    def dot(a, b, dims):
        return lax.dot_general(a, b, dims, preferred_element_type=jnp.float32)

    def columns(ref, q):
        if blocks == 1:
            return ref.at[:, :, 0]
        span = pl.ds(pl.multiple_of(flip(w, q) * part, 128), part)
        return ref.at[:, :, 0, :, span]

    def piece(ref, q):
        return columns(ref, q)[...].reshape(rows, part)

    def offset(q):
        return 0 if blocks == 1 else pl.multiple_of(flip(w, q) * part, 128)

    inner_width = tall_refs[0].shape[3]
    for q in range(blocks):
        span = pl.ds(offset(q), part)
        tall_all[span, :inner_width] = tall_refs[q][0, 0]
        tall_all[span, inner_width:] = tall_refs[q][0, 1]
        flat_all[:, span] = down_refs[q][0]
    x = x_ref[...].reshape(rows, width)
    g = g_ref[...].reshape(rows, width)
    gate = dot(x, tall_all[:, :inner_width], nn)
    up = dot(x, tall_all[:, inner_width:], nn)
    grad_inner = dot(g, flat_all[...], nt)
    sigmoid = jax.nn.sigmoid(gate)
    activated = gate * sigmoid
    inner = (activated * up).astype(jnp.bfloat16)
    grad_gate = (grad_inner * up * (sigmoid * (1.0 + gate * (1.0 - sigmoid)))).astype(jnp.bfloat16)
    grad_up = (grad_inner * activated).astype(jnp.bfloat16)
    grad_both = jnp.concatenate([grad_gate, grad_up], axis=1)
    scale = scale_ref[...].reshape(rows, 128)[:, :1]
    chunk = 512
    for first in range(0, width, chunk):
        span = slice(first, first + chunk)
        result = dot(inner, flat_all[:, span], nn) * scale
        result_ref[:, :, 0, :, span] = result.astype(jnp.bfloat16).reshape(chips, sides, depth, chunk)
        back = dot(grad_both, tall_all[span, :], nt)
        back_ref[:, :, 0, :, span] = back.astype(jnp.bfloat16).reshape(chips, sides, depth, chunk)
        flat_grad[:, span] = dot(inner, g[:, span], tn).astype(jnp.bfloat16)
    for q in range(blocks):
        more = dot(piece(x_ref, q), grad_both, tn).astype(jnp.bfloat16)
        grad_gate_refs[q // 2][q % 2, 0] = more[:, :inner_width]
        grad_up_refs[q // 2][q % 2, 0] = more[:, inner_width:]
        grad_down_refs[q // 2][q % 2, 0] = flat_grad[:, pl.ds(offset(q), part)]


def run_experts(x, g, scale, talls, downs):
    chips, sides, local, depth, width = x.shape
    blocks = len(talls)
    part, inner = talls[0].shape[2:]
    large = chips * sides * depth > 1024
    rows = pl.BlockSpec((chips, sides, 1, depth, width), lambda e: (0, 0, e, 0, 0))
    sources = pl.BlockSpec(
        (chips, sides, 1, depth, width),
        lambda e: (0, 0, e, 0, 0),
        pipeline_mode=pl.Buffered(1 if large else 2),
    )
    scales = pl.BlockSpec((chips, sides, 1, depth, 128), lambda e: (0, 0, e, 0, 0))
    tall = pl.BlockSpec((1, 2, part, inner), lambda e: (e, 0, 0, 0))
    flat = pl.BlockSpec((1, inner, part), lambda e: (e, 0, 0))
    hops, each = max(blocks // 2, 1), min(blocks, 2)
    tall_out = pl.BlockSpec((each, 1, part, inner), lambda e: (0, e, 0, 0))
    flat_out = pl.BlockSpec((each, 1, inner, part), lambda e: (0, e, 0, 0))
    return pl.pallas_call(
        functools.partial(expert_kernel, blocks),
        grid=(local,),
        out_shape=(
            jax.ShapeDtypeStruct(x.shape, jnp.bfloat16),
            jax.ShapeDtypeStruct(x.shape, jnp.bfloat16),
            *[jax.ShapeDtypeStruct((each, local, part, inner), jnp.bfloat16)] * (2 * hops),
            *[jax.ShapeDtypeStruct((each, local, inner, part), jnp.bfloat16)] * hops,
        ),
        in_specs=[sources, sources, scales] + [tall] * blocks + [flat] * blocks,
        out_specs=(rows, rows) + (tall_out,) * (2 * hops) + (flat_out,) * hops,
        scratch_shapes=[
            pltpu.VMEM((width, 2 * inner), jnp.bfloat16),
            pltpu.VMEM((inner, width), jnp.bfloat16),
            pltpu.VMEM((inner, width), jnp.bfloat16),
        ],
        compiler_params=pltpu.CompilerParams(vmem_limit_bytes=60 * 2**20),
        cost_estimate=CHEAP,
        name="experts",
    )(x, g, scale, *talls, *downs)


def place_kernel(arrivals, side_ref, *refs):
    own, other, more, outs = refs[:3], refs[3:6], refs[6 : 6 + 3 * arrivals], refs[6 + 3 * arrivals :]
    mine = pl.program_id(0) == side_ref[0]

    @pl.when(mine)
    def _():
        for i in range(3):
            value = own[i][0, 0].astype(jnp.float32)
            for m in more[i * arrivals : (i + 1) * arrivals]:
                value = value + m[0, 0].astype(jnp.float32)
            outs[i][0] = value

    @pl.when(jnp.logical_not(mine))
    def _():
        for i in range(3):
            outs[i][0] = other[i][0].astype(jnp.float32)


def place_experts(side, own, more, other):
    local = other[0].shape[0]
    arrivals = len(more[0])
    shapes = [o.shape[1:] for o in other]
    paired = [pl.BlockSpec((1, 1) + s, lambda h, e: (0, e, 0, 0)) for s in shapes]
    single = [pl.BlockSpec((1,) + s, lambda h, e: (e, 0, 0)) for s in shapes]
    return pl.pallas_call(
        functools.partial(place_kernel, arrivals),
        grid=(2, local),
        out_shape=[jax.ShapeDtypeStruct((2 * local,) + s, jnp.float32) for s in shapes],
        in_specs=[pl.BlockSpec(memory_space=pltpu.SMEM)]
        + paired
        + single
        + [p for p in paired for _ in range(arrivals)],
        out_specs=[pl.BlockSpec((1,) + s, lambda h, e: (h * local + e, 0, 0)) for s in shapes],
        compiler_params=pltpu.CompilerParams(vmem_limit_bytes=WIDE),
        cost_estimate=CHEAP,
        name="place_experts",
    )(side, *own, *other, *[m for group in more for m in group])


def swap_pairs(value, axis, distance):
    count = lax.axis_size(axis)
    return lax.ppermute(value, axis, [(i, i ^ distance) for i in range(count)])


def own_and_other(stacked, mine):
    return (
        lax.dynamic_index_in_dim(stacked, mine, 0, keepdims=False),
        lax.dynamic_index_in_dim(stacked, 1 - mine, 0, keepdims=False),
    )


def collect_expert(shard, side, pairs):
    local = shard.shape[0]
    kept, given = own_and_other(shard.reshape((2, local // 2) + shard.shape[1:]), side)
    return kept, swap_pairs(given, "wt", 1), [swap_pairs(kept, "wt", 2 * d) for d in range(1, pairs)]


def settle_blocks(blocks, index, axis):
    stacked = jnp.stack(blocks)
    return jnp.concatenate(
        [
            lax.dynamic_index_in_dim(stacked, jnp.bitwise_xor(j, index), 0, False)
            for j in range(len(blocks))
        ],
        axis=axis,
    )


def split_blocks(whole, index, count, axis):
    parts = jnp.stack(jnp.split(whole, count, axis=axis))
    return jnp.stack(
        [
            lax.dynamic_index_in_dim(parts, jnp.bitwise_xor(q, index), 0, False)
            for q in range(count)
        ]
    )


def body(
    hidden,
    segment_ids,
    routes,
    gates,
    cotangent,
    norm_one_gain,
    w_query,
    w_key,
    w_value,
    w_out,
    norm_two_gain,
    shared_gate,
    shared_up,
    shared_down,
    expert_gate,
    expert_up,
    expert_down,
):
    wt_index = lax.axis_index("wt")
    wt_count = lax.axis_size("wt")
    ctx_count = lax.axis_size("ctx")
    chips = ctx_count // 2
    pairs = wt_count // 2
    tokens, width_model = hidden.shape[1:]
    wide, kv_width = w_query.shape[1], w_key.shape[1]
    shared_width = shared_gate.shape[1]
    gates_here = gates[0]
    gate_high = gates_here.astype(jnp.bfloat16)
    gate_rest = gates_here - gate_high.astype(jnp.float32)
    gate_middle = gate_rest.astype(jnp.bfloat16)
    gate_low = (gate_rest - gate_middle.astype(jnp.float32)).astype(jnp.bfloat16)
    table = jnp.concatenate(
        [routes[0].astype(jnp.bfloat16), gate_high, gate_middle, gate_low], axis=1
    )
    grad_rows = cotangent[0]
    depth = norm_one_gain.shape[0]
    extra_rows = 16
    packed = jnp.pad(
        jnp.swapaxes(table, 0, 1).reshape(4, width_model), ((0, extra_rows - 4), (0, 0))
    )
    extended = jnp.concatenate([grad_rows, packed], axis=0)
    gain_pair = jnp.concatenate(
        [norm_one_gain[None], norm_two_gain[None], jnp.zeros((62, depth), jnp.bfloat16)]
    )
    query_weight, key_weight, value_weight, gains, grad_pair, zero = gather_weights(
        (w_query, w_key, w_value, gain_pair), (extended,)
    )
    query_weight = query_weight.reshape(-1, wide)
    key_weight = key_weight.reshape(-1, kv_width)
    value_weight = value_weight.reshape(-1, kv_width)
    zero = zero[0, 0]
    side = lax.rem(wt_index, 2)
    later = side + zero
    collected = [
        collect_expert(jnp.stack([expert_gate, expert_up], axis=1), later, pairs),
        collect_expert(expert_down, later, pairs),
    ]
    gain_one, gain_two = gains[:, 0].reshape(-1), gains[:, 1].reshape(-1)
    local = expert_gate.shape[0] // 2
    first_expert = (lax.axis_index("ctx") * 2 + side) * local

    inputs = hidden[0].astype(jnp.float32)
    offset = lax.axis_index("ctx") * tokens
    seg_all = segment_ids[0]
    query_seg = lax.dynamic_slice_in_dim(seg_all, offset, tokens)
    scale_one = inverse_rms(inputs)
    gain_one_full = gain_one.astype(jnp.float32)
    normed = (inputs * scale_one * gain_one_full).astype(jnp.bfloat16)

    def project(weight):
        return jnp.dot(normed, weight, preferred_element_type=jnp.float32).astype(jnp.bfloat16)

    queries = project(query_weight)
    fresh = jnp.stack(
        [
            project(key_weight).reshape(tokens, KV_HEADS, HEAD_DIM),
            project(value_weight).reshape(tokens, KV_HEADS, HEAD_DIM),
        ],
        axis=2,
    ).reshape(tokens, 2 * kv_width)
    both, out_weight, both_weight, down_weight, zero = gather_rows(
        fresh,
        2,
        False,
        False,
        "gather_keys",
        (w_out, jnp.concatenate([shared_gate, shared_up], axis=1), shared_down),
    )
    out_weight = out_weight.reshape(-1, out_weight.shape[2])
    both_weight = both_weight.reshape(-1, both_weight.shape[2])
    down_weight = down_weight.reshape(-1, down_weight.shape[2])
    both = both.reshape(-1, 2 * kv_width)

    grad_pair, both = lax.optimization_barrier((grad_pair, both))
    all_grads = lax.all_gather(grad_pair, "ctx", axis=0).reshape(
        chips, 2, 2, tokens + extra_rows, width_model
    )

    place = lax.axis_index("ctx").astype(jnp.int32).reshape(1)
    seg_row, seg_column = seg_all[None, :], seg_all[:, None]
    attended_full, logs = attend(place, queries, both, seg_row, query_seg[:, None])
    attended = attended_full.astype(jnp.bfloat16)
    middle = inputs + jnp.dot(attended, out_weight, preferred_element_type=jnp.float32)
    scale_two = inverse_rms(middle)
    gain_two_full = gain_two.astype(jnp.float32)
    normed_two = (middle * scale_two * gain_two_full).astype(jnp.bfloat16)

    shared_parts = jnp.dot(normed_two, both_weight, preferred_element_type=jnp.float32)
    shared_gate_part, shared_up_part = shared_parts[:, :shared_width], shared_parts[:, shared_width:]
    shared_inner = (jax.nn.silu(shared_gate_part) * shared_up_part).astype(jnp.bfloat16)
    shared_result = jnp.dot(shared_inner, down_weight, preferred_element_type=jnp.float32)
    grad_out = grad_rows.astype(jnp.float32)
    grad_shared_down = jnp.einsum(
        "tf,td->fd", shared_inner, grad_rows, preferred_element_type=jnp.float32
    )
    grad_shared_inner = jnp.einsum(
        "td,fd->tf", grad_rows, down_weight, preferred_element_type=jnp.float32
    )
    grad_shared_gate_part = (
        grad_shared_inner * shared_up_part * silu_slope(shared_gate_part)
    ).astype(jnp.bfloat16)
    grad_shared_up_part = (grad_shared_inner * jax.nn.silu(shared_gate_part)).astype(jnp.bfloat16)
    grad_shared_parts = jnp.concatenate([grad_shared_gate_part, grad_shared_up_part], axis=1)
    grad_shared_both = jnp.einsum(
        "td,tf->df", normed_two, grad_shared_parts, preferred_element_type=jnp.float32
    )
    grad_shared_rows = jnp.einsum(
        "tf,df->td", grad_shared_parts, both_weight, preferred_element_type=jnp.float32
    )
    grad_shared_both = grad_shared_both.astype(jnp.bfloat16)
    grad_shared_down = grad_shared_down.astype(jnp.bfloat16)
    normed_two, collected, shared_result, grad_shared_both, grad_shared_down, grad_shared_rows = (
        lax.optimization_barrier(
            (normed_two, collected, shared_result, grad_shared_both, grad_shared_down, grad_shared_rows)
        )
    )
    all_rows, *landed, zero = gather_rows(
        normed_two, 3, True, True, "gather_tokens", (), [c[1] for c in collected]
    )

    def blocks_of(i):
        kept, paired, straight = collected[i]
        blocks = [kept, paired]
        for d in range(pairs - 1):
            blocks += [straight[d], landed[i * (pairs - 1) + d]]
        return blocks

    tall_blocks, down_blocks = blocks_of(0), blocks_of(1)
    grad_received, row_gates, slots = pick_grads(
        all_grads, first_expert.astype(jnp.int32).reshape(1), local, tokens
    )
    received_rows = pick_tokens(all_rows, slots)
    if down_blocks[0].shape[2] % 128:
        results, backs, grads_gate, grads_up, grads_down = run_experts(
            received_rows,
            grad_received,
            row_gates,
            [settle_blocks(tall_blocks, wt_index, 2)],
            [settle_blocks(down_blocks, wt_index, 2)],
        )
        wholes = [
            split_blocks(grads_gate[0], wt_index, wt_count, 1),
            split_blocks(grads_up[0], wt_index, wt_count, 1),
            split_blocks(grads_down[0], wt_index, wt_count, 2),
        ]
        hop_grads = [[g[2 * d : 2 * d + 2] for d in range(pairs)] for g in wholes]
    else:
        results, backs, *rest = run_experts(
            received_rows, grad_received, row_gates, tall_blocks, down_blocks
        )
        hop_grads = [rest[i * pairs : (i + 1) * pairs] for i in range(3)]
    later_arrived = [[swap_pairs(g[d], "wt", 2 * d) for d in range(1, pairs)] for g in hop_grads[1:]]
    if chips > 4:
        routed_grad, *gate_arrived = scatter_rows(
            spread_rows(backs, slots, "spread_grads", False),
            5,
            True,
            True,
            "scatter_grads",
            moved=hop_grads[0][1:],
        )
    else:
        routed_grad, *gate_arrived = scatter_rows(
            backs, 5, True, True, "scatter_grads", slots, hop_grads[0][1:]
        )
    routed_grad, results = lax.optimization_barrier((routed_grad, results))
    partial = lax.psum_scatter(
        spread_rows(results, slots, "spread_results", True).reshape(ctx_count, 2, tokens, width_model),
        "ctx",
        scatter_dimension=0,
        tiled=True,
    )[0]

    def crossed(own, more):
        total = own[1].astype(jnp.float32)
        for m in more:
            total = total + m[1].astype(jnp.float32)
        return swap_pairs(total.astype(jnp.bfloat16), "wt", 1)

    gate_other = crossed(hop_grads[0][0], gate_arrived)
    grad_normed_two = grad_shared_rows + routed_grad
    grad_gain_two = jnp.sum(grad_normed_two * middle * scale_two, axis=0)
    scaled_two = grad_normed_two * gain_two_full
    grad_middle = (
        grad_out
        + scale_two * scaled_two
        - middle * scale_two**3 * jnp.mean(scaled_two * middle, axis=-1, keepdims=True)
    )
    grad_branch = grad_middle.astype(jnp.bfloat16)
    grad_out_weight = jnp.einsum(
        "tq,td->qd", attended, grad_branch, preferred_element_type=jnp.float32
    )
    grad_attended = jnp.einsum(
        "td,qd->tq", grad_branch, out_weight, preferred_element_type=jnp.float32
    ).astype(jnp.bfloat16)
    grad_queries, grad_parts = attend_back(
        place, queries, both, query_seg[None, :], seg_column, attended_full, grad_attended, logs
    )
    (grad_both,) = scatter_rows(
        grad_parts.reshape(chips, 1, 2, tokens, 2 * kv_width),
        6,
        False,
        False,
        "scatter_keys",
    )
    grad_both = grad_both.astype(jnp.bfloat16)
    grad_both, gate_other, up_arrived = lax.optimization_barrier(
        (grad_both, gate_other, later_arrived[0])
    )
    up_other = crossed(hop_grads[1][0], up_arrived)
    grad_both = grad_both.reshape(tokens, KV_HEADS, 2, HEAD_DIM)
    grad_keys = grad_both[:, :, 0].reshape(tokens, kv_width)
    grad_values = grad_both[:, :, 1].reshape(tokens, kv_width)

    def weight_grad(grad):
        return jnp.einsum("tc,tq->cq", normed, grad, preferred_element_type=jnp.float32).astype(
            jnp.bfloat16
        )

    def input_grad(grad, weight):
        return jnp.einsum("tq,cq->tc", grad, weight, preferred_element_type=jnp.float32)

    grad_normed = (
        input_grad(grad_queries, query_weight)
        + input_grad(grad_keys, key_weight)
        + input_grad(grad_values, value_weight)
    )
    grad_gain_one = jnp.sum(grad_normed * inputs * scale_one, axis=0)
    scaled_one = grad_normed * gain_one_full
    grad_inputs = (
        grad_middle
        + scale_one * scaled_one
        - inputs * scale_one**3 * jnp.mean(scaled_one * inputs, axis=-1, keepdims=True)
    )

    gain_grads = jnp.stack([grad_gain_one, grad_gain_two]).reshape(2, wt_count, 1, depth)
    gain_grads = jnp.pad(gain_grads.astype(jnp.bfloat16), ((0, 0), (0, 0), (0, 15), (0, 0)))
    gain_grads = jnp.swapaxes(gain_grads, 0, 1).reshape(wt_count * 32, depth)
    dense_grads = [
        weight_grad(grad_queries),
        grad_shared_both,
        grad_out_weight.astype(jnp.bfloat16),
        grad_shared_down,
        weight_grad(grad_keys),
        weight_grad(grad_values),
        gain_grads,
    ]
    dense_grads, down_arrived = lax.optimization_barrier((dense_grads, later_arrived[1]))
    arrived = [gate_arrived, up_arrived, down_arrived]
    down_other = crossed(hop_grads[2][0], down_arrived)
    totals = reduce_dense(dense_grads)
    totals, up_other, down_other, partial = lax.optimization_barrier(
        (totals, up_other, down_other, partial)
    )
    others = [gate_other, up_other, down_other]
    kept, given = own_and_other(partial, side)
    crossing = swap_pairs(given, "wt", 1)
    routed = kept.astype(jnp.float32) + crossing.astype(jnp.float32)
    output = (middle + shared_result + routed).astype(jnp.bfloat16)
    sum_experts_gate, sum_experts_up, sum_experts_down = place_experts(
        side.astype(jnp.int32).reshape(1), [g[0] for g in hop_grads], arrived, others
    )
    final_query, final_shared, final_out, final_down, final_key, final_value, final_gains = [
        total.astype(jnp.float32) for total in totals
    ]
    final_gate, final_up = final_shared[:, :shared_width], final_shared[:, shared_width:]
    final_gain_one, final_gain_two = final_gains[0], final_gains[16]
    return (
        output[None],
        grad_inputs[None],
        final_gain_one,
        final_query,
        final_key,
        final_value,
        final_out,
        final_gain_two,
        final_gate,
        final_up,
        final_down,
        sum_experts_gate,
        sum_experts_up,
        sum_experts_down,
    )


def solution(mesh):
    placed = (
        P("wt", "ctx", None),
        P("wt", None),
        P("wt", "ctx", None),
        P("wt", "ctx", None),
        P("wt", "ctx", None),
        P("wt"),
        P("wt", None),
        P("wt", None),
        P("wt", None),
        P("wt", None),
        P("wt"),
        P("wt", None),
        P("wt", None),
        P("wt", None),
        P("ctx", "wt", None),
        P("ctx", "wt", None),
        P("ctx", None, "wt"),
    )
    return jax.shard_map(
        body,
        mesh=mesh,
        in_specs=placed,
        out_specs=(
            P("wt", "ctx", None),
            P("wt", "ctx", None),
            P("wt"),
            P("wt", None),
            P("wt", None),
            P("wt", None),
            P("wt", None),
            P("wt"),
            P("wt", None),
            P("wt", None),
            P("wt", None),
            P("ctx", "wt", None),
            P("ctx", "wt", None),
            P("ctx", None, "wt"),
        ),
        check_vma=False,
    )
```

```python
import functools
import math

import jax
import jax.numpy as jnp
from jax import lax
from jax.experimental import pallas as pl
from jax.experimental.pallas import tpu as pltpu
from jax.sharding import PartitionSpec as P

HEADS = 12
KV_HEADS = 4
HEAD_DIM = 128
EXPERTS = 64
TOPK = 6
CAP = 40


epsilon = 1e-05
masked_value = -1e30


def inverse_rms(rows):
    return lax.rsqrt(jnp.mean(rows * rows, axis=-1, keepdims=True) + epsilon)


def silu_slope(gate_part):
    sigmoid = jax.nn.sigmoid(gate_part)
    return sigmoid * (1.0 + gate_part * (1.0 - sigmoid))


MESH = pl.DeviceIdType.MESH
WIDE = 56 * 2**20
LONG = pl.CostEstimate(flops=0, bytes_accessed=2_000_000_000, transcendentals=0)
CHEAP = pl.CostEstimate(flops=0, bytes_accessed=4096, transcendentals=0)


def flip(index, distance):
    result = index
    bit = 1
    while bit <= distance:
        if distance // bit % 2:
            result = result + bit - 2 * bit * (index // bit % 2)
        bit *= 2
    return result


def remote(src, dst, send_sem, recv_sem, device):
    return pltpu.make_async_remote_copy(
        src_ref=src,
        dst_ref=dst,
        send_sem=send_sem,
        recv_sem=recv_sem,
        device_id=device,
        device_id_type=MESH,
    )


def greet(devices):
    barrier = pltpu.get_barrier_semaphore()
    for device in devices:
        pl.semaphore_signal(barrier, inc=1, device_id=device, device_id_type=MESH)
    pl.semaphore_wait(barrier, len(devices))


class Slabs:
    def __init__(self, count, sources, targets, here, there, send, recv, near_send, near_recv, *stages):
        self.c, self.w = lax.axis_index("ctx"), lax.axis_index("wt")
        self.core = lax.rem(self.c, 2)
        self.near = (flip(self.c, 1), self.w)
        self.count = count
        self.pairs = list(zip(sources, targets))
        self.here, self.there, self.send, self.recv = here, there, send, recv
        self.near_send, self.near_recv = near_send, near_recv
        self.stages = stages
        dims = [1 << i for i in range(count.bit_length() - 1)]
        self.orders = [dims, dims[::-1]]

    def devices(self):
        return [(self.c, flip(self.w, d)) for d in self.orders[0]]

    def rows(self, s, p, core):
        rows = self.pairs[s][0].shape[0] // 4
        return pl.ds(pl.multiple_of((core * 2 + p) * rows, 16), rows)

    def block(self, s, p, f, core):
        return self.pairs[s][1].at[flip(self.w, f), self.rows(s, p, core)]

    def push(self, s, p, stage, held):
        step = self.orders[p][stage]
        part = self.rows(s, p, self.core)
        source = self.pairs[s][0].at[part] if held == 0 else self.block(s, p, held, self.core)
        index = (s, p, (step ^ held) - 1)
        return remote(
            source,
            self.block(s, p, held, self.core),
            self.send.at[index],
            self.recv.at[index],
            (self.c, flip(self.w, step)),
        )

    def arrival(self, s, p, f):
        spot = self.block(s, p, f, self.core)
        return remote(spot, spot, self.send.at[s, p, f - 1], self.recv.at[s, p, f - 1], self.near)

    def hand(self, s, p, f, core):
        spot = self.block(s, p, f, core)
        return remote(spot, spot, self.near_send.at[s, p, f - 1], self.near_recv.at[s, p, f - 1], self.near)

    def load(self, s):
        return pltpu.make_async_copy(self.pairs[s][0], self.stages[s], self.here.at[s])

    def keep(self, s):
        return pltpu.make_async_copy(self.stages[s], self.pairs[s][1].at[self.w], self.there.at[s])

    def last_stage(self, p, f):
        return max(i for i, d in enumerate(self.orders[p]) if f & d)

    def every(self):
        return [(s, p) for s in range(len(self.pairs)) for p in range(2)]

    def start(self):
        for stage in range(len(self.orders[0])):
            for s, p in self.every():
                self.push(s, p, stage, 0).start()
        for s in range(len(self.pairs)):
            self.load(s).start()

    def relay(self):
        for s in range(len(self.pairs)):
            self.load(s).wait()
            self.keep(s).start()
        last = len(self.orders[0])
        for stage in range(last):
            for s, p in self.every():
                for f in range(1, self.count):
                    if self.last_stage(p, f) == stage:
                        self.arrival(s, p, f).wait_recv()
                        for onward in range(stage + 1, last):
                            self.push(s, p, onward, f).start()
                        self.hand(s, p, f, self.core).start()

    def finish(self):
        for s, p in self.every():
            for f in range(1, self.count):
                stage = self.last_stage(p, f)
                self.hand(s, p, f, 1 - self.core).wait_recv()
                self.hand(s, p, f, self.core).wait_send()
                self.push(s, p, stage, f ^ self.orders[p][stage]).wait_send()
        for s in range(len(self.pairs)):
            self.keep(s).wait()

    @staticmethod
    def scratch(slabs, count):
        dma = pltpu.SemaphoreType.DMA
        number = len(slabs)
        return (
            [dma((number,))] * 2
            + [dma((number, 2, count - 1))] * 4
            + [pltpu.VMEM(s.shape, s.dtype) for s in slabs]
        )

    @staticmethod
    def shapes(slabs, count):
        return tuple(jax.ShapeDtypeStruct((count,) + s.shape, s.dtype) for s in slabs)


def weights_kernel(count, slabs, swaps, *refs):
    refs = list(refs)

    def take(number):
        taken = refs[:number]
        del refs[:number]
        return taken

    sources, given = take(slabs), take(swaps)
    targets, paired, (zero_ref,) = take(slabs), take(swaps), take(1)
    stages = take(swaps)
    load_sem, keep_sem, swap_send, swap_recv = take(4)
    plan = Slabs(count, sources, targets, *refs)
    c, w = lax.axis_index("ctx"), lax.axis_index("wt")
    side = lax.rem(w, 2)
    partner = (c, flip(w, 1))
    greet(plan.devices() + [plan.near])

    def swap(i):
        return remote(given[i], paired[i].at[side], swap_send.at[i], swap_recv.at[i], partner)

    def load(i):
        return pltpu.make_async_copy(given[i], stages[i], load_sem.at[i])

    def keep(i):
        return pltpu.make_async_copy(stages[i], paired[i].at[side], keep_sem.at[i])

    plan.start()
    for i in range(swaps):
        swap(i).start()
        load(i).start()
    zero_ref[...] = jnp.zeros_like(zero_ref)
    for i in range(swaps):
        load(i).wait()
        keep(i).start()
    plan.relay()
    plan.finish()
    for i in range(swaps):
        keep(i).wait()
        swap(i).wait()


def gather_weights(slabs, swaps):
    count = lax.axis_size("wt")
    dma = pltpu.SemaphoreType.DMA((len(swaps),))
    pairs = tuple(jax.ShapeDtypeStruct((2,) + s.shape, s.dtype) for s in swaps)
    shapes = Slabs.shapes(slabs, count) + pairs
    return pl.pallas_call(
        functools.partial(weights_kernel, count, len(slabs), len(swaps)),
        out_shape=shapes + (jax.ShapeDtypeStruct((8, 128), jnp.int32),),
        in_specs=[pl.BlockSpec(memory_space=pl.ANY)] * (len(slabs) + len(swaps)),
        out_specs=(pl.BlockSpec(memory_space=pl.ANY),) * len(shapes)
        + (pl.BlockSpec(memory_space=pltpu.VMEM),),
        scratch_shapes=[pltpu.VMEM(s.shape, s.dtype) for s in swaps]
        + [dma] * 4
        + Slabs.scratch(slabs, count),
        compiler_params=pltpu.CompilerParams(
            collective_id=1, has_side_effects=True, vmem_limit_bytes=WIDE
        ),
        cost_estimate=LONG,
        name="gather_weights",
    )(*slabs, *swaps)


def gather_kernel(chips, downward, paired, count, slabs, passed, rows_ref, *refs):
    refs = list(refs)

    def take(number):
        taken = refs[:number]
        del refs[:number]
        return taken

    hops = count // 2 - 1
    sources, moved = take(slabs), take(passed)
    (out_ref,), targets, landed, (zero_ref,) = take(1), take(slabs), take(passed * hops), take(1)
    (stage,) = take(1)
    here, up_send, up_recv, down_send, down_recv, pair_send, pair_recv, near_send, near_recv = take(9)
    plan = Slabs(count, sources, targets, *take(6 + slabs)) if slabs else None
    pass_send, pass_recv = take(2) if passed else (None, None)
    zero_ref[...] = jnp.zeros_like(zero_ref)
    c, w = lax.axis_index("ctx"), lax.axis_index("wt")
    z = c // 2
    core = lax.rem(c, 2)
    side = lax.rem(w, 2) if paired else 0
    near, partner = (flip(c, 1), w), (c, flip(w, 1))
    above = (lax.rem(c + 2, 2 * chips), w)
    below = (lax.rem(c + 2 * chips - 2, 2 * chips), w)
    far = [(c, flip(w, 2 * d + 2)) for d in range(hops)]
    greet([near, above, below] + ([partner] if paired else []) + (plan.devices() if plan else []) + (far if passed else []))

    def onward(i, d):
        return remote(
            moved[i], landed[i * hops + d], pass_send.at[i, d], pass_recv.at[i, d], far[d]
        )

    def spot(chip, which, parity):
        return out_ref.at[chip, which, parity]

    def lift(chip, source):
        return remote(source, spot(chip, side, core), up_send.at[chip], up_recv.at[chip], above)

    def drop(chip, source):
        return remote(source, spot(chip, side, core), down_send.at[chip], down_recv.at[chip], below)

    def give(chip, source):
        return remote(source, spot(chip, side, core), pair_send.at[chip], pair_recv.at[chip], partner)

    def taken(chip):
        return remote(
            spot(chip, 1 - side, core), spot(chip, 1 - side, core), pair_send.at[chip], pair_recv.at[chip], partner
        )

    def hand(chip, which, source):
        return remote(source, spot(chip, which, core), near_send.at[chip, which], near_recv.at[chip, which], near)

    def handed(chip, which):
        there = spot(chip, which, 1 - core)
        return remote(there, there, near_send.at[chip, which], near_recv.at[chip, which], near)

    def settle_pair(chip):
        taken(chip).wait_recv()
        hand(chip, 1 - side, spot(chip, 1 - side, core)).start()

    load = pltpu.make_async_copy(rows_ref, stage, here.at[0])
    keep = pltpu.make_async_copy(stage, spot(z, side, core), here.at[1])
    load.start()
    pl.when(z < chips - 1)(lambda: lift(z, rows_ref).start())
    if downward:
        pl.when(z > 0)(lambda: drop(z, rows_ref).start())
    if paired:
        give(z, rows_ref).start()
    hand(z, side, rows_ref).start()
    if plan:
        plan.start()
    for d in range(hops):
        for i in range(passed):
            onward(i, d).start()
    load.wait()
    keep.start()
    for step in range(1, chips):
        low, high = z - step, z + step

        @pl.when(low >= 0)
        def _():
            lift(low, spot(low, side, core)).wait_recv()
            pl.when(z < chips - 1)(lambda: lift(low, spot(low, side, core)).start())
            if paired:
                give(low, spot(low, side, core)).start()
            hand(low, side, spot(low, side, core)).start()

        if downward:

            @pl.when(high < chips)
            def _():
                drop(high, spot(high, side, core)).wait_recv()
                pl.when(z > 0)(lambda: drop(high, spot(high, side, core)).start())
                if paired:
                    give(high, spot(high, side, core)).start()
                hand(high, side, spot(high, side, core)).start()

        if paired:
            if step == 1:
                settle_pair(z)
            else:
                pl.when(z - step + 1 >= 0)(lambda: settle_pair(z - step + 1))
                pl.when(z + step - 1 < chips)(lambda: settle_pair(z + step - 1))
    if paired:
        pl.when(z - chips + 1 >= 0)(lambda: settle_pair(z - chips + 1))
        pl.when(z + chips - 1 < chips)(lambda: settle_pair(z + chips - 1))
    keep.wait()
    if plan:
        plan.relay()
        plan.finish()

    def finish(chip):
        here_now = spot(chip, side, core)
        pl.when((z < chips - 1) & (chip <= z))(lambda: lift(chip, here_now).wait_send())
        if downward:
            pl.when((z > 0) & (chip >= z))(lambda: drop(chip, here_now).wait_send())
        if paired:
            give(chip, here_now).wait_send()
            for which in range(2):
                hand(chip, which, spot(chip, which, core)).wait_send()
                handed(chip, which).wait_recv()
        else:
            hand(chip, side, here_now).wait_send()
            handed(chip, side).wait_recv()

    for chip in range(chips):
        if downward:
            finish(chip)
        else:
            pl.when(chip <= z)(lambda: finish(chip))
    for d in range(hops):
        for i in range(passed):
            onward(i, d).wait()


def gather_rows(rows, collective_id, downward, paired, name, slabs=(), moved=()):
    chips = lax.axis_size("ctx") // 2
    count = lax.axis_size("wt")
    hops = count // 2 - 1
    line = pltpu.SemaphoreType.DMA((chips,))
    both = pltpu.SemaphoreType.DMA((chips, 2))
    shape = jax.ShapeDtypeStruct((chips, 2 if paired else 1, 2) + rows.shape, rows.dtype)
    landed = tuple(jax.ShapeDtypeStruct(m.shape, m.dtype) for m in moved for _ in range(hops))
    shapes = (shape,) + Slabs.shapes(slabs, count) + landed
    *results, zero = pl.pallas_call(
        functools.partial(gather_kernel, chips, downward, paired, count, len(slabs), len(moved)),
        out_shape=shapes + (jax.ShapeDtypeStruct((8, 128), jnp.int32),),
        in_specs=[pl.BlockSpec(memory_space=pl.ANY)] * (1 + len(slabs) + len(moved)),
        out_specs=(pl.BlockSpec(memory_space=pl.ANY),) * len(shapes)
        + (pl.BlockSpec(memory_space=pltpu.VMEM),),
        scratch_shapes=[pltpu.VMEM(rows.shape, rows.dtype), pltpu.SemaphoreType.DMA((2,))]
        + [line] * 6
        + [both] * 2
        + (Slabs.scratch(slabs, count) if slabs else [])
        + ([pltpu.SemaphoreType.DMA((len(moved), hops))] * 2 if moved else []),
        compiler_params=pltpu.CompilerParams(
            collective_id=collective_id, has_side_effects=True, vmem_limit_bytes=WIDE
        ),
        cost_estimate=LONG,
        name=name,
    )(rows, *slabs, *moved)
    return results + [zero[0, 0]]


def scatter_kernel(chips, upward, paired, pieces, fused, passed, extra, *refs):
    refs = list(refs)

    def take(number):
        taken = refs[:number]
        del refs[:number]
        return taken

    if fused:
        rows_ref, slot_ref = take(2)
        partial_ref = None
    else:
        (partial_ref,) = take(1)
    moved = take(passed)
    (extra_ref,) = take(1) if extra else (None,)
    (out_ref,) = take(1)
    landed = take(passed)
    (spread_ref, extra_stage, extra_sem) = take(1) + [None, None] if extra else (None, None, None)
    (built,) = take(1) if fused else (None,)
    if extra:
        extra_stage, extra_sem = take(2)
    pass_send, pass_recv = take(2) if passed else (None, None)
    own, sib, mate, low_in, high_in, load, near_send, near_recv, *refs = refs
    pair_send, pair_recv, up_send, up_recv, down_send, down_recv = refs
    c, w = lax.axis_index("ctx"), lax.axis_index("wt")
    z = c // 2
    core = lax.rem(c, 2)
    side = lax.rem(w, 2) if paired else 0
    sides = 2 if paired else 1
    near, partner = (flip(c, 1), w), (c, flip(w, 1))
    above = (lax.rem(c + 2, 2 * chips), w)
    below = (lax.rem(c + 2 * chips - 2, 2 * chips), w)
    rows = own.shape[2] // pieces
    far = [(c, flip(w, 2 * d + 2)) for d in range(passed)]
    greet([near, above, below] + ([partner] if paired else []) + far)

    def onward(d):
        return remote(moved[d], landed[d], pass_send.at[d], pass_recv.at[d], far[d])

    order = []
    for i in range(chips // 2):
        order += [chips - 1 - i, i]
    if chips % 2:
        order.append(chips // 2)
    if not upward:
        order = list(range(chips))

    def wanted(chip, action):
        if upward:
            action()
        else:
            pl.when(chip <= z)(action)

    def fetch(chip, which):
        return pltpu.make_async_copy(
            partial_ref.at[chip, which, core], own.at[chip, which], load.at[chip, which]
        )

    def hand(chip, which):
        return remote(
            built.at[chip, which] if fused else partial_ref.at[chip, which, 1 - core],
            sib.at[chip, which],
            near_send.at[chip, which],
            near_recv.at[chip, which],
            near,
        )

    def cut(piece):
        return pl.ds(piece * rows, rows)

    def give(chip, piece):
        return remote(
            own.at[chip, 1 - side, cut(piece)],
            mate.at[chip, cut(piece)],
            pair_send.at[chip, piece],
            pair_recv.at[chip, piece],
            partner,
        )

    def lift(chip, piece):
        return remote(
            own.at[chip, side, cut(piece)],
            low_in.at[chip, cut(piece)],
            up_send.at[chip, piece],
            up_recv.at[chip, piece],
            above,
        )

    def drop(chip, piece):
        return remote(
            own.at[chip, side, cut(piece)],
            high_in.at[chip, cut(piece)],
            down_send.at[chip, piece],
            down_recv.at[chip, piece],
            below,
        )

    def add_into(chip, which, piece, other):
        spot = own.at[chip, which, cut(piece)]
        spot[...] = spot[...] + other[...]

    def spread(chip, which, parity, spot, source=None):
        source = rows_ref if source is None else source
        local, depth, width = source.shape[2:]
        tokens = spot.shape[0]
        span = pl.ds(pl.multiple_of(parity * tokens, tokens), tokens)
        place = lax.broadcasted_iota(jnp.int32, (depth, tokens), 0)
        ones = jnp.concatenate(
            [
                (slot_ref[chip, which, e : e + 1, span] == place).astype(jnp.float32)
                for e in range(local)
            ],
            axis=0,
        ).astype(jnp.bfloat16)
        spot[...] = lax.dot_general(
            ones,
            source[chip, which].reshape(local * depth, width),
            (((0,), (0,)), ((), ())),
            preferred_element_type=jnp.float32,
        ).astype(jnp.bfloat16)

    def aside(chip, which, parity):
        slot = which * 2 + parity
        return pltpu.make_async_copy(
            extra_stage.at[slot], spread_ref.at[chip, parity, which], extra_sem.at[slot]
        )

    def put_aside(i, chip):
        for which in range(sides):
            for parity in range(2):
                if i > 0:
                    aside(order[i - 1], which, parity).wait()
                spread(chip, which, parity, extra_stage.at[which * 2 + parity], extra_ref)
                aside(chip, which, parity).start()

    def begin(chip):
        for which in range(sides):
            if fused:
                spread(chip, which, 1 - core, built.at[chip, which])
            hand(chip, which).start()
            if fused:
                spread(chip, which, core, own.at[chip, which])
            else:
                fetch(chip, which).start()

    if not fused:
        for chip in order:
            wanted(chip, lambda: begin(chip))
    else:
        begin(order[0])
    for d in range(passed):
        onward(d).start()

    def meet(chip):
        for which in range(sides):
            if not fused:
                fetch(chip, which).wait()
            hand(chip, which).wait_recv()
        for piece in range(pieces):
            if paired:
                add_into(chip, 1 - side, piece, sib.at[chip, 1 - side, cut(piece)])
                give(chip, piece).start()
            add_into(chip, side, piece, sib.at[chip, side, cut(piece)])

    def travel(chip):
        for piece in range(pieces):
            if paired:
                give(chip, piece).wait_recv()
                add_into(chip, side, piece, mate.at[chip, cut(piece)])
            if upward:

                @pl.when(z < chip)
                def _():
                    @pl.when(z > 0)
                    def _():
                        lift(chip, piece).wait_recv()
                        add_into(chip, side, piece, low_in.at[chip, cut(piece)])

                    lift(chip, piece).start()

            @pl.when(z > chip)
            def _():
                @pl.when(z < chips - 1)
                def _():
                    drop(chip, piece).wait_recv()
                    add_into(chip, side, piece, high_in.at[chip, cut(piece)])

                drop(chip, piece).start()

    for i, chip in enumerate(order):
        if fused and i + 1 < len(order):
            begin(order[i + 1])
        wanted(chip, lambda: meet(chip))
        if i >= 1:
            wanted(order[i - 1], lambda: travel(order[i - 1]))
        if extra:
            put_aside(i, chip)
    wanted(order[-1], lambda: travel(order[-1]))
    for piece in range(pieces):
        out_ref[cut(piece), :] = own.at[z, side, cut(piece)][...].astype(jnp.float32)
    for piece in range(pieces):
        if upward:

            @pl.when(z > 0)
            def _():
                lift(z, piece).wait_recv()
                out_ref[cut(piece), :] += low_in.at[z, cut(piece)][...].astype(jnp.float32)

        @pl.when(z < chips - 1)
        def _():
            drop(z, piece).wait_recv()
            out_ref[cut(piece), :] += high_in.at[z, cut(piece)][...].astype(jnp.float32)

    def finish(chip):
        for which in range(sides):
            hand(chip, which).wait_send()
        for piece in range(pieces):
            if paired:
                give(chip, piece).wait_send()
            if upward:
                pl.when(z < chip)(lambda: lift(chip, piece).wait_send())
            pl.when(z > chip)(lambda: drop(chip, piece).wait_send())

    for chip in order:
        wanted(chip, lambda: finish(chip))
    for d in range(passed):
        onward(d).wait()
    if extra:
        for which in range(sides):
            for parity in range(2):
                aside(order[-1], which, parity).wait()


def scatter_rows(partial, collective_id, upward, paired, name, slots=None, moved=(), extra=None):
    fused = slots is not None
    dma = pltpu.SemaphoreType.DMA
    pieces = 2
    if fused:
        chips, sides, _, _, width = partial.shape
        tokens = slots.shape[3] // 2
    else:
        chips, sides, _, tokens, width = partial.shape
    block = (tokens, width)
    has_extra = int(extra is not None)
    several = pltpu.VMEM((chips, sides) + block, jnp.bfloat16)
    return pl.pallas_call(
        functools.partial(scatter_kernel, chips, upward, paired, pieces, fused, len(moved), extra is not None),
        out_shape=[jax.ShapeDtypeStruct(block, jnp.float32)]
        + [jax.ShapeDtypeStruct(m.shape, m.dtype) for m in moved]
        + ([jax.ShapeDtypeStruct((chips, 2, sides) + block, jnp.bfloat16)] if has_extra else []),
        in_specs=(
            [pl.BlockSpec(memory_space=pltpu.VMEM)] * 2 if fused else [pl.BlockSpec(memory_space=pl.ANY)]
        )
        + [pl.BlockSpec(memory_space=pl.ANY)] * len(moved)
        + [pl.BlockSpec(memory_space=pltpu.VMEM)] * has_extra,
        out_specs=[pl.BlockSpec(memory_space=pltpu.VMEM)]
        + [pl.BlockSpec(memory_space=pl.ANY)] * (len(moved) + has_extra),
        scratch_shapes=([several] if fused else [])
        + ([pltpu.VMEM((2 * sides,) + block, jnp.bfloat16), dma((2 * sides,))] if has_extra else [])
        + ([dma((len(moved),))] * 2 if moved else [])
        + [
            several,
            several,
            pltpu.VMEM((chips if paired else 1,) + block, jnp.bfloat16),
            pltpu.VMEM((chips if upward else 1,) + block, jnp.bfloat16),
            pltpu.VMEM((chips,) + block, jnp.bfloat16),
            dma((chips, 2)),
            dma((chips, 2)),
            dma((chips, 2)),
        ]
        + [dma((chips, pieces))] * 6,
        compiler_params=pltpu.CompilerParams(
            collective_id=collective_id, has_side_effects=True, vmem_limit_bytes=WIDE
        ),
        cost_estimate=LONG if paired else CHEAP,
        name=name,
    )(*((partial, slots) if fused else (partial,)), *moved, *([extra] if has_extra else []))


def dense_kernel(chips, count, matrices, pieces, crossings, *refs):
    refs = list(refs)

    def take(number):
        taken = refs[:number]
        del refs[:number]
        return taken

    grads, moved, outs, landed = take(matrices), take(crossings), take(matrices), take(crossings)
    cross_send, cross_recv = take(2)
    own, sib, mates, low, final = (take(matrices) for _ in range(5))
    (load, near_send, near_recv, send, recv, low_send, low_recv, back_send, back_recv, last_send, last_recv, keep) = refs
    c, w = lax.axis_index("ctx"), lax.axis_index("wt")
    z = c // 2
    core = lax.rem(c, 2)
    near = (flip(c, 1), w)
    above = (lax.rem(c + 2, 2 * chips), w)
    below = (lax.rem(c + 2 * chips - 2, 2 * chips), w)
    dims = [1 << i for i in range(count.bit_length() - 1)]
    greet([near, above, below] + [(c, flip(w, d)) for d in dims])

    def order(j):
        return dims if pieces[j][3] else dims[::-1]

    def sends(j, stage):
        step, rest = order(j)[stage], order(j)[stage + 1 :]
        offsets = [step]
        for r in rest:
            offsets += [o ^ r for o in offsets]
        return offsets

    def cross(i):
        return remote(
            moved[i], landed[i], cross_send.at[i], cross_recv.at[i], (c, flip(w, 1))
        )

    def span(j, parity=None):
        m, first, rows, _ = pieces[j]
        if parity is None:
            return pl.ds(first, rows)
        half = grads[m].shape[1] // 2
        return pl.ds(pl.multiple_of(parity * half + first, 16), rows)

    def fetch(j):
        m = pieces[j][0]
        return pltpu.make_async_copy(grads[m].at[:, span(j, core)], own[m].at[:, span(j)], load.at[j])

    def hand(j):
        m = pieces[j][0]
        return remote(
            grads[m].at[:, span(j, 1 - core)], sib[m].at[:, span(j)], near_send.at[j], near_recv.at[j], near
        )

    def give(j, stage, o):
        m = pieces[j][0]
        step = order(j)[stage]
        return remote(
            own[m].at[flip(w, o), span(j)],
            mates[m].at[o - 1, span(j)],
            send.at[j, o - 1],
            recv.at[j, o - 1],
            (c, flip(w, step)),
        )

    def total(j):
        return own[pieces[j][0]].at[w, span(j)]

    def add(spot, other):
        spot[...] = spot[...] + other[...]

    def start(j):
        hand(j).start()
        fetch(j).start()

    def share(j):
        m = pieces[j][0]
        fetch(j).wait()
        hand(j).wait_recv()
        for o in sends(j, 0):
            add(own[m].at[flip(w, o), span(j)], sib[m].at[flip(w, o), span(j)])
            give(j, 0, o).start()
        for o in range(count):
            if o not in sends(j, 0):
                add(own[m].at[flip(w, o), span(j)], sib[m].at[flip(w, o), span(j)])

    def collect(j, stage):
        m = pieces[j][0]
        step = order(j)[stage]
        for o in sends(j, stage):
            give(j, stage, o).wait_recv()
        last = stage + 1 == len(dims)
        onward_blocks = [] if last else sends(j, stage + 1)
        for o in sends(j, stage):
            kept = o ^ step
            if kept in onward_blocks:
                add(own[m].at[flip(w, kept), span(j)], mates[m].at[o - 1, span(j)])
                give(j, stage + 1, kept).start()
        for o in sends(j, stage):
            kept = o ^ step
            if kept not in onward_blocks:
                add(own[m].at[flip(w, kept), span(j)], mates[m].at[o - 1, span(j)])

    def line(j):
        return (z, above, below) if j % 2 == 0 else (chips - 1 - z, below, above)

    def onward(j):
        m = pieces[j][0]
        return remote(total(j), low[m].at[span(j)], low_send.at[j], low_recv.at[j], line(j)[1])

    def backward(j):
        spot = final[pieces[j][0]].at[span(j)]
        return remote(spot, spot, back_send.at[j], back_recv.at[j], line(j)[2])

    def across(j, parity):
        m = pieces[j][0]
        return remote(
            final[m].at[span(j)], outs[m].at[span(j, parity)], last_send.at[j], last_recv.at[j], near
        )

    def store(j):
        m = pieces[j][0]
        return pltpu.make_async_copy(final[m].at[span(j)], outs[m].at[span(j, core)], keep.at[j])

    def accumulate(j):
        place = line(j)[0]
        m = pieces[j][0]

        @pl.when(place > 0)
        def _():
            onward(j).wait_recv()
            add(total(j), low[m].at[span(j)])

        @pl.when(place < chips - 1)
        def _():
            onward(j).start()

        @pl.when(place == chips - 1)
        def _():
            final[m][span(j), :] = total(j)[...]
            backward(j).start()
            across(j, core).start()
            store(j).start()

    def spread(j):
        place = line(j)[0]

        @pl.when(place < chips - 1)
        def _():
            backward(j).wait_recv()
            pl.when(place > 0)(lambda: backward(j).start())
            across(j, core).start()
            store(j).start()

    number = len(pieces)
    for j in range(number):
        start(j)
    last = chips - 1
    lead, gap = 2, 1
    behind = lead + gap * (len(dims) - 1)
    for t in range(number + 2 * last + behind):
        if t < number:
            share(t)
        if t == number:
            for i in range(crossings):
                cross(i).start()
        for stage in range(len(dims)):
            if 0 <= t - lead - gap * stage < number:
                collect(t - lead - gap * stage, stage)
        for hop in range(2 * last, -1, -1):
            j = t - hop - behind
            if not 0 <= j < number:
                continue
            if hop <= last:
                pl.when(line(j)[0] == hop)(lambda: accumulate(j))
            if hop > last:
                pl.when(line(j)[0] == 2 * last - hop)(lambda: spread(j))
    for i in range(crossings):
        cross(i).wait()
    for j in range(number):
        place = line(j)[0]
        hand(j).wait_send()
        for stage in range(len(dims)):
            for o in sends(j, stage):
                give(j, stage, o).wait_send()
        pl.when(place < chips - 1)(lambda: onward(j).wait_send())
        pl.when(place > 0)(lambda: backward(j).wait_send())
        across(j, core).wait_send()
        across(j, 1 - core).wait_recv()
        store(j).wait()


def reduce_dense(grads, moved):
    count = lax.axis_size("wt")
    chips = lax.axis_size("ctx") // 2
    shapes = [(g.shape[0] // count, g.shape[1]) for g in grads]
    pieces = []
    for m, (rows, _) in enumerate(shapes):
        half, width = rows // 2, shapes[m][1]
        cuts = max(n for n in range(1, 9) if half % (16 * n) == 0 and (n == 1 or half * width > 60000 * (n - 1)))
        for i in range(cuts):
            pieces.append((m, i * (rows // 2 // cuts), rows // 2 // cuts, len(pieces) % 2))
    halves = [(rows // 2, width) for rows, width in shapes]
    dma = pltpu.SemaphoreType.DMA
    one, many = dma((len(pieces),)), dma((len(pieces), count - 1))
    return pl.pallas_call(
        functools.partial(dense_kernel, chips, count, len(grads), tuple(pieces), len(moved)),
        out_shape=[jax.ShapeDtypeStruct(s, jnp.bfloat16) for s in shapes]
        + [jax.ShapeDtypeStruct(m.shape, m.dtype) for m in moved],
        in_specs=[pl.BlockSpec(memory_space=pl.ANY)] * (len(grads) + len(moved)),
        out_specs=[pl.BlockSpec(memory_space=pl.ANY)] * (len(grads) + len(moved)),
        scratch_shapes=[dma((len(moved),))] * 2
        + [pltpu.VMEM((count,) + h, jnp.bfloat16) for h in halves]
        + [pltpu.VMEM((count,) + h, jnp.bfloat16) for h in halves]
        + [pltpu.VMEM((count - 1,) + h, jnp.bfloat16) for h in halves]
        + [pltpu.VMEM(h, jnp.bfloat16) for h in halves]
        + [pltpu.VMEM(h, jnp.bfloat16) for h in halves]
        + [one, one, one, many, many, one, one, one, one, one, one, one],
        compiler_params=pltpu.CompilerParams(
            collective_id=7, has_side_effects=True, vmem_limit_bytes=WIDE
        ),
        cost_estimate=LONG,
        name="reduce_dense",
    )(*[g.reshape((count,) + s) for g, s in zip(grads, shapes)], *moved)


def dot_of(a, b, left, right):
    return lax.dot_general(
        a, b, (((left,), (right,)), ((), ())), preferred_element_type=jnp.float32
    )


def stacked_heads(ref):
    return jnp.concatenate(
        [ref[:, h * HEAD_DIM : (h + 1) * HEAD_DIM] for h in range(ref.shape[1] // HEAD_DIM)], axis=0
    )


exponent_scale = HEAD_DIM ** (-0.5) * math.log2(math.e)


def attend_kernel(place_ref, query_ref, both_ref, row_ref, column_ref, out_ref, log_ref, best, total, accum):
    tokens = query_ref.shape[0]
    group = query_ref.shape[1] // HEAD_DIM
    width = 2 * tokens
    place = place_ref[0]
    queries = stacked_heads(query_ref)
    best[...] = jnp.full_like(best, masked_value)
    total[...] = jnp.zeros_like(total)
    accum[...] = jnp.zeros_like(accum)
    query_pos = place * tokens + lax.broadcasted_iota(jnp.int32, (tokens, width), 0)
    key_pos = lax.broadcasted_iota(jnp.int32, (tokens, width), 1)

    def step(j, carry):
        span = pl.ds(pl.multiple_of(j * width, width), width)
        allowed = (key_pos + j * width <= query_pos) & (row_ref[0:1, span] == column_ref[:, 0:1])
        bias = jnp.where(allowed, 0.0, masked_value)
        scores = dot_of(queries, both_ref[span, :HEAD_DIM], 1, 1)
        scores = (scores.reshape(group, tokens, width) + bias[None]).reshape(group * tokens, width)
        newest = jnp.maximum(best[...], jnp.max(scores, axis=1, keepdims=True))
        factor = jnp.exp2((best[...] - newest) * exponent_scale)
        weights = jnp.exp2((scores - newest[:, :1]) * exponent_scale)
        total[...] = total[...] * factor + jnp.sum(weights, axis=1, keepdims=True)
        accum[...] = accum[...] * factor + dot_of(
            weights.astype(jnp.bfloat16), both_ref[span, HEAD_DIM:], 1, 0
        )
        best[...] = newest
        return carry

    lax.fori_loop(0, place // 2 + 1, step, 0)
    heads = accum[...] / total[...]
    for h in range(group):
        out_ref[:, h * HEAD_DIM : (h + 1) * HEAD_DIM] = heads[h * tokens : (h + 1) * tokens]
    logs = best[...] * exponent_scale + jnp.log2(total[...])
    log_ref[0] = jnp.transpose(logs)[:8]


def attend(place, projected, both, seg_row, seg_column):
    tokens = projected.shape[0]
    group = HEADS // KV_HEADS
    rows, span = group * tokens, both.shape[0]
    stat = pltpu.VMEM((rows, HEAD_DIM), jnp.float32)
    return pl.pallas_call(
        attend_kernel,
        grid=(KV_HEADS,),
        out_shape=(
            jax.ShapeDtypeStruct((tokens, HEADS * HEAD_DIM), jnp.float32),
            jax.ShapeDtypeStruct((KV_HEADS, 8, rows), jnp.float32),
        ),
        in_specs=[
            pl.BlockSpec(memory_space=pltpu.SMEM),
            pl.BlockSpec((tokens, group * HEAD_DIM), lambda g: (0, g)),
            pl.BlockSpec((span, 2 * HEAD_DIM), lambda g: (0, g)),
            pl.BlockSpec((1, span), lambda g: (0, 0)),
            pl.BlockSpec((tokens, 1), lambda g: (0, 0)),
        ],
        out_specs=(
            pl.BlockSpec((tokens, group * HEAD_DIM), lambda g: (0, g)),
            pl.BlockSpec((1, 8, rows), lambda g: (g, 0, 0)),
        ),
        scratch_shapes=[stat, stat, stat],
        compiler_params=pltpu.CompilerParams(vmem_limit_bytes=WIDE),
        cost_estimate=CHEAP,
        name="attend",
    )(place, projected, both, seg_row, seg_column)


def attend_back_kernel(place_ref, query_ref, both_ref, row_ref, column_ref, heads_ref, grad_ref, log_ref, grad_query_ref, grad_both_ref, accum):
    tokens = query_ref.shape[0]
    group = query_ref.shape[1] // HEAD_DIM
    width = 2 * tokens
    rows = group * tokens
    scale = HEAD_DIM ** (-0.5)
    place = place_ref[0]
    queries, grads = stacked_heads(query_ref), stacked_heads(grad_ref)
    product = grads.astype(jnp.float32) * stacked_heads(heads_ref)
    delta = jnp.sum(product, axis=1, keepdims=True)
    delta = jnp.transpose(jnp.broadcast_to(delta, (rows, HEAD_DIM)))[0:1]
    logs = log_ref[0, 0:1, :]
    accum[...] = jnp.zeros_like(accum)
    grad_both_ref[...] = jnp.zeros_like(grad_both_ref)
    query_pos = place * tokens + lax.broadcasted_iota(jnp.int32, (width, tokens), 1)
    key_pos = lax.broadcasted_iota(jnp.int32, (width, tokens), 0)

    def step(j, carry):
        span = pl.ds(pl.multiple_of(j * width, width), width)
        allowed = (key_pos + j * width <= query_pos) & (column_ref[span, 0:1] == row_ref[0:1, :])
        bias = jnp.where(allowed, 0.0, masked_value)
        bias = jnp.concatenate([bias] * group, axis=1)
        keys, values = both_ref[span, :HEAD_DIM], both_ref[span, HEAD_DIM:]
        scores = dot_of(keys, queries, 1, 1)
        probs = jnp.exp2(scores * exponent_scale + bias - logs)
        grad_probs = dot_of(values, grads, 1, 1)
        grad_scores = (probs * (grad_probs - delta)).astype(jnp.bfloat16)
        accum[...] += dot_of(grad_scores, keys, 0, 0)
        grad_both_ref[span, :HEAD_DIM] = (dot_of(grad_scores, queries, 1, 0) * scale).astype(jnp.bfloat16)
        grad_both_ref[span, HEAD_DIM:] = dot_of(probs.astype(jnp.bfloat16), grads, 1, 0).astype(jnp.bfloat16)
        return carry

    lax.fori_loop(0, place // 2 + 1, step, 0)
    grad_queries = (accum[...] * scale).astype(jnp.bfloat16)
    for h in range(group):
        grad_query_ref[:, h * HEAD_DIM : (h + 1) * HEAD_DIM] = grad_queries[h * tokens : (h + 1) * tokens]


def attend_back(place, projected, both, query_seg_row, seg_column, heads_out, grad_attended, logs):
    tokens = projected.shape[0]
    group = HEADS // KV_HEADS
    rows, span = group * tokens, both.shape[0]
    per_group = pl.BlockSpec((tokens, group * HEAD_DIM), lambda g: (0, g))
    return pl.pallas_call(
        attend_back_kernel,
        grid=(KV_HEADS,),
        out_shape=(
            jax.ShapeDtypeStruct((tokens, HEADS * HEAD_DIM), jnp.bfloat16),
            jax.ShapeDtypeStruct(both.shape, jnp.bfloat16),
        ),
        in_specs=[
            pl.BlockSpec(memory_space=pltpu.SMEM),
            per_group,
            pl.BlockSpec((span, 2 * HEAD_DIM), lambda g: (0, g)),
            pl.BlockSpec((1, tokens), lambda g: (0, 0)),
            pl.BlockSpec((span, 1), lambda g: (0, 0)),
            per_group,
            per_group,
            pl.BlockSpec((1, 8, rows), lambda g: (g, 0, 0)),
        ],
        out_specs=(per_group, pl.BlockSpec((span, 2 * HEAD_DIM), lambda g: (0, g))),
        scratch_shapes=[pltpu.VMEM((rows, HEAD_DIM), jnp.float32)],
        compiler_params=pltpu.CompilerParams(vmem_limit_bytes=WIDE),
        cost_estimate=CHEAP,
        name="attend_back",
    )(place, projected, both, query_seg_row, seg_column, heads_out, grad_attended, logs)


def pick_rows_of(slot_rows, rows_of, local, depth, tokens):
    place = lax.broadcasted_iota(jnp.int32, (depth, tokens), 0)
    total, masks = None, []
    for core in range(2):
        chosen = [slot_rows[core][e : e + 1] == place for e in range(local)]
        ones = jnp.concatenate([c.astype(jnp.float32) for c in chosen], axis=0).astype(jnp.bfloat16)
        term = jnp.dot(ones, rows_of(core), preferred_element_type=jnp.float32)
        total = term if total is None else total + term
        masks.append(chosen)
    return total, masks


def pick_grads_kernel(local, first_ref, earlier_ref, rows_ref, out_ref, scale_ref, slot_ref):
    depth = out_ref.shape[3]
    tokens = slot_ref.shape[3] // 2
    slot_rows, gate_rows, count = [], [], None
    for core in range(2):
        table = rows_ref[0, core, 0, tokens : tokens + 16, :].astype(jnp.float32)
        member, gate = [], []
        for e in range(local):
            expert = (first_ref[0] + e).astype(jnp.float32)
            found, weight = None, None
            for k in range(TOPK):
                span = slice(k * tokens, (k + 1) * tokens)
                named = table[0:1, span] == expert
                value = jnp.where(named, table[1:2, span] + table[2:3, span] + table[3:4, span], 0.0)
                mark = jnp.where(named, 1.0, 0.0)
                found = mark if k == 0 else found + mark
                weight = value if k == 0 else weight + value
            member.append(found)
            gate.append(weight)
        member = jnp.concatenate(member + [jnp.zeros((8 - local, tokens), jnp.float32)], axis=0)
        rank = jnp.dot(member.astype(jnp.bfloat16), earlier_ref[...], preferred_element_type=jnp.float32)
        if core:
            rank = rank + count
        count = jnp.sum(member, axis=1, keepdims=True)
        slots = jnp.where(member > 0.5, rank.astype(jnp.int32), -1)[:local]
        slot_ref[0, 0, :, core * tokens : (core + 1) * tokens] = slots
        slot_rows.append(slots)
        gate_rows.append(gate)
    total, masks = pick_rows_of(
        slot_rows, lambda core: rows_ref[0, core, 0, :tokens, :], local, depth, tokens
    )
    weight = None
    for core in range(2):
        gates = jnp.concatenate(
            [
                jnp.sum(jnp.where(masks[core][e], gate_rows[core][e], 0.0), axis=1, keepdims=True)
                for e in range(local)
            ],
            axis=0,
        )
        weight = gates if core == 0 else weight + gates
    scale_ref[0, 0] = jnp.broadcast_to(weight, (local * depth, 128)).reshape(local, depth, 128)
    out_ref[0, 0] = (total * weight).astype(jnp.bfloat16).reshape(local, depth, total.shape[1])


def pick_grads(rows, first, local, tokens):
    chips, _, sides, long, width = rows.shape
    depth = 2 * CAP
    earlier = jnp.arange(tokens)[:, None] < jnp.arange(tokens)[None, :]
    return pl.pallas_call(
        functools.partial(pick_grads_kernel, local),
        grid=(chips, sides),
        out_shape=(
            jax.ShapeDtypeStruct((chips, sides, local, depth, width), jnp.bfloat16),
            jax.ShapeDtypeStruct((chips, sides, local, depth, 128), jnp.float32),
            jax.ShapeDtypeStruct((chips, sides, local, 2 * tokens), jnp.int32),
        ),
        in_specs=[
            pl.BlockSpec(memory_space=pltpu.SMEM),
            pl.BlockSpec((tokens, tokens), lambda z, s: (0, 0)),
            pl.BlockSpec((1, 2, 1, long, width), lambda z, s: (z, 0, s, 0, 0)),
        ],
        out_specs=(
            pl.BlockSpec((1, 1, local, depth, width), lambda z, s: (z, s, 0, 0, 0)),
            pl.BlockSpec((1, 1, local, depth, 128), lambda z, s: (z, s, 0, 0, 0)),
            pl.BlockSpec((1, 1, local, 2 * tokens), lambda z, s: (z, s, 0, 0)),
        ),
        compiler_params=pltpu.CompilerParams(vmem_limit_bytes=WIDE),
        cost_estimate=CHEAP,
        name="pick_grads",
    )(first, earlier.astype(jnp.bfloat16), rows)


def pick_tokens_kernel(slot_ref, rows_ref, out_ref):
    local, depth = out_ref.shape[2], out_ref.shape[3]
    tokens = rows_ref.shape[3]
    slot_rows = [slot_ref[0, 0, :, core * tokens : (core + 1) * tokens] for core in range(2)]
    total, _ = pick_rows_of(slot_rows, lambda core: rows_ref[0, 0, core], local, depth, tokens)
    out_ref[0, 0] = total.astype(jnp.bfloat16).reshape(local, depth, total.shape[1])


def pick_tokens(rows, slots):
    chips, sides, local, both = slots.shape
    tokens, width = rows.shape[3:]
    depth = 2 * CAP
    return pl.pallas_call(
        pick_tokens_kernel,
        grid=(chips, sides),
        out_shape=jax.ShapeDtypeStruct((chips, sides, local, depth, width), jnp.bfloat16),
        in_specs=[
            pl.BlockSpec((1, 1, local, both), lambda z, s: (z, s, 0, 0)),
            pl.BlockSpec((1, 1, 2, tokens, width), lambda z, s: (z, s, 0, 0, 0)),
        ],
        out_specs=pl.BlockSpec((1, 1, local, depth, width), lambda z, s: (z, s, 0, 0, 0)),
        compiler_params=pltpu.CompilerParams(vmem_limit_bytes=WIDE),
        cost_estimate=CHEAP,
        name="pick_tokens",
    )(slots, rows)


def spread_kernel(apart, slot_ref, rows_ref, out_ref):
    local, depth, width = rows_ref.shape[2:]
    tokens = out_ref.shape[3]
    place = lax.broadcasted_iota(jnp.int32, (depth, tokens), 0)
    rows = rows_ref[0, 0].reshape(local * depth, width)
    for core in range(2):
        span = slice(core * tokens, (core + 1) * tokens)
        ones = jnp.concatenate(
            [(slot_ref[0, 0, e : e + 1, span] == place).astype(jnp.float32) for e in range(local)], axis=0
        ).astype(jnp.bfloat16)
        spot = out_ref.at[0, core, 0] if apart else out_ref.at[0, 0, core]
        spot[...] = lax.dot_general(
            ones, rows, (((0,), (0,)), ((), ())), preferred_element_type=jnp.float32
        ).astype(jnp.bfloat16)


def spread_rows(rows, slots, name, apart):
    chips, sides, local, both = slots.shape
    depth, width = rows.shape[3:]
    tokens = both // 2
    return pl.pallas_call(
        functools.partial(spread_kernel, apart),
        grid=(chips, sides),
        out_shape=jax.ShapeDtypeStruct(
            (chips, 2, sides, tokens, width) if apart else (chips, sides, 2, tokens, width), jnp.bfloat16
        ),
        in_specs=[
            pl.BlockSpec((1, 1, local, both), lambda z, s: (z, s, 0, 0)),
            pl.BlockSpec((1, 1, local, depth, width), lambda z, s: (z, s, 0, 0, 0)),
        ],
        out_specs=pl.BlockSpec((1, 2, 1, tokens, width), lambda z, s: (z, 0, s, 0, 0))
        if apart
        else pl.BlockSpec((1, 1, 2, tokens, width), lambda z, s: (z, s, 0, 0, 0)),
        compiler_params=pltpu.CompilerParams(vmem_limit_bytes=WIDE),
        cost_estimate=CHEAP,
        name=name,
    )(slots, rows)


def expert_kernel(blocks, x_ref, g_ref, scale_ref, *refs):
    tall_refs, down_refs = refs[:blocks], refs[blocks : 2 * blocks]
    result_ref, back_ref, *grad_refs = refs[2 * blocks : -3]
    tall_all, flat_all, flat_grad = refs[-3:]
    hops = len(grad_refs) // 3
    grad_gate_refs, grad_up_refs = grad_refs[:hops], grad_refs[hops : 2 * hops]
    grad_down_refs = grad_refs[2 * hops :]
    w = lax.axis_index("wt")
    chips, sides, _, depth, width = x_ref.shape
    rows = chips * sides * depth
    part = tall_refs[0].shape[2]
    nn, nt, tn = (((1,), (0,)), ((), ())), (((1,), (1,)), ((), ())), (((0,), (0,)), ((), ()))

    def dot(a, b, dims):
        return lax.dot_general(a, b, dims, preferred_element_type=jnp.float32)

    def columns(ref, q):
        if blocks == 1:
            return ref.at[:, :, 0]
        span = pl.ds(pl.multiple_of(flip(w, q) * part, 128), part)
        return ref.at[:, :, 0, :, span]

    def piece(ref, q):
        return columns(ref, q)[...].reshape(rows, part)

    def offset(q):
        return 0 if blocks == 1 else pl.multiple_of(flip(w, q) * part, 128)

    inner_width = tall_refs[0].shape[3]
    for q in range(blocks):
        span = pl.ds(offset(q), part)
        tall_all[span, :inner_width] = tall_refs[q][0, 0]
        tall_all[span, inner_width:] = tall_refs[q][0, 1]
        flat_all[:, span] = down_refs[q][0]
    x = x_ref[...].reshape(rows, width)
    g = g_ref[...].reshape(rows, width)
    gate = dot(x, tall_all[:, :inner_width], nn)
    up = dot(x, tall_all[:, inner_width:], nn)
    grad_inner = dot(g, flat_all[...], nt)
    sigmoid = jax.nn.sigmoid(gate)
    activated = gate * sigmoid
    inner = (activated * up).astype(jnp.bfloat16)
    grad_gate = (grad_inner * up * (sigmoid * (1.0 + gate * (1.0 - sigmoid)))).astype(jnp.bfloat16)
    grad_up = (grad_inner * activated).astype(jnp.bfloat16)
    grad_both = jnp.concatenate([grad_gate, grad_up], axis=1)
    scale = scale_ref[...].reshape(rows, 128)[:, :1]
    chunk = 512
    for first in range(0, width, chunk):
        span = slice(first, first + chunk)
        result = dot(inner, flat_all[:, span], nn) * scale
        result_ref[:, :, 0, :, span] = result.astype(jnp.bfloat16).reshape(chips, sides, depth, chunk)
        back = dot(grad_both, tall_all[span, :], nt)
        back_ref[:, :, 0, :, span] = back.astype(jnp.bfloat16).reshape(chips, sides, depth, chunk)
        flat_grad[:, span] = dot(inner, g[:, span], tn).astype(jnp.bfloat16)
    for q in range(blocks):
        more = dot(piece(x_ref, q), grad_both, tn).astype(jnp.bfloat16)
        grad_gate_refs[q // 2][q % 2, 0] = more[:, :inner_width]
        grad_up_refs[q // 2][q % 2, 0] = more[:, inner_width:]
        grad_down_refs[q // 2][q % 2, 0] = flat_grad[:, pl.ds(offset(q), part)]


def run_experts(x, g, scale, talls, downs):
    chips, sides, local, depth, width = x.shape
    blocks = len(talls)
    part, inner = talls[0].shape[2:]
    large = chips * sides * depth > 1024
    rows = pl.BlockSpec((chips, sides, 1, depth, width), lambda e: (0, 0, e, 0, 0))
    sources = pl.BlockSpec(
        (chips, sides, 1, depth, width),
        lambda e: (0, 0, e, 0, 0),
        pipeline_mode=pl.Buffered(1 if large else 2),
    )
    scales = pl.BlockSpec((chips, sides, 1, depth, 128), lambda e: (0, 0, e, 0, 0))
    tall = pl.BlockSpec((1, 2, part, inner), lambda e: (e, 0, 0, 0))
    flat = pl.BlockSpec((1, inner, part), lambda e: (e, 0, 0))
    hops, each = max(blocks // 2, 1), min(blocks, 2)
    tall_out = pl.BlockSpec((each, 1, part, inner), lambda e: (0, e, 0, 0))
    flat_out = pl.BlockSpec((each, 1, inner, part), lambda e: (0, e, 0, 0))
    return pl.pallas_call(
        functools.partial(expert_kernel, blocks),
        grid=(local,),
        out_shape=(
            jax.ShapeDtypeStruct(x.shape, jnp.bfloat16),
            jax.ShapeDtypeStruct(x.shape, jnp.bfloat16),
            *[jax.ShapeDtypeStruct((each, local, part, inner), jnp.bfloat16)] * (2 * hops),
            *[jax.ShapeDtypeStruct((each, local, inner, part), jnp.bfloat16)] * hops,
        ),
        in_specs=[sources, sources, scales] + [tall] * blocks + [flat] * blocks,
        out_specs=(rows, rows) + (tall_out,) * (2 * hops) + (flat_out,) * hops,
        scratch_shapes=[
            pltpu.VMEM((width, 2 * inner), jnp.bfloat16),
            pltpu.VMEM((inner, width), jnp.bfloat16),
            pltpu.VMEM((inner, width), jnp.bfloat16),
        ],
        compiler_params=pltpu.CompilerParams(vmem_limit_bytes=60 * 2**20),
        cost_estimate=CHEAP,
        name="experts",
    )(x, g, scale, *talls, *downs)


def place_kernel(arrivals, side_ref, *refs):
    own, other, more, outs = refs[:3], refs[3:6], refs[6 : 6 + 3 * arrivals], refs[6 + 3 * arrivals :]
    mine = pl.program_id(0) == side_ref[0]

    @pl.when(mine)
    def _():
        for i in range(3):
            value = own[i][0, 0].astype(jnp.float32)
            for m in more[i * arrivals : (i + 1) * arrivals]:
                value = value + m[0, 0].astype(jnp.float32)
            outs[i][0] = value

    @pl.when(jnp.logical_not(mine))
    def _():
        for i in range(3):
            outs[i][0] = other[i][0].astype(jnp.float32)


def place_experts(side, own, more, other):
    local = other[0].shape[0]
    arrivals = len(more[0])
    shapes = [o.shape[1:] for o in other]
    paired = [pl.BlockSpec((1, 1) + s, lambda h, e: (0, e, 0, 0)) for s in shapes]
    single = [pl.BlockSpec((1,) + s, lambda h, e: (e, 0, 0)) for s in shapes]
    return pl.pallas_call(
        functools.partial(place_kernel, arrivals),
        grid=(2, local),
        out_shape=[jax.ShapeDtypeStruct((2 * local,) + s, jnp.float32) for s in shapes],
        in_specs=[pl.BlockSpec(memory_space=pltpu.SMEM)]
        + paired
        + single
        + [p for p in paired for _ in range(arrivals)],
        out_specs=[pl.BlockSpec((1,) + s, lambda h, e: (h * local + e, 0, 0)) for s in shapes],
        compiler_params=pltpu.CompilerParams(vmem_limit_bytes=WIDE),
        cost_estimate=CHEAP,
        name="place_experts",
    )(side, *own, *other, *[m for group in more for m in group])


def swap_pairs(value, axis, distance):
    count = lax.axis_size(axis)
    return lax.ppermute(value, axis, [(i, i ^ distance) for i in range(count)])


def own_and_other(stacked, mine):
    return (
        lax.dynamic_index_in_dim(stacked, mine, 0, keepdims=False),
        lax.dynamic_index_in_dim(stacked, 1 - mine, 0, keepdims=False),
    )


def collect_expert(shard, side, pairs):
    local = shard.shape[0]
    kept, given = own_and_other(shard.reshape((2, local // 2) + shard.shape[1:]), side)
    return kept, swap_pairs(given, "wt", 1), [swap_pairs(kept, "wt", 2 * d) for d in range(1, pairs)]


def settle_blocks(blocks, index, axis):
    stacked = jnp.stack(blocks)
    return jnp.concatenate(
        [
            lax.dynamic_index_in_dim(stacked, jnp.bitwise_xor(j, index), 0, False)
            for j in range(len(blocks))
        ],
        axis=axis,
    )


def split_blocks(whole, index, count, axis):
    parts = jnp.stack(jnp.split(whole, count, axis=axis))
    return jnp.stack(
        [
            lax.dynamic_index_in_dim(parts, jnp.bitwise_xor(q, index), 0, False)
            for q in range(count)
        ]
    )


def body(
    hidden,
    segment_ids,
    routes,
    gates,
    cotangent,
    norm_one_gain,
    w_query,
    w_key,
    w_value,
    w_out,
    norm_two_gain,
    shared_gate,
    shared_up,
    shared_down,
    expert_gate,
    expert_up,
    expert_down,
):
    wt_index = lax.axis_index("wt")
    wt_count = lax.axis_size("wt")
    ctx_count = lax.axis_size("ctx")
    chips = ctx_count // 2
    pairs = wt_count // 2
    tokens, width_model = hidden.shape[1:]
    wide, kv_width = w_query.shape[1], w_key.shape[1]
    shared_width = shared_gate.shape[1]
    gates_here = gates[0]
    gate_high = gates_here.astype(jnp.bfloat16)
    gate_rest = gates_here - gate_high.astype(jnp.float32)
    gate_middle = gate_rest.astype(jnp.bfloat16)
    gate_low = (gate_rest - gate_middle.astype(jnp.float32)).astype(jnp.bfloat16)
    table = jnp.concatenate(
        [routes[0].astype(jnp.bfloat16), gate_high, gate_middle, gate_low], axis=1
    )
    grad_rows = cotangent[0]
    depth = norm_one_gain.shape[0]
    extra_rows = 16
    packed = jnp.pad(
        jnp.swapaxes(table, 0, 1).reshape(4, width_model), ((0, extra_rows - 4), (0, 0))
    )
    extended = jnp.concatenate([grad_rows, packed], axis=0)
    gain_pair = jnp.concatenate(
        [norm_one_gain[None], norm_two_gain[None], jnp.zeros((62, depth), jnp.bfloat16)]
    )
    query_weight, key_weight, value_weight, gains, grad_pair, zero = gather_weights(
        (w_query, w_key, w_value, gain_pair), (extended,)
    )
    query_weight = query_weight.reshape(-1, wide)
    key_weight = key_weight.reshape(-1, kv_width)
    value_weight = value_weight.reshape(-1, kv_width)
    zero = zero[0, 0]
    side = lax.rem(wt_index, 2)
    later = side + zero
    collected = [
        collect_expert(jnp.stack([expert_gate, expert_up], axis=1), later, pairs),
        collect_expert(expert_down, later, pairs),
    ]
    gain_one, gain_two = gains[:, 0].reshape(-1), gains[:, 1].reshape(-1)
    local = expert_gate.shape[0] // 2
    first_expert = (lax.axis_index("ctx") * 2 + side) * local

    inputs = hidden[0].astype(jnp.float32)
    offset = lax.axis_index("ctx") * tokens
    seg_all = segment_ids[0]
    query_seg = lax.dynamic_slice_in_dim(seg_all, offset, tokens)
    scale_one = inverse_rms(inputs)
    gain_one_full = gain_one.astype(jnp.float32)
    normed = (inputs * scale_one * gain_one_full).astype(jnp.bfloat16)

    def project(weight):
        return jnp.dot(normed, weight, preferred_element_type=jnp.float32).astype(jnp.bfloat16)

    queries = project(query_weight)
    fresh = jnp.stack(
        [
            project(key_weight).reshape(tokens, KV_HEADS, HEAD_DIM),
            project(value_weight).reshape(tokens, KV_HEADS, HEAD_DIM),
        ],
        axis=2,
    ).reshape(tokens, 2 * kv_width)
    both, out_weight, both_weight, down_weight, zero = gather_rows(
        fresh,
        2,
        False,
        False,
        "gather_keys",
        (w_out, jnp.concatenate([shared_gate, shared_up], axis=1), shared_down),
    )
    out_weight = out_weight.reshape(-1, out_weight.shape[2])
    both_weight = both_weight.reshape(-1, both_weight.shape[2])
    down_weight = down_weight.reshape(-1, down_weight.shape[2])
    both = both.reshape(-1, 2 * kv_width)

    grad_pair, both = lax.optimization_barrier((grad_pair, both))
    all_grads = lax.all_gather(grad_pair, "ctx", axis=0).reshape(
        chips, 2, 2, tokens + extra_rows, width_model
    )

    place = lax.axis_index("ctx").astype(jnp.int32).reshape(1)
    seg_row, seg_column = seg_all[None, :], seg_all[:, None]
    attended_full, logs = attend(place, queries, both, seg_row, query_seg[:, None])
    attended = attended_full.astype(jnp.bfloat16)
    middle = inputs + jnp.dot(attended, out_weight, preferred_element_type=jnp.float32)
    scale_two = inverse_rms(middle)
    gain_two_full = gain_two.astype(jnp.float32)
    normed_two = (middle * scale_two * gain_two_full).astype(jnp.bfloat16)

    shared_parts = jnp.dot(normed_two, both_weight, preferred_element_type=jnp.float32)
    shared_gate_part, shared_up_part = shared_parts[:, :shared_width], shared_parts[:, shared_width:]
    shared_inner = (jax.nn.silu(shared_gate_part) * shared_up_part).astype(jnp.bfloat16)
    shared_result = jnp.dot(shared_inner, down_weight, preferred_element_type=jnp.float32)
    grad_out = grad_rows.astype(jnp.float32)
    grad_shared_down = jnp.einsum(
        "tf,td->fd", shared_inner, grad_rows, preferred_element_type=jnp.float32
    )
    grad_shared_inner = jnp.einsum(
        "td,fd->tf", grad_rows, down_weight, preferred_element_type=jnp.float32
    )
    grad_shared_gate_part = (
        grad_shared_inner * shared_up_part * silu_slope(shared_gate_part)
    ).astype(jnp.bfloat16)
    grad_shared_up_part = (grad_shared_inner * jax.nn.silu(shared_gate_part)).astype(jnp.bfloat16)
    grad_shared_parts = jnp.concatenate([grad_shared_gate_part, grad_shared_up_part], axis=1)
    grad_shared_both = jnp.einsum(
        "td,tf->df", normed_two, grad_shared_parts, preferred_element_type=jnp.float32
    )
    grad_shared_rows = jnp.einsum(
        "tf,df->td", grad_shared_parts, both_weight, preferred_element_type=jnp.float32
    )
    grad_shared_both = grad_shared_both.astype(jnp.bfloat16)
    grad_shared_down = grad_shared_down.astype(jnp.bfloat16)
    normed_two, collected, shared_result, grad_shared_both, grad_shared_down, grad_shared_rows = (
        lax.optimization_barrier(
            (normed_two, collected, shared_result, grad_shared_both, grad_shared_down, grad_shared_rows)
        )
    )
    all_rows, *landed, zero = gather_rows(
        normed_two, 3, True, True, "gather_tokens", (), [c[1] for c in collected]
    )

    def blocks_of(i):
        kept, paired, straight = collected[i]
        blocks = [kept, paired]
        for d in range(pairs - 1):
            blocks += [straight[d], landed[i * (pairs - 1) + d]]
        return blocks

    tall_blocks, down_blocks = blocks_of(0), blocks_of(1)
    grad_received, row_gates, slots = pick_grads(
        all_grads, first_expert.astype(jnp.int32).reshape(1), local, tokens
    )
    received_rows = pick_tokens(all_rows, slots)
    if down_blocks[0].shape[2] % 128:
        results, backs, grads_gate, grads_up, grads_down = run_experts(
            received_rows,
            grad_received,
            row_gates,
            [settle_blocks(tall_blocks, wt_index, 2)],
            [settle_blocks(down_blocks, wt_index, 2)],
        )
        wholes = [
            split_blocks(grads_gate[0], wt_index, wt_count, 1),
            split_blocks(grads_up[0], wt_index, wt_count, 1),
            split_blocks(grads_down[0], wt_index, wt_count, 2),
        ]
        hop_grads = [[g[2 * d : 2 * d + 2] for d in range(pairs)] for g in wholes]
    else:
        results, backs, *rest = run_experts(
            received_rows, grad_received, row_gates, tall_blocks, down_blocks
        )
        hop_grads = [rest[i * pairs : (i + 1) * pairs] for i in range(3)]
    later_arrived = [[swap_pairs(g[d], "wt", 2 * d) for d in range(1, pairs)] for g in hop_grads[1:]]
    if chips > 4:
        routed_grad, *gate_arrived = scatter_rows(
            spread_rows(backs, slots, "spread_grads", False),
            5,
            True,
            True,
            "scatter_grads",
            moved=hop_grads[0][1:],
        )
        routed_grad, results = lax.optimization_barrier((routed_grad, results))
        spread = spread_rows(results, slots, "spread_results", True)
    else:
        routed_grad, *gate_arrived, spread = scatter_rows(
            backs, 5, True, True, "scatter_grads", slots, hop_grads[0][1:], results
        )
    partial = lax.psum_scatter(
        spread.reshape(ctx_count, 2, tokens, width_model),
        "ctx",
        scatter_dimension=0,
        tiled=True,
    )[0]

    def across(own, more):
        total = own[1].astype(jnp.float32)
        for m in more:
            total = total + m[1].astype(jnp.float32)
        return total.astype(jnp.bfloat16)

    gate_other = swap_pairs(across(hop_grads[0][0], gate_arrived), "wt", 1)
    grad_normed_two = grad_shared_rows + routed_grad
    grad_gain_two = jnp.sum(grad_normed_two * middle * scale_two, axis=0)
    scaled_two = grad_normed_two * gain_two_full
    grad_middle = (
        grad_out
        + scale_two * scaled_two
        - middle * scale_two**3 * jnp.mean(scaled_two * middle, axis=-1, keepdims=True)
    )
    grad_branch = grad_middle.astype(jnp.bfloat16)
    grad_out_weight = jnp.einsum(
        "tq,td->qd", attended, grad_branch, preferred_element_type=jnp.float32
    )
    grad_attended = jnp.einsum(
        "td,qd->tq", grad_branch, out_weight, preferred_element_type=jnp.float32
    ).astype(jnp.bfloat16)
    grad_queries, grad_parts = attend_back(
        place, queries, both, query_seg[None, :], seg_column, attended_full, grad_attended, logs
    )
    (grad_both,) = scatter_rows(
        grad_parts.reshape(chips, 1, 2, tokens, 2 * kv_width),
        6,
        False,
        False,
        "scatter_keys",
    )
    grad_both = grad_both.astype(jnp.bfloat16)
    grad_both, gate_other, up_arrived = lax.optimization_barrier(
        (grad_both, gate_other, later_arrived[0])
    )
    up_given = across(hop_grads[1][0], up_arrived)
    grad_both = grad_both.reshape(tokens, KV_HEADS, 2, HEAD_DIM)
    grad_keys = grad_both[:, :, 0].reshape(tokens, kv_width)
    grad_values = grad_both[:, :, 1].reshape(tokens, kv_width)

    def weight_grad(grad):
        return jnp.einsum("tc,tq->cq", normed, grad, preferred_element_type=jnp.float32).astype(
            jnp.bfloat16
        )

    def input_grad(grad, weight):
        return jnp.einsum("tq,cq->tc", grad, weight, preferred_element_type=jnp.float32)

    grad_normed = (
        input_grad(grad_queries, query_weight)
        + input_grad(grad_keys, key_weight)
        + input_grad(grad_values, value_weight)
    )
    grad_gain_one = jnp.sum(grad_normed * inputs * scale_one, axis=0)
    scaled_one = grad_normed * gain_one_full
    grad_inputs = (
        grad_middle
        + scale_one * scaled_one
        - inputs * scale_one**3 * jnp.mean(scaled_one * inputs, axis=-1, keepdims=True)
    )

    gain_grads = jnp.stack([grad_gain_one, grad_gain_two]).reshape(2, wt_count, 1, depth)
    gain_grads = jnp.pad(gain_grads.astype(jnp.bfloat16), ((0, 0), (0, 0), (0, 15), (0, 0)))
    gain_grads = jnp.swapaxes(gain_grads, 0, 1).reshape(wt_count * 32, depth)
    dense_grads = [
        weight_grad(grad_queries),
        grad_shared_both,
        grad_out_weight.astype(jnp.bfloat16),
        grad_shared_down,
        weight_grad(grad_keys),
        weight_grad(grad_values),
        gain_grads,
    ]
    dense_grads, down_arrived = lax.optimization_barrier((dense_grads, later_arrived[1]))
    arrived = [gate_arrived, up_arrived, down_arrived]
    down_given = across(hop_grads[2][0], down_arrived)
    *totals, up_other, down_other = reduce_dense(dense_grads, [up_given, down_given])
    totals, partial = lax.optimization_barrier((totals, partial))
    others = [gate_other, up_other, down_other]
    kept, given = own_and_other(partial, side)
    crossing = swap_pairs(given, "wt", 1)
    routed = kept.astype(jnp.float32) + crossing.astype(jnp.float32)
    output = (middle + shared_result + routed).astype(jnp.bfloat16)
    sum_experts_gate, sum_experts_up, sum_experts_down = place_experts(
        side.astype(jnp.int32).reshape(1), [g[0] for g in hop_grads], arrived, others
    )
    final_query, final_shared, final_out, final_down, final_key, final_value, final_gains = [
        total.astype(jnp.float32) for total in totals
    ]
    final_gate, final_up = final_shared[:, :shared_width], final_shared[:, shared_width:]
    final_gain_one, final_gain_two = final_gains[0], final_gains[16]
    return (
        output[None],
        grad_inputs[None],
        final_gain_one,
        final_query,
        final_key,
        final_value,
        final_out,
        final_gain_two,
        final_gate,
        final_up,
        final_down,
        sum_experts_gate,
        sum_experts_up,
        sum_experts_down,
    )


def solution(mesh):
    placed = (
        P("wt", "ctx", None),
        P("wt", None),
        P("wt", "ctx", None),
        P("wt", "ctx", None),
        P("wt", "ctx", None),
        P("wt"),
        P("wt", None),
        P("wt", None),
        P("wt", None),
        P("wt", None),
        P("wt"),
        P("wt", None),
        P("wt", None),
        P("wt", None),
        P("ctx", "wt", None),
        P("ctx", "wt", None),
        P("ctx", None, "wt"),
    )
    return jax.shard_map(
        body,
        mesh=mesh,
        in_specs=placed,
        out_specs=(
            P("wt", "ctx", None),
            P("wt", "ctx", None),
            P("wt"),
            P("wt", None),
            P("wt", None),
            P("wt", None),
            P("wt", None),
            P("wt"),
            P("wt", None),
            P("wt", None),
            P("wt", None),
            P("ctx", "wt", None),
            P("ctx", "wt", None),
            P("ctx", None, "wt"),
        ),
        check_vma=False,
    )
```
